32 devices in a mesh: fsdp: 16 (over z, y, core), ns: 2 (over x).
Axes of the slice: x: 2, y: 2, z: 4, core: 2. Of those that a mesh axis runs over, the one named last changes fastest.
Arguments:
- patches: bfloat16 [32, 256, 768], P(('fsdp', 'ns')), may hold values from -6 to 6
- pad_mask: int32 [32, 256], P(('fsdp', 'ns')), may hold values from 0 to 1, as said below
- labels: int32 [32], P(('fsdp', 'ns')), may hold values from 0 to 999
- loss_weights: int32 [32], P(('fsdp', 'ns')), may hold values from 1 to 15
- class_emb: bfloat16 [1000, 512], replicated, may hold values from -6 to 6
- layer_mats: float32 [2, 9216, 768], P(None, 'fsdp')
- layer_zero: float32 [2, 9216, 768], P(None, 'fsdp')
- layer_ema: float32 [2, 9216, 768], P(None, 'fsdp')
- layer_momentum: float32 [2, 9216, 768], P(None, 'fsdp'), may hold values from -3.8146973e-06 to 3.8146973e-06
- row_params: float32 [1564, 768], P(None, 'fsdp')
- row_zero: float32 [1564, 768], P(None, 'fsdp')
- row_ema: float32 [1564, 768], P(None, 'fsdp')
- row_first: float32 [1564, 768], P(None, 'fsdp'), may hold values from -4.172325e-07 to 4.172325e-07
- row_second: float32 [1564, 768], P(None, 'fsdp'), may hold values from 1.3283907e-15 to 5.3135626e-15
Outputs:
- loss_sum: float32 [], replicated
- weight_sum: float32 [], replicated
- grad_norm: float32 [], replicated
- new_mats: float32 [2, 9216, 768], P(None, 'fsdp')
- new_momentum: float32 [2, 9216, 768], P(None, 'fsdp')
- ema_mats: float32 [2, 9216, 768], P(None, 'fsdp')
- mixed_mats: float32 [2, 9216, 768], P(None, 'fsdp')
- new_rows: float32 [1564, 768], P(None, 'fsdp')
- new_first: float32 [1564, 768], P(None, 'fsdp')
- new_second: float32 [1564, 768], P(None, 'fsdp')
- ema_rows: float32 [1564, 768], P(None, 'fsdp')
- mixed_rows: float32 [1564, 768], P(None, 'fsdp')
- down_bias_grad: float32 [2, 768], P(None, 'fsdp')
The draws below stay inside these ranges and needn't reach their ends.
Inputs may be any that keep to these rules, and one draw needn't show every extreme that they name: `pad_mask`: in each image the ones are the first 128 to 256 slots; image 0 has all 256.
All inputs are finite; a program needn't handle non-finite values.
Results may differ from the reference program's by a relative error of at most 0.015.
Values may be sent and summed in bfloat16 or wider, within the bound.
A program may use at most 256 MiB of HBM per device.

```python
import math
import jax
import jax.numpy as jnp
from jax import lax

D = 768
HEADS = 12
HDIM = 64
FF = 3072
PIX = 768
EMB = 512
CLASSES = 1000
SEQ = 256
LAYERS = 2
NS_STEPS = 5
STEPS_DONE = 10
IMG_DEV = 1
IMAGES = 32
WCOLS = 9216
COLS_DEV = 576
ROWS = 1564
N_FSDP = 16
N_NS = 2


def layer_law(key):
    columns = 4 * D + 2 * FF
    noise = jax.random.normal(key, (LAYERS, columns, D), jnp.float32)
    column_id = jnp.arange(columns)
    scale = jnp.where(column_id < 3 * D, D ** (-0.5), jnp.where(column_id < 4 * D, 3.0 * D ** (-0.5), jnp.where(column_id < 4 * D + FF, D ** (-0.5), FF ** (-0.5))))
    return noise * scale[None, :, None]


def row_law(key, rising):
    key_gain, key_noise = jax.random.split(key)
    lanes = jnp.arange(D, dtype=jnp.float32) / (D - 1)
    gains = (0.6 + rising * lanes)[None, :] * jax.random.uniform(key_gain, (ROWS, D), jnp.float32, 0.85, 1.15)
    noise = jax.random.normal(key_noise, (ROWS, D), jnp.float32)
    row_id = jnp.arange(ROWS)[:, None]
    front = PIX + EMB + SEQ
    inner = (row_id - front - 4) % 12
    is_gain = (row_id == front) | (row_id == front + 2) | (row_id >= front + 4) & ((inner == 0) | (inner == 5))
    scale = jnp.where(row_id < PIX, PIX ** (-0.5), jnp.where(row_id < PIX + EMB, D ** (-0.5), jnp.where(row_id < front, 0.5, 0.3)))
    return jnp.where(is_gain, gains, scale * noise)


def draw_layer_mats(key, part):
    key = jax.random.fold_in(key, 1)
    return layer_law(key)


def draw_layer_zero(key, part):
    key = jax.random.fold_in(key, 2)
    return layer_law(key)


def draw_layer_ema(key, part):
    key = jax.random.fold_in(key, 3)
    return layer_law(key)


def draw_row_params(key, part):
    key = jax.random.fold_in(key, 4)
    return row_law(key, 1.2)


def draw_row_zero(key, part):
    key = jax.random.fold_in(key, 5)
    return row_law(key, 1.2)


def draw_row_ema(key, part):
    key = jax.random.fold_in(key, 6)
    return row_law(key, 1.2)


def draw_pad_mask(key, part):
    key = jax.random.fold_in(key, 11)
    lengths = jax.random.randint(key, (IMAGES,), SEQ // 2, SEQ + 1)
    lengths = lengths.at[0].set(SEQ)
    position = jnp.arange(SEQ)[None, :]
    return (position < lengths[:, None]).astype(jnp.int32)


def draw_loss_weights(key, part):
    key = jax.random.fold_in(key, 12)
    image_id = jnp.arange(IMAGES)
    device_id = image_id // IMG_DEV
    column_id = device_id // N_NS
    lane_id = device_id % N_NS
    ceiling = 1 + 5 * column_id // N_FSDP
    drawn = jax.random.randint(key, (IMAGES,), 1, ceiling + 1)
    drawn = drawn.at[IMAGES - 1].set(5)
    return (drawn * (1 + 2 * lane_id)).astype(jnp.int32)


def set_ends(values, key, low, top_value):
    index_at = [jax.random.randint(jax.random.fold_in(key, axis), (), 0, length) for axis, length in enumerate(values.shape)]
    longest = values.shape.index(max(values.shape))
    next_to = index_at[:longest] + [(index_at[longest] + 1) % values.shape[longest]] + index_at[longest + 1:]
    return values.at[tuple(index_at)].set(low).at[tuple(next_to)].set(top_value)


def levels(stream_key, extent, pieces, low, high):
    loudness = 1.0
    for dim, shards_of in pieces:
        heights = jax.random.uniform(jax.random.fold_in(jax.random.fold_in(stream_key, 6), dim), (shards_of,), jnp.float32, low / len(pieces), high / len(pieces))
        loudness = loudness * jnp.repeat(jnp.exp(heights), extent[dim] // shards_of).reshape((-1,) + (1,) * (len(extent) - 1 - dim))
    return loudness


def gaussian(key, shape, deviation, bound, cuts=(), kind=jnp.bfloat16):
    factor_of = levels(key, shape, cuts, -0.22, 0.18) if cuts else 1.0
    array = jax.random.normal(key, shape, jnp.float32) * deviation * factor_of
    return jnp.minimum(jnp.maximum(array, -bound), bound).astype(kind)


def setup_inputs(seed: int = 0) -> dict:
    key_list = jax.random.split(jax.random.key(seed), 15)
    patches = gaussian(key_list[0], (IMAGES, SEQ, PIX), 1.0, 6.0, ((0, 32),))
    pad_mask = draw_pad_mask(jax.random.fold_in(key_list[14], 71), 0)
    labels = set_ends(jax.random.randint(key_list[2], (IMAGES,), 0, CLASSES), jax.random.fold_in(key_list[2], 1), 0, CLASSES - 1).astype(jnp.int32)
    loss_weights = draw_loss_weights(jax.random.fold_in(key_list[14], 71), 0)
    class_emb = gaussian(key_list[4], (CLASSES, EMB), 1.0, 6.0)
    layer_mats = draw_layer_mats(jax.random.fold_in(key_list[14], 71), 0)
    layer_zero = draw_layer_zero(jax.random.fold_in(key_list[14], 71), 0)
    layer_ema = draw_layer_ema(jax.random.fold_in(key_list[14], 71), 0)
    layer_momentum = gaussian(key_list[8], (LAYERS, WCOLS, D), (0.001 * (LAYERS * D * WCOLS + ROWS * D) ** -0.5), 3.814697265625e-06, ((1, 16),), jnp.float32)
    row_params = draw_row_params(jax.random.fold_in(key_list[14], 71), 0)
    row_zero = draw_row_zero(jax.random.fold_in(key_list[14], 71), 0)
    row_ema = draw_row_ema(jax.random.fold_in(key_list[14], 71), 0)
    row_first = gaussian(key_list[12], (ROWS, D), (0.111 * 0.001 * (LAYERS * D * WCOLS + ROWS * D) ** -0.5), 4.172325134277344e-07, ((1, 16),), jnp.float32)
    row_second = jnp.clip(jnp.exp(math.log(5.313562615485946e-15) - 1.3862944 * jax.random.uniform(key_list[13], (ROWS, D), jnp.float32) ** levels(key_list[13], (ROWS, D), ((1, 16),), -0.2, 0.2)), 1.3283906538714865e-15, 5.313562615485946e-15)
    return dict(patches=patches, pad_mask=pad_mask, labels=labels, loss_weights=loss_weights, class_emb=class_emb, layer_mats=layer_mats, layer_zero=layer_zero, layer_ema=layer_ema, layer_momentum=layer_momentum, row_params=row_params, row_zero=row_zero, row_ema=row_ema, row_first=row_first, row_second=row_second)


HIGHEST = lax.Precision.HIGHEST
norm_epsilon = 1e-05
unit_epsilon = 1e-06
logit_scale = 50.0
clip_bound = 0.001
momentum_decay = 0.95
muon_rate = 0.05
weight_decay = 0.05
adam_rate = 0.2
first_decay = 0.9
second_decay = 0.98
adam_floor = 1e-08
ema_decay = 0.9
mix_share = 0.5
coeff_linear = 3.4445
coeff_cubic = -4.775
coeff_quintic = 2.0315

@jax.custom_vjp
def low(v):
    return lax.optimization_barrier(v.astype(jnp.bfloat16)).astype(jnp.float32)

@jax.custom_vjp
def low_back(v):
    return v

def low_keep(v):
    return (low(v), None)

def low_pass(kept, grad):
    return (grad,)

def back_keep(v):
    return (v, None)

def back_low(kept, grad):
    return (low(grad),)
low.defvjp(low_keep, low_pass)
low_back.defvjp(back_keep, back_low)

def matmul(left, right):
    return jnp.dot(left, right, precision=HIGHEST)

def layer_norm(inputs, gain, shift):
    center = inputs - lax.optimization_barrier(jnp.mean(inputs, -1, keepdims=True))
    variance = lax.optimization_barrier(jnp.mean(center * center, -1, keepdims=True))
    return center * lax.rsqrt(variance + norm_epsilon) * gain + shift

def block(resid, weight_tensors, vector, valid_mask):
    groups = resid.shape[0]
    normed = low(layer_norm(resid, vector[0], vector[1]))
    bias = jnp.concatenate([vector[2], jnp.zeros((D,), jnp.float32), vector[3]])
    project = low(low_back(jnp.einsum('gsd,ed->gse', normed, weight_tensors[:3 * D], precision=HIGHEST) + bias))
    parts = project.reshape(groups, SEQ, 3, HEADS, HDIM)
    scores = low_back(jnp.einsum('gqhd,gkhd->ghqk', parts[:, :, 0], parts[:, :, 1], precision=HIGHEST) * HDIM ** (-0.5))
    scores = jnp.where(valid_mask[:, None, None, :] > 0, scores, -1000000000.0)
    probs = jax.nn.softmax(scores, -1)
    context = jnp.einsum('ghqk,gkhd->gqhd', low(probs), parts[:, :, 2], precision=HIGHEST)
    context = low(low_back(context)).reshape(groups, SEQ, D)
    attn = low_back(jnp.einsum('gsd,ed->gse', context, weight_tensors[3 * D:4 * D], precision=HIGHEST) + vector[4])
    mixed = resid + attn
    normed_two = low(layer_norm(mixed, vector[5], vector[6]))
    hidden_pre = low_back(jnp.einsum('gsd,fd->gsf', normed_two, weight_tensors[4 * D:4 * D + FF], precision=HIGHEST) + vector[8:12].reshape(FF))
    hidden = low(hidden_pre * jax.nn.sigmoid(1.702 * hidden_pre))
    output = low_back(jnp.einsum('gsf,fd->gsd', hidden, weight_tensors[4 * D + FF:], precision=HIGHEST) + vector[7])
    return mixed + output

def group_loss(mats, rows, class_unit, patches, valid_mask, labels, weight_tensors):
    front = PIX + EMB + SEQ
    patch_weight = rows[:PIX]
    proj_rows = rows[PIX:PIX + EMB]
    position = rows[PIX + EMB:front]
    head_vec = rows[front:front + 4]
    layer_vector_params = rows[front + 4:].reshape(LAYERS, 12, D)
    embedded = low_back(jnp.einsum('gsp,pd->gsd', patches, patch_weight, precision=HIGHEST)) + position
    resid = layer_norm(embedded, head_vec[0], head_vec[1])
    for layer_number in range(LAYERS):
        resid = block(resid, mats[layer_number], layer_vector_params[layer_number], valid_mask)
    counts = lax.optimization_barrier(jnp.sum(valid_mask, -1, keepdims=True))
    pooled = lax.optimization_barrier(jnp.sum(resid * valid_mask[..., None], 1)) / counts
    normed = low(layer_norm(pooled, head_vec[2], head_vec[3]))
    feature = matmul(normed, proj_rows.T)
    unit_feat = low(feature * lax.rsqrt(lax.optimization_barrier(jnp.sum(feature * feature, -1, keepdims=True)) + unit_epsilon))
    logits = logit_scale * matmul(unit_feat, class_unit.T)
    log_norm = jax.nn.logsumexp(logits, -1)
    picked = lax.optimization_barrier(jnp.sum(jnp.where(jnp.arange(CLASSES)[None, :] == labels[:, None], logits, 0.0), -1))
    return jnp.sum(weight_tensors * (log_norm - picked))

def orthogonalize(momentum):
    blocks = momentum.reshape(LAYERS, N_FSDP, COLS_DEV, D)
    gram = jnp.einsum('lncd,lned->lnce', blocks, blocks, precision=HIGHEST)
    frob = jnp.sqrt(jnp.trace(gram, axis1=2, axis2=3))[..., None, None] + 1e-07
    blocks = blocks / frob
    gram = gram / (frob * frob)
    for turn in range(NS_STEPS):
        poly = coeff_cubic * gram + coeff_quintic * jnp.einsum('lnce,lnef->lncf', gram, gram, precision=HIGHEST)
        blocks = coeff_linear * blocks + jnp.einsum('lnce,lned->lncd', poly, blocks, precision=HIGHEST)
        if turn + 1 < NS_STEPS:
            gram = jnp.einsum('lncd,lned->lnce', blocks, blocks, precision=HIGHEST)
    return blocks.reshape(LAYERS, WCOLS, D)

def reference(patches, pad_mask, labels, loss_weights, class_emb, layer_mats, layer_zero, layer_ema, layer_momentum, row_params, row_zero, row_ema, row_first, row_second):
    valid_mask = pad_mask.astype(jnp.float32)
    weight_tensors = loss_weights.astype(jnp.float32)
    weight_sum = jnp.sum(weight_tensors)
    classes = class_emb.astype(jnp.float32)
    class_unit = low(classes * lax.rsqrt(lax.optimization_barrier(jnp.sum(classes * classes, -1, keepdims=True)) + unit_epsilon))
    group = math.gcd(IMAGES, max(1, 4096 // SEQ))
    count = IMAGES // group
    stacked = (patches.astype(jnp.float32).reshape(count, group, SEQ, PIX), valid_mask.reshape(count, group, SEQ), labels.reshape(count, group), weight_tensors.reshape(count, group))

    def total(mats, rows):
        mats_low = low(mats)
        rows_low = low(rows)

        def scan_step(carry, item):
            return (carry + group_loss(mats_low, rows_low, class_unit, *item), None)
        result, _ = lax.scan(jax.checkpoint(scan_step), jnp.zeros((), jnp.float32), stacked)
        return result
    loss_sum, pull_back = jax.vjp(total, layer_mats, row_params)
    grad_mats, grad_rows = pull_back(jnp.ones((), jnp.float32) / weight_sum)
    grad_norm = jnp.sqrt(jnp.sum(grad_mats * grad_mats) + jnp.sum(grad_rows * grad_rows))
    clip = jnp.minimum(1.0, clip_bound / (grad_norm + 1e-06))
    new_momentum = momentum_decay * layer_momentum + clip * grad_mats
    orth = orthogonalize(new_momentum)
    new_mats = layer_mats - muon_rate * (0.2 * math.sqrt(D) * orth + weight_decay * layer_mats)
    ema_mats = ema_decay * layer_ema + (1.0 - ema_decay) * new_mats
    mixed_mats = mix_share * new_mats + (1.0 - mix_share) * layer_zero
    clipped = clip * grad_rows
    new_first = first_decay * row_first + (1.0 - first_decay) * clipped
    new_second = second_decay * row_second + (1.0 - second_decay) * clipped * clipped
    down_bias_grad = clipped[PIX + EMB + SEQ + 4:].reshape(LAYERS, 12, D)[:, 7]
    step_size = new_first / (1.0 - first_decay ** STEPS_DONE) / (jnp.sqrt(new_second / (1.0 - second_decay ** STEPS_DONE)) + adam_floor)
    new_rows = row_params - adam_rate * (step_size + weight_decay * row_params)
    ema_rows = ema_decay * row_ema + (1.0 - ema_decay) * new_rows
    mixed_rows = mix_share * new_rows + (1.0 - mix_share) * row_zero
    return (loss_sum, weight_sum, grad_norm, new_mats, new_momentum, ema_mats, mixed_mats, new_rows, new_first, new_second, ema_rows, mixed_rows, down_bias_grad)
```

```python
import math

import jax
import jax.numpy as jnp
from jax import lax
from jax.sharding import PartitionSpec as P

HEADS = 12
HDIM = 64
PIX = 768
EMB = 512
SEQ = 256
NS_STEPS = 5
STEPS_DONE = 10


HIGHEST = lax.Precision.HIGHEST
norm_epsilon = 1e-05
unit_epsilon = 1e-06
logit_scale = 50.0
clip_bound = 0.001
momentum_decay = 0.95
muon_rate = 0.05
weight_decay = 0.05
adam_rate = 0.2
first_decay = 0.9
second_decay = 0.98
adam_floor = 1e-08
ema_decay = 0.9
mix_share = 0.5
coeff_linear = 3.4445
coeff_cubic = -4.775
coeff_quintic = 2.0315


def matmul(left, right):
    return jnp.dot(left, right, preferred_element_type=jnp.float32)


def matmul_nt(left, right):
    return lax.dot_general(
        left, right, (((1,), (1,)), ((), ())), preferred_element_type=jnp.float32
    )


def matmul_tn(left, right):
    return lax.dot_general(
        left, right, (((0,), (0,)), ((), ())), preferred_element_type=jnp.float32
    )


def norm_forward(inputs, gain, shift):
    center = inputs - jnp.mean(inputs, -1, keepdims=True)
    scale = lax.rsqrt(jnp.mean(center * center, -1, keepdims=True) + norm_epsilon)
    return center * scale * gain + shift


def norm_backward(inputs, gain, upstream):
    center = inputs - jnp.mean(inputs, -1, keepdims=True)
    scale = lax.rsqrt(jnp.mean(center * center, -1, keepdims=True) + norm_epsilon)
    normal = center * scale
    scaled_up = upstream * gain
    inner = scale * (
        scaled_up
        - jnp.mean(scaled_up, -1, keepdims=True)
        - normal * jnp.mean(scaled_up * normal, -1, keepdims=True)
    )
    return (inner, jnp.sum(upstream * normal, 0), jnp.sum(upstream, 0))


def attention_scores(parts, valid_mask):
    raw = jnp.einsum(
        "iqhd,ikhd->ihqk", parts[:, :, 0], parts[:, :, 1], preferred_element_type=jnp.float32
    )
    return jnp.where(valid_mask[:, None, None, :] > 0, raw * HDIM ** (-0.5), -1000000000.0)


def gather_layer(shard):
    return lax.all_gather(shard.astype(jnp.bfloat16), "fsdp", axis=0, tiled=True)


def layer_forward(resid, weight_tensors, vector, valid_mask):
    images, seq = valid_mask.shape
    width = resid.shape[1]
    ffn = 4 * width
    normed = norm_forward(resid, vector[0], vector[1]).astype(jnp.bfloat16)
    bias = jnp.concatenate([vector[2], jnp.zeros_like(vector[2]), vector[3]])
    project = (matmul_nt(normed, weight_tensors[: 3 * width]) + bias).astype(jnp.bfloat16)
    parts = project.reshape(images, seq, 3, HEADS, HDIM)
    scores = attention_scores(parts, valid_mask)
    top_score = jnp.max(scores, -1, keepdims=True)
    expo = jnp.exp(scores - top_score)
    totals = jnp.sum(expo, -1, keepdims=True)
    log_total = top_score + jnp.log(totals)
    probs = (expo / totals).astype(jnp.bfloat16)
    context = jnp.einsum(
        "ihqk,ikhd->iqhd", probs, parts[:, :, 2], preferred_element_type=jnp.float32
    )
    context = context.reshape(images * seq, width).astype(jnp.bfloat16)
    mixed = resid + (matmul_nt(context, weight_tensors[3 * width : 4 * width]) + vector[4])
    normed_two = norm_forward(mixed, vector[5], vector[6]).astype(jnp.bfloat16)
    hidden_pre = matmul_nt(normed_two, weight_tensors[4 * width : 4 * width + ffn]) + vector[
        8:12
    ].reshape(ffn)
    hidden = (hidden_pre * jax.nn.sigmoid(1.702 * hidden_pre)).astype(jnp.bfloat16)
    output = mixed + (matmul(hidden, weight_tensors[4 * width + ffn :]) + vector[7])
    return (
        output,
        (resid, normed, project, log_total, context, mixed, normed_two, hidden_pre, hidden),
    )


def layer_backward(upstream, weight_tensors, vector, valid_mask, saved_activation):
    resid, normed, project, log_total, context, mixed, normed_two, hidden_pre, hidden = (
        saved_activation
    )
    images, seq = valid_mask.shape
    width = resid.shape[1]
    ffn = 4 * width
    out_grad = upstream.astype(jnp.bfloat16)
    grad_down = matmul_tn(hidden, out_grad)
    hidden_grad = matmul_nt(out_grad, weight_tensors[4 * width + ffn :])
    gate = jax.nn.sigmoid(1.702 * hidden_pre)
    pre_grad = (hidden_grad * (gate + 1.702 * hidden_pre * gate * (1.0 - gate))).astype(
        jnp.bfloat16
    )
    grad_up = matmul_tn(pre_grad, normed_two)
    second_in, gain_two, shift_two = norm_backward(
        mixed, vector[5], matmul(pre_grad, weight_tensors[4 * width : 4 * width + ffn])
    )
    mixed_grad = upstream + second_in
    attn_grad = mixed_grad.astype(jnp.bfloat16)
    grad_out = matmul_tn(attn_grad, context)
    context_grad = matmul(attn_grad, weight_tensors[3 * width : 4 * width]).astype(jnp.bfloat16)
    context_grad = context_grad.reshape(images, seq, HEADS, HDIM)
    parts = project.reshape(images, seq, 3, HEADS, HDIM)
    probs = jnp.exp(attention_scores(parts, valid_mask) - log_total)
    prob_grad = jnp.einsum(
        "iqhd,ikhd->ihqk", context_grad, parts[:, :, 2], preferred_element_type=jnp.float32
    )
    value_grad = jnp.einsum(
        "ihqk,iqhd->ikhd",
        probs.astype(jnp.bfloat16),
        context_grad,
        preferred_element_type=jnp.float32,
    )
    score_grad = (probs * (prob_grad - jnp.sum(prob_grad * probs, -1, keepdims=True))).astype(
        jnp.bfloat16
    )
    query_grad = jnp.einsum(
        "ihqk,ikhd->iqhd", score_grad, parts[:, :, 1], preferred_element_type=jnp.float32
    ) * HDIM ** (-0.5)
    key_grad = jnp.einsum(
        "ihqk,iqhd->ikhd", score_grad, parts[:, :, 0], preferred_element_type=jnp.float32
    ) * HDIM ** (-0.5)
    project_grad = (
        jnp.stack([query_grad, key_grad, value_grad], 2)
        .reshape(images * seq, 3 * width)
        .astype(jnp.bfloat16)
    )
    project_sum = jnp.sum(project_grad.astype(jnp.float32), 0)
    grad_qkv = matmul_tn(project_grad, normed)
    first_in, gain_one, shift_one = norm_backward(
        resid, vector[0], matmul(project_grad, weight_tensors[: 3 * width])
    )
    residual_gradient = mixed_grad + first_in
    grad_matrix = jnp.concatenate(
        [part.astype(jnp.bfloat16) for part in (grad_qkv, grad_out, grad_up, grad_down)], 0
    )
    grad_vector = jnp.concatenate(
        [
            jnp.stack(
                [
                    gain_one,
                    shift_one,
                    project_sum[:width],
                    project_sum[2 * width :],
                    jnp.sum(attn_grad.astype(jnp.float32), 0),
                    gain_two,
                    shift_two,
                    jnp.sum(out_grad.astype(jnp.float32), 0),
                ]
            ),
            jnp.sum(pre_grad.astype(jnp.float32), 0).reshape(4, width),
        ],
        0,
    )
    return (residual_gradient, grad_matrix, grad_vector)


def gram_of(blocks):
    return jnp.einsum("lcd,led->lce", blocks, blocks, precision=HIGHEST)


def newton_schulz(blocks):
    gram = gram_of(blocks)
    frob = jnp.sqrt(jnp.trace(gram, axis1=1, axis2=2))[:, None, None] + 1e-07
    blocks = blocks / frob
    gram = gram / (frob * frob)
    for turn in range(NS_STEPS):
        poly = coeff_cubic * gram + coeff_quintic * jnp.einsum(
            "lce,lef->lcf", gram, gram, precision=HIGHEST
        )
        blocks = coeff_linear * blocks + jnp.einsum("lce,led->lcd", poly, blocks, precision=HIGHEST)
        if turn + 1 < NS_STEPS:
            gram = gram_of(blocks)
    return blocks


def body(
    patches,
    pad_mask,
    labels,
    loss_weights,
    class_emb,
    layer_mats,
    layer_zero,
    layer_ema,
    layer_momentum,
    row_params,
    row_zero,
    row_ema,
    row_first,
    row_second,
):
    layers, columns, width = layer_mats.shape
    images, seq, pixels = patches.shape
    front = PIX + EMB + SEQ + 4
    valid_mask = pad_mask.astype(jnp.float32)
    gathered_rows = lax.all_gather(row_params.astype(jnp.bfloat16), "fsdp", axis=1, tiled=True)
    rows_value = gathered_rows.astype(jnp.float32)
    patch_weight = gathered_rows[:PIX]
    proj_rows = gathered_rows[PIX : PIX + EMB]
    position = rows_value[PIX + EMB : PIX + EMB + SEQ]
    head_vec = rows_value[PIX + EMB + SEQ : front]
    layer_vector_params = rows_value[front:].reshape(layers, 12, width)
    flat_patches = patches.reshape(images * seq, pixels)
    embedded = (matmul(flat_patches, patch_weight).reshape(images, seq, width) + position).reshape(
        images * seq, width
    )
    resid = norm_forward(embedded, head_vec[0], head_vec[1])
    kept_weights = []
    saved_activations = []
    for layer_number in range(layers):
        weight_tensors = gather_layer(layer_mats[layer_number])
        kept_weights.append(weight_tensors)
        resid, saved_activation = layer_forward(
            resid, weight_tensors, layer_vector_params[layer_number], valid_mask
        )
        saved_activations.append(saved_activation)
    counts = jnp.sum(valid_mask, -1, keepdims=True)
    pooled = jnp.sum(resid.reshape(images, seq, width) * valid_mask[..., None], 1) / counts
    pooled_norm = norm_forward(pooled, head_vec[2], head_vec[3]).astype(jnp.bfloat16)
    feature = matmul_nt(pooled_norm, proj_rows)
    inv_length = lax.rsqrt(jnp.sum(feature * feature, -1, keepdims=True) + unit_epsilon)
    unit_feat = (feature * inv_length).astype(jnp.bfloat16)
    classes = class_emb.astype(jnp.float32)
    class_unit = (
        classes * lax.rsqrt(jnp.sum(classes * classes, -1, keepdims=True) + unit_epsilon)
    ).astype(jnp.bfloat16)
    logits = logit_scale * matmul_nt(unit_feat, class_unit)
    top_logit = jnp.max(logits, -1, keepdims=True)
    shifted = jnp.exp(logits - top_logit)
    total_exp = jnp.sum(shifted, -1, keepdims=True)
    log_norm = top_logit + jnp.log(total_exp)
    onehot = (jnp.arange(logits.shape[1])[None, :] == labels[:, None]).astype(jnp.float32)
    losses = log_norm[:, 0] - jnp.sum(onehot * logits, -1)
    weights_value = loss_weights.astype(jnp.float32)
    loss_sum, weight_sum = lax.psum(
        (jnp.sum(weights_value * losses), jnp.sum(weights_value)), ("fsdp", "ns")
    )
    seed = weights_value / weight_sum
    logit_grad = seed[:, None] * (shifted / total_exp - onehot)
    unit_grad = logit_scale * jnp.dot(logit_grad, class_unit.astype(jnp.float32), precision=HIGHEST)
    feat_grad = inv_length * unit_grad - feature * inv_length**3 * jnp.sum(
        unit_grad * feature, -1, keepdims=True
    )
    grad_proj = jnp.dot(feat_grad.T, pooled_norm.astype(jnp.float32), precision=HIGHEST)
    pooled_grad, gain_post, shift_post = norm_backward(
        pooled, head_vec[2], jnp.dot(feat_grad, proj_rows.astype(jnp.float32), precision=HIGHEST)
    )
    residual_gradient = (valid_mask[..., None] * (pooled_grad / counts)[:, None, :]).reshape(
        images * seq, width
    )
    grad_mats = [None] * layers
    grad_vecs = [None] * layers
    for layer_number in reversed(range(layers)):
        weight_tensors = kept_weights[layer_number]
        residual_gradient, grad_matrix, grad_vector = layer_backward(
            residual_gradient,
            weight_tensors,
            layer_vector_params[layer_number],
            valid_mask,
            saved_activations[layer_number],
        )
        grad_mats[layer_number], grad_vecs[layer_number] = (
            lax.psum_scatter(grad_matrix, "fsdp", scatter_dimension=0, tiled=True),
            lax.psum_scatter(grad_vector, "fsdp", scatter_dimension=1, tiled=True),
        )
    embed_grad, gain_pre, shift_pre = norm_backward(embedded, head_vec[0], residual_gradient)
    position_grad = jnp.sum(embed_grad.reshape(images, seq, width), 0)
    patch_grad = matmul_tn(flat_patches, embed_grad.astype(jnp.bfloat16))
    front_grad = jnp.concatenate(
        [
            patch_grad,
            grad_proj,
            position_grad,
            jnp.stack([gain_pre, shift_pre, gain_post, shift_post]),
        ],
        0,
    )
    front_shard = lax.psum_scatter(front_grad, "fsdp", scatter_dimension=1, tiled=True)
    mat_grad = jnp.stack(grad_mats)
    row_grad = jnp.concatenate([front_shard] + grad_vecs, 0)
    pairs = lax.axis_size("ns")
    side = lax.axis_index("ns")
    half_depth = width // pairs
    half_rows = row_grad.shape[0] // pairs
    shard_width = row_grad.shape[1]
    mat_total, row_total = (
        lax.psum(mat_grad.astype(jnp.bfloat16), "ns").astype(jnp.float32),
        lax.psum(row_grad.astype(jnp.bfloat16), "ns").astype(jnp.float32),
    )
    mat_half = lax.dynamic_slice_in_dim(mat_total, side * half_depth, half_depth, 2)
    row_half = lax.dynamic_slice_in_dim(row_total, side * half_rows, half_rows, 0)
    squares = jnp.sum(mat_half * mat_half) + jnp.sum(row_half * row_half)
    grad_norm = jnp.sqrt(lax.psum(squares, ("fsdp", "ns")))
    clip = jnp.minimum(1.0, clip_bound / (grad_norm + 1e-06))
    momentum = momentum_decay * layer_momentum + clip * mat_total
    orth = newton_schulz(momentum)
    clipped = clip * row_total
    new_first = first_decay * row_first + (1.0 - first_decay) * clipped
    new_second = second_decay * row_second + (1.0 - second_decay) * clipped * clipped
    down_bias_grad = clipped[front:].reshape(layers, 12, shard_width)[:, 7]
    new_mats = layer_mats - muon_rate * (0.2 * math.sqrt(width) * orth + weight_decay * layer_mats)
    ema_mats = ema_decay * layer_ema + (1.0 - ema_decay) * new_mats
    mixed_mats = mix_share * new_mats + (1.0 - mix_share) * layer_zero
    step_size = (
        new_first
        / (1.0 - first_decay**STEPS_DONE)
        / (jnp.sqrt(new_second / (1.0 - second_decay**STEPS_DONE)) + adam_floor)
    )
    new_rows = row_params - adam_rate * (step_size + weight_decay * row_params)
    ema_rows = ema_decay * row_ema + (1.0 - ema_decay) * new_rows
    mixed_rows = mix_share * new_rows + (1.0 - mix_share) * row_zero
    return (
        loss_sum,
        weight_sum,
        grad_norm,
        new_mats,
        momentum,
        ema_mats,
        mixed_mats,
        new_rows,
        new_first,
        new_second,
        ema_rows,
        mixed_rows,
        down_bias_grad,
    )


def solution(mesh):
    in_specs = (
        P(("fsdp", "ns"), None, None),
        P(("fsdp", "ns"), None),
        P(("fsdp", "ns")),
        P(("fsdp", "ns")),
        P(),
        P(None, "fsdp", None),
        P(None, "fsdp", None),
        P(None, "fsdp", None),
        P(None, "fsdp", None),
        P(None, "fsdp"),
        P(None, "fsdp"),
        P(None, "fsdp"),
        P(None, "fsdp"),
        P(None, "fsdp"),
    )
    out_specs = (
        P(),
        P(),
        P(),
        P(None, "fsdp", None),
        P(None, "fsdp", None),
        P(None, "fsdp", None),
        P(None, "fsdp", None),
        P(None, "fsdp"),
        P(None, "fsdp"),
        P(None, "fsdp"),
        P(None, "fsdp"),
        P(None, "fsdp"),
        P(None, "fsdp"),
    )
    return jax.shard_map(body, mesh=mesh, in_specs=in_specs, out_specs=out_specs, check_vma=False)
```

```python
import functools
import math

import jax
import jax.numpy as jnp
from jax import lax
from jax.experimental import pallas as pl
from jax.experimental.pallas import tpu as pltpu
from jax.sharding import PartitionSpec as P

HEADS = 12
HDIM = 64
PIX = 768
EMB = 512
SEQ = 256
NS_STEPS = 5
STEPS_DONE = 10


HIGHEST = lax.Precision.HIGHEST
norm_epsilon = 1e-05
unit_epsilon = 1e-06
logit_scale = 50.0
clip_bound = 0.001
momentum_decay = 0.95
muon_rate = 0.05
weight_decay = 0.05
adam_rate = 0.2
first_decay = 0.9
second_decay = 0.98
adam_floor = 1e-08
ema_decay = 0.9
mix_share = 0.5
coeff_linear = 3.4445
coeff_cubic = -4.775
coeff_quintic = 2.0315


def matmul(left, right):
    return jnp.dot(left, right, preferred_element_type=jnp.float32)


def matmul_nt(left, right):
    return lax.dot_general(
        left, right, (((1,), (1,)), ((), ())), preferred_element_type=jnp.float32
    )


def matmul_tn(left, right):
    return lax.dot_general(
        left, right, (((0,), (0,)), ((), ())), preferred_element_type=jnp.float32
    )


def norm_forward(inputs, gain, shift):
    center = inputs - jnp.mean(inputs, -1, keepdims=True)
    scale = lax.rsqrt(jnp.mean(center * center, -1, keepdims=True) + norm_epsilon)
    return center * scale * gain + shift


def norm_backward(inputs, gain, upstream):
    center = inputs - jnp.mean(inputs, -1, keepdims=True)
    scale = lax.rsqrt(jnp.mean(center * center, -1, keepdims=True) + norm_epsilon)
    normal = center * scale
    scaled_up = upstream * gain
    inner = scale * (
        scaled_up
        - jnp.mean(scaled_up, -1, keepdims=True)
        - normal * jnp.mean(scaled_up * normal, -1, keepdims=True)
    )
    return (inner, jnp.sum(upstream * normal, 0), jnp.sum(upstream, 0))


def attention_scores(parts, valid_mask):
    raw = jnp.einsum(
        "iqhd,ikhd->ihqk", parts[:, :, 0], parts[:, :, 1], preferred_element_type=jnp.float32
    )
    return jnp.where(valid_mask[:, None, None, :] > 0, raw * HDIM ** (-0.5), -1000000000.0)


BF = jnp.bfloat16
F32 = jnp.float32
MESH = pl.DeviceIdType.MESH
PLANE = 4


def guarded(pred, run):
    if pred is None:
        run()
    else:
        pl.when(pred)(run)


def both(first, second):
    if first is None:
        return second
    return first if second is None else jnp.logical_and(first, second)


def rows_at(start, count):
    return pl.ds(start if isinstance(start, int) else pl.multiple_of(start, 16), count)


class Links:
    def __init__(self, depth, send_sem, recv_sem):
        self.depth, self.send_sem, self.recv_sem = depth, send_sem, recv_sem
        self.me, self.x = lax.axis_index("fsdp"), lax.axis_index("ns")
        self.z, self.y, self.c = self.me // PLANE, lax.rem(self.me // 2, 2), lax.rem(self.me, 2)
        self.up = (self.at(self.z + 1, self.y, self.c), self.x)
        self.down = (self.at(self.z - 1, self.y, self.c), self.x)
        self.y_peer = (self.at(self.z, 1 - self.y, self.c), self.x)
        self.c_peer = (self.at(self.z, self.y, 1 - self.c), self.x)
        self.x_peer = (self.me, 1 - self.x)
        self.count, self.sent, self.waited = 0, [], set()

    def at(self, z, y, c):
        return PLANE * z + 2 * y + c

    def slot(self):
        self.count += 1
        return self.count - 1

    def greet(self):
        barrier = pltpu.get_barrier_semaphore()

        def signal(device):
            pl.semaphore_signal(barrier, inc=1, device_id=device, device_id_type=MESH)

        for device in (self.y_peer, self.x_peer, self.c_peer):
            signal(device)
        pl.when(self.z < self.depth - 1)(lambda: signal(self.up))
        pl.when(self.z > 0)(lambda: signal(self.down))
        inner = (self.z < self.depth - 1).astype(jnp.int32) + (self.z > 0).astype(jnp.int32)
        pl.semaphore_wait(barrier, 3 + inner)

    def copy(self, slot, source, target, device):
        return pltpu.make_async_remote_copy(
            src_ref=source,
            dst_ref=target,
            send_sem=self.send_sem.at[slot],
            recv_sem=self.recv_sem.at[slot],
            device_id=device,
            device_id_type=MESH,
        )

    def send(self, slot, source, target, device, pred=None):
        copy = self.copy(slot, source, target, device)
        guarded(pred, copy.start)
        self.sent.append((slot, pred, copy))

    def receive(self, slot, target, pred=None):
        guarded(pred, self.copy(slot, target, target, self.c_peer).wait_recv)

    def finish(self, slot=None):
        for number, pred, copy in self.sent:
            if number not in self.waited and (slot is None or number == slot):
                guarded(pred, copy.wait_send)
        if slot is not None:
            self.waited.add(slot)


def gather_item(links, own, target, count):
    depth, z, y, c, x = links.depth, links.z, links.y, links.c, links.x
    third = count // 3
    begin = x * third
    origin = (0, 0)
    keys = [(side, far) for far in range(1, depth) for side in (-1, 1)]
    z_slot = {key: links.slot() for key in keys}
    y_slot = {key: links.slot() for key in keys + [origin]}
    x_slot = {(key, o): links.slot() for key in keys + [origin] for o in (0, 1)}
    c_slot = {(key, o): links.slot() for key in keys + [origin] for o in (0, 1)}

    def part(shard):
        return target(shard).at[rows_at(begin, 2 * third)]

    def own_part():
        return own.at[rows_at(begin, 2 * third)]

    def third_of(shard, side):
        return target(shard).at[rows_at(side * 2 * third, third)]

    def shard(key, other, core=None):
        return links.at(z + key[0] * key[1], 1 - y if other else y, c if core is None else core)

    def exists(key):
        if key == origin:
            return None
        return z >= key[1] if key[0] < 0 else z + key[1] < depth

    def z_send(key):
        for side in (-1, 1) if key == origin else (key[0],):
            if key[1] + 1 < depth:
                source = own_part() if key == origin else part(shard(key, 0))
                links.send(
                    z_slot[(side, key[1] + 1)],
                    source,
                    part(shard(key, 0)),
                    links.up if side < 0 else links.down,
                    both(exists(key), z < depth - 1 if side < 0 else z > 0),
                )

    def y_send(key):
        source = own_part() if key == origin else part(shard(key, 0))
        links.send(y_slot[key], source, part(shard(key, 0)), links.y_peer, exists(key))

    def x_send(key, other):
        block = third_of(shard(key, other), x)
        links.send(x_slot[(key, other)], block, block, links.x_peer, exists(key))

    def c_send(key, other):
        whole = target(shard(key, other))
        source = own if (key, other) == (origin, 0) else whole
        links.send(c_slot[(key, other)], source, whole, links.c_peer, exists(key))

    order = []
    for far in range(1, depth):
        order += [((side, far), 0) for side in (-1, 1)]
        order += [(key, 1) for key in ([origin] if far == 1 else [(-1, far - 1), (1, far - 1)])]
    order += [((side, depth - 1), 1) for side in (-1, 1)]

    def start():
        z_send(origin)
        y_send(origin)
        c_send(origin, 0)

    def cross(keys_now):
        for key in keys_now:
            links.receive(y_slot[key], part(shard(key, 1)), exists(key))
            x_send(key, 1)

    def step(far):
        for side in (-1, 1):
            key = (side, far)
            links.receive(z_slot[key], part(shard(key, 0)), exists(key))
            z_send(key)
            y_send(key)
            x_send(key, 0)
        cross([origin] if far == 1 else [(-1, far - 1), (1, far - 1)])
        if far == depth - 1:
            cross([(-1, far), (1, far)])

    def share():
        for key, other in order:
            links.receive(x_slot[(key, other)], third_of(shard(key, other), 1 - x), exists(key))
            c_send(key, other)

    def settle():
        for key, other in [(origin, 0)] + order:
            links.receive(c_slot[(key, other)], target(shard(key, other, 1 - c)), exists(key))

    return start, step, share, settle


def gather_kernel(depth, halves, rows, mats, all_rows, all_mats, send_sem, recv_sem, local_sem):
    links = Links(depth, send_sem, recv_sem)
    links.greet()
    layers, count = mats.shape[:2]
    size = count // halves
    own = [pltpu.make_async_copy(rows, all_rows.at[links.me], local_sem.at[0])]
    items = [gather_item(links, rows, lambda shard: all_rows.at[shard], rows.shape[0])]
    for layer in range(layers):
        own.append(
            pltpu.make_async_copy(
                mats.at[layer], all_mats.at[layer, links.me], local_sem.at[1 + layer]
            )
        )
        for half in range(halves):
            block = pl.ds(half * size, size)

            def target(shard, layer=layer, block=block):
                return all_mats.at[layer, shard, block]

            items.append(gather_item(links, mats.at[layer, block], target, size))
    for copy in own:
        copy.start()
    items[0][0]()
    for number, (_, step, _, _) in enumerate(items):
        step(1)
        step(2)
        if number + 1 < len(items):
            items[number + 1][0]()
        if number > 0:
            items[number - 1][2]()
        for far in range(3, depth):
            step(far)
    items[-1][2]()
    for item in items:
        item[3]()
    links.finish()
    for copy in own:
        copy.wait()


def gather(depth, rows, mats):
    layers, count, width = mats.shape
    shards = PLANE * depth
    halves = 2
    slots = (1 + layers * halves) * 60
    any_space = pl.BlockSpec(memory_space=pl.ANY)
    return pl.pallas_call(
        functools.partial(gather_kernel, depth, halves),
        out_shape=(
            jax.ShapeDtypeStruct((shards,) + rows.shape, BF),
            jax.ShapeDtypeStruct((layers, shards, count, width), BF),
        ),
        in_specs=[any_space] * 2,
        out_specs=[any_space] * 2,
        scratch_shapes=[
            pltpu.SemaphoreType.DMA((slots,)),
            pltpu.SemaphoreType.DMA((slots,)),
            pltpu.SemaphoreType.DMA((1 + layers,)),
        ],
        name="gather_weights",
        compiler_params=pltpu.CompilerParams(collective_id=1, has_side_effects=True),
    )(rows, mats)


def accumulate(target, start, source, begin, count, step):
    @pl.loop(0, count // step)
    def _(turn):
        here = rows_at(start + turn * step, step)
        there = rows_at(begin + turn * step, step)
        target[here, :] = (target[here, :].astype(F32) + source[there, :].astype(F32)).astype(BF)


def scatter_group(links, dest, load, sizes, bufs, emit):
    depth, z, y, c, x = links.depth, links.z, links.y, links.c, links.x
    n, p, q, step = sizes
    mine, core_in, x_in, y_in, z_in, z_last, final = bufs
    core_slot, x_slot = [links.slot(), links.slot()], [links.slot(), links.slot()]
    q_slot, p_slot, low_slot, high_slot, last_slot = (links.slot() for _ in range(5))
    m = p + q
    first = x * p
    own_p, peer_p = x * m, (1 - x) * m
    sides = ((0, 1 - y), (1, y))

    def begin():
        for i, side in sides:
            load(i, side, mine.at[side], core_in.at[side], core_slot[i])

    def stage_core():
        for i, side in sides:
            load(i, side, mine.at[side], None, None)
            links.receive(core_slot[i], core_in.at[side])
            accumulate(mine.at[side], 0, core_in.at[side], 0, n, step)
            links.send(x_slot[i], mine.at[side, rows_at(peer_p, p)], x_in.at[side], links.x_peer)
            if i == 0:
                links.send(q_slot, mine.at[side, pl.ds(p, q)], y_in.at[pl.ds(0, q)], links.y_peer)

    def stage_x():
        for i, side in sides:
            links.receive(x_slot[i], x_in.at[side])
            accumulate(mine.at[side], own_p, x_in.at[side], 0, p, step)
            if i == 0:
                links.send(
                    p_slot, mine.at[side, rows_at(own_p, p)], y_in.at[pl.ds(q, p)], links.y_peer
                )
        links.receive(q_slot, y_in.at[pl.ds(0, q)])
        accumulate(mine.at[y], p, y_in, 0, q, step)

    def stage_y():
        links.receive(p_slot, y_in.at[pl.ds(q, p)])
        accumulate(mine.at[y], own_p, y_in, q, p, step)

    def stage_z(hop):
        block = mine.at[y, rows_at(first, m)]

        def take(slot, source, pred):
            @pl.when(pred)
            def _():
                links.receive(slot, source)
                accumulate(mine.at[y], first, source, 0, m, step)

        if dest > 0:
            if 1 <= hop <= dest:
                take(low_slot, z_in, z == hop)
            if hop < dest:
                links.send(low_slot, block, z_in, links.up, z == hop)
        if dest < depth - 1:
            turn = depth - 1 - hop
            if hop >= 1 and turn > dest:
                take(high_slot, z_in, z == turn)
            if turn > dest + 1:
                links.send(high_slot, block, z_in, links.down, z == turn)
            if turn == dest + 1:
                links.send(high_slot, block, z_last, links.down, z == turn)
            if turn == dest and hop >= 1:
                take(high_slot, z_last, z == dest)
        if hop == max(dest, depth - 1 - dest):
            links.send(last_slot, block, final, links.x_peer, z == dest)

    def stage_last():
        links.finish(x_slot[1])
        links.finish(last_slot)

        @pl.when(z == dest)
        def _():
            links.receive(last_slot, final)
            accumulate(mine.at[y], p, final, jnp.where(x == 0, 0, p), q, step)

            @pl.loop(0, p // 16)
            def _(turn):
                there = rows_at(jnp.where(x == 0, q, 0) + turn * 16, 16)
                mine[y, rows_at(peer_p + turn * 16, 16), :] = final[there, :]

            emit(mine.at[y])

    hops = [functools.partial(stage_z, hop) for hop in range(depth)]
    return begin, [stage_core, stage_x, stage_y] + hops + [stage_last]


def scatter_kernel(depth, layers, sub, lags, *refs):
    grads, row_grad = refs[: 4 * layers], refs[4 * layers]
    out, row_out = refs[4 * layers + 1 : 4 * layers + 3]
    big, small = refs[4 * layers + 3 : 4 * layers + 10], refs[4 * layers + 10 : 4 * layers + 17]
    send_sem, recv_sem, local_sem = refs[4 * layers + 17 :]
    links = Links(depth, send_sem, recv_sem)
    links.greet()
    y, c = links.y, links.c
    count = out.shape[1]
    n = count // sub
    p = n // 4 // 16 * 16
    groups = []

    def block_of(layer, shard, part):
        row = shard * count + part * n
        for matrix in grads[4 * layer : 4 * layer + 4]:
            if row < matrix.shape[0]:
                return matrix.at[pl.ds(row, n)]
            row -= matrix.shape[0]

    def add_group(dest, source, sizes, bufs, emit):
        number = len(groups)

        def load(i, side, mine, core_in, slot):
            sem = local_sem.at[2 * number + i]
            if core_in is None:
                pltpu.make_async_copy(source(0, 0), mine, sem).wait()
                return
            for y_now in (0, 1):
                for core in (0, 1):

                    @pl.when(jnp.logical_and(side == y_now, c == core))
                    def _():
                        pltpu.make_async_copy(source(y_now, core), mine, sem).start()
                        links.copy(slot, source(y_now, 1 - core), core_in, links.c_peer).start()

            links.sent.append((slot, None, links.copy(slot, source(0, 0), core_in, links.c_peer)))

        groups.append(scatter_group(links, dest, load, sizes, bufs, emit))

    def write(target, sem):
        def emit(result):
            copy = pltpu.make_async_copy(result, target, sem)
            copy.start()
            copy.wait()

        return emit

    end_sem = local_sem.at[local_sem.shape[0] - 1]
    for layer in reversed(range(layers)):
        for part in range(sub):
            for dest in (3, 0, 2, 1) if depth == 4 else reversed(range(depth)):
                number, spot = len(groups), layer * sub + part
                add_group(
                    dest,
                    lambda y_now, core, layer=layer, part=part, dest=dest: block_of(
                        layer, links.at(dest, y_now, core), part
                    ),
                    (n, p, n - 2 * p, 48),
                    [ref.at[number] for ref in big[:5]] + [ref.at[spot] for ref in big[5:]],
                    write(out.at[layer, pl.ds(part * n, n)], end_sem),
                )
    rows = row_out.shape[0]
    for dest in reversed(range(depth)):
        add_group(
            dest,
            lambda y_now, core, dest=dest: row_grad.at[links.at(dest, y_now, core)],
            (rows, 16, rows - 32, 16),
            [ref.at[dest] for ref in small[:5]] + list(small[5:]),
            write(row_out, end_sem),
        )
    for begin, _ in groups:
        begin()
    for turn in range(len(groups) + max(lags)):
        for place, lag in enumerate(lags):
            if 0 <= turn - lag < len(groups):
                groups[turn - lag][1][place]()
    links.finish()


def scatter(depth, grads, row_grad):
    layers = len(grads)
    shards = PLANE * depth
    width = grads[0][0].shape[1]
    count = sum(part.shape[0] for part in grads[0]) // shards
    sub = 3
    n = count // sub
    p = n // 4 // 16 * 16
    m = n - p
    blocks = layers * depth * sub
    rows, lanes = row_grad.shape[1:]
    row_m = rows - 16
    lags = [0, 3, 6] + [9 + 3 * hop for hop in range(depth)] + [9 + 3 * depth]

    def room(*shape):
        return pltpu.VMEM(shape, BF)

    any_space = pl.BlockSpec(memory_space=pl.ANY)
    slots = (blocks + depth) * 9
    return pl.pallas_call(
        functools.partial(scatter_kernel, depth, layers, sub, lags),
        out_shape=(
            jax.ShapeDtypeStruct((layers, count, width), BF),
            jax.ShapeDtypeStruct((rows, lanes), BF),
        ),
        in_specs=[any_space] * (4 * layers + 1),
        out_specs=[any_space] * 2,
        scratch_shapes=[
            room(blocks, 2, n, width),
            room(blocks, 2, n, width),
            room(blocks, 2, p, width),
            room(blocks, m, width),
            room(blocks, m, width),
            room(layers * sub, m, width),
            room(layers * sub, m, width),
            room(depth, 2, rows, lanes),
            room(depth, 2, rows, lanes),
            room(depth, 2, 16, lanes),
            room(depth, row_m, lanes),
            room(depth, row_m, lanes),
            room(row_m, lanes),
            room(row_m, lanes),
            pltpu.SemaphoreType.DMA((slots,)),
            pltpu.SemaphoreType.DMA((slots,)),
            pltpu.SemaphoreType.DMA((2 * (blocks + depth) + 1,)),
        ],
        name="scatter_gradients",
        compiler_params=pltpu.CompilerParams(
            collective_id=2, has_side_effects=True, vmem_limit_bytes=60 * 1024 * 1024
        ),
    )(*[part for layer in grads for part in layer], row_grad)


def gather_layer(shard):
    return lax.all_gather(shard.astype(jnp.bfloat16), "fsdp", axis=0, tiled=True)


def layer_forward(resid, weight_tensors, vector, valid_mask):
    images, seq = valid_mask.shape
    width = resid.shape[1]
    ffn = 4 * width
    normed = norm_forward(resid, vector[0], vector[1]).astype(jnp.bfloat16)
    bias = jnp.concatenate([vector[2], jnp.zeros_like(vector[2]), vector[3]])
    project = (matmul_nt(normed, weight_tensors[: 3 * width]) + bias).astype(jnp.bfloat16)
    parts = project.reshape(images, seq, 3, HEADS, HDIM)
    scores = attention_scores(parts, valid_mask)
    top_score = jnp.max(scores, -1, keepdims=True)
    expo = jnp.exp(scores - top_score)
    totals = jnp.sum(expo, -1, keepdims=True)
    log_total = top_score + jnp.log(totals)
    probs = (expo / totals).astype(jnp.bfloat16)
    context = jnp.einsum(
        "ihqk,ikhd->iqhd", probs, parts[:, :, 2], preferred_element_type=jnp.float32
    )
    context = context.reshape(images * seq, width).astype(jnp.bfloat16)
    mixed = resid + (matmul_nt(context, weight_tensors[3 * width : 4 * width]) + vector[4])
    normed_two = norm_forward(mixed, vector[5], vector[6]).astype(jnp.bfloat16)
    hidden_pre = matmul_nt(normed_two, weight_tensors[4 * width : 4 * width + ffn]) + vector[
        8:12
    ].reshape(ffn)
    hidden = (hidden_pre * jax.nn.sigmoid(1.702 * hidden_pre)).astype(jnp.bfloat16)
    output = mixed + (matmul(hidden, weight_tensors[4 * width + ffn :]) + vector[7])
    return (
        output,
        (resid, normed, project, log_total, context, mixed, normed_two, hidden_pre, hidden),
    )


def layer_backward(upstream, weight_tensors, vector, valid_mask, saved_activation):
    resid, normed, project, log_total, context, mixed, normed_two, hidden_pre, hidden = (
        saved_activation
    )
    images, seq = valid_mask.shape
    width = resid.shape[1]
    ffn = 4 * width
    out_grad = upstream.astype(jnp.bfloat16)
    grad_down = matmul_tn(hidden, out_grad)
    hidden_grad = matmul_nt(out_grad, weight_tensors[4 * width + ffn :])
    gate = jax.nn.sigmoid(1.702 * hidden_pre)
    pre_grad = (hidden_grad * (gate + 1.702 * hidden_pre * gate * (1.0 - gate))).astype(
        jnp.bfloat16
    )
    grad_up = matmul_tn(pre_grad, normed_two)
    second_in, gain_two, shift_two = norm_backward(
        mixed, vector[5], matmul(pre_grad, weight_tensors[4 * width : 4 * width + ffn])
    )
    mixed_grad = upstream + second_in
    attn_grad = mixed_grad.astype(jnp.bfloat16)
    grad_out = matmul_tn(attn_grad, context)
    context_grad = matmul(attn_grad, weight_tensors[3 * width : 4 * width]).astype(jnp.bfloat16)
    context_grad = context_grad.reshape(images, seq, HEADS, HDIM)
    parts = project.reshape(images, seq, 3, HEADS, HDIM)
    probs = jnp.exp(attention_scores(parts, valid_mask) - log_total)
    prob_grad = jnp.einsum(
        "iqhd,ikhd->ihqk", context_grad, parts[:, :, 2], preferred_element_type=jnp.float32
    )
    value_grad = jnp.einsum(
        "ihqk,iqhd->ikhd",
        probs.astype(jnp.bfloat16),
        context_grad,
        preferred_element_type=jnp.float32,
    )
    score_grad = (probs * (prob_grad - jnp.sum(prob_grad * probs, -1, keepdims=True))).astype(
        jnp.bfloat16
    )
    query_grad = jnp.einsum(
        "ihqk,ikhd->iqhd", score_grad, parts[:, :, 1], preferred_element_type=jnp.float32
    ) * HDIM ** (-0.5)
    key_grad = jnp.einsum(
        "ihqk,iqhd->ikhd", score_grad, parts[:, :, 0], preferred_element_type=jnp.float32
    ) * HDIM ** (-0.5)
    project_grad = (
        jnp.stack([query_grad, key_grad, value_grad], 2)
        .reshape(images * seq, 3 * width)
        .astype(jnp.bfloat16)
    )
    project_sum = jnp.sum(project_grad.astype(jnp.float32), 0)
    grad_qkv = matmul_tn(project_grad, normed)
    first_in, gain_one, shift_one = norm_backward(
        resid, vector[0], matmul(project_grad, weight_tensors[: 3 * width])
    )
    residual_gradient = mixed_grad + first_in
    grad_matrix = [part.astype(BF) for part in (grad_qkv, grad_out, grad_up, grad_down)]
    grad_vector = jnp.concatenate(
        [
            jnp.stack(
                [
                    gain_one,
                    shift_one,
                    project_sum[:width],
                    project_sum[2 * width :],
                    jnp.sum(attn_grad.astype(jnp.float32), 0),
                    gain_two,
                    shift_two,
                    jnp.sum(out_grad.astype(jnp.float32), 0),
                ]
            ),
            jnp.sum(pre_grad.astype(jnp.float32), 0).reshape(4, width),
        ],
        0,
    )
    return (residual_gradient, grad_matrix, grad_vector)


def newton_schulz(blocks):
    frob = jnp.sqrt(jnp.sum(blocks * blocks, axis=(1, 2), keepdims=True)) + 1e-07
    blocks = blocks / frob
    unit = jnp.eye(blocks.shape[1], dtype=jnp.float32)
    for turn in range(NS_STEPS):
        shift = 1.0 if turn >= NS_STEPS - 2 else 0.0
        short = blocks.astype(BF)
        gram = jnp.einsum("lcd,led->lce", short, short, preferred_element_type=F32) - shift * unit
        low = gram.astype(BF)
        square = jnp.einsum("lce,lef->lcf", low, low, preferred_element_type=F32)
        poly = (coeff_cubic + 2.0 * shift * coeff_quintic) * gram + coeff_quintic * square
        stay = coeff_linear + shift * (coeff_cubic + shift * coeff_quintic)
        blocks = stay * blocks + jnp.einsum(
            "lce,led->lcd", poly.astype(BF), short, preferred_element_type=F32
        )
    return blocks


def updates(
    clipped,
    momentum,
    orth,
    layer_mats,
    layer_zero,
    layer_ema,
    row_params,
    row_zero,
    row_ema,
    row_first,
    row_second,
):
    layers, _, width = layer_mats.shape
    shard_width = row_params.shape[1]
    front = PIX + EMB + SEQ + 4
    new_first = first_decay * row_first + (1.0 - first_decay) * clipped
    new_second = second_decay * row_second + (1.0 - second_decay) * clipped * clipped
    down_bias_grad = clipped[front:].reshape(layers, 12, shard_width)[:, 7]
    new_mats = layer_mats - muon_rate * (0.2 * math.sqrt(width) * orth + weight_decay * layer_mats)
    ema_mats = ema_decay * layer_ema + (1.0 - ema_decay) * new_mats
    mixed_mats = mix_share * new_mats + (1.0 - mix_share) * layer_zero
    step_size = (
        new_first
        / (1.0 - first_decay**STEPS_DONE)
        / (jnp.sqrt(new_second / (1.0 - second_decay**STEPS_DONE)) + adam_floor)
    )
    new_rows = row_params - adam_rate * (step_size + weight_decay * row_params)
    ema_rows = ema_decay * row_ema + (1.0 - ema_decay) * new_rows
    mixed_rows = mix_share * new_rows + (1.0 - mix_share) * row_zero
    return (
        new_mats,
        momentum,
        ema_mats,
        mixed_mats,
        new_rows,
        new_first,
        new_second,
        ema_rows,
        mixed_rows,
        down_bias_grad,
    )


def plain_body(
    patches,
    pad_mask,
    labels,
    loss_weights,
    class_emb,
    layer_mats,
    layer_zero,
    layer_ema,
    layer_momentum,
    row_params,
    row_zero,
    row_ema,
    row_first,
    row_second,
):
    layers, columns, width = layer_mats.shape
    images, seq, pixels = patches.shape
    front = PIX + EMB + SEQ + 4
    valid_mask = pad_mask.astype(jnp.float32)
    gathered_rows = lax.all_gather(row_params.astype(jnp.bfloat16), "fsdp", axis=1, tiled=True)
    rows_value = gathered_rows.astype(jnp.float32)
    patch_weight = gathered_rows[:PIX]
    proj_rows = gathered_rows[PIX : PIX + EMB]
    position = rows_value[PIX + EMB : PIX + EMB + SEQ]
    head_vec = rows_value[PIX + EMB + SEQ : front]
    layer_vector_params = rows_value[front:].reshape(layers, 12, width)
    flat_patches = patches.reshape(images * seq, pixels)
    embedded = (matmul(flat_patches, patch_weight).reshape(images, seq, width) + position).reshape(
        images * seq, width
    )
    resid = norm_forward(embedded, head_vec[0], head_vec[1])
    kept_weights = []
    saved_activations = []
    for layer_number in range(layers):
        weight_tensors = gather_layer(layer_mats[layer_number])
        kept_weights.append(weight_tensors)
        resid, saved_activation = layer_forward(
            resid, weight_tensors, layer_vector_params[layer_number], valid_mask
        )
        saved_activations.append(saved_activation)
    counts = jnp.sum(valid_mask, -1, keepdims=True)
    pooled = jnp.sum(resid.reshape(images, seq, width) * valid_mask[..., None], 1) / counts
    pooled_norm = norm_forward(pooled, head_vec[2], head_vec[3]).astype(jnp.bfloat16)
    feature = matmul_nt(pooled_norm, proj_rows)
    inv_length = lax.rsqrt(jnp.sum(feature * feature, -1, keepdims=True) + unit_epsilon)
    unit_feat = (feature * inv_length).astype(jnp.bfloat16)
    classes = class_emb.astype(jnp.float32)
    class_unit = (
        classes * lax.rsqrt(jnp.sum(classes * classes, -1, keepdims=True) + unit_epsilon)
    ).astype(jnp.bfloat16)
    logits = logit_scale * matmul_nt(unit_feat, class_unit)
    top_logit = jnp.max(logits, -1, keepdims=True)
    shifted = jnp.exp(logits - top_logit)
    total_exp = jnp.sum(shifted, -1, keepdims=True)
    log_norm = top_logit + jnp.log(total_exp)
    onehot = (jnp.arange(logits.shape[1])[None, :] == labels[:, None]).astype(jnp.float32)
    losses = log_norm[:, 0] - jnp.sum(onehot * logits, -1)
    weights_value = loss_weights.astype(jnp.float32)
    loss_sum, weight_sum = lax.psum(
        (jnp.sum(weights_value * losses), jnp.sum(weights_value)), ("fsdp", "ns")
    )
    seed = weights_value / weight_sum
    logit_grad = seed[:, None] * (shifted / total_exp - onehot)
    unit_grad = logit_scale * jnp.dot(logit_grad, class_unit.astype(jnp.float32), precision=HIGHEST)
    feat_grad = inv_length * unit_grad - feature * inv_length**3 * jnp.sum(
        unit_grad * feature, -1, keepdims=True
    )
    grad_proj = jnp.dot(feat_grad.T, pooled_norm.astype(jnp.float32), precision=HIGHEST)
    pooled_grad, gain_post, shift_post = norm_backward(
        pooled, head_vec[2], jnp.dot(feat_grad, proj_rows.astype(jnp.float32), precision=HIGHEST)
    )
    residual_gradient = (valid_mask[..., None] * (pooled_grad / counts)[:, None, :]).reshape(
        images * seq, width
    )
    grad_mats = [None] * layers
    grad_vecs = [None] * layers
    for layer_number in reversed(range(layers)):
        weight_tensors = kept_weights[layer_number]
        residual_gradient, grad_matrix, grad_vector = layer_backward(
            residual_gradient,
            weight_tensors,
            layer_vector_params[layer_number],
            valid_mask,
            saved_activations[layer_number],
        )
        grad_mats[layer_number], grad_vecs[layer_number] = (
            lax.psum_scatter(
                jnp.concatenate(grad_matrix, 0), "fsdp", scatter_dimension=0, tiled=True
            ),
            lax.psum_scatter(grad_vector, "fsdp", scatter_dimension=1, tiled=True),
        )
    embed_grad, gain_pre, shift_pre = norm_backward(embedded, head_vec[0], residual_gradient)
    position_grad = jnp.sum(embed_grad.reshape(images, seq, width), 0)
    patch_grad = matmul_tn(flat_patches, embed_grad.astype(jnp.bfloat16))
    front_grad = jnp.concatenate(
        [
            patch_grad,
            grad_proj,
            position_grad,
            jnp.stack([gain_pre, shift_pre, gain_post, shift_post]),
        ],
        0,
    )
    front_shard = lax.psum_scatter(front_grad, "fsdp", scatter_dimension=1, tiled=True)
    mat_grad = jnp.stack(grad_mats)
    row_grad = jnp.concatenate([front_shard] + grad_vecs, 0)
    pairs = lax.axis_size("ns")
    side = lax.axis_index("ns")
    half_depth = width // pairs
    half_rows = row_grad.shape[0] // pairs
    mat_total, row_total = (
        lax.psum(mat_grad.astype(jnp.bfloat16), "ns").astype(jnp.float32),
        lax.psum(row_grad.astype(jnp.bfloat16), "ns").astype(jnp.float32),
    )
    mat_half = lax.dynamic_slice_in_dim(mat_total, side * half_depth, half_depth, 2)
    row_half = lax.dynamic_slice_in_dim(row_total, side * half_rows, half_rows, 0)
    squares = jnp.sum(mat_half * mat_half) + jnp.sum(row_half * row_half)
    grad_norm = jnp.sqrt(lax.psum(squares, ("fsdp", "ns")))
    clip = jnp.minimum(1.0, clip_bound / (grad_norm + 1e-06))
    momentum = momentum_decay * layer_momentum + clip * mat_total
    orth = newton_schulz(momentum)
    return (loss_sum, weight_sum, grad_norm) + updates(
        clip * row_total,
        momentum,
        orth,
        layer_mats,
        layer_zero,
        layer_ema,
        row_params,
        row_zero,
        row_ema,
        row_first,
        row_second,
    )


def fast_body(
    patches,
    pad_mask,
    labels,
    loss_weights,
    class_emb,
    layer_mats,
    layer_zero,
    layer_ema,
    layer_momentum,
    row_params,
    row_zero,
    row_ema,
    row_first,
    row_second,
):
    layers, columns, width = layer_mats.shape
    images, seq, pixels = patches.shape
    shards = lax.axis_size("fsdp")
    depth = shards // PLANE
    rows, share = row_params.shape
    front = PIX + EMB + SEQ + 4
    lanes = -(-rows // 128) * 128
    valid_mask = pad_mask.astype(F32)
    sent_rows = jnp.pad(row_params.T.astype(BF), ((0, 0), (0, lanes - rows)))
    all_rows, all_mats = gather(depth, sent_rows, layer_mats.astype(BF))
    table = all_rows.reshape(width, lanes)
    weights = all_mats.reshape(layers, shards * columns, width)
    patch_weight, proj = table[:, :PIX], table[:, PIX : PIX + EMB]
    position = table[:, PIX + EMB : PIX + EMB + SEQ].T.astype(F32)
    vectors = table[:, PIX + EMB + SEQ : rows].T.astype(F32)
    head_vec = vectors[:4]
    layer_vector_params = vectors[4:].reshape(layers, 12, width)
    flat_patches = patches.reshape(images * seq, pixels)
    embedded = (
        matmul_nt(flat_patches, patch_weight).reshape(images, seq, width) + position
    ).reshape(images * seq, width)
    resid = norm_forward(embedded, head_vec[0], head_vec[1])
    saved_activations = []
    for layer_number in range(layers):
        resid, saved_activation = layer_forward(
            resid, weights[layer_number], layer_vector_params[layer_number], valid_mask
        )
        saved_activations.append(saved_activation)
    counts = jnp.sum(valid_mask, -1, keepdims=True)
    pooled = jnp.sum(resid.reshape(images, seq, width) * valid_mask[..., None], 1) / counts
    pooled_norm = norm_forward(pooled, head_vec[2], head_vec[3]).astype(BF)
    feature = matmul(pooled_norm, proj)
    inv_length = lax.rsqrt(jnp.sum(feature * feature, -1, keepdims=True) + unit_epsilon)
    unit_feat = (feature * inv_length).astype(BF)
    classes = class_emb.astype(F32)
    class_unit = (
        classes * lax.rsqrt(jnp.sum(classes * classes, -1, keepdims=True) + unit_epsilon)
    ).astype(BF)
    logits = logit_scale * matmul_nt(unit_feat, class_unit)
    top_logit = jnp.max(logits, -1, keepdims=True)
    shifted = jnp.exp(logits - top_logit)
    total_exp = jnp.sum(shifted, -1, keepdims=True)
    log_norm = top_logit + jnp.log(total_exp)
    onehot = (jnp.arange(logits.shape[1])[None, :] == labels[:, None]).astype(F32)
    losses = log_norm[:, 0] - jnp.sum(onehot * logits, -1)
    weights_value = loss_weights.astype(F32)
    logit_grad = weights_value[:, None] * (shifted / total_exp - onehot)
    unit_grad = logit_scale * jnp.dot(logit_grad, class_unit.astype(F32), precision=HIGHEST)
    feat_grad = inv_length * unit_grad - feature * inv_length**3 * jnp.sum(
        unit_grad * feature, -1, keepdims=True
    )
    grad_proj = jnp.dot(pooled_norm.astype(F32).T, feat_grad, precision=HIGHEST)
    pooled_grad, gain_post, shift_post = norm_backward(
        pooled,
        head_vec[2],
        lax.dot_general(
            feat_grad, proj.astype(F32), (((1,), (1,)), ((), ())), precision=HIGHEST
        ),
    )
    upstream = (valid_mask[..., None] * (pooled_grad / counts)[:, None, :]).reshape(
        images * seq, width
    )
    grad_mats = [None] * layers
    grad_vecs = [None] * layers
    for layer_number in reversed(range(layers)):
        upstream, grad_mats[layer_number], grad_vecs[layer_number] = layer_backward(
            upstream,
            weights[layer_number],
            layer_vector_params[layer_number],
            valid_mask,
            saved_activations[layer_number],
        )
    embed_grad, gain_pre, shift_pre = norm_backward(embedded, head_vec[0], upstream)
    position_grad = jnp.sum(embed_grad.reshape(images, seq, width), 0)
    patch_grad = matmul_tn(embed_grad.astype(BF), flat_patches)
    vector_grad = jnp.concatenate(
        [jnp.stack([gain_pre, shift_pre, gain_post, shift_post])] + grad_vecs, 0
    )
    row_grad = jnp.concatenate(
        [patch_grad, grad_proj, position_grad.T, vector_grad.T, jnp.zeros((width, lanes - rows))], 1
    )
    mat_total, row_total = scatter(
        depth, grad_mats, row_grad.astype(BF).reshape(shards, share, lanes)
    )
    mat_total = mat_total.astype(F32)
    row_total = row_total.astype(F32)[:, :rows].T
    squares = jnp.sum(mat_total * mat_total) + jnp.sum(row_total * row_total)
    loss_sum, weight_sum, squares = lax.psum(
        (jnp.sum(weights_value * losses), jnp.sum(weights_value), squares), ("fsdp", "ns")
    )
    grad_norm = jnp.sqrt(squares / lax.axis_size("ns")) / weight_sum
    clip = jnp.minimum(1.0, clip_bound / (grad_norm + 1e-06)) / weight_sum
    momentum = momentum_decay * layer_momentum + clip * mat_total
    orth = newton_schulz(momentum)
    return (loss_sum, weight_sum, grad_norm) + updates(
        clip * row_total,
        momentum,
        orth,
        layer_mats,
        layer_zero,
        layer_ema,
        row_params,
        row_zero,
        row_ema,
        row_first,
        row_second,
    )


def body(*args):
    count, share = args[5].shape[1], args[9].shape[1]
    planes = lax.axis_size("fsdp") % PLANE == 0 and lax.axis_size("ns") == 2
    if planes and count % 192 == 0 and share % 48 == 0:
        return fast_body(*args)
    return plain_body(*args)


def solution(mesh):
    in_specs = (
        P(("fsdp", "ns"), None, None),
        P(("fsdp", "ns"), None),
        P(("fsdp", "ns")),
        P(("fsdp", "ns")),
        P(),
        P(None, "fsdp", None),
        P(None, "fsdp", None),
        P(None, "fsdp", None),
        P(None, "fsdp", None),
        P(None, "fsdp"),
        P(None, "fsdp"),
        P(None, "fsdp"),
        P(None, "fsdp"),
        P(None, "fsdp"),
    )
    out_specs = (
        P(),
        P(),
        P(),
        P(None, "fsdp", None),
        P(None, "fsdp", None),
        P(None, "fsdp", None),
        P(None, "fsdp", None),
        P(None, "fsdp"),
        P(None, "fsdp"),
        P(None, "fsdp"),
        P(None, "fsdp"),
        P(None, "fsdp"),
        P(None, "fsdp"),
    )
    return jax.shard_map(body, mesh=mesh, in_specs=in_specs, out_specs=out_specs, check_vma=False)
```

```python
import functools
import math

import jax
import jax.numpy as jnp
from jax import lax
from jax.experimental import pallas as pl
from jax.experimental.pallas import tpu as pltpu
from jax.sharding import PartitionSpec as P

HEADS = 12
HDIM = 64
PIX = 768
EMB = 512
SEQ = 256
NS_STEPS = 5
STEPS_DONE = 10


HIGHEST = lax.Precision.HIGHEST
norm_epsilon = 1e-05
unit_epsilon = 1e-06
logit_scale = 50.0
clip_bound = 0.001
momentum_decay = 0.95
muon_rate = 0.05
weight_decay = 0.05
adam_rate = 0.2
first_decay = 0.9
second_decay = 0.98
adam_floor = 1e-08
ema_decay = 0.9
mix_share = 0.5
coeff_linear = 3.4445
coeff_cubic = -4.775
coeff_quintic = 2.0315


def matmul(left, right):
    return jnp.dot(left, right, preferred_element_type=jnp.float32)


def matmul_nt(left, right):
    return lax.dot_general(
        left, right, (((1,), (1,)), ((), ())), preferred_element_type=jnp.float32
    )


def matmul_tn(left, right):
    return lax.dot_general(
        left, right, (((0,), (0,)), ((), ())), preferred_element_type=jnp.float32
    )


def norm_forward(inputs, gain, shift):
    center = inputs - jnp.mean(inputs, -1, keepdims=True)
    scale = lax.rsqrt(jnp.mean(center * center, -1, keepdims=True) + norm_epsilon)
    return center * scale * gain + shift


def norm_backward(inputs, gain, upstream):
    center = inputs - jnp.mean(inputs, -1, keepdims=True)
    scale = lax.rsqrt(jnp.mean(center * center, -1, keepdims=True) + norm_epsilon)
    normal = center * scale
    scaled_up = upstream * gain
    inner = scale * (
        scaled_up
        - jnp.mean(scaled_up, -1, keepdims=True)
        - normal * jnp.mean(scaled_up * normal, -1, keepdims=True)
    )
    return (inner, jnp.sum(upstream * normal, 0), jnp.sum(upstream, 0))


def attention_scores(parts, valid_mask):
    raw = jnp.einsum(
        "iqhd,ikhd->ihqk", parts[:, :, 0], parts[:, :, 1], preferred_element_type=jnp.float32
    )
    return jnp.where(valid_mask[:, None, None, :] > 0, raw * HDIM ** (-0.5), -1000000000.0)


BF = jnp.bfloat16
F32 = jnp.float32
MESH = pl.DeviceIdType.MESH
PLANE = 4


def guarded(pred, run):
    if pred is None:
        run()
    else:
        pl.when(pred)(run)


def both(first, second):
    if first is None:
        return second
    return first if second is None else jnp.logical_and(first, second)


def rows_at(start, count):
    return pl.ds(start if isinstance(start, int) else pl.multiple_of(start, 16), count)


class Links:
    def __init__(self, depth, send_sem, recv_sem):
        self.depth, self.send_sem, self.recv_sem = depth, send_sem, recv_sem
        self.me, self.x = lax.axis_index("fsdp"), lax.axis_index("ns")
        self.z, self.y, self.c = self.me // PLANE, lax.rem(self.me // 2, 2), lax.rem(self.me, 2)
        self.up = (self.at(self.z + 1, self.y, self.c), self.x)
        self.down = (self.at(self.z - 1, self.y, self.c), self.x)
        self.y_peer = (self.at(self.z, 1 - self.y, self.c), self.x)
        self.c_peer = (self.at(self.z, self.y, 1 - self.c), self.x)
        self.x_peer = (self.me, 1 - self.x)
        self.count, self.sent, self.waited = 0, [], set()

    def at(self, z, y, c):
        return PLANE * z + 2 * y + c

    def slot(self):
        self.count += 1
        return self.count - 1

    def greet(self):
        barrier = pltpu.get_barrier_semaphore()

        def signal(device):
            pl.semaphore_signal(barrier, inc=1, device_id=device, device_id_type=MESH)

        for device in (self.y_peer, self.x_peer, self.c_peer):
            signal(device)
        pl.when(self.z < self.depth - 1)(lambda: signal(self.up))
        pl.when(self.z > 0)(lambda: signal(self.down))
        inner = (self.z < self.depth - 1).astype(jnp.int32) + (self.z > 0).astype(jnp.int32)
        pl.semaphore_wait(barrier, 3 + inner)

    def copy(self, slot, source, target, device):
        return pltpu.make_async_remote_copy(
            src_ref=source,
            dst_ref=target,
            send_sem=self.send_sem.at[slot],
            recv_sem=self.recv_sem.at[slot],
            device_id=device,
            device_id_type=MESH,
        )

    def send(self, slot, source, target, device, pred=None):
        copy = self.copy(slot, source, target, device)
        guarded(pred, copy.start)
        self.sent.append((slot, pred, copy))

    def receive(self, slot, target, pred=None):
        guarded(pred, self.copy(slot, target, target, self.c_peer).wait_recv)

    def finish(self, slot=None):
        for number, pred, copy in self.sent:
            if number not in self.waited and (slot is None or number == slot):
                guarded(pred, copy.wait_send)
        if slot is not None:
            self.waited.add(slot)


def gather_item(links, own, target, count):
    depth, z, y, c, x = links.depth, links.z, links.y, links.c, links.x
    third = count // 3
    begin = x * third
    origin = (0, 0)
    keys = [(side, far) for far in range(1, depth) for side in (-1, 1)]
    z_slot = {key: links.slot() for key in keys}
    y_slot = {key: links.slot() for key in keys + [origin]}
    x_slot = {(key, o): links.slot() for key in keys + [origin] for o in (0, 1)}
    c_slot = {(key, o): links.slot() for key in keys + [origin] for o in (0, 1)}

    def part(shard):
        return target(shard).at[rows_at(begin, 2 * third)]

    def own_part():
        return own.at[rows_at(begin, 2 * third)]

    def third_of(shard, side):
        return target(shard).at[rows_at(side * 2 * third, third)]

    def shard(key, other, core=None):
        return links.at(z + key[0] * key[1], 1 - y if other else y, c if core is None else core)

    def exists(key):
        if key == origin:
            return None
        return z >= key[1] if key[0] < 0 else z + key[1] < depth

    def z_send(key):
        for side in (-1, 1) if key == origin else (key[0],):
            if key[1] + 1 < depth:
                source = own_part() if key == origin else part(shard(key, 0))
                links.send(
                    z_slot[(side, key[1] + 1)],
                    source,
                    part(shard(key, 0)),
                    links.up if side < 0 else links.down,
                    both(exists(key), z < depth - 1 if side < 0 else z > 0),
                )

    def y_send(key):
        source = own_part() if key == origin else part(shard(key, 0))
        links.send(y_slot[key], source, part(shard(key, 0)), links.y_peer, exists(key))

    def x_send(key, other):
        block = third_of(shard(key, other), x)
        links.send(x_slot[(key, other)], block, block, links.x_peer, exists(key))

    def c_send(key, other):
        whole = target(shard(key, other))
        source = own if (key, other) == (origin, 0) else whole
        links.send(c_slot[(key, other)], source, whole, links.c_peer, exists(key))

    order = []
    for far in range(1, depth):
        order += [((side, far), 0) for side in (-1, 1)]
        order += [(key, 1) for key in ([origin] if far == 1 else [(-1, far - 1), (1, far - 1)])]
    order += [((side, depth - 1), 1) for side in (-1, 1)]

    def start():
        z_send(origin)
        y_send(origin)
        c_send(origin, 0)

    def cross(keys_now):
        for key in keys_now:
            links.receive(y_slot[key], part(shard(key, 1)), exists(key))
            x_send(key, 1)

    def step(far):
        for side in (-1, 1):
            key = (side, far)
            links.receive(z_slot[key], part(shard(key, 0)), exists(key))
            z_send(key)
            y_send(key)
            x_send(key, 0)
        cross([origin] if far == 1 else [(-1, far - 1), (1, far - 1)])
        if far == depth - 1:
            cross([(-1, far), (1, far)])

    def share():
        for key, other in order:
            links.receive(x_slot[(key, other)], third_of(shard(key, other), 1 - x), exists(key))
            c_send(key, other)

    def settle():
        for key, other in [(origin, 0)] + order:
            links.receive(c_slot[(key, other)], target(shard(key, other, 1 - c)), exists(key))

    return start, step, share, settle


def gather_kernel(depth, halves, rows, mats, all_rows, all_mats, send_sem, recv_sem, local_sem):
    links = Links(depth, send_sem, recv_sem)
    links.greet()
    layers, count = mats.shape[:2]
    size = count // halves
    own = [pltpu.make_async_copy(rows, all_rows.at[links.me], local_sem.at[0])]
    items = [gather_item(links, rows, lambda shard: all_rows.at[shard], rows.shape[0])]
    for layer in range(layers):
        own.append(
            pltpu.make_async_copy(
                mats.at[layer], all_mats.at[layer, links.me], local_sem.at[1 + layer]
            )
        )
        for half in range(halves):
            block = pl.ds(half * size, size)

            def target(shard, layer=layer, block=block):
                return all_mats.at[layer, shard, block]

            items.append(gather_item(links, mats.at[layer, block], target, size))
    for copy in own:
        copy.start()
    items[0][0]()
    for number, (_, step, _, _) in enumerate(items):
        step(1)
        step(2)
        if number + 1 < len(items):
            items[number + 1][0]()
        if number > 0:
            items[number - 1][2]()
        for far in range(3, depth):
            step(far)
    items[-1][2]()
    for item in items:
        item[3]()
    links.finish()
    for copy in own:
        copy.wait()


def gather(depth, rows, mats):
    layers, count, width = mats.shape
    shards = PLANE * depth
    halves = 2
    slots = (1 + layers * halves) * 60
    any_space = pl.BlockSpec(memory_space=pl.ANY)
    return pl.pallas_call(
        functools.partial(gather_kernel, depth, halves),
        out_shape=(
            jax.ShapeDtypeStruct((shards,) + rows.shape, BF),
            jax.ShapeDtypeStruct((layers, shards, count, width), BF),
        ),
        in_specs=[any_space] * 2,
        out_specs=[any_space] * 2,
        scratch_shapes=[
            pltpu.SemaphoreType.DMA((slots,)),
            pltpu.SemaphoreType.DMA((slots,)),
            pltpu.SemaphoreType.DMA((1 + layers,)),
        ],
        name="gather_weights",
        compiler_params=pltpu.CompilerParams(collective_id=1, has_side_effects=True),
    )(rows, mats)


def accumulate(target, start, source, begin, count, step):
    @pl.loop(0, count // step)
    def _(turn):
        here = rows_at(start + turn * step, step)
        there = rows_at(begin + turn * step, step)
        target[here, :] = (target[here, :].astype(F32) + source[there, :].astype(F32)).astype(BF)


def scatter_group(links, dest, load, sizes, bufs, emit):
    depth, z, y, c, x = links.depth, links.z, links.y, links.c, links.x
    n, p, q, step = sizes
    mine, core_in, x_in, y_in, z_in, z_last, final = bufs
    core_slot, x_slot = [links.slot(), links.slot()], [links.slot(), links.slot()]
    q_slot, p_slot, low_slot, high_slot, last_slot = (links.slot() for _ in range(5))
    m = p + q
    first = x * p
    own_p, peer_p = x * m, (1 - x) * m
    sides = ((0, 1 - y), (1, y))

    def begin():
        for i, side in sides:
            load(i, side, mine.at[side], core_in.at[side], core_slot[i])

    def stage_core():
        for i, side in sides:
            load(i, side, mine.at[side], None, None)
            links.receive(core_slot[i], core_in.at[side])
            accumulate(mine.at[side], 0, core_in.at[side], 0, n, step)
            links.send(x_slot[i], mine.at[side, rows_at(peer_p, p)], x_in.at[side], links.x_peer)
            if i == 0:
                links.send(q_slot, mine.at[side, pl.ds(p, q)], y_in.at[pl.ds(0, q)], links.y_peer)

    def stage_x():
        for i, side in sides:
            links.receive(x_slot[i], x_in.at[side])
            accumulate(mine.at[side], own_p, x_in.at[side], 0, p, step)
            if i == 0:
                links.send(
                    p_slot, mine.at[side, rows_at(own_p, p)], y_in.at[pl.ds(q, p)], links.y_peer
                )
        links.receive(q_slot, y_in.at[pl.ds(0, q)])
        accumulate(mine.at[y], p, y_in, 0, q, step)

    def stage_y():
        links.receive(p_slot, y_in.at[pl.ds(q, p)])
        accumulate(mine.at[y], own_p, y_in, q, p, step)

    def stage_z(hop):
        block = mine.at[y, rows_at(first, m)]

        def take(slot, source, pred):
            @pl.when(pred)
            def _():
                links.receive(slot, source)
                accumulate(mine.at[y], first, source, 0, m, step)

        if dest > 0:
            if 1 <= hop <= dest:
                take(low_slot, z_in, z == hop)
            if hop < dest:
                links.send(low_slot, block, z_in, links.up, z == hop)
        if dest < depth - 1:
            turn = depth - 1 - hop
            if hop >= 1 and turn > dest:
                take(high_slot, z_in, z == turn)
            if turn > dest + 1:
                links.send(high_slot, block, z_in, links.down, z == turn)
            if turn == dest + 1:
                links.send(high_slot, block, z_last, links.down, z == turn)
            if turn == dest and hop >= 1:
                take(high_slot, z_last, z == dest)
        if hop == max(dest, depth - 1 - dest):
            links.send(last_slot, block, final, links.x_peer, z == dest)

    def stage_last():
        links.finish(x_slot[1])
        links.finish(last_slot)

        @pl.when(z == dest)
        def _():
            links.receive(last_slot, final)
            accumulate(mine.at[y], p, final, jnp.where(x == 0, 0, p), q, step)

            @pl.loop(0, p // 16)
            def _(turn):
                there = rows_at(jnp.where(x == 0, q, 0) + turn * 16, 16)
                mine[y, rows_at(peer_p + turn * 16, 16), :] = final[there, :]

            emit(mine.at[y])

    hops = [functools.partial(stage_z, hop) for hop in range(depth)]
    return begin, [stage_core, stage_x, stage_y] + hops + [stage_last]


def scatter_kernel(depth, layers, sub, lags, *refs):
    grads, row_grad = refs[: 4 * layers], refs[4 * layers]
    out, row_out = refs[4 * layers + 1 : 4 * layers + 3]
    big, small = refs[4 * layers + 3 : 4 * layers + 10], refs[4 * layers + 10 : 4 * layers + 17]
    send_sem, recv_sem, local_sem = refs[4 * layers + 17 :]
    links = Links(depth, send_sem, recv_sem)
    links.greet()
    y, c = links.y, links.c
    count = out.shape[1]
    n = count // sub
    p = n // 4 // 16 * 16
    groups = []

    def block_of(layer, shard, part):
        row = shard * count + part * n
        for matrix in grads[4 * layer : 4 * layer + 4]:
            if row < matrix.shape[0]:
                return matrix.at[pl.ds(row, n)]
            row -= matrix.shape[0]

    def add_group(dest, source, sizes, bufs, emit):
        number = len(groups)

        def load(i, side, mine, core_in, slot):
            sem = local_sem.at[2 * number + i]
            if core_in is None:
                pltpu.make_async_copy(source(0, 0), mine, sem).wait()
                return
            for y_now in (0, 1):
                for core in (0, 1):

                    @pl.when(jnp.logical_and(side == y_now, c == core))
                    def _():
                        pltpu.make_async_copy(source(y_now, core), mine, sem).start()
                        links.copy(slot, source(y_now, 1 - core), core_in, links.c_peer).start()

            links.sent.append((slot, None, links.copy(slot, source(0, 0), core_in, links.c_peer)))

        groups.append(scatter_group(links, dest, load, sizes, bufs, emit))

    def write(target, sem):
        def emit(result):
            copy = pltpu.make_async_copy(result, target, sem)
            copy.start()
            copy.wait()

        return emit

    end_sem = local_sem.at[local_sem.shape[0] - 1]
    for layer in reversed(range(layers)):
        for part in range(sub):
            for dest in (3, 0, 2, 1) if depth == 4 else reversed(range(depth)):
                number, spot = len(groups), layer * sub + part
                add_group(
                    dest,
                    lambda y_now, core, layer=layer, part=part, dest=dest: block_of(
                        layer, links.at(dest, y_now, core), part
                    ),
                    (n, p, n - 2 * p, 48),
                    [ref.at[number] for ref in big[:5]] + [ref.at[spot] for ref in big[5:]],
                    write(out.at[layer, pl.ds(part * n, n)], end_sem),
                )
    rows = row_out.shape[0]
    for dest in reversed(range(depth)):
        add_group(
            dest,
            lambda y_now, core, dest=dest: row_grad.at[links.at(dest, y_now, core)],
            (rows, 16, rows - 32, 16),
            [ref.at[dest] for ref in small[:5]] + list(small[5:]),
            write(row_out, end_sem),
        )
    for begin, _ in groups:
        begin()
    for turn in range(len(groups) + max(lags)):
        for place, lag in enumerate(lags):
            if 0 <= turn - lag < len(groups):
                groups[turn - lag][1][place]()
    links.finish()


def scatter(depth, grads, row_grad):
    layers = len(grads)
    shards = PLANE * depth
    width = grads[0][0].shape[1]
    count = sum(part.shape[0] for part in grads[0]) // shards
    sub = 3
    n = count // sub
    p = n // 4 // 16 * 16
    m = n - p
    blocks = layers * depth * sub
    rows, lanes = row_grad.shape[1:]
    row_m = rows - 16
    lags = [0, 3, 6] + [9 + 3 * hop for hop in range(depth)] + [9 + 3 * depth]

    def room(*shape):
        return pltpu.VMEM(shape, BF)

    any_space = pl.BlockSpec(memory_space=pl.ANY)
    slots = (blocks + depth) * 9
    return pl.pallas_call(
        functools.partial(scatter_kernel, depth, layers, sub, lags),
        out_shape=(
            jax.ShapeDtypeStruct((layers, count, width), BF),
            jax.ShapeDtypeStruct((rows, lanes), BF),
        ),
        in_specs=[any_space] * (4 * layers + 1),
        out_specs=[any_space] * 2,
        scratch_shapes=[
            room(blocks, 2, n, width),
            room(blocks, 2, n, width),
            room(blocks, 2, p, width),
            room(blocks, m, width),
            room(blocks, m, width),
            room(layers * sub, m, width),
            room(layers * sub, m, width),
            room(depth, 2, rows, lanes),
            room(depth, 2, rows, lanes),
            room(depth, 2, 16, lanes),
            room(depth, row_m, lanes),
            room(depth, row_m, lanes),
            room(row_m, lanes),
            room(row_m, lanes),
            pltpu.SemaphoreType.DMA((slots,)),
            pltpu.SemaphoreType.DMA((slots,)),
            pltpu.SemaphoreType.DMA((2 * (blocks + depth) + 1,)),
        ],
        name="scatter_gradients",
        compiler_params=pltpu.CompilerParams(
            collective_id=2, has_side_effects=True, vmem_limit_bytes=60 * 1024 * 1024
        ),
    )(*[part for layer in grads for part in layer], row_grad)


def finish_kernel(
    shards,
    sides,
    hyper,
    stats,
    grad,
    row_grad,
    momentum,
    mats,
    zero,
    ema,
    totals,
    new_momentum,
    new_mats,
    new_ema,
    new_mixed,
    grad_v,
    row_v,
    m_v,
    mats_v,
    zero_v,
    ema_v,
    x_v,
    short_v,
    low_v,
    note,
    inbox,
    send_sem,
    recv_sem,
    in_sem,
    out_sem,
):
    me = lax.axis_index("fsdp") * sides + lax.axis_index("ns")
    everyone = shards * sides
    layers, count, width = grad.shape
    pairs = [(grad, grad_v), (row_grad, row_v), (momentum, m_v)]
    pairs += [(mats, mats_v), (zero, zero_v), (ema, ema_v)]
    loads = [pltpu.make_async_copy(a, b, in_sem.at[i]) for i, (a, b) in enumerate(pairs)]
    for load in loads:
        load.start()
    barrier = pltpu.get_barrier_semaphore()

    def others(run):
        for number in range(everyone):
            pl.when(me != number)(functools.partial(run, number))

    def place(number):
        return (number // sides, number % sides)

    others(
        lambda number: pl.semaphore_signal(
            barrier, inc=1, device_id=place(number), device_id_type=MESH
        )
    )
    loads[0].wait()
    loads[1].wait()
    part = count // 3

    def blocks(run):
        @pl.loop(0, layers * 3)
        def _(turn):
            run(turn // 3, rows_at(lax.rem(turn, 3) * part, part))

    note[...] = stats[...]
    lane = lax.broadcasted_iota(jnp.int32, (8, 128), 1)
    sub = lax.broadcasted_iota(jnp.int32, (8, 128), 0)

    def add_squares(block):
        value = block.astype(F32)
        total = jnp.sum(value * value)
        note[...] += jnp.where((lane == 0) & (sub == 0), total, 0.0)

    blocks(lambda layer, rows: add_squares(grad_v[layer, rows, :]))
    add_squares(row_v[...])
    pl.semaphore_wait(barrier, everyone - 1)

    def mail(number):
        return pltpu.make_async_remote_copy(
            src_ref=note,
            dst_ref=inbox.at[me],
            send_sem=send_sem.at[number],
            recv_sem=recv_sem.at[me],
            device_id=place(number),
            device_id_type=MESH,
        )

    def collect(number):
        pltpu.make_async_remote_copy(
            src_ref=note,
            dst_ref=inbox.at[number],
            send_sem=send_sem.at[number],
            recv_sem=recv_sem.at[number],
            device_id=place(number),
            device_id_type=MESH,
        ).wait_recv()

    others(lambda number: mail(number).start())
    inbox[pl.ds(me, 1)] = note[...][None]
    others(collect)
    summed = jnp.sum(inbox[...], 0)
    others(lambda number: mail(number).wait_send())

    def pick(index):
        return jnp.sum(jnp.where((lane == index) & (sub == 0), summed, 0.0))

    loss_sum, weight_sum = pick(1), pick(2)
    norm = jnp.sqrt(jnp.full((8, 128), pick(0) / sides)) / weight_sum
    clip = jnp.minimum(1.0, clip_bound / (norm + 1e-06)) / weight_sum
    totals[...] = jnp.where(
        lane == 0,
        loss_sum,
        jnp.where(lane == 1, weight_sum, jnp.where(lane == 2, norm, clip)),
    )
    factor = clip[:1, :1]
    loads[2].wait()
    stores = []
    for layer in range(layers):
        total = jnp.zeros((1, 1), F32)
        for third in range(3):
            rows = pl.ds(third * part, part)
            value = momentum_decay * m_v[layer, rows, :] + factor * grad_v[layer, rows, :].astype(F32)
            m_v[layer, rows, :] = value
            total += jnp.sum(value * value, keepdims=True)
        store = pltpu.make_async_copy(m_v.at[layer], new_momentum.at[layer], out_sem.at[layer])
        store.start()
        stores.append(store)
        inverse = 1.0 / (jnp.sqrt(total) + 1e-07)
        for third in range(3):
            rows = pl.ds(third * part, part)
            value = m_v[layer, rows, :] * inverse
            x_v[layer, rows, :] = value
            short_v[0, layer, rows, :] = value.astype(BF)

    row_id = lax.broadcasted_iota(jnp.int32, (part, count), 0)
    col_id = lax.broadcasted_iota(jnp.int32, (part, count), 1)

    @pl.loop(0, NS_STEPS)
    def _(turn):
        now, later = lax.rem(turn, 2), 1 - lax.rem(turn, 2)
        shift = jnp.where(turn >= NS_STEPS - 2, 1.0, 0.0)
        linear = coeff_cubic + 2.0 * shift * coeff_quintic
        stay = coeff_linear + shift * (coeff_cubic + shift * coeff_quintic)
        for layer in range(layers):
            for third in range(3):
                rows = pl.ds(third * part, part)
                gram = matmul_nt(short_v[now, layer, rows, :], short_v[now, layer])
                gram -= jnp.where(row_id + third * part == col_id, shift, 0.0)
                low_v[layer, rows, :] = gram.astype(BF)
        for layer in range(layers):
            for third in range(3):
                rows = pl.ds(third * part, part)
                low = low_v[layer, rows, :]
                poly = linear * low.astype(F32) + coeff_quintic * matmul(low, low_v[layer])
                value = stay * x_v[layer, rows, :] + matmul(poly.astype(BF), short_v[now, layer])
                x_v[layer, rows, :] = value
                short_v[later, layer, rows, :] = value.astype(BF)

    for load in loads[3:]:
        load.wait()
    for layer in range(layers):
        for third in range(3):
            rows = pl.ds(third * part, part)
            old = mats_v[layer, rows, :]
            value = old - muon_rate * (
                hyper * x_v[layer, rows, :] + weight_decay * old
            )
            mats_v[layer, rows, :] = value
            ema_v[layer, rows, :] = ema_decay * ema_v[layer, rows, :] + (1.0 - ema_decay) * value
            zero_v[layer, rows, :] = mix_share * value + (1.0 - mix_share) * zero_v[layer, rows, :]
            for turn, (source, target) in enumerate(
                ((mats_v, new_mats), (ema_v, new_ema), (zero_v, new_mixed))
            ):
                sem = out_sem.at[layers + (layer * 3 + third) * 3 + turn]
                store = pltpu.make_async_copy(source.at[layer, rows], target.at[layer, rows], sem)
                store.start()
                stores.append(store)
    for store in stores:
        store.wait()


def finish(shards, sides, stats, grad, row_grad, momentum, mats, zero, ema):
    layers, count, width = grad.shape
    everyone = shards * sides
    full = jax.ShapeDtypeStruct(mats.shape, F32)
    any_space = pl.BlockSpec(memory_space=pl.ANY)
    vmem = pl.BlockSpec(memory_space=pltpu.VMEM)
    return pl.pallas_call(
        functools.partial(finish_kernel, shards, sides, 0.2 * math.sqrt(width)),
        out_shape=(jax.ShapeDtypeStruct((8, 128), F32), full, full, full, full),
        in_specs=[vmem] + [any_space] * 6,
        out_specs=[vmem] + [any_space] * 4,
        scratch_shapes=[
            pltpu.VMEM(grad.shape, BF),
            pltpu.VMEM(row_grad.shape, BF),
            pltpu.VMEM(mats.shape, F32),
            pltpu.VMEM(mats.shape, F32),
            pltpu.VMEM(mats.shape, F32),
            pltpu.VMEM(mats.shape, F32),
            pltpu.VMEM(mats.shape, F32),
            pltpu.VMEM((2,) + mats.shape, BF),
            pltpu.VMEM((layers, count, count), BF),
            pltpu.VMEM((8, 128), F32),
            pltpu.VMEM((everyone, 8, 128), F32),
            pltpu.SemaphoreType.DMA((everyone,)),
            pltpu.SemaphoreType.DMA((everyone,)),
            pltpu.SemaphoreType.DMA((6,)),
            pltpu.SemaphoreType.DMA((layers * 10,)),
        ],
        name="clip_and_orthogonalize",
        compiler_params=pltpu.CompilerParams(
            collective_id=3, has_side_effects=True, vmem_limit_bytes=56 * 1024 * 1024
        ),
    )(stats, grad, row_grad, momentum, mats, zero, ema)


def gather_layer(shard):
    return lax.all_gather(shard.astype(jnp.bfloat16), "fsdp", axis=0, tiled=True)


def layer_forward(resid, weight_tensors, vector, valid_mask):
    images, seq = valid_mask.shape
    width = resid.shape[1]
    ffn = 4 * width
    normed = norm_forward(resid, vector[0], vector[1]).astype(jnp.bfloat16)
    bias = jnp.concatenate([vector[2], jnp.zeros_like(vector[2]), vector[3]])
    project = (matmul_nt(normed, weight_tensors[: 3 * width]) + bias).astype(jnp.bfloat16)
    parts = project.reshape(images, seq, 3, HEADS, HDIM)
    scores = attention_scores(parts, valid_mask)
    top_score = jnp.max(scores, -1, keepdims=True)
    expo = jnp.exp(scores - top_score)
    totals = jnp.sum(expo, -1, keepdims=True)
    log_total = top_score + jnp.log(totals)
    probs = (expo / totals).astype(jnp.bfloat16)
    context = jnp.einsum(
        "ihqk,ikhd->iqhd", probs, parts[:, :, 2], preferred_element_type=jnp.float32
    )
    context = context.reshape(images * seq, width).astype(jnp.bfloat16)
    mixed = resid + (matmul_nt(context, weight_tensors[3 * width : 4 * width]) + vector[4])
    normed_two = norm_forward(mixed, vector[5], vector[6]).astype(jnp.bfloat16)
    hidden_pre = matmul_nt(normed_two, weight_tensors[4 * width : 4 * width + ffn]) + vector[
        8:12
    ].reshape(ffn)
    hidden = (hidden_pre * jax.nn.sigmoid(1.702 * hidden_pre)).astype(jnp.bfloat16)
    output = mixed + (matmul(hidden, weight_tensors[4 * width + ffn :]) + vector[7])
    return (
        output,
        (resid, normed, project, log_total, context, mixed, normed_two, hidden_pre, hidden),
    )


def layer_backward(upstream, weight_tensors, vector, valid_mask, saved_activation):
    resid, normed, project, log_total, context, mixed, normed_two, hidden_pre, hidden = (
        saved_activation
    )
    images, seq = valid_mask.shape
    width = resid.shape[1]
    ffn = 4 * width
    out_grad = upstream.astype(jnp.bfloat16)
    grad_down = matmul_tn(hidden, out_grad)
    hidden_grad = matmul_nt(out_grad, weight_tensors[4 * width + ffn :])
    gate = jax.nn.sigmoid(1.702 * hidden_pre)
    pre_grad = (hidden_grad * (gate + 1.702 * hidden_pre * gate * (1.0 - gate))).astype(
        jnp.bfloat16
    )
    grad_up = matmul_tn(pre_grad, normed_two)
    second_in, gain_two, shift_two = norm_backward(
        mixed, vector[5], matmul(pre_grad, weight_tensors[4 * width : 4 * width + ffn])
    )
    mixed_grad = upstream + second_in
    attn_grad = mixed_grad.astype(jnp.bfloat16)
    grad_out = matmul_tn(attn_grad, context)
    context_grad = matmul(attn_grad, weight_tensors[3 * width : 4 * width]).astype(jnp.bfloat16)
    context_grad = context_grad.reshape(images, seq, HEADS, HDIM)
    parts = project.reshape(images, seq, 3, HEADS, HDIM)
    probs = jnp.exp(attention_scores(parts, valid_mask) - log_total)
    prob_grad = jnp.einsum(
        "iqhd,ikhd->ihqk", context_grad, parts[:, :, 2], preferred_element_type=jnp.float32
    )
    value_grad = jnp.einsum(
        "ihqk,iqhd->ikhd",
        probs.astype(jnp.bfloat16),
        context_grad,
        preferred_element_type=jnp.float32,
    )
    score_grad = (probs * (prob_grad - jnp.sum(prob_grad * probs, -1, keepdims=True))).astype(
        jnp.bfloat16
    )
    query_grad = jnp.einsum(
        "ihqk,ikhd->iqhd", score_grad, parts[:, :, 1], preferred_element_type=jnp.float32
    ) * HDIM ** (-0.5)
    key_grad = jnp.einsum(
        "ihqk,iqhd->ikhd", score_grad, parts[:, :, 0], preferred_element_type=jnp.float32
    ) * HDIM ** (-0.5)
    project_grad = (
        jnp.stack([query_grad, key_grad, value_grad], 2)
        .reshape(images * seq, 3 * width)
        .astype(jnp.bfloat16)
    )
    project_sum = jnp.sum(project_grad.astype(jnp.float32), 0)
    grad_qkv = matmul_tn(project_grad, normed)
    first_in, gain_one, shift_one = norm_backward(
        resid, vector[0], matmul(project_grad, weight_tensors[: 3 * width])
    )
    residual_gradient = mixed_grad + first_in
    grad_matrix = [part.astype(BF) for part in (grad_qkv, grad_out, grad_up, grad_down)]
    grad_vector = jnp.concatenate(
        [
            jnp.stack(
                [
                    gain_one,
                    shift_one,
                    project_sum[:width],
                    project_sum[2 * width :],
                    jnp.sum(attn_grad.astype(jnp.float32), 0),
                    gain_two,
                    shift_two,
                    jnp.sum(out_grad.astype(jnp.float32), 0),
                ]
            ),
            jnp.sum(pre_grad.astype(jnp.float32), 0).reshape(4, width),
        ],
        0,
    )
    return (residual_gradient, grad_matrix, grad_vector)


def newton_schulz(blocks):
    frob = jnp.sqrt(jnp.sum(blocks * blocks, axis=(1, 2), keepdims=True)) + 1e-07
    blocks = blocks / frob
    unit = jnp.eye(blocks.shape[1], dtype=jnp.float32)
    for turn in range(NS_STEPS):
        shift = 1.0 if turn >= NS_STEPS - 2 else 0.0
        short = blocks.astype(BF)
        gram = jnp.einsum("lcd,led->lce", short, short, preferred_element_type=F32) - shift * unit
        low = gram.astype(BF)
        square = jnp.einsum("lce,lef->lcf", low, low, preferred_element_type=F32)
        poly = (coeff_cubic + 2.0 * shift * coeff_quintic) * gram + coeff_quintic * square
        stay = coeff_linear + shift * (coeff_cubic + shift * coeff_quintic)
        blocks = stay * blocks + jnp.einsum(
            "lce,led->lcd", poly.astype(BF), short, preferred_element_type=F32
        )
    return blocks


def row_updates(clipped, layers, row_params, row_zero, row_ema, row_first, row_second):
    front = PIX + EMB + SEQ + 4
    new_first = first_decay * row_first + (1.0 - first_decay) * clipped
    new_second = second_decay * row_second + (1.0 - second_decay) * clipped * clipped
    down_bias_grad = clipped[front:].reshape(layers, 12, row_params.shape[1])[:, 7]
    step_size = (
        new_first
        / (1.0 - first_decay**STEPS_DONE)
        / (jnp.sqrt(new_second / (1.0 - second_decay**STEPS_DONE)) + adam_floor)
    )
    new_rows = row_params - adam_rate * (step_size + weight_decay * row_params)
    ema_rows = ema_decay * row_ema + (1.0 - ema_decay) * new_rows
    mixed_rows = mix_share * new_rows + (1.0 - mix_share) * row_zero
    return (new_rows, new_first, new_second, ema_rows, mixed_rows, down_bias_grad)


def plain_body(
    patches,
    pad_mask,
    labels,
    loss_weights,
    class_emb,
    layer_mats,
    layer_zero,
    layer_ema,
    layer_momentum,
    row_params,
    row_zero,
    row_ema,
    row_first,
    row_second,
):
    layers, columns, width = layer_mats.shape
    images, seq, pixels = patches.shape
    front = PIX + EMB + SEQ + 4
    valid_mask = pad_mask.astype(jnp.float32)
    gathered_rows = lax.all_gather(row_params.astype(jnp.bfloat16), "fsdp", axis=1, tiled=True)
    rows_value = gathered_rows.astype(jnp.float32)
    patch_weight = gathered_rows[:PIX]
    proj_rows = gathered_rows[PIX : PIX + EMB]
    position = rows_value[PIX + EMB : PIX + EMB + SEQ]
    head_vec = rows_value[PIX + EMB + SEQ : front]
    layer_vector_params = rows_value[front:].reshape(layers, 12, width)
    flat_patches = patches.reshape(images * seq, pixels)
    embedded = (matmul(flat_patches, patch_weight).reshape(images, seq, width) + position).reshape(
        images * seq, width
    )
    resid = norm_forward(embedded, head_vec[0], head_vec[1])
    kept_weights = []
    saved_activations = []
    for layer_number in range(layers):
        weight_tensors = gather_layer(layer_mats[layer_number])
        kept_weights.append(weight_tensors)
        resid, saved_activation = layer_forward(
            resid, weight_tensors, layer_vector_params[layer_number], valid_mask
        )
        saved_activations.append(saved_activation)
    counts = jnp.sum(valid_mask, -1, keepdims=True)
    pooled = jnp.sum(resid.reshape(images, seq, width) * valid_mask[..., None], 1) / counts
    pooled_norm = norm_forward(pooled, head_vec[2], head_vec[3]).astype(jnp.bfloat16)
    feature = matmul_nt(pooled_norm, proj_rows)
    inv_length = lax.rsqrt(jnp.sum(feature * feature, -1, keepdims=True) + unit_epsilon)
    unit_feat = (feature * inv_length).astype(jnp.bfloat16)
    classes = class_emb.astype(jnp.float32)
    class_unit = (
        classes * lax.rsqrt(jnp.sum(classes * classes, -1, keepdims=True) + unit_epsilon)
    ).astype(jnp.bfloat16)
    logits = logit_scale * matmul_nt(unit_feat, class_unit)
    top_logit = jnp.max(logits, -1, keepdims=True)
    shifted = jnp.exp(logits - top_logit)
    total_exp = jnp.sum(shifted, -1, keepdims=True)
    log_norm = top_logit + jnp.log(total_exp)
    onehot = (jnp.arange(logits.shape[1])[None, :] == labels[:, None]).astype(jnp.float32)
    losses = log_norm[:, 0] - jnp.sum(onehot * logits, -1)
    weights_value = loss_weights.astype(jnp.float32)
    loss_sum, weight_sum = lax.psum(
        (jnp.sum(weights_value * losses), jnp.sum(weights_value)), ("fsdp", "ns")
    )
    seed = weights_value / weight_sum
    logit_grad = seed[:, None] * (shifted / total_exp - onehot)
    unit_grad = logit_scale * jnp.dot(logit_grad, class_unit.astype(jnp.float32), precision=HIGHEST)
    feat_grad = inv_length * unit_grad - feature * inv_length**3 * jnp.sum(
        unit_grad * feature, -1, keepdims=True
    )
    grad_proj = jnp.dot(feat_grad.T, pooled_norm.astype(jnp.float32), precision=HIGHEST)
    pooled_grad, gain_post, shift_post = norm_backward(
        pooled, head_vec[2], jnp.dot(feat_grad, proj_rows.astype(jnp.float32), precision=HIGHEST)
    )
    residual_gradient = (valid_mask[..., None] * (pooled_grad / counts)[:, None, :]).reshape(
        images * seq, width
    )
    grad_mats = [None] * layers
    grad_vecs = [None] * layers
    for layer_number in reversed(range(layers)):
        weight_tensors = kept_weights[layer_number]
        residual_gradient, grad_matrix, grad_vector = layer_backward(
            residual_gradient,
            weight_tensors,
            layer_vector_params[layer_number],
            valid_mask,
            saved_activations[layer_number],
        )
        grad_mats[layer_number], grad_vecs[layer_number] = (
            lax.psum_scatter(
                jnp.concatenate(grad_matrix, 0), "fsdp", scatter_dimension=0, tiled=True
            ),
            lax.psum_scatter(grad_vector, "fsdp", scatter_dimension=1, tiled=True),
        )
    embed_grad, gain_pre, shift_pre = norm_backward(embedded, head_vec[0], residual_gradient)
    position_grad = jnp.sum(embed_grad.reshape(images, seq, width), 0)
    patch_grad = matmul_tn(flat_patches, embed_grad.astype(jnp.bfloat16))
    front_grad = jnp.concatenate(
        [
            patch_grad,
            grad_proj,
            position_grad,
            jnp.stack([gain_pre, shift_pre, gain_post, shift_post]),
        ],
        0,
    )
    front_shard = lax.psum_scatter(front_grad, "fsdp", scatter_dimension=1, tiled=True)
    mat_grad = jnp.stack(grad_mats)
    row_grad = jnp.concatenate([front_shard] + grad_vecs, 0)
    pairs = lax.axis_size("ns")
    side = lax.axis_index("ns")
    half_depth = width // pairs
    half_rows = row_grad.shape[0] // pairs
    mat_total, row_total = (
        lax.psum(mat_grad.astype(jnp.bfloat16), "ns").astype(jnp.float32),
        lax.psum(row_grad.astype(jnp.bfloat16), "ns").astype(jnp.float32),
    )
    mat_half = lax.dynamic_slice_in_dim(mat_total, side * half_depth, half_depth, 2)
    row_half = lax.dynamic_slice_in_dim(row_total, side * half_rows, half_rows, 0)
    squares = jnp.sum(mat_half * mat_half) + jnp.sum(row_half * row_half)
    grad_norm = jnp.sqrt(lax.psum(squares, ("fsdp", "ns")))
    clip = jnp.minimum(1.0, clip_bound / (grad_norm + 1e-06))
    momentum = momentum_decay * layer_momentum + clip * mat_total
    orth = newton_schulz(momentum)
    new_mats = layer_mats - muon_rate * (0.2 * math.sqrt(width) * orth + weight_decay * layer_mats)
    ema_mats = ema_decay * layer_ema + (1.0 - ema_decay) * new_mats
    mixed_mats = mix_share * new_mats + (1.0 - mix_share) * layer_zero
    return (loss_sum, weight_sum, grad_norm, new_mats, momentum, ema_mats, mixed_mats) + row_updates(
        clip * row_total, layers, row_params, row_zero, row_ema, row_first, row_second
    )


def fast_body(
    patches,
    pad_mask,
    labels,
    loss_weights,
    class_emb,
    layer_mats,
    layer_zero,
    layer_ema,
    layer_momentum,
    row_params,
    row_zero,
    row_ema,
    row_first,
    row_second,
):
    layers, columns, width = layer_mats.shape
    images, seq, pixels = patches.shape
    shards = lax.axis_size("fsdp")
    depth = shards // PLANE
    rows, share = row_params.shape
    front = PIX + EMB + SEQ + 4
    lanes = -(-rows // 128) * 128
    valid_mask = pad_mask.astype(F32)
    sent_rows = jnp.pad(row_params.T.astype(BF), ((0, 0), (0, lanes - rows)))
    all_rows, all_mats = gather(depth, sent_rows, layer_mats.astype(BF))
    table = all_rows.reshape(width, lanes)
    weights = all_mats.reshape(layers, shards * columns, width)
    patch_weight, proj = table[:, :PIX], table[:, PIX : PIX + EMB]
    position = table[:, PIX + EMB : PIX + EMB + SEQ].T.astype(F32)
    vectors = table[:, PIX + EMB + SEQ : rows].T.astype(F32)
    head_vec = vectors[:4]
    layer_vector_params = vectors[4:].reshape(layers, 12, width)
    flat_patches = patches.reshape(images * seq, pixels)
    embedded = (
        matmul_nt(flat_patches, patch_weight).reshape(images, seq, width) + position
    ).reshape(images * seq, width)
    resid = norm_forward(embedded, head_vec[0], head_vec[1])
    saved_activations = []
    for layer_number in range(layers):
        resid, saved_activation = layer_forward(
            resid, weights[layer_number], layer_vector_params[layer_number], valid_mask
        )
        saved_activations.append(saved_activation)
    counts = jnp.sum(valid_mask, -1, keepdims=True)
    pooled = jnp.sum(resid.reshape(images, seq, width) * valid_mask[..., None], 1) / counts
    pooled_norm = norm_forward(pooled, head_vec[2], head_vec[3]).astype(BF)
    feature = matmul(pooled_norm, proj)
    inv_length = lax.rsqrt(jnp.sum(feature * feature, -1, keepdims=True) + unit_epsilon)
    unit_feat = (feature * inv_length).astype(BF)
    classes = class_emb.astype(F32)
    class_unit = (
        classes * lax.rsqrt(jnp.sum(classes * classes, -1, keepdims=True) + unit_epsilon)
    ).astype(BF)
    logits = logit_scale * matmul_nt(unit_feat, class_unit)
    top_logit = jnp.max(logits, -1, keepdims=True)
    shifted = jnp.exp(logits - top_logit)
    total_exp = jnp.sum(shifted, -1, keepdims=True)
    log_norm = top_logit + jnp.log(total_exp)
    onehot = (jnp.arange(logits.shape[1])[None, :] == labels[:, None]).astype(F32)
    losses = log_norm[:, 0] - jnp.sum(onehot * logits, -1)
    weights_value = loss_weights.astype(F32)
    logit_grad = weights_value[:, None] * (shifted / total_exp - onehot)
    unit_grad = logit_scale * jnp.dot(logit_grad, class_unit.astype(F32), precision=HIGHEST)
    feat_grad = inv_length * unit_grad - feature * inv_length**3 * jnp.sum(
        unit_grad * feature, -1, keepdims=True
    )
    grad_proj = jnp.dot(pooled_norm.astype(F32).T, feat_grad, precision=HIGHEST)
    pooled_grad, gain_post, shift_post = norm_backward(
        pooled,
        head_vec[2],
        lax.dot_general(
            feat_grad, proj.astype(F32), (((1,), (1,)), ((), ())), precision=HIGHEST
        ),
    )
    upstream = (valid_mask[..., None] * (pooled_grad / counts)[:, None, :]).reshape(
        images * seq, width
    )
    grad_mats = [None] * layers
    grad_vecs = [None] * layers
    for layer_number in reversed(range(layers)):
        upstream, grad_mats[layer_number], grad_vecs[layer_number] = layer_backward(
            upstream,
            weights[layer_number],
            layer_vector_params[layer_number],
            valid_mask,
            saved_activations[layer_number],
        )
    embed_grad, gain_pre, shift_pre = norm_backward(embedded, head_vec[0], upstream)
    position_grad = jnp.sum(embed_grad.reshape(images, seq, width), 0)
    patch_grad = matmul_tn(embed_grad.astype(BF), flat_patches)
    vector_grad = jnp.concatenate(
        [jnp.stack([gain_pre, shift_pre, gain_post, shift_post])] + grad_vecs, 0
    )
    row_grad = jnp.concatenate(
        [patch_grad, grad_proj, position_grad.T, vector_grad.T, jnp.zeros((width, lanes - rows))], 1
    )
    mat_total, row_total = scatter(
        depth, grad_mats, row_grad.astype(BF).reshape(shards, share, lanes)
    )
    lane = lax.broadcasted_iota(jnp.int32, (8, 128), 1)
    first = lax.broadcasted_iota(jnp.int32, (8, 128), 0) == 0
    stats = jnp.where(first & (lane == 1), jnp.sum(weights_value * losses), 0.0)
    stats = jnp.where(first & (lane == 2), jnp.sum(weights_value), stats)
    totals, momentum, new_mats, ema_mats, mixed_mats = finish(
        shards,
        lax.axis_size("ns"),
        stats,
        mat_total,
        row_total,
        layer_momentum,
        layer_mats,
        layer_zero,
        layer_ema,
    )
    loss_sum, weight_sum, grad_norm, clip = (totals[0, turn] for turn in range(4))
    clipped = clip * row_total.astype(F32)[:, :rows].T
    return (loss_sum, weight_sum, grad_norm, new_mats, momentum, ema_mats, mixed_mats) + row_updates(
        clipped, layers, row_params, row_zero, row_ema, row_first, row_second
    )


def body(*args):
    count, share = args[5].shape[1], args[9].shape[1]
    planes = lax.axis_size("fsdp") % PLANE == 0 and lax.axis_size("ns") == 2
    if planes and count % 192 == 0 and share % 48 == 0:
        return fast_body(*args)
    return plain_body(*args)


def solution(mesh):
    in_specs = (
        P(("fsdp", "ns"), None, None),
        P(("fsdp", "ns"), None),
        P(("fsdp", "ns")),
        P(("fsdp", "ns")),
        P(),
        P(None, "fsdp", None),
        P(None, "fsdp", None),
        P(None, "fsdp", None),
        P(None, "fsdp", None),
        P(None, "fsdp"),
        P(None, "fsdp"),
        P(None, "fsdp"),
        P(None, "fsdp"),
        P(None, "fsdp"),
    )
    out_specs = (
        P(),
        P(),
        P(),
        P(None, "fsdp", None),
        P(None, "fsdp", None),
        P(None, "fsdp", None),
        P(None, "fsdp", None),
        P(None, "fsdp"),
        P(None, "fsdp"),
        P(None, "fsdp"),
        P(None, "fsdp"),
        P(None, "fsdp"),
        P(None, "fsdp"),
    )
    return jax.shard_map(body, mesh=mesh, in_specs=in_specs, out_specs=out_specs, check_vma=False)
```

```python
import functools
import math
from typing import NamedTuple

import jax
import jax.numpy as jnp
from jax import lax
from jax.experimental import pallas as pl
from jax.experimental.pallas import tpu as pltpu
from jax.sharding import PartitionSpec as P

HEADS = 12
HDIM = 64
PIX = 768
EMB = 512
SEQ = 256
NS_STEPS = 5
STEPS_DONE = 10


HIGHEST = lax.Precision.HIGHEST
norm_epsilon = 1e-05
unit_epsilon = 1e-06
logit_scale = 50.0
clip_bound = 0.001
momentum_decay = 0.95
muon_rate = 0.05
weight_decay = 0.05
adam_rate = 0.2
first_decay = 0.9
second_decay = 0.98
adam_floor = 1e-08
ema_decay = 0.9
mix_share = 0.5
coeff_linear = 3.4445
coeff_cubic = -4.775
coeff_quintic = 2.0315


def matmul(left, right):
    return jnp.dot(left, right, preferred_element_type=jnp.float32)


def matmul_nt(left, right):
    return lax.dot_general(
        left, right, (((1,), (1,)), ((), ())), preferred_element_type=jnp.float32
    )


def matmul_tn(left, right):
    return lax.dot_general(
        left, right, (((0,), (0,)), ((), ())), preferred_element_type=jnp.float32
    )


def norm_forward(inputs, gain, shift):
    center = inputs - jnp.mean(inputs, -1, keepdims=True)
    scale = lax.rsqrt(jnp.mean(center * center, -1, keepdims=True) + norm_epsilon)
    return center * scale * gain + shift


def norm_backward(inputs, gain, upstream):
    center = inputs - jnp.mean(inputs, -1, keepdims=True)
    scale = lax.rsqrt(jnp.mean(center * center, -1, keepdims=True) + norm_epsilon)
    normal = center * scale
    scaled_up = upstream * gain
    inner = scale * (
        scaled_up
        - jnp.mean(scaled_up, -1, keepdims=True)
        - normal * jnp.mean(scaled_up * normal, -1, keepdims=True)
    )
    return (inner, jnp.sum(upstream * normal, 0), jnp.sum(upstream, 0))


def attention_scores(parts, valid_mask):
    raw = jnp.einsum(
        "iqhd,ikhd->ihqk", parts[:, :, 0], parts[:, :, 1], preferred_element_type=jnp.float32
    )
    return jnp.where(valid_mask[:, None, None, :] > 0, raw * HDIM ** (-0.5), -1000000000.0)


BF = jnp.bfloat16
F32 = jnp.float32
MESH = pl.DeviceIdType.MESH
PLANE = 4


def guarded(pred, run):
    if pred is None:
        run()
    else:
        pl.when(pred)(run)


def both(first, second):
    if first is None:
        return second
    return first if second is None else jnp.logical_and(first, second)


def rows_at(start, count):
    return pl.ds(start if isinstance(start, int) else pl.multiple_of(start, 16), count)


class Links:
    def __init__(self, depth, send_sem, recv_sem):
        self.depth, self.send_sem, self.recv_sem = depth, send_sem, recv_sem
        self.me, self.x = lax.axis_index("fsdp"), lax.axis_index("ns")
        self.z, self.y, self.c = self.me // PLANE, lax.rem(self.me // 2, 2), lax.rem(self.me, 2)
        self.up = (self.at(self.z + 1, self.y, self.c), self.x)
        self.down = (self.at(self.z - 1, self.y, self.c), self.x)
        self.y_peer = (self.at(self.z, 1 - self.y, self.c), self.x)
        self.c_peer = (self.at(self.z, self.y, 1 - self.c), self.x)
        self.x_peer = (self.me, 1 - self.x)
        self.count, self.sent, self.waited = 0, [], set()

    def at(self, z, y, c):
        return PLANE * z + 2 * y + c

    def slot(self):
        self.count += 1
        return self.count - 1

    def greet(self):
        barrier = pltpu.get_barrier_semaphore()

        def signal(device):
            pl.semaphore_signal(barrier, inc=1, device_id=device, device_id_type=MESH)

        for device in (self.y_peer, self.x_peer, self.c_peer):
            signal(device)
        pl.when(self.z < self.depth - 1)(lambda: signal(self.up))
        pl.when(self.z > 0)(lambda: signal(self.down))
        inner = (self.z < self.depth - 1).astype(jnp.int32) + (self.z > 0).astype(jnp.int32)
        pl.semaphore_wait(barrier, 3 + inner)

    def copy(self, slot, source, target, device):
        return pltpu.make_async_remote_copy(
            src_ref=source,
            dst_ref=target,
            send_sem=self.send_sem.at[slot],
            recv_sem=self.recv_sem.at[slot],
            device_id=device,
            device_id_type=MESH,
        )

    def send(self, slot, source, target, device, pred=None):
        copy = self.copy(slot, source, target, device)
        guarded(pred, copy.start)
        self.sent.append((slot, pred, copy))

    def receive(self, slot, target, pred=None):
        guarded(pred, self.copy(slot, target, target, self.c_peer).wait_recv)

    def finish(self, slot=None):
        for number, pred, copy in self.sent:
            if number not in self.waited and (slot is None or number == slot):
                guarded(pred, copy.wait_send)
        if slot is not None:
            self.waited.add(slot)


def gather_item(links, own, target, count):
    depth, z, y, c, x = links.depth, links.z, links.y, links.c, links.x
    third = count // 3
    begin = x * third
    origin = (0, 0)
    keys = [(side, far) for far in range(1, depth) for side in (-1, 1)]
    z_slot = {key: links.slot() for key in keys}
    y_slot = {key: links.slot() for key in keys + [origin]}
    x_slot = {(key, o): links.slot() for key in keys + [origin] for o in (0, 1)}
    c_slot = {(key, o): links.slot() for key in keys + [origin] for o in (0, 1)}

    def part(shard):
        return target(shard).at[rows_at(begin, 2 * third)]

    def own_part():
        return own.at[rows_at(begin, 2 * third)]

    def third_of(shard, side):
        return target(shard).at[rows_at(side * 2 * third, third)]

    def shard(key, other, core=None):
        return links.at(z + key[0] * key[1], 1 - y if other else y, c if core is None else core)

    def exists(key):
        if key == origin:
            return None
        return z >= key[1] if key[0] < 0 else z + key[1] < depth

    def z_send(key):
        for side in (-1, 1) if key == origin else (key[0],):
            if key[1] + 1 < depth:
                source = own_part() if key == origin else part(shard(key, 0))
                links.send(
                    z_slot[(side, key[1] + 1)],
                    source,
                    part(shard(key, 0)),
                    links.up if side < 0 else links.down,
                    both(exists(key), z < depth - 1 if side < 0 else z > 0),
                )

    def y_send(key):
        source = own_part() if key == origin else part(shard(key, 0))
        links.send(y_slot[key], source, part(shard(key, 0)), links.y_peer, exists(key))

    def x_send(key, other):
        block = third_of(shard(key, other), x)
        links.send(x_slot[(key, other)], block, block, links.x_peer, exists(key))

    def c_send(key, other):
        whole = target(shard(key, other))
        source = own if (key, other) == (origin, 0) else whole
        links.send(c_slot[(key, other)], source, whole, links.c_peer, exists(key))

    order = []
    for far in range(1, depth):
        order += [((side, far), 0) for side in (-1, 1)]
        order += [(key, 1) for key in ([origin] if far == 1 else [(-1, far - 1), (1, far - 1)])]
    order += [((side, depth - 1), 1) for side in (-1, 1)]

    def start():
        z_send(origin)
        y_send(origin)
        c_send(origin, 0)

    def cross(keys_now):
        for key in keys_now:
            links.receive(y_slot[key], part(shard(key, 1)), exists(key))
            x_send(key, 1)

    def step(far):
        for side in (-1, 1):
            key = (side, far)
            links.receive(z_slot[key], part(shard(key, 0)), exists(key))
            z_send(key)
            y_send(key)
            x_send(key, 0)
        cross([origin] if far == 1 else [(-1, far - 1), (1, far - 1)])
        if far == depth - 1:
            cross([(-1, far), (1, far)])

    def share():
        for key, other in order:
            links.receive(x_slot[(key, other)], third_of(shard(key, other), 1 - x), exists(key))
            c_send(key, other)

    def settle():
        for key, other in [(origin, 0)] + order:
            links.receive(c_slot[(key, other)], target(shard(key, other, 1 - c)), exists(key))

    return start, step, share, settle


def gather_kernel(depth, halves, rows, mats, all_rows, all_mats, send_sem, recv_sem, local_sem):
    links = Links(depth, send_sem, recv_sem)
    links.greet()
    layers, count = mats.shape[:2]
    size = count // halves
    own = [pltpu.make_async_copy(rows, all_rows.at[links.me], local_sem.at[0])]
    items = [gather_item(links, rows, lambda shard: all_rows.at[shard], rows.shape[0])]
    for layer in range(layers):
        own.append(
            pltpu.make_async_copy(
                mats.at[layer], all_mats.at[layer, links.me], local_sem.at[1 + layer]
            )
        )
        for half in range(halves):
            block = pl.ds(half * size, size)

            def target(shard, layer=layer, block=block):
                return all_mats.at[layer, shard, block]

            items.append(gather_item(links, mats.at[layer, block], target, size))
    for copy in own:
        copy.start()
    items[0][0]()
    for number, (_, step, _, _) in enumerate(items):
        step(1)
        step(2)
        if number + 1 < len(items):
            items[number + 1][0]()
        if number > 0:
            items[number - 1][2]()
        for far in range(3, depth):
            step(far)
    items[-1][2]()
    for item in items:
        item[3]()
    links.finish()
    for copy in own:
        copy.wait()


def gather(depth, rows, mats):
    layers, count, width = mats.shape
    shards = PLANE * depth
    halves = 2
    slots = (1 + layers * halves) * 60
    any_space = pl.BlockSpec(memory_space=pl.ANY)
    return pl.pallas_call(
        functools.partial(gather_kernel, depth, halves),
        out_shape=(
            jax.ShapeDtypeStruct((shards,) + rows.shape, BF),
            jax.ShapeDtypeStruct((layers, shards, count, width), BF),
        ),
        in_specs=[any_space] * 2,
        out_specs=[any_space] * 2,
        scratch_shapes=[
            pltpu.SemaphoreType.DMA((slots,)),
            pltpu.SemaphoreType.DMA((slots,)),
            pltpu.SemaphoreType.DMA((1 + layers,)),
        ],
        name="gather_weights",
        compiler_params=pltpu.CompilerParams(collective_id=1, has_side_effects=True),
    )(rows, mats)


def accumulate(target, start, source, begin, count, step):
    @pl.loop(0, count // step)
    def _(turn):
        here = rows_at(start + turn * step, step)
        there = rows_at(begin + turn * step, step)
        target[here, :] = (target[here, :].astype(F32) + source[there, :].astype(F32)).astype(BF)


class Group(NamedTuple):
    begin: object
    stages: list
    core_slot: list


def scatter_group(links, dest, load, sizes, bufs, emit, used=None):
    depth, z, y, c, x = links.depth, links.z, links.y, links.c, links.x
    n, p, q, step = sizes
    mine, core_in, x_in, y_in, z_in, z_last, final = bufs
    core_slot, x_slot = [links.slot(), links.slot()], [links.slot(), links.slot()]
    q_slot, p_slot, low_slot, high_slot, last_slot = (links.slot() for _ in range(5))
    m = p + q
    first = x * p
    own_p, peer_p = x * m, (1 - x) * m
    sides = ((0, 1 - y), (1, y))

    def begin():
        for i, side in sides:
            load(i, side, mine.at[side], core_in.at[side], core_slot[i])

    def stage_core():
        for i, side in sides:
            load(i, side, mine.at[side], None, None)
            links.receive(core_slot[i], core_in.at[side])
            accumulate(mine.at[side], 0, core_in.at[side], 0, n, step)
            links.send(x_slot[i], mine.at[side, rows_at(peer_p, p)], x_in.at[side], links.x_peer)
            if i == 0:
                links.send(q_slot, mine.at[side, pl.ds(p, q)], y_in.at[pl.ds(0, q)], links.y_peer)
        if used is not None:
            used()

    def stage_x():
        for i, side in sides:
            links.receive(x_slot[i], x_in.at[side])
            accumulate(mine.at[side], own_p, x_in.at[side], 0, p, step)
            if i == 0:
                links.send(
                    p_slot, mine.at[side, rows_at(own_p, p)], y_in.at[pl.ds(q, p)], links.y_peer
                )
        links.receive(q_slot, y_in.at[pl.ds(0, q)])
        accumulate(mine.at[y], p, y_in, 0, q, step)

    def stage_y():
        links.receive(p_slot, y_in.at[pl.ds(q, p)])
        accumulate(mine.at[y], own_p, y_in, q, p, step)

    def stage_z(hop):
        block = mine.at[y, rows_at(first, m)]

        def take(slot, source, pred):
            @pl.when(pred)
            def _():
                links.receive(slot, source)
                accumulate(mine.at[y], first, source, 0, m, step)

        if dest > 0:
            if 1 <= hop <= dest:
                take(low_slot, z_in, z == hop)
            if hop < dest:
                links.send(low_slot, block, z_in, links.up, z == hop)
        if dest < depth - 1:
            turn = depth - 1 - hop
            if hop >= 1 and turn > dest:
                take(high_slot, z_in, z == turn)
            if turn > dest + 1:
                links.send(high_slot, block, z_in, links.down, z == turn)
            if turn == dest + 1:
                links.send(high_slot, block, z_last, links.down, z == turn)
            if turn == dest and hop >= 1:
                take(high_slot, z_last, z == dest)
        if hop == max(dest, depth - 1 - dest):
            links.send(last_slot, block, final, links.x_peer, z == dest)

    def stage_last():
        links.finish(x_slot[1])
        links.finish(last_slot)

        @pl.when(z == dest)
        def _():
            links.receive(last_slot, final)
            accumulate(mine.at[y], p, final, jnp.where(x == 0, 0, p), q, step)

            @pl.loop(0, p // 16)
            def _(turn):
                there = rows_at(jnp.where(x == 0, q, 0) + turn * 16, 16)
                mine[y, rows_at(peer_p + turn * 16, 16), :] = final[there, :]

            emit(mine.at[y])

    hops = [functools.partial(stage_z, hop) for hop in range(depth)]
    return Group(begin, [stage_core, stage_x, stage_y] + hops + [stage_last], core_slot)

def norm_back(value, gain, upstream):
    center = value - jnp.mean(value, -1, keepdims=True)
    scale = lax.rsqrt(jnp.mean(center * center, -1, keepdims=True) + norm_epsilon)
    normal = center * scale
    scaled = upstream * gain
    inner = scale * (
        scaled
        - jnp.mean(scaled, -1, keepdims=True)
        - normal * jnp.mean(scaled * normal, -1, keepdims=True)
    )
    return (
        inner,
        jnp.sum(upstream * normal, 0, keepdims=True),
        jnp.sum(upstream, 0, keepdims=True),
    )


VMEM_LIMIT = 62 * 1024 * 1024
SUB = 3
IN_FLIGHT = 2 * SUB
LAGS = (1, 3, 5, 7, 9, 11, 13, 15)


def backward_kernel(
    depth,
    sides,
    layers,
    weights,
    resid,
    normed,
    project,
    log_total,
    context,
    mixed,
    normed_two,
    embedded,
    patches,
    vectors,
    keep,
    keep_column,
    pooled_row,
    z_column,
    feature_row,
    vector_start,
    stats,
    out,
    row_out,
    totals,
    blocks_v,
    core_in,
    x_in,
    y_in,
    z_in,
    z_last,
    final,
    rows_v,
    row_mine,
    row_core,
    row_x,
    row_y,
    row_z,
    row_z_last,
    row_final,
    resid_v,
    normed_v,
    project_v,
    log_v,
    context_v,
    mixed_v,
    two_v,
    weight_v,
    patch_v,
    hidden_v,
    pre_v,
    up_v,
    short_v,
    total_v,
    context_grad_v,
    vector_v,
    note,
    inbox,
    send_sem,
    recv_sem,
    local_sem,
    weight_sem,
    load_sem,
    mail_send,
    mail_recv,
    free_sem,
):
    links = Links(depth, send_sem, recv_sem)
    y, c, z = links.y, links.c, links.z
    me = links.me * sides + links.x
    everyone = PLANE * depth * sides
    width = up_v.shape[1]
    count = out.shape[1]
    n = count // SUB
    p = n // 4 // 16 * 16
    per_layer = depth * SUB
    own = 2 * layers * per_layer
    piece = 2 * n

    saved = (
        (normed_two, two_v),
        (mixed, mixed_v),
        (context, context_v),
        (resid, resid_v),
        (normed, normed_v),
        (project, project_v),
        (log_total, log_v),
    )

    def load(layer, which):
        source, target = saved[which]
        return pltpu.make_async_copy(source.at[layer], target, load_sem.at[which])

    chunks = []
    for layer in reversed(range(layers)):
        for turn in (3, 2, 1, 0):
            chunks += [(layer, 8 + turn), (layer, 4 + turn)]
        chunks += [(layer, 3), (layer, 0), (layer, 1), (layer, 2)]

    def chunk_copy(number):
        layer, index = chunks[number]
        return pltpu.make_async_copy(
            weights.at[layer, pl.ds(index * width, width)],
            weight_v.at[number % 4],
            weight_sem.at[number % 4],
        )

    def chunk(number):
        chunk_copy(number).wait()
        return weight_v[number % 4]

    def refill(*numbers):
        for number in numbers:
            if number < len(chunks):
                chunk_copy(number).start()

    for which in range(len(saved)):
        load(layers - 1, which).start()
    refill(0, 1, 2, 3)
    patch_load = pltpu.make_async_copy(patches, patch_v, load_sem.at[7])
    patch_load.start()

    def others(run):
        for number in range(everyone):
            pl.when(me != number)(functools.partial(run, number))

    def place(number):
        return (number // sides, number % sides)

    barrier = pltpu.get_barrier_semaphore()
    others(
        lambda number: pl.semaphore_signal(
            barrier, inc=1, device_id=place(number), device_id_type=MESH
        )
    )
    note[...] = stats[...]
    vector_v[...] = vector_start[...]
    up_v[...] = keep_column[...] * pooled_row[...]
    lane = lax.broadcasted_iota(jnp.int32, (8, 128), 1)
    first = lax.broadcasted_iota(jnp.int32, (8, 128), 0) == 0

    def add_squares(block):
        value = block.astype(F32)
        note[...] += jnp.where(first & (lane == 0), jnp.sum(value * value), 0.0)

    groups, closers = [], []
    starts = {}

    def add_group(dest, send_out, take_in, sizes, bufs, emit, used=None):
        def load_block(i, side, mine, target, slot):
            if target is None:
                take_in(i, side, mine)
            else:
                send_out(i, side, mine, target, slot)

        groups.append(scatter_group(links, dest, load_block, sizes, bufs, emit, used))

    for order, layer in enumerate(reversed(range(layers))):
        for turn, dest in enumerate(reversed(range(depth))):
            ring = own
            for part in range(SUB):
                number, spot = len(groups), layer * SUB + part
                starts[(layer, dest, part)] = number
                slot = number % IN_FLIGHT

                def send_out(i, side, mine, target, sem_slot, ring=ring, part=part):
                    source = blocks_v.at[ring + 2 * part + side]
                    links.send(sem_slot, source, target, links.c_peer)

                def write(source, layer=layer, part=part, spot=spot):
                    target = out.at[layer, pl.ds(part * n, n)]
                    return pltpu.make_async_copy(source, target, local_sem.at[spot])

                def emit(result, write=write):
                    add_squares(result[...])
                    write(result).start()

                closers.append((dest, write, blocks_v.at[2 * number]))

                def used(number=number):
                    if number < layers * per_layer - IN_FLIGHT:
                        pl.semaphore_signal(
                            free_sem, inc=1, device_id=links.c_peer, device_id_type=MESH
                        )

                add_group(
                    dest,
                    send_out,
                    lambda i, side, mine: None,
                    (n, p, n - 2 * p, n // 4),
                    [blocks_v.at[pl.ds(2 * number, 2)], core_in.at[slot]]
                    + [ref.at[number] for ref in (x_in, y_in, z_in)]
                    + [z_last.at[spot], final.at[spot]],
                    emit,
                    used,
                )
    first_row_group = len(groups)
    rows = row_out.shape[0]
    for dest in reversed(range(depth)):
        number = len(groups)

        def row_copy(i, side, mine, dest=dest):
            sem = local_sem.at[layers * SUB + 2 * dest + i]
            return pltpu.make_async_copy(rows_v.at[links.at(dest, side, c)], mine, sem)

        def row_send(i, side, mine, target, slot, dest=dest, row_copy=row_copy):
            row_copy(i, side, mine).start()
            source = rows_v.at[links.at(dest, side, 1 - c)]
            links.send(slot, source, target, links.c_peer)

        def row_emit(result, dest=dest):
            add_squares(result[...])
            row_out[...] = result[...]

        add_group(
            dest,
            row_send,
            lambda i, side, mine, row_copy=row_copy: row_copy(i, side, mine).wait(),
            (rows, 16, rows - 32, 16),
            [ref.at[dest] for ref in (row_mine, row_core, row_x, row_y, row_z)]
            + [row_z_last, row_final],
            row_emit,
        )

    begun = []

    def release(layer, dest):
        for part in range(SUB):
            number = starts[(layer, dest, part)]
            if number >= IN_FLIGHT:
                pl.semaphore_wait(free_sem, 1)
            groups[number].begin()
            begun.append(number)

    def recycle(layer, dest):
        for part in range(SUB):
            number = starts[(layer, dest, part)]
            if number >= SUB:
                for slot in groups[number - SUB].core_slot:
                    links.finish(slot)

    last_turn = [0]

    def advance():
        turn = last_turn[0]
        for stage, lag in enumerate(LAGS):
            if 0 <= turn - lag < len(groups):
                groups[turn - lag].stages[stage]()
        last_turn[0] += 1

    def grad_pieces(layer, dest, left, column, amount, right, begin):
        number = starts[(layer, dest, 0)]
        ring = own

        @pl.loop(0, amount)
        def _(turn):
            columns = pl.ds(pl.multiple_of(column + turn * piece, 128), piece)
            result = matmul_tn(left[:, columns], right[...])
            for half in range(2):
                block = 2 * (begin + turn) + half
                shard = block // SUB
                part = lax.rem(block, SUB)
                side, core = shard // 2, lax.rem(shard, 2)
                index = jnp.where(
                    core == c, 2 * (number + part) + side, ring + 2 * part + side
                )
                blocks_v[index] = result[half * n : (half + 1) * n].astype(BF)

    half_lane = lax.broadcasted_iota(jnp.int32, (1, 128), 1) < HDIM
    scale = HDIM ** (-0.5)

    def attention_pair(pair):
        def lanes(base):
            return pl.ds(pl.multiple_of(base + pair * 128, 128), 128)

        query, key = project_v[:, lanes(0)], project_v[:, lanes(width)]
        value, grad = project_v[:, lanes(2 * width)], context_grad_v[:, lanes(0)]
        totals_now = log_v[...]
        column = lax.broadcasted_iota(jnp.int32, totals_now.shape, 1)
        query_grad = key_grad = value_grad = 0.0
        zero = jnp.zeros_like(query)
        for head in range(2):
            here = half_lane if head == 0 else jnp.logical_not(half_lane)
            query_h, key_h = jnp.where(here, query, zero), jnp.where(here, key, zero)
            grad_h = jnp.where(here, grad, zero)
            total = jnp.sum(
                jnp.where(column == 2 * pair + head, totals_now, 0.0), -1, keepdims=True
            )
            scores = jnp.where(keep[...] > 0, matmul_nt(query_h, key) * scale, -1000000000.0)
            probs = jnp.exp(scores - total)
            prob_grad = matmul_nt(grad_h, value)
            value_grad += matmul_tn(probs.astype(BF), grad_h)
            score_grad = (
                probs * (prob_grad - jnp.sum(prob_grad * probs, -1, keepdims=True))
            ).astype(BF)
            query_grad += matmul(score_grad, key_h)
            key_grad += matmul_tn(score_grad, query_h)
        pre_v[:, lanes(0)] = (query_grad * scale).astype(BF)
        pre_v[:, lanes(width)] = (key_grad * scale).astype(BF)
        pre_v[:, lanes(2 * width)] = value_grad.astype(BF)

    def layer_steps(order, layer):
        base = 4 + 12 * layer
        chunk0 = 12 * order

        def vector(index):
            return vectors[pl.ds(base + index, 1), :]

        def put(index, value):
            vector_v[pl.ds(base + index, 1), :] = value

        def column_sum(value):
            return jnp.sum(value.astype(F32), 0, keepdims=True)

        load(layer, 0).wait()
        short_v[...] = up_v[...].astype(BF)
        put(7, column_sum(short_v[...]))
        total_v[...] = jnp.zeros_like(total_v)
        recycle(layer, 3)
        for turn, part in enumerate((3, 2, 1, 0)):
            number = chunk0 + 2 * turn
            down, up = chunk(number), chunk(number + 1)
            pre = matmul_nt(two_v[...], up) + vector(8 + part)
            gate = jax.nn.sigmoid(1.702 * pre)
            hidden_v[...] = (pre * gate).astype(BF)
            slope = gate + 1.702 * pre * gate * (1.0 - gate)
            pre_grad = (matmul_nt(short_v[...], down) * slope).astype(BF)
            pre_v[:, pl.ds(part * width, width)] = pre_grad
            put(8 + part, column_sum(pre_grad))
            total_v[...] += matmul(pre_grad, up)
            refill(number + 4, number + 5)
            yield None
            if part == 0:
                recycle(layer, 2)
            if part > 0:
                grad_pieces(layer, 3, hidden_v, 0, 2, short_v, 2 * (part - 1))
            else:
                grad_pieces(layer, 2, hidden_v, 0, 2, short_v, 4)
            if part == 1:
                release(layer, 3)
                yield 3
            else:
                yield None
        grad_pieces(layer, 2, pre_v, 2 * width, 2, two_v, 0)
        yield None
        grad_pieces(layer, 2, pre_v, 3 * width, 2, two_v, 2)
        release(layer, 2)
        yield 2
        load(layer, 1).wait()
        inner, gain, shift = norm_back(mixed_v[...], vector(5), total_v[...])
        put(5, gain)
        put(6, shift)
        up_v[...] += inner
        short_v[...] = up_v[...].astype(BF)
        put(4, column_sum(short_v[...]))
        yield None
        load(layer, 2).wait()
        recycle(layer, 1)
        grad_pieces(layer, 1, short_v, 0, 2, context_v, 0)
        context_grad_v[...] = matmul(short_v[...], chunk(chunk0 + 8)).astype(BF)
        refill(chunk0 + 12)
        yield None
        grad_pieces(layer, 1, pre_v, 0, 2, two_v, 2)
        yield None
        grad_pieces(layer, 1, pre_v, width, 2, two_v, 4)
        release(layer, 1)
        if layer > 0:
            for which in range(3):
                load(layer - 1, which).start()
        else:
            embed_load.start()
        yield 1
        load(layer, 5).wait()
        load(layer, 6).wait()
        for third in range(3):

            @pl.loop(0, 2)
            def _(turn, third=third):
                attention_pair(2 * third + turn)

            yield None
        load(layer, 4).wait()
        recycle(layer, 0)
        put(2, column_sum(pre_v[:, pl.ds(0, width)]))
        put(3, column_sum(pre_v[:, pl.ds(2 * width, width)]))
        for third in range(3):
            grad_pieces(layer, 0, pre_v, third * width, 2, normed_v, 2 * third)
            if third < 2:
                yield None
        release(layer, 0)
        yield 0
        load(layer, 3).wait()
        back = matmul(pre_v[:, pl.ds(0, width)], chunk(chunk0 + 9))
        back += matmul(pre_v[:, pl.ds(width, width)], chunk(chunk0 + 10))
        back += matmul(pre_v[:, pl.ds(2 * width, width)], chunk(chunk0 + 11))
        refill(chunk0 + 13, chunk0 + 14, chunk0 + 15)
        inner, gain, shift = norm_back(resid_v[...], vector(0), back)
        put(0, gain)
        put(1, shift)
        up_v[...] += inner
        if layer > 0:
            for which in range(3, len(saved)):
                load(layer - 1, which).start()
        yield None

    embed_load = pltpu.make_async_copy(embedded, mixed_v, load_sem.at[8])
    pl.semaphore_wait(barrier, everyone - 1)
    pending = 0
    for order, layer in enumerate(reversed(range(layers))):
        for ready in layer_steps(order, layer):
            if ready is not None:
                pending += SUB
            if pending > 0:
                advance()
                pending -= 1
    embed_load.wait()
    inner, gain, shift = norm_back(mixed_v[...], vectors[pl.ds(0, 1), :], up_v[...])
    vector_v[pl.ds(0, 1), :] = gain
    vector_v[pl.ds(1, 1), :] = shift
    short_v[...] = inner.astype(BF)
    total_v[...] = inner
    patch_load.wait()
    pixels, embeds, seq = patch_v.shape[1], feature_row.shape[1], inner.shape[0]
    for turn in range(width // piece):
        columns = pl.ds(turn * piece, piece)
        patch_grad = matmul_tn(short_v[:, columns], patch_v[...])
        position = total_v[:, columns].T
        vector_grad = vector_v[:, columns].T
        for part in range(piece // rows):
            shard, inside = turn * (piece // rows) + part, slice(part * rows, (part + 1) * rows)
            rows_v[shard, :, pl.ds(0, pixels)] = patch_grad[inside].astype(BF)
            proj = z_column[pl.ds(shard * rows, rows), :] * feature_row[...]
            rows_v[shard, :, pl.ds(pixels, embeds)] = proj.astype(BF)
            rows_v[shard, :, pl.ds(pixels + embeds, seq)] = position[inside].astype(BF)
            rows_v[shard, :, pl.ds(pixels + embeds + seq, 128)] = vector_grad[inside].astype(BF)
    for number in range(first_row_group, len(groups)):
        groups[number].begin()
    while last_turn[0] < len(groups) + max(LAGS):
        advance()

    def mail(number, slot):
        return pltpu.make_async_remote_copy(
            src_ref=note,
            dst_ref=inbox.at[slot],
            send_sem=mail_send.at[number],
            recv_sem=mail_recv.at[slot],
            device_id=place(number),
            device_id_type=MESH,
        )

    others(lambda number: mail(number, me).start())
    inbox[pl.ds(me, 1)] = note[...][None]
    links.finish()
    for dest, write, source in closers:
        pl.when(z == dest)(lambda write=write, source=source: write(source).wait())
    others(lambda number: mail(number, number).wait_recv())
    summed = jnp.sum(inbox[...], 0)
    others(lambda number: mail(number, me).wait_send())

    def pick(index):
        return jnp.sum(jnp.where(first & (lane == index), summed, 0.0))

    loss_sum, weight_sum = pick(1), pick(2)
    norm = jnp.sqrt(jnp.full((8, 128), pick(0) / sides)) / weight_sum
    clip = jnp.minimum(1.0, clip_bound / (norm + 1e-06)) / weight_sum
    totals[...] = jnp.where(
        lane == 0,
        loss_sum,
        jnp.where(lane == 1, weight_sum, jnp.where(lane == 2, norm, clip)),
    )


def backward(
    depth, sides, weights, saved, embedded, patches, vectors, keep, keep_column, head, start, stats
):
    layers, rows_all, width = weights.shape
    seq, pixels = patches.shape
    shards = PLANE * depth
    count, rows = rows_all // shards, width // shards
    lanes = -(-(pixels + EMB + SEQ + 4 + 12 * layers) // 128) * 128
    n = count // SUB
    p = n // 4 // 16 * 16
    m = n - p
    per_layer = depth * SUB
    blocks = layers * per_layer
    row_m = rows - 16
    everyone = shards * sides

    def room(*shape, dtype=BF):
        return pltpu.VMEM(shape, dtype)

    any_space = pl.BlockSpec(memory_space=pl.ANY)
    vmem = pl.BlockSpec(memory_space=pltpu.VMEM)
    slots = (blocks + depth) * 9
    return pl.pallas_call(
        functools.partial(backward_kernel, depth, sides, layers),
        out_shape=(
            jax.ShapeDtypeStruct((layers, count, width), BF),
            jax.ShapeDtypeStruct((rows, lanes), BF),
            jax.ShapeDtypeStruct((8, 128), F32),
        ),
        in_specs=[any_space] * (1 + len(saved) + 2) + [vmem] * 8,
        out_specs=[any_space, vmem, vmem],
        scratch_shapes=[
            room(2 * blocks + 2 * SUB, n, width),
            room(IN_FLIGHT, 2, n, width),
            room(blocks, 2, p, width),
            room(blocks, m, width),
            room(blocks, m, width),
            room(layers * SUB, m, width),
            room(layers * SUB, m, width),
            room(shards, rows, lanes),
            room(depth, 2, rows, lanes),
            room(depth, 2, rows, lanes),
            room(depth, 2, 16, lanes),
            room(depth, row_m, lanes),
            room(depth, row_m, lanes),
            room(row_m, lanes),
            room(row_m, lanes),
            room(seq, width, dtype=F32),
            room(seq, width),
            room(seq, 3 * width),
            room(seq, 128, dtype=F32),
            room(seq, width),
            room(seq, width, dtype=F32),
            room(seq, width),
            room(4, width, width),
            room(seq, pixels),
            room(seq, width),
            room(seq, 4 * width),
            room(seq, width, dtype=F32),
            room(seq, width),
            room(seq, width, dtype=F32),
            room(seq, width),
            room(128, width, dtype=F32),
            room(8, 128, dtype=F32),
            room(everyone, 8, 128, dtype=F32),
            pltpu.SemaphoreType.DMA((slots,)),
            pltpu.SemaphoreType.DMA((slots,)),
            pltpu.SemaphoreType.DMA((layers * SUB + 2 * depth,)),
            pltpu.SemaphoreType.DMA((4,)),
            pltpu.SemaphoreType.DMA((9,)),
            pltpu.SemaphoreType.DMA((everyone,)),
            pltpu.SemaphoreType.DMA((everyone,)),
            pltpu.SemaphoreType.REGULAR,
        ],
        name="backward_and_sum",
        compiler_params=pltpu.CompilerParams(
            collective_id=2, has_side_effects=True, vmem_limit_bytes=VMEM_LIMIT
        ),
    )(weights, *saved, embedded, patches, vectors, keep, keep_column, *head, start, stats)


def finish_kernel(
    hyper,
    totals,
    grad,
    momentum,
    mats,
    zero,
    ema,
    new_momentum,
    new_mats,
    new_ema,
    new_mixed,
    grad_v,
    m_v,
    mats_v,
    zero_v,
    ema_v,
    x_v,
    short_v,
    low_v,
    in_sem,
    out_sem,
):
    layers, count, width = grad.shape
    pairs = [(grad, grad_v), (momentum, m_v)]
    pairs += [(mats, mats_v), (zero, zero_v), (ema, ema_v)]
    loads = [pltpu.make_async_copy(a, b, in_sem.at[i]) for i, (a, b) in enumerate(pairs)]
    for load in loads:
        load.start()
    part = count // 3
    factor = totals[pl.ds(0, 1), pl.ds(3, 1)]
    loads[0].wait()
    loads[1].wait()
    stores = []
    for layer in range(layers):
        total = jnp.zeros((1, 1), F32)
        for third in range(3):
            rows = pl.ds(third * part, part)
            value = momentum_decay * m_v[layer, rows, :] + factor * grad_v[layer, rows, :].astype(F32)
            m_v[layer, rows, :] = value
            total += jnp.sum(value * value, keepdims=True)
        store = pltpu.make_async_copy(m_v.at[layer], new_momentum.at[layer], out_sem.at[layer])
        store.start()
        stores.append(store)
        inverse = 1.0 / (jnp.sqrt(total) + 1e-07)
        for third in range(3):
            rows = pl.ds(third * part, part)
            value = m_v[layer, rows, :] * inverse
            x_v[layer, rows, :] = value
            short_v[0, layer, rows, :] = value.astype(BF)

    row_id = lax.broadcasted_iota(jnp.int32, (part, count), 0)
    col_id = lax.broadcasted_iota(jnp.int32, (part, count), 1)

    @pl.loop(0, NS_STEPS)
    def _(turn):
        now, later = lax.rem(turn, 2), 1 - lax.rem(turn, 2)
        shift = jnp.where(turn >= NS_STEPS - 2, 1.0, 0.0)
        linear = coeff_cubic + 2.0 * shift * coeff_quintic
        stay = coeff_linear + shift * (coeff_cubic + shift * coeff_quintic)
        for layer in range(layers):
            for third in range(3):
                rows = pl.ds(third * part, part)
                gram = matmul_nt(short_v[now, layer, rows, :], short_v[now, layer])
                gram -= jnp.where(row_id + third * part == col_id, shift, 0.0)
                low_v[layer, rows, :] = gram.astype(BF)
        for layer in range(layers):
            for third in range(3):
                rows = pl.ds(third * part, part)
                low = low_v[layer, rows, :]
                poly = linear * low.astype(F32) + coeff_quintic * matmul(low, low_v[layer])
                value = stay * x_v[layer, rows, :] + matmul(poly.astype(BF), short_v[now, layer])
                x_v[layer, rows, :] = value
                short_v[later, layer, rows, :] = value.astype(BF)

    for load in loads[2:]:
        load.wait()
    for layer in range(layers):
        for third in range(3):
            rows = pl.ds(third * part, part)
            old = mats_v[layer, rows, :]
            value = old - muon_rate * (
                hyper * x_v[layer, rows, :] + weight_decay * old
            )
            mats_v[layer, rows, :] = value
            ema_v[layer, rows, :] = ema_decay * ema_v[layer, rows, :] + (1.0 - ema_decay) * value
            zero_v[layer, rows, :] = mix_share * value + (1.0 - mix_share) * zero_v[layer, rows, :]
            for turn, (source, target) in enumerate(
                ((mats_v, new_mats), (ema_v, new_ema), (zero_v, new_mixed))
            ):
                sem = out_sem.at[layers + (layer * 3 + third) * 3 + turn]
                store = pltpu.make_async_copy(source.at[layer, rows], target.at[layer, rows], sem)
                store.start()
                stores.append(store)
    for store in stores:
        store.wait()


def finish(totals, grad, momentum, mats, zero, ema):
    layers, count, width = grad.shape
    full = jax.ShapeDtypeStruct(mats.shape, F32)
    any_space = pl.BlockSpec(memory_space=pl.ANY)
    vmem = pl.BlockSpec(memory_space=pltpu.VMEM)
    return pl.pallas_call(
        functools.partial(finish_kernel, 0.2 * math.sqrt(width)),
        out_shape=(full, full, full, full),
        in_specs=[vmem] + [any_space] * 5,
        out_specs=[any_space] * 4,
        scratch_shapes=[
            pltpu.VMEM(grad.shape, BF),
            pltpu.VMEM(mats.shape, F32),
            pltpu.VMEM(mats.shape, F32),
            pltpu.VMEM(mats.shape, F32),
            pltpu.VMEM(mats.shape, F32),
            pltpu.VMEM(mats.shape, F32),
            pltpu.VMEM((2,) + mats.shape, BF),
            pltpu.VMEM((layers, count, count), BF),
            pltpu.SemaphoreType.DMA((5,)),
            pltpu.SemaphoreType.DMA((layers * 10,)),
        ],
        name="orthogonalize",
        compiler_params=pltpu.CompilerParams(vmem_limit_bytes=56 * 1024 * 1024),
    )(totals, grad, momentum, mats, zero, ema)


def gather_layer(shard):
    return lax.all_gather(shard.astype(jnp.bfloat16), "fsdp", axis=0, tiled=True)


def layer_forward(resid, weight_tensors, vector, valid_mask):
    images, seq = valid_mask.shape
    width = resid.shape[1]
    ffn = 4 * width
    normed = norm_forward(resid, vector[0], vector[1]).astype(jnp.bfloat16)
    bias = jnp.concatenate([vector[2], jnp.zeros_like(vector[2]), vector[3]])
    project = (matmul_nt(normed, weight_tensors[: 3 * width]) + bias).astype(jnp.bfloat16)
    parts = project.reshape(images, seq, 3, HEADS, HDIM)
    scores = attention_scores(parts, valid_mask)
    top_score = jnp.max(scores, -1, keepdims=True)
    expo = jnp.exp(scores - top_score)
    totals = jnp.sum(expo, -1, keepdims=True)
    log_total = top_score + jnp.log(totals)
    probs = (expo / totals).astype(jnp.bfloat16)
    context = jnp.einsum(
        "ihqk,ikhd->iqhd", probs, parts[:, :, 2], preferred_element_type=jnp.float32
    )
    context = context.reshape(images * seq, width).astype(jnp.bfloat16)
    mixed = resid + (matmul_nt(context, weight_tensors[3 * width : 4 * width]) + vector[4])
    normed_two = norm_forward(mixed, vector[5], vector[6]).astype(jnp.bfloat16)
    hidden_pre = matmul_nt(normed_two, weight_tensors[4 * width : 4 * width + ffn]) + vector[
        8:12
    ].reshape(ffn)
    hidden = (hidden_pre * jax.nn.sigmoid(1.702 * hidden_pre)).astype(jnp.bfloat16)
    output = mixed + (matmul(hidden, weight_tensors[4 * width + ffn :]) + vector[7])
    return (
        output,
        (resid, normed, project, log_total, context, mixed, normed_two, hidden_pre, hidden),
    )


def layer_backward(upstream, weight_tensors, vector, valid_mask, saved_activation):
    resid, normed, project, log_total, context, mixed, normed_two, hidden_pre, hidden = (
        saved_activation
    )
    images, seq = valid_mask.shape
    width = resid.shape[1]
    ffn = 4 * width
    out_grad = upstream.astype(jnp.bfloat16)
    grad_down = matmul_tn(hidden, out_grad)
    hidden_grad = matmul_nt(out_grad, weight_tensors[4 * width + ffn :])
    gate = jax.nn.sigmoid(1.702 * hidden_pre)
    pre_grad = (hidden_grad * (gate + 1.702 * hidden_pre * gate * (1.0 - gate))).astype(
        jnp.bfloat16
    )
    grad_up = matmul_tn(pre_grad, normed_two)
    second_in, gain_two, shift_two = norm_backward(
        mixed, vector[5], matmul(pre_grad, weight_tensors[4 * width : 4 * width + ffn])
    )
    mixed_grad = upstream + second_in
    attn_grad = mixed_grad.astype(jnp.bfloat16)
    grad_out = matmul_tn(attn_grad, context)
    context_grad = matmul(attn_grad, weight_tensors[3 * width : 4 * width]).astype(jnp.bfloat16)
    context_grad = context_grad.reshape(images, seq, HEADS, HDIM)
    parts = project.reshape(images, seq, 3, HEADS, HDIM)
    probs = jnp.exp(attention_scores(parts, valid_mask) - log_total)
    prob_grad = jnp.einsum(
        "iqhd,ikhd->ihqk", context_grad, parts[:, :, 2], preferred_element_type=jnp.float32
    )
    value_grad = jnp.einsum(
        "ihqk,iqhd->ikhd",
        probs.astype(jnp.bfloat16),
        context_grad,
        preferred_element_type=jnp.float32,
    )
    score_grad = (probs * (prob_grad - jnp.sum(prob_grad * probs, -1, keepdims=True))).astype(
        jnp.bfloat16
    )
    query_grad = jnp.einsum(
        "ihqk,ikhd->iqhd", score_grad, parts[:, :, 1], preferred_element_type=jnp.float32
    ) * HDIM ** (-0.5)
    key_grad = jnp.einsum(
        "ihqk,iqhd->ikhd", score_grad, parts[:, :, 0], preferred_element_type=jnp.float32
    ) * HDIM ** (-0.5)
    project_grad = (
        jnp.stack([query_grad, key_grad, value_grad], 2)
        .reshape(images * seq, 3 * width)
        .astype(jnp.bfloat16)
    )
    project_sum = jnp.sum(project_grad.astype(jnp.float32), 0)
    grad_qkv = matmul_tn(project_grad, normed)
    first_in, gain_one, shift_one = norm_backward(
        resid, vector[0], matmul(project_grad, weight_tensors[: 3 * width])
    )
    residual_gradient = mixed_grad + first_in
    grad_matrix = [part.astype(BF) for part in (grad_qkv, grad_out, grad_up, grad_down)]
    grad_vector = jnp.concatenate(
        [
            jnp.stack(
                [
                    gain_one,
                    shift_one,
                    project_sum[:width],
                    project_sum[2 * width :],
                    jnp.sum(attn_grad.astype(jnp.float32), 0),
                    gain_two,
                    shift_two,
                    jnp.sum(out_grad.astype(jnp.float32), 0),
                ]
            ),
            jnp.sum(pre_grad.astype(jnp.float32), 0).reshape(4, width),
        ],
        0,
    )
    return (residual_gradient, grad_matrix, grad_vector)


def newton_schulz(blocks):
    frob = jnp.sqrt(jnp.sum(blocks * blocks, axis=(1, 2), keepdims=True)) + 1e-07
    blocks = blocks / frob
    unit = jnp.eye(blocks.shape[1], dtype=jnp.float32)
    for turn in range(NS_STEPS):
        shift = 1.0 if turn >= NS_STEPS - 2 else 0.0
        short = blocks.astype(BF)
        gram = jnp.einsum("lcd,led->lce", short, short, preferred_element_type=F32) - shift * unit
        low = gram.astype(BF)
        square = jnp.einsum("lce,lef->lcf", low, low, preferred_element_type=F32)
        poly = (coeff_cubic + 2.0 * shift * coeff_quintic) * gram + coeff_quintic * square
        stay = coeff_linear + shift * (coeff_cubic + shift * coeff_quintic)
        blocks = stay * blocks + jnp.einsum(
            "lce,led->lcd", poly.astype(BF), short, preferred_element_type=F32
        )
    return blocks


def row_updates(clipped, layers, row_params, row_zero, row_ema, row_first, row_second):
    front = PIX + EMB + SEQ + 4
    new_first = first_decay * row_first + (1.0 - first_decay) * clipped
    new_second = second_decay * row_second + (1.0 - second_decay) * clipped * clipped
    down_bias_grad = clipped[front:].reshape(layers, 12, row_params.shape[1])[:, 7]
    step_size = (
        new_first
        / (1.0 - first_decay**STEPS_DONE)
        / (jnp.sqrt(new_second / (1.0 - second_decay**STEPS_DONE)) + adam_floor)
    )
    new_rows = row_params - adam_rate * (step_size + weight_decay * row_params)
    ema_rows = ema_decay * row_ema + (1.0 - ema_decay) * new_rows
    mixed_rows = mix_share * new_rows + (1.0 - mix_share) * row_zero
    return (new_rows, new_first, new_second, ema_rows, mixed_rows, down_bias_grad)


def plain_body(
    patches,
    pad_mask,
    labels,
    loss_weights,
    class_emb,
    layer_mats,
    layer_zero,
    layer_ema,
    layer_momentum,
    row_params,
    row_zero,
    row_ema,
    row_first,
    row_second,
):
    layers, columns, width = layer_mats.shape
    images, seq, pixels = patches.shape
    front = PIX + EMB + SEQ + 4
    valid_mask = pad_mask.astype(jnp.float32)
    gathered_rows = lax.all_gather(row_params.astype(jnp.bfloat16), "fsdp", axis=1, tiled=True)
    rows_value = gathered_rows.astype(jnp.float32)
    patch_weight = gathered_rows[:PIX]
    proj_rows = gathered_rows[PIX : PIX + EMB]
    position = rows_value[PIX + EMB : PIX + EMB + SEQ]
    head_vec = rows_value[PIX + EMB + SEQ : front]
    layer_vector_params = rows_value[front:].reshape(layers, 12, width)
    flat_patches = patches.reshape(images * seq, pixels)
    embedded = (matmul(flat_patches, patch_weight).reshape(images, seq, width) + position).reshape(
        images * seq, width
    )
    resid = norm_forward(embedded, head_vec[0], head_vec[1])
    kept_weights = []
    saved_activations = []
    for layer_number in range(layers):
        weight_tensors = gather_layer(layer_mats[layer_number])
        kept_weights.append(weight_tensors)
        resid, saved_activation = layer_forward(
            resid, weight_tensors, layer_vector_params[layer_number], valid_mask
        )
        saved_activations.append(saved_activation)
    counts = jnp.sum(valid_mask, -1, keepdims=True)
    pooled = jnp.sum(resid.reshape(images, seq, width) * valid_mask[..., None], 1) / counts
    pooled_norm = norm_forward(pooled, head_vec[2], head_vec[3]).astype(jnp.bfloat16)
    feature = matmul_nt(pooled_norm, proj_rows)
    inv_length = lax.rsqrt(jnp.sum(feature * feature, -1, keepdims=True) + unit_epsilon)
    unit_feat = (feature * inv_length).astype(jnp.bfloat16)
    classes = class_emb.astype(jnp.float32)
    class_unit = (
        classes * lax.rsqrt(jnp.sum(classes * classes, -1, keepdims=True) + unit_epsilon)
    ).astype(jnp.bfloat16)
    logits = logit_scale * matmul_nt(unit_feat, class_unit)
    top_logit = jnp.max(logits, -1, keepdims=True)
    shifted = jnp.exp(logits - top_logit)
    total_exp = jnp.sum(shifted, -1, keepdims=True)
    log_norm = top_logit + jnp.log(total_exp)
    onehot = (jnp.arange(logits.shape[1])[None, :] == labels[:, None]).astype(jnp.float32)
    losses = log_norm[:, 0] - jnp.sum(onehot * logits, -1)
    weights_value = loss_weights.astype(jnp.float32)
    loss_sum, weight_sum = lax.psum(
        (jnp.sum(weights_value * losses), jnp.sum(weights_value)), ("fsdp", "ns")
    )
    seed = weights_value / weight_sum
    logit_grad = seed[:, None] * (shifted / total_exp - onehot)
    unit_grad = logit_scale * jnp.dot(logit_grad, class_unit.astype(jnp.float32), precision=HIGHEST)
    feat_grad = inv_length * unit_grad - feature * inv_length**3 * jnp.sum(
        unit_grad * feature, -1, keepdims=True
    )
    grad_proj = jnp.dot(feat_grad.T, pooled_norm.astype(jnp.float32), precision=HIGHEST)
    pooled_grad, gain_post, shift_post = norm_backward(
        pooled, head_vec[2], jnp.dot(feat_grad, proj_rows.astype(jnp.float32), precision=HIGHEST)
    )
    residual_gradient = (valid_mask[..., None] * (pooled_grad / counts)[:, None, :]).reshape(
        images * seq, width
    )
    grad_mats = [None] * layers
    grad_vecs = [None] * layers
    for layer_number in reversed(range(layers)):
        weight_tensors = kept_weights[layer_number]
        residual_gradient, grad_matrix, grad_vector = layer_backward(
            residual_gradient,
            weight_tensors,
            layer_vector_params[layer_number],
            valid_mask,
            saved_activations[layer_number],
        )
        grad_mats[layer_number], grad_vecs[layer_number] = (
            lax.psum_scatter(
                jnp.concatenate(grad_matrix, 0), "fsdp", scatter_dimension=0, tiled=True
            ),
            lax.psum_scatter(grad_vector, "fsdp", scatter_dimension=1, tiled=True),
        )
    embed_grad, gain_pre, shift_pre = norm_backward(embedded, head_vec[0], residual_gradient)
    position_grad = jnp.sum(embed_grad.reshape(images, seq, width), 0)
    patch_grad = matmul_tn(flat_patches, embed_grad.astype(jnp.bfloat16))
    front_grad = jnp.concatenate(
        [
            patch_grad,
            grad_proj,
            position_grad,
            jnp.stack([gain_pre, shift_pre, gain_post, shift_post]),
        ],
        0,
    )
    front_shard = lax.psum_scatter(front_grad, "fsdp", scatter_dimension=1, tiled=True)
    mat_grad = jnp.stack(grad_mats)
    row_grad = jnp.concatenate([front_shard] + grad_vecs, 0)
    pairs = lax.axis_size("ns")
    side = lax.axis_index("ns")
    half_depth = width // pairs
    half_rows = row_grad.shape[0] // pairs
    mat_total, row_total = (
        lax.psum(mat_grad.astype(jnp.bfloat16), "ns").astype(jnp.float32),
        lax.psum(row_grad.astype(jnp.bfloat16), "ns").astype(jnp.float32),
    )
    mat_half = lax.dynamic_slice_in_dim(mat_total, side * half_depth, half_depth, 2)
    row_half = lax.dynamic_slice_in_dim(row_total, side * half_rows, half_rows, 0)
    squares = jnp.sum(mat_half * mat_half) + jnp.sum(row_half * row_half)
    grad_norm = jnp.sqrt(lax.psum(squares, ("fsdp", "ns")))
    clip = jnp.minimum(1.0, clip_bound / (grad_norm + 1e-06))
    momentum = momentum_decay * layer_momentum + clip * mat_total
    orth = newton_schulz(momentum)
    new_mats = layer_mats - muon_rate * (0.2 * math.sqrt(width) * orth + weight_decay * layer_mats)
    ema_mats = ema_decay * layer_ema + (1.0 - ema_decay) * new_mats
    mixed_mats = mix_share * new_mats + (1.0 - mix_share) * layer_zero
    return (loss_sum, weight_sum, grad_norm, new_mats, momentum, ema_mats, mixed_mats) + row_updates(
        clip * row_total, layers, row_params, row_zero, row_ema, row_first, row_second
    )


def fast_body(
    patches,
    pad_mask,
    labels,
    loss_weights,
    class_emb,
    layer_mats,
    layer_zero,
    layer_ema,
    layer_momentum,
    row_params,
    row_zero,
    row_ema,
    row_first,
    row_second,
):
    layers, columns, width = layer_mats.shape
    images, seq, pixels = patches.shape
    shards = lax.axis_size("fsdp")
    depth = shards // PLANE
    rows, share = row_params.shape
    front = PIX + EMB + SEQ + 4
    lanes = -(-rows // 128) * 128
    valid_mask = pad_mask.astype(F32)
    sent_rows = jnp.pad(row_params.T.astype(BF), ((0, 0), (0, lanes - rows)))
    all_rows, all_mats = gather(depth, sent_rows, layer_mats.astype(BF))
    table = all_rows.reshape(width, lanes)
    weights = all_mats.reshape(layers, shards * columns, width)
    patch_weight, proj = table[:, :PIX], table[:, PIX : PIX + EMB]
    position = table[:, PIX + EMB : PIX + EMB + SEQ].T.astype(F32)
    vectors = table[:, PIX + EMB + SEQ : rows].T.astype(F32)
    head_vec = vectors[:4]
    layer_vector_params = vectors[4:].reshape(layers, 12, width)
    flat_patches = patches.reshape(images * seq, pixels)
    embedded = (
        matmul_nt(flat_patches, patch_weight).reshape(images, seq, width) + position
    ).reshape(images * seq, width)
    resid = norm_forward(embedded, head_vec[0], head_vec[1])
    saved_activations = []
    for layer_number in range(layers):
        resid, saved_activation = layer_forward(
            resid, weights[layer_number], layer_vector_params[layer_number], valid_mask
        )
        before, normed, project, log_total, context, mixed, normed_two, _, _ = saved_activation
        log_total = jnp.pad(log_total.reshape(HEADS, seq).T, ((0, 0), (0, 128 - HEADS)))
        saved_activations.append(
            (before, normed, project, log_total, context, mixed, normed_two)
        )
    saved = [jnp.stack(parts) for parts in zip(*saved_activations)]
    counts = jnp.sum(valid_mask, -1, keepdims=True)
    pooled = jnp.sum(resid.reshape(images, seq, width) * valid_mask[..., None], 1) / counts
    pooled_norm = norm_forward(pooled, head_vec[2], head_vec[3]).astype(BF)
    feature = matmul(pooled_norm, proj)
    inv_length = lax.rsqrt(jnp.sum(feature * feature, -1, keepdims=True) + unit_epsilon)
    unit_feat = (feature * inv_length).astype(BF)
    classes = class_emb.astype(F32)
    class_unit = (
        classes * lax.rsqrt(jnp.sum(classes * classes, -1, keepdims=True) + unit_epsilon)
    ).astype(BF)
    logits = logit_scale * matmul_nt(unit_feat, class_unit)
    top_logit = jnp.max(logits, -1, keepdims=True)
    shifted = jnp.exp(logits - top_logit)
    total_exp = jnp.sum(shifted, -1, keepdims=True)
    log_norm = top_logit + jnp.log(total_exp)
    onehot = (jnp.arange(logits.shape[1])[None, :] == labels[:, None]).astype(F32)
    losses = log_norm[:, 0] - jnp.sum(onehot * logits, -1)
    weights_value = loss_weights.astype(F32)
    logit_grad = weights_value[:, None] * (shifted / total_exp - onehot)
    unit_grad = logit_scale * jnp.dot(logit_grad, class_unit.astype(F32), precision=HIGHEST)
    feat_grad = inv_length * unit_grad - feature * inv_length**3 * jnp.sum(
        unit_grad * feature, -1, keepdims=True
    )
    pooled_grad, gain_post, shift_post = norm_backward(
        pooled,
        head_vec[2],
        lax.dot_general(
            feat_grad, proj.astype(F32), (((1,), (1,)), ((), ())), precision=HIGHEST
        ),
    )
    lane = lax.broadcasted_iota(jnp.int32, (8, 128), 1)
    first = lax.broadcasted_iota(jnp.int32, (8, 128), 0) == 0
    stats = jnp.where(first & (lane == 1), jnp.sum(weights_value * losses), 0.0)
    stats = jnp.where(first & (lane == 2), jnp.sum(weights_value), stats)
    mat_total, row_total, totals = backward(
        depth,
        lax.axis_size("ns"),
        weights,
        saved,
        embedded,
        flat_patches,
        vectors,
        valid_mask,
        valid_mask.T,
        (pooled_grad / counts, pooled_norm.astype(F32).T, feat_grad),
        jnp.pad(jnp.stack([gain_post, shift_post]), ((2, 124), (0, 0))),
        stats,
    )
    loss_sum, weight_sum, grad_norm, clip = (totals[0, turn] for turn in range(4))
    momentum, new_mats, ema_mats, mixed_mats = finish(
        totals, mat_total, layer_momentum, layer_mats, layer_zero, layer_ema
    )
    clipped = clip * row_total.astype(F32)[:, :rows].T
    return (loss_sum, weight_sum, grad_norm, new_mats, momentum, ema_mats, mixed_mats) + row_updates(
        clipped, layers, row_params, row_zero, row_ema, row_first, row_second
    )


def body(*args):
    count, share = args[5].shape[1], args[9].shape[1]
    planes = lax.axis_size("fsdp") == 4 * PLANE and lax.axis_size("ns") == 2
    if planes and count % 192 == 0 and share % 48 == 0 and args[0].shape[0] == 1:
        return fast_body(*args)
    return plain_body(*args)


def solution(mesh):
    in_specs = (
        P(("fsdp", "ns"), None, None),
        P(("fsdp", "ns"), None),
        P(("fsdp", "ns")),
        P(("fsdp", "ns")),
        P(),
        P(None, "fsdp", None),
        P(None, "fsdp", None),
        P(None, "fsdp", None),
        P(None, "fsdp", None),
        P(None, "fsdp"),
        P(None, "fsdp"),
        P(None, "fsdp"),
        P(None, "fsdp"),
        P(None, "fsdp"),
    )
    out_specs = (
        P(),
        P(),
        P(),
        P(None, "fsdp", None),
        P(None, "fsdp", None),
        P(None, "fsdp", None),
        P(None, "fsdp", None),
        P(None, "fsdp"),
        P(None, "fsdp"),
        P(None, "fsdp"),
        P(None, "fsdp"),
        P(None, "fsdp"),
        P(None, "fsdp"),
    )
    return jax.shard_map(body, mesh=mesh, in_specs=in_specs, out_specs=out_specs, check_vma=False)
```

```python
import functools
import math
from typing import NamedTuple

import jax
import jax.numpy as jnp
from jax import lax
from jax.experimental import pallas as pl
from jax.experimental.pallas import tpu as pltpu
from jax.sharding import PartitionSpec as P

HEADS = 12
HDIM = 64
PIX = 768
EMB = 512
CLASSES = 1000
SEQ = 256
NS_STEPS = 5
STEPS_DONE = 10


HIGHEST = lax.Precision.HIGHEST
norm_epsilon = 1e-05
unit_epsilon = 1e-06
logit_scale = 50.0
clip_bound = 0.001
momentum_decay = 0.95
muon_rate = 0.05
weight_decay = 0.05
adam_rate = 0.2
first_decay = 0.9
second_decay = 0.98
adam_floor = 1e-08
ema_decay = 0.9
mix_share = 0.5
coeff_linear = 3.4445
coeff_cubic = -4.775
coeff_quintic = 2.0315


def matmul(left, right):
    return jnp.dot(left, right, preferred_element_type=jnp.float32)


def matmul_nt(left, right):
    return lax.dot_general(
        left, right, (((1,), (1,)), ((), ())), preferred_element_type=jnp.float32
    )


def matmul_tn(left, right):
    return lax.dot_general(
        left, right, (((0,), (0,)), ((), ())), preferred_element_type=jnp.float32
    )


def norm_forward(inputs, gain, shift):
    center = inputs - jnp.mean(inputs, -1, keepdims=True)
    scale = lax.rsqrt(jnp.mean(center * center, -1, keepdims=True) + norm_epsilon)
    return center * scale * gain + shift


def norm_backward(inputs, gain, upstream):
    center = inputs - jnp.mean(inputs, -1, keepdims=True)
    scale = lax.rsqrt(jnp.mean(center * center, -1, keepdims=True) + norm_epsilon)
    normal = center * scale
    scaled_up = upstream * gain
    inner = scale * (
        scaled_up
        - jnp.mean(scaled_up, -1, keepdims=True)
        - normal * jnp.mean(scaled_up * normal, -1, keepdims=True)
    )
    return (inner, jnp.sum(upstream * normal, 0), jnp.sum(upstream, 0))


def attention_scores(parts, valid_mask):
    raw = jnp.einsum(
        "iqhd,ikhd->ihqk", parts[:, :, 0], parts[:, :, 1], preferred_element_type=jnp.float32
    )
    return jnp.where(valid_mask[:, None, None, :] > 0, raw * HDIM ** (-0.5), -1000000000.0)


BF = jnp.bfloat16
F32 = jnp.float32
MESH = pl.DeviceIdType.MESH
PLANE = 4


def guarded(pred, run):
    if pred is None:
        run()
    else:
        pl.when(pred)(run)


def both(first, second):
    if first is None:
        return second
    return first if second is None else jnp.logical_and(first, second)


def rows_at(start, count):
    return pl.ds(start if isinstance(start, int) else pl.multiple_of(start, 16), count)


class Links:
    def __init__(self, depth, send_sem, recv_sem):
        self.depth, self.send_sem, self.recv_sem = depth, send_sem, recv_sem
        self.me, self.x = lax.axis_index("fsdp"), lax.axis_index("ns")
        self.z, self.y, self.c = self.me // PLANE, lax.rem(self.me // 2, 2), lax.rem(self.me, 2)
        self.up = (self.at(self.z + 1, self.y, self.c), self.x)
        self.down = (self.at(self.z - 1, self.y, self.c), self.x)
        self.y_peer = (self.at(self.z, 1 - self.y, self.c), self.x)
        self.c_peer = (self.at(self.z, self.y, 1 - self.c), self.x)
        self.x_peer = (self.me, 1 - self.x)
        self.count, self.sent, self.waited = 0, [], set()

    def at(self, z, y, c):
        return PLANE * z + 2 * y + c

    def slot(self):
        self.count += 1
        return self.count - 1

    def greet(self):
        barrier = pltpu.get_barrier_semaphore()

        def signal(device):
            pl.semaphore_signal(barrier, inc=1, device_id=device, device_id_type=MESH)

        for device in (self.y_peer, self.x_peer, self.c_peer):
            signal(device)
        pl.when(self.z < self.depth - 1)(lambda: signal(self.up))
        pl.when(self.z > 0)(lambda: signal(self.down))
        inner = (self.z < self.depth - 1).astype(jnp.int32) + (self.z > 0).astype(jnp.int32)
        pl.semaphore_wait(barrier, 3 + inner)

    def copy(self, slot, source, target, device):
        return pltpu.make_async_remote_copy(
            src_ref=source,
            dst_ref=target,
            send_sem=self.send_sem.at[slot],
            recv_sem=self.recv_sem.at[slot],
            device_id=device,
            device_id_type=MESH,
        )

    def send(self, slot, source, target, device, pred=None):
        copy = self.copy(slot, source, target, device)
        guarded(pred, copy.start)
        self.sent.append((slot, pred, copy))

    def receive(self, slot, target, pred=None):
        guarded(pred, self.copy(slot, target, target, self.c_peer).wait_recv)

    def finish(self, slot=None):
        for number, pred, copy in self.sent:
            if number not in self.waited and (slot is None or number == slot):
                guarded(pred, copy.wait_send)
        if slot is not None:
            self.waited.add(slot)


def gather_item(links, own, target, count):
    depth, z, y, c, x = links.depth, links.z, links.y, links.c, links.x
    third = count // 3
    begin = x * third
    origin = (0, 0)
    keys = [(side, far) for far in range(1, depth) for side in (-1, 1)]
    z_slot = {key: links.slot() for key in keys}
    y_slot = {key: links.slot() for key in keys + [origin]}
    x_slot = {(key, o): links.slot() for key in keys + [origin] for o in (0, 1)}
    c_slot = {(key, o): links.slot() for key in keys + [origin] for o in (0, 1)}

    def part(shard):
        return target(shard).at[rows_at(begin, 2 * third)]

    def own_part():
        return own.at[rows_at(begin, 2 * third)]

    def third_of(shard, side):
        return target(shard).at[rows_at(side * 2 * third, third)]

    def shard(key, other, core=None):
        return links.at(z + key[0] * key[1], 1 - y if other else y, c if core is None else core)

    def exists(key):
        if key == origin:
            return None
        return z >= key[1] if key[0] < 0 else z + key[1] < depth

    def z_send(key):
        for side in (-1, 1) if key == origin else (key[0],):
            if key[1] + 1 < depth:
                source = own_part() if key == origin else part(shard(key, 0))
                links.send(
                    z_slot[(side, key[1] + 1)],
                    source,
                    part(shard(key, 0)),
                    links.up if side < 0 else links.down,
                    both(exists(key), z < depth - 1 if side < 0 else z > 0),
                )

    def y_send(key):
        source = own_part() if key == origin else part(shard(key, 0))
        links.send(y_slot[key], source, part(shard(key, 0)), links.y_peer, exists(key))

    def x_send(key, other):
        block = third_of(shard(key, other), x)
        links.send(x_slot[(key, other)], block, block, links.x_peer, exists(key))

    def c_send(key, other):
        whole = target(shard(key, other))
        source = own if (key, other) == (origin, 0) else whole
        links.send(c_slot[(key, other)], source, whole, links.c_peer, exists(key))

    order = []
    for far in range(1, depth):
        order += [((side, far), 0) for side in (-1, 1)]
        order += [(key, 1) for key in ([origin] if far == 1 else [(-1, far - 1), (1, far - 1)])]
    order += [((side, depth - 1), 1) for side in (-1, 1)]

    def start():
        z_send(origin)
        y_send(origin)
        c_send(origin, 0)

    def cross(keys_now):
        for key in keys_now:
            links.receive(y_slot[key], part(shard(key, 1)), exists(key))
            x_send(key, 1)

    def step(far):
        for side in (-1, 1):
            key = (side, far)
            links.receive(z_slot[key], part(shard(key, 0)), exists(key))
            z_send(key)
            y_send(key)
            x_send(key, 0)
        cross([origin] if far == 1 else [(-1, far - 1), (1, far - 1)])
        if far == depth - 1:
            cross([(-1, far), (1, far)])

    def share():
        for key, other in order:
            links.receive(x_slot[(key, other)], third_of(shard(key, other), 1 - x), exists(key))
            c_send(key, other)

    def settle():
        for key, other in [(origin, 0)] + order:
            links.receive(c_slot[(key, other)], target(shard(key, other, 1 - c)), exists(key))

    return start, step, share, settle

def split(value):
    high = value.astype(BF)
    return high, (value - high.astype(F32)).astype(BF)


def forward_kernel(
    depth,
    halves,
    rows,
    mats,
    patches,
    keep,
    keep_column,
    classes,
    label,
    weight,
    all_mats,
    resid,
    normed,
    project,
    log_total,
    context,
    mixed,
    normed_two,
    embedded,
    vectors,
    pooled_row,
    z_rows,
    feature_rows,
    vector_start,
    stats,
    rows_v,
    resid_v,
    normed_v,
    project_v,
    log_v,
    context_v,
    mixed_v,
    two_v,
    embed_v,
    weight_v,
    total_v,
    class_v,
    send_sem,
    recv_sem,
    local_sem,
    weight_sem,
    save_sem,
):
    links = Links(depth, send_sem, recv_sem)
    links.greet()
    layers, count, width = mats.shape
    size = count // halves
    own = [pltpu.make_async_copy(rows, rows_v.at[links.me], local_sem.at[0])]
    items = [gather_item(links, rows, lambda shard: rows_v.at[shard], rows.shape[0])]
    for layer in range(layers):
        own.append(
            pltpu.make_async_copy(
                mats.at[layer],
                all_mats.at[layer, pl.ds(links.me * count, count)],
                local_sem.at[1 + layer],
            )
        )
        for half in range(halves):

            def target(shard, layer=layer, half=half):
                return all_mats.at[layer, rows_at(shard * count + half * size, size)]

            items.append(gather_item(links, mats.at[layer, pl.ds(half * size, size)], target, size))
    for copy in own:
        copy.start()
    saves = []

    def save(source, target):
        copy = pltpu.make_async_copy(source, target, save_sem.at[len(saves)])
        copy.start()
        saves.append(copy)

    def table(begin, amount):
        return rows_v[:, :, pl.ds(begin, amount)].reshape(width, amount)

    pixels, seq = patches.shape[1], patches.shape[0]

    def column(index):
        return vectors[pl.ds(index, 1), :]

    def embed():
        own[0].wait()
        vectors[...] = table(pixels + EMB + SEQ, 128).astype(F32).T
        position = table(pixels + EMB, SEQ).astype(F32).T
        embed_v[...] = matmul_nt(patches[...], table(0, pixels)) + position
        save(embed_v, embedded)
        resid_v[0] = norm_forward(embed_v[...], column(0), column(1))

    order = []
    for layer in range(layers):
        order += [(layer, index) for index in (0, 1, 2, 3, 4, 8, 5, 9, 6, 10, 7, 11)]

    def chunk_copy(number):
        layer, index = order[number]
        return pltpu.make_async_copy(
            all_mats.at[layer, pl.ds(index * width, width)],
            weight_v.at[number % 4],
            weight_sem.at[number % 4],
        )

    def chunk(number):
        chunk_copy(number).wait()
        return weight_v[number % 4]

    half_lane = lax.broadcasted_iota(jnp.int32, (1, 128), 1) < HDIM
    scale = HDIM ** (-0.5)

    def attention_pair(layer, pair):
        def lanes(base):
            return pl.ds(pl.multiple_of(base + pair * 128, 128), 128)

        query, key = project_v[layer, :, lanes(0)], project_v[layer, :, lanes(width)]
        value = project_v[layer, :, lanes(2 * width)]
        results = []
        kept = log_v[layer]
        lane = lax.broadcasted_iota(jnp.int32, kept.shape, 1)
        for head in range(2):
            here = half_lane if head == 0 else jnp.logical_not(half_lane)
            query_h = jnp.where(here, query, jnp.zeros_like(query))
            scores = jnp.where(keep[...] > 0, matmul_nt(query_h, key) * scale, -1000000000.0)
            top = jnp.max(scores, -1, keepdims=True)
            expo = jnp.exp(scores - top)
            total = jnp.sum(expo, -1, keepdims=True)
            kept = jnp.where(lane == 2 * pair + head, top + jnp.log(total), kept)
            results.append(matmul((expo / total).astype(BF), value))
        log_v[layer] = kept
        context_v[layer, :, lanes(0)] = jnp.where(half_lane, results[0], results[1]).astype(BF)

    def layer_steps(layer):
        base, first = 4 + 12 * layer, 12 * layer

        def vector(index):
            return column(base + index)

        for number in range(first, first + 4):
            chunk_copy(number).start()
        log_v[layer] = jnp.zeros_like(log_v[layer])
        save(resid_v.at[layer], resid.at[layer])
        normed_v[layer] = norm_forward(resid_v[layer], vector(0), vector(1)).astype(BF)
        save(normed_v.at[layer], normed.at[layer])
        for part in range(3):
            result = matmul_nt(normed_v[layer], chunk(first + part))
            if part != 1:
                result += vector(2 if part == 0 else 3)
            project_v[layer, :, pl.ds(part * width, width)] = result.astype(BF)
            chunk_copy(first + 4 + part).start()
        save(project_v.at[layer], project.at[layer])
        yield
        for third in range(3):

            @pl.loop(0, 2)
            def _(turn, third=third):
                attention_pair(layer, 2 * third + turn)

            yield
        save(context_v.at[layer], context.at[layer])
        save(log_v.at[layer], log_total.at[layer])
        mixed_v[layer] = resid_v[layer] + (
            matmul_nt(context_v[layer], chunk(first + 3)) + vector(4)
        )
        chunk_copy(first + 7).start()
        save(mixed_v.at[layer], mixed.at[layer])
        two_v[layer] = norm_forward(mixed_v[layer], vector(5), vector(6)).astype(BF)
        save(two_v.at[layer], normed_two.at[layer])
        yield
        total_v[...] = mixed_v[layer] + vector(7)
        for part in range(4):
            number = first + 4 + 2 * part
            pre = matmul_nt(two_v[layer], chunk(number)) + vector(8 + part)
            hidden = (pre * jax.nn.sigmoid(1.702 * pre)).astype(BF)
            total_v[...] += matmul(hidden, chunk(number + 1))
            for ahead in (number + 4, number + 5):
                if ahead < first + 12:
                    chunk_copy(ahead).start()
            if part < 3:
                yield
        resid_v[layer + 1] = total_v[...]
        yield

    def class_units():
        value = classes[...].astype(F32)
        length = lax.rsqrt(jnp.sum(value * value, -1, keepdims=True) + unit_epsilon)
        class_v[...] = (value * length).astype(BF)

    def head():
        number = jnp.sum(keep[...], -1, keepdims=True)
        pooled = jnp.sum(resid_v[layers] * keep_column[...], 0, keepdims=True) / number
        center = pooled - jnp.mean(pooled, -1, keepdims=True)
        spread = lax.rsqrt(jnp.mean(center * center, -1, keepdims=True) + norm_epsilon)
        normal = center * spread
        z_value = jnp.broadcast_to(normal * column(2) + column(3), (16, width)).astype(BF)
        proj = table(pixels, EMB)
        feature = matmul(z_value, proj)
        inverse = lax.rsqrt(jnp.sum(feature * feature, -1, keepdims=True) + unit_epsilon)
        unit = (feature * inverse).astype(BF)
        logits = logit_scale * matmul_nt(unit, class_v[...])
        lane = lax.broadcasted_iota(jnp.int32, logits.shape, 1)
        logits = jnp.where(lane < CLASSES, logits, -1e30)
        top = jnp.max(logits, -1, keepdims=True)
        shifted = jnp.exp(logits - top)
        total = jnp.sum(shifted, -1, keepdims=True)
        chosen = lane == label[...]
        loss = top + jnp.log(total) - jnp.sum(jnp.where(chosen, logits, 0.0), -1, keepdims=True)
        logit_grad = weight[...] * (shifted / total - chosen.astype(F32))
        high, low = split(logit_grad)
        unit_grad = logit_scale * (matmul(high, class_v[...]) + matmul(low, class_v[...]))
        feature_grad = inverse * unit_grad - feature * inverse**3 * jnp.sum(
            unit_grad * feature, -1, keepdims=True
        )
        high, low = split(feature_grad)
        z_grad = (matmul_nt(high, proj) + matmul_nt(low, proj))[:1]
        scaled = z_grad * column(2)
        inner = spread * (
            scaled
            - jnp.mean(scaled, -1, keepdims=True)
            - normal * jnp.mean(scaled * normal, -1, keepdims=True)
        )
        pooled_row[...] = jnp.broadcast_to(inner / number, pooled_row.shape)
        spot = lax.broadcasted_iota(jnp.int32, (16, 1), 0)
        z_rows[...] = jnp.where(spot < 2, z_value, jnp.zeros_like(z_value))
        picked = jnp.where(spot == 0, high, jnp.where(spot == 1, low, jnp.zeros_like(low)))
        feature_rows[...] = picked
        vector_start[...] = jnp.zeros_like(vector_start)
        vector_start[pl.ds(2, 1), :] = z_grad * normal
        vector_start[pl.ds(3, 1), :] = z_grad
        here = lax.broadcasted_iota(jnp.int32, (8, 128), 1)
        first = lax.broadcasted_iota(jnp.int32, (8, 128), 0) == 0
        value = jnp.where(first & (here == 1), (loss * weight[...])[:8], 0.0)
        stats[...] = jnp.where(first & (here == 2), jnp.broadcast_to(weight[...], (8, 128)), value)

    running = None

    def work(amount):
        nonlocal running
        for _ in range(amount):
            if running is None:
                return
            if next(running, 0) == 0:
                running = None

    items[0][0]()
    class_units()
    for number, (_, step, _, _) in enumerate(items):
        step(1)
        work(1)
        step(2)
        if number + 1 < len(items):
            items[number + 1][0]()
        work(1)
        if number > 0:
            items[number - 1][2]()
        work(1)
        for far in range(3, depth):
            step(far)
        work(1)
        if number > 0:
            items[number - 1][3]()
            if number == 1:
                embed()
            for layer in range(layers - 1):
                if number - 1 == halves * (layer + 1):
                    own[1 + layer].wait()
                    work(1000)
                    running = counted(layer_steps(layer))
        work(1)
    items[-1][2]()
    work(2)
    items[-1][3]()
    work(1000)
    own[layers].wait()
    for _ in layer_steps(layers - 1):
        pass
    head()
    links.finish()
    for copy in saves:
        copy.wait()


def counted(steps):
    for _ in steps:
        yield 1


def forward(depth, rows, mats, patches, keep, keep_column, classes, label, weight):
    layers, count, width = mats.shape
    shards = PLANE * depth
    halves = 2
    seq = patches.shape[0]
    slots = (1 + layers * halves) * 60
    any_space = pl.BlockSpec(memory_space=pl.ANY)
    vmem = pl.BlockSpec(memory_space=pltpu.VMEM)

    def shape(*sizes, dtype=F32):
        return jax.ShapeDtypeStruct(sizes, dtype)

    saved = (
        shape(layers, seq, width),
        shape(layers, seq, width, dtype=BF),
        shape(layers, seq, 3 * width, dtype=BF),
        shape(layers, seq, 128),
        shape(layers, seq, width, dtype=BF),
        shape(layers, seq, width),
        shape(layers, seq, width, dtype=BF),
    )
    return pl.pallas_call(
        functools.partial(forward_kernel, depth, halves),
        out_shape=(shape(layers, shards * count, width, dtype=BF),)
        + saved
        + (
            shape(seq, width),
            shape(128, width),
            shape(8, width),
            shape(16, width, dtype=BF),
            shape(16, EMB, dtype=BF),
            shape(128, width),
            shape(8, 128),
        ),
        in_specs=[any_space] * 2 + [vmem] * 6,
        out_specs=[any_space] * 9 + [vmem] * 6,
        scratch_shapes=[
            pltpu.VMEM((shards,) + rows.shape, BF),
            pltpu.VMEM((layers + 1, seq, width), F32),
        ]
        + [pltpu.VMEM(array.shape, array.dtype) for array in saved[1:]]
        + [
            pltpu.VMEM((seq, width), F32),
            pltpu.VMEM((4, width, width), BF),
            pltpu.VMEM((seq, width), F32),
            pltpu.VMEM(classes.shape, BF),
            pltpu.SemaphoreType.DMA((slots,)),
            pltpu.SemaphoreType.DMA((slots,)),
            pltpu.SemaphoreType.DMA((1 + layers,)),
            pltpu.SemaphoreType.DMA((4,)),
            pltpu.SemaphoreType.DMA((1 + 7 * layers,)),
        ],
        name="gather_and_forward",
        compiler_params=pltpu.CompilerParams(
            collective_id=1, has_side_effects=True, vmem_limit_bytes=56 * 1024 * 1024
        ),
    )(rows, mats, patches, keep, keep_column, classes, label, weight)


def accumulate(target, start, source, begin, count, step):
    @pl.loop(0, count // step)
    def _(turn):
        here = rows_at(start + turn * step, step)
        there = rows_at(begin + turn * step, step)
        target[here, :] = (target[here, :].astype(F32) + source[there, :].astype(F32)).astype(BF)


class Group(NamedTuple):
    begin: object
    stages: list
    core_slot: list


def scatter_group(links, dest, load, sizes, bufs, emit, used=None):
    depth, z, y, c, x = links.depth, links.z, links.y, links.c, links.x
    n, p, q, step = sizes
    mine, core_in, x_in, y_in, z_in, z_last, final = bufs
    core_slot, x_slot = [links.slot(), links.slot()], [links.slot(), links.slot()]
    q_slot, p_slot, low_slot, high_slot, last_slot = (links.slot() for _ in range(5))
    m = p + q
    first = x * p
    own_p, peer_p = x * m, (1 - x) * m
    sides = ((0, 1 - y), (1, y))

    def begin():
        for i, side in sides:
            load(i, side, mine.at[side], core_in.at[side], core_slot[i])

    def stage_core():
        for i, side in sides:
            load(i, side, mine.at[side], None, None)
            links.receive(core_slot[i], core_in.at[side])
            accumulate(mine.at[side], 0, core_in.at[side], 0, n, step)
            links.send(x_slot[i], mine.at[side, rows_at(peer_p, p)], x_in.at[side], links.x_peer)
            if i == 0:
                links.send(q_slot, mine.at[side, pl.ds(p, q)], y_in.at[pl.ds(0, q)], links.y_peer)
        if used is not None:
            used()

    def stage_x():
        for i, side in sides:
            links.receive(x_slot[i], x_in.at[side])
            accumulate(mine.at[side], own_p, x_in.at[side], 0, p, step)
            if i == 0:
                links.send(
                    p_slot, mine.at[side, rows_at(own_p, p)], y_in.at[pl.ds(q, p)], links.y_peer
                )
        links.receive(q_slot, y_in.at[pl.ds(0, q)])
        accumulate(mine.at[y], p, y_in, 0, q, step)

    def stage_y():
        links.receive(p_slot, y_in.at[pl.ds(q, p)])
        accumulate(mine.at[y], own_p, y_in, q, p, step)

    def stage_z(hop):
        block = mine.at[y, rows_at(first, m)]

        def take(slot, source, pred):
            @pl.when(pred)
            def _():
                links.receive(slot, source)
                accumulate(mine.at[y], first, source, 0, m, step)

        if dest > 0:
            if 1 <= hop <= dest:
                take(low_slot, z_in, z == hop)
            if hop < dest:
                links.send(low_slot, block, z_in, links.up, z == hop)
        if dest < depth - 1:
            turn = depth - 1 - hop
            if hop >= 1 and turn > dest:
                take(high_slot, z_in, z == turn)
            if turn > dest + 1:
                links.send(high_slot, block, z_in, links.down, z == turn)
            if turn == dest + 1:
                links.send(high_slot, block, z_last, links.down, z == turn)
            if turn == dest and hop >= 1:
                take(high_slot, z_last, z == dest)
        if hop == max(dest, depth - 1 - dest):
            links.send(last_slot, block, final, links.x_peer, z == dest)

    def stage_last():
        links.finish(x_slot[1])
        links.finish(last_slot)

        @pl.when(z == dest)
        def _():
            links.receive(last_slot, final)
            accumulate(mine.at[y], p, final, jnp.where(x == 0, 0, p), q, step)

            @pl.loop(0, p // 16)
            def _(turn):
                there = rows_at(jnp.where(x == 0, q, 0) + turn * 16, 16)
                mine[y, rows_at(peer_p + turn * 16, 16), :] = final[there, :]

            emit(mine.at[y])

    hops = [functools.partial(stage_z, hop) for hop in range(depth)]
    return Group(begin, [stage_core, stage_x, stage_y] + hops + [stage_last], core_slot)

def norm_back(value, gain, upstream):
    center = value - jnp.mean(value, -1, keepdims=True)
    scale = lax.rsqrt(jnp.mean(center * center, -1, keepdims=True) + norm_epsilon)
    normal = center * scale
    scaled = upstream * gain
    inner = scale * (
        scaled
        - jnp.mean(scaled, -1, keepdims=True)
        - normal * jnp.mean(scaled * normal, -1, keepdims=True)
    )
    return (
        inner,
        jnp.sum(upstream * normal, 0, keepdims=True),
        jnp.sum(upstream, 0, keepdims=True),
    )


VMEM_LIMIT = 62 * 1024 * 1024
SUB = 3
IN_FLIGHT = 2 * SUB
LAGS = (1, 3, 5, 7, 9, 11, 13, 15)


def backward_kernel(
    depth,
    sides,
    layers,
    weights,
    resid,
    normed,
    project,
    log_total,
    context,
    mixed,
    normed_two,
    embedded,
    patches,
    vectors,
    keep,
    keep_column,
    pooled_row,
    z_rows,
    feature_rows,
    vector_start,
    stats,
    out,
    row_out,
    totals,
    blocks_v,
    core_in,
    x_in,
    y_in,
    z_in,
    z_last,
    final,
    rows_v,
    row_mine,
    row_core,
    row_x,
    row_y,
    row_z,
    row_z_last,
    row_final,
    resid_v,
    normed_v,
    project_v,
    log_v,
    context_v,
    mixed_v,
    two_v,
    weight_v,
    patch_v,
    hidden_v,
    pre_v,
    up_v,
    short_v,
    total_v,
    context_grad_v,
    vector_v,
    note,
    inbox,
    send_sem,
    recv_sem,
    local_sem,
    weight_sem,
    load_sem,
    mail_send,
    mail_recv,
    free_sem,
):
    links = Links(depth, send_sem, recv_sem)
    y, c, z = links.y, links.c, links.z
    me = links.me * sides + links.x
    everyone = PLANE * depth * sides
    width = up_v.shape[1]
    count = out.shape[1]
    n = count // SUB
    p = n // 4 // 16 * 16
    per_layer = depth * SUB
    own = 2 * layers * per_layer
    piece = 2 * n

    saved = (
        (normed_two, two_v),
        (mixed, mixed_v),
        (context, context_v),
        (resid, resid_v),
        (normed, normed_v),
        (project, project_v),
        (log_total, log_v),
    )

    def load(layer, which):
        source, target = saved[which]
        return pltpu.make_async_copy(source.at[layer], target, load_sem.at[which])

    chunks = []
    for layer in reversed(range(layers)):
        for turn in (3, 2, 1, 0):
            chunks += [(layer, 8 + turn), (layer, 4 + turn)]
        chunks += [(layer, 3), (layer, 0), (layer, 1), (layer, 2)]

    def chunk_copy(number):
        layer, index = chunks[number]
        return pltpu.make_async_copy(
            weights.at[layer, pl.ds(index * width, width)],
            weight_v.at[number % 4],
            weight_sem.at[number % 4],
        )

    def chunk(number):
        chunk_copy(number).wait()
        return weight_v[number % 4]

    def refill(*numbers):
        for number in numbers:
            if number < len(chunks):
                chunk_copy(number).start()

    for which in range(len(saved)):
        load(layers - 1, which).start()
    refill(0, 1, 2, 3)
    patch_load = pltpu.make_async_copy(patches, patch_v, load_sem.at[7])
    patch_load.start()

    def others(run):
        for number in range(everyone):
            pl.when(me != number)(functools.partial(run, number))

    def place(number):
        return (number // sides, number % sides)

    barrier = pltpu.get_barrier_semaphore()
    others(
        lambda number: pl.semaphore_signal(
            barrier, inc=1, device_id=place(number), device_id_type=MESH
        )
    )
    note[...] = stats[...]
    vector_v[...] = vector_start[...]
    up_v[...] = keep_column[...] * pooled_row[pl.ds(0, 1), :]
    lane = lax.broadcasted_iota(jnp.int32, (8, 128), 1)
    first = lax.broadcasted_iota(jnp.int32, (8, 128), 0) == 0

    def add_squares(block):
        value = block.astype(F32)
        note[...] += jnp.where(first & (lane == 0), jnp.sum(value * value), 0.0)

    groups, closers = [], []
    starts = {}

    def add_group(dest, send_out, take_in, sizes, bufs, emit, used=None):
        def load_block(i, side, mine, target, slot):
            if target is None:
                take_in(i, side, mine)
            else:
                send_out(i, side, mine, target, slot)

        groups.append(scatter_group(links, dest, load_block, sizes, bufs, emit, used))

    for order, layer in enumerate(reversed(range(layers))):
        for turn, dest in enumerate(reversed(range(depth))):
            ring = own
            for part in range(SUB):
                number, spot = len(groups), layer * SUB + part
                starts[(layer, dest, part)] = number
                slot = number % IN_FLIGHT

                def send_out(i, side, mine, target, sem_slot, ring=ring, part=part):
                    source = blocks_v.at[ring + 2 * part + side]
                    links.send(sem_slot, source, target, links.c_peer)

                def write(source, layer=layer, part=part, spot=spot):
                    target = out.at[layer, pl.ds(part * n, n)]
                    return pltpu.make_async_copy(source, target, local_sem.at[spot])

                def emit(result, write=write):
                    add_squares(result[...])
                    write(result).start()

                closers.append((dest, write, blocks_v.at[2 * number]))

                def used(number=number):
                    if number < layers * per_layer - IN_FLIGHT:
                        pl.semaphore_signal(
                            free_sem, inc=1, device_id=links.c_peer, device_id_type=MESH
                        )

                add_group(
                    dest,
                    send_out,
                    lambda i, side, mine: None,
                    (n, p, n - 2 * p, n // 4),
                    [blocks_v.at[pl.ds(2 * number, 2)], core_in.at[slot]]
                    + [ref.at[number] for ref in (x_in, y_in, z_in)]
                    + [z_last.at[spot], final.at[spot]],
                    emit,
                    used,
                )
    first_row_group = len(groups)
    rows = row_out.shape[0]
    for dest in reversed(range(depth)):
        number = len(groups)

        def row_copy(i, side, mine, dest=dest):
            sem = local_sem.at[layers * SUB + 2 * dest + i]
            return pltpu.make_async_copy(rows_v.at[links.at(dest, side, c)], mine, sem)

        def row_send(i, side, mine, target, slot, dest=dest, row_copy=row_copy):
            row_copy(i, side, mine).start()
            source = rows_v.at[links.at(dest, side, 1 - c)]
            links.send(slot, source, target, links.c_peer)

        def row_emit(result, dest=dest):
            add_squares(result[...])
            row_out[...] = result[...]

        add_group(
            dest,
            row_send,
            lambda i, side, mine, row_copy=row_copy: row_copy(i, side, mine).wait(),
            (rows, 16, rows - 32, 16),
            [ref.at[dest] for ref in (row_mine, row_core, row_x, row_y, row_z)]
            + [row_z_last, row_final],
            row_emit,
        )

    begun = []

    def release(layer, dest):
        for part in range(SUB):
            number = starts[(layer, dest, part)]
            if number >= IN_FLIGHT:
                pl.semaphore_wait(free_sem, 1)
            groups[number].begin()
            begun.append(number)

    def recycle(layer, dest):
        for part in range(SUB):
            number = starts[(layer, dest, part)]
            if number >= SUB:
                for slot in groups[number - SUB].core_slot:
                    links.finish(slot)

    last_turn = [0]

    def advance():
        turn = last_turn[0]
        for stage, lag in enumerate(LAGS):
            if 0 <= turn - lag < len(groups):
                groups[turn - lag].stages[stage]()
        last_turn[0] += 1

    def grad_pieces(layer, dest, left, column, amount, right, begin):
        number = starts[(layer, dest, 0)]
        ring = own

        @pl.loop(0, amount)
        def _(turn):
            columns = pl.ds(pl.multiple_of(column + turn * piece, 128), piece)
            result = matmul_tn(left[:, columns], right[...])
            for half in range(2):
                block = 2 * (begin + turn) + half
                shard = block // SUB
                part = lax.rem(block, SUB)
                side, core = shard // 2, lax.rem(shard, 2)
                index = jnp.where(
                    core == c, 2 * (number + part) + side, ring + 2 * part + side
                )
                blocks_v[index] = result[half * n : (half + 1) * n].astype(BF)

    half_lane = lax.broadcasted_iota(jnp.int32, (1, 128), 1) < HDIM
    scale = HDIM ** (-0.5)

    def attention_pair(pair):
        def lanes(base):
            return pl.ds(pl.multiple_of(base + pair * 128, 128), 128)

        query, key = project_v[:, lanes(0)], project_v[:, lanes(width)]
        value, grad = project_v[:, lanes(2 * width)], context_grad_v[:, lanes(0)]
        totals_now = log_v[...]
        column = lax.broadcasted_iota(jnp.int32, totals_now.shape, 1)
        query_grad = key_grad = value_grad = 0.0
        zero = jnp.zeros_like(query)
        for head in range(2):
            here = half_lane if head == 0 else jnp.logical_not(half_lane)
            query_h, key_h = jnp.where(here, query, zero), jnp.where(here, key, zero)
            grad_h = jnp.where(here, grad, zero)
            total = jnp.sum(
                jnp.where(column == 2 * pair + head, totals_now, 0.0), -1, keepdims=True
            )
            scores = jnp.where(keep[...] > 0, matmul_nt(query_h, key) * scale, -1000000000.0)
            probs = jnp.exp(scores - total)
            prob_grad = matmul_nt(grad_h, value)
            value_grad += matmul_tn(probs.astype(BF), grad_h)
            score_grad = (
                probs * (prob_grad - jnp.sum(prob_grad * probs, -1, keepdims=True))
            ).astype(BF)
            query_grad += matmul(score_grad, key_h)
            key_grad += matmul_tn(score_grad, query_h)
        pre_v[:, lanes(0)] = (query_grad * scale).astype(BF)
        pre_v[:, lanes(width)] = (key_grad * scale).astype(BF)
        pre_v[:, lanes(2 * width)] = value_grad.astype(BF)

    def layer_steps(order, layer):
        base = 4 + 12 * layer
        chunk0 = 12 * order

        def vector(index):
            return vectors[pl.ds(base + index, 1), :]

        def put(index, value):
            vector_v[pl.ds(base + index, 1), :] = value

        def column_sum(value):
            return jnp.sum(value.astype(F32), 0, keepdims=True)

        load(layer, 0).wait()
        short_v[...] = up_v[...].astype(BF)
        put(7, column_sum(short_v[...]))
        total_v[...] = jnp.zeros_like(total_v)
        recycle(layer, 3)
        for turn, part in enumerate((3, 2, 1, 0)):
            number = chunk0 + 2 * turn
            down, up = chunk(number), chunk(number + 1)
            pre = matmul_nt(two_v[...], up) + vector(8 + part)
            gate = jax.nn.sigmoid(1.702 * pre)
            hidden_v[...] = (pre * gate).astype(BF)
            slope = gate + 1.702 * pre * gate * (1.0 - gate)
            pre_grad = (matmul_nt(short_v[...], down) * slope).astype(BF)
            pre_v[:, pl.ds(part * width, width)] = pre_grad
            put(8 + part, column_sum(pre_grad))
            total_v[...] += matmul(pre_grad, up)
            refill(number + 4, number + 5)
            yield None
            if part == 0:
                recycle(layer, 2)
            if part > 0:
                grad_pieces(layer, 3, hidden_v, 0, 2, short_v, 2 * (part - 1))
            else:
                grad_pieces(layer, 2, hidden_v, 0, 2, short_v, 4)
            if part == 1:
                release(layer, 3)
                yield 3
            else:
                yield None
        grad_pieces(layer, 2, pre_v, 2 * width, 2, two_v, 0)
        yield None
        grad_pieces(layer, 2, pre_v, 3 * width, 2, two_v, 2)
        release(layer, 2)
        yield 2
        load(layer, 1).wait()
        inner, gain, shift = norm_back(mixed_v[...], vector(5), total_v[...])
        put(5, gain)
        put(6, shift)
        up_v[...] += inner
        short_v[...] = up_v[...].astype(BF)
        put(4, column_sum(short_v[...]))
        yield None
        load(layer, 2).wait()
        recycle(layer, 1)
        grad_pieces(layer, 1, short_v, 0, 2, context_v, 0)
        context_grad_v[...] = matmul(short_v[...], chunk(chunk0 + 8)).astype(BF)
        refill(chunk0 + 12)
        yield None
        grad_pieces(layer, 1, pre_v, 0, 2, two_v, 2)
        yield None
        grad_pieces(layer, 1, pre_v, width, 2, two_v, 4)
        release(layer, 1)
        if layer > 0:
            for which in range(3):
                load(layer - 1, which).start()
        else:
            embed_load.start()
        yield 1
        load(layer, 5).wait()
        load(layer, 6).wait()
        for third in range(3):

            @pl.loop(0, 2)
            def _(turn, third=third):
                attention_pair(2 * third + turn)

            yield None
        load(layer, 4).wait()
        recycle(layer, 0)
        put(2, column_sum(pre_v[:, pl.ds(0, width)]))
        put(3, column_sum(pre_v[:, pl.ds(2 * width, width)]))
        for third in range(3):
            grad_pieces(layer, 0, pre_v, third * width, 2, normed_v, 2 * third)
            if third < 2:
                yield None
        release(layer, 0)
        yield 0
        load(layer, 3).wait()
        back = matmul(pre_v[:, pl.ds(0, width)], chunk(chunk0 + 9))
        back += matmul(pre_v[:, pl.ds(width, width)], chunk(chunk0 + 10))
        back += matmul(pre_v[:, pl.ds(2 * width, width)], chunk(chunk0 + 11))
        refill(chunk0 + 13, chunk0 + 14, chunk0 + 15)
        inner, gain, shift = norm_back(resid_v[...], vector(0), back)
        put(0, gain)
        put(1, shift)
        up_v[...] += inner
        if layer > 0:
            for which in range(3, len(saved)):
                load(layer - 1, which).start()
        yield None

    embed_load = pltpu.make_async_copy(embedded, mixed_v, load_sem.at[8])
    pl.semaphore_wait(barrier, everyone - 1)
    pending = 0
    for order, layer in enumerate(reversed(range(layers))):
        for ready in layer_steps(order, layer):
            if ready is not None:
                pending += SUB
            if pending > 0:
                advance()
                pending -= 1
    embed_load.wait()
    inner, gain, shift = norm_back(mixed_v[...], vectors[pl.ds(0, 1), :], up_v[...])
    vector_v[pl.ds(0, 1), :] = gain
    vector_v[pl.ds(1, 1), :] = shift
    short_v[...] = inner.astype(BF)
    total_v[...] = inner
    patch_load.wait()
    pixels, embeds, seq = patch_v.shape[1], feature_rows.shape[1], inner.shape[0]
    for turn in range(width // piece):
        columns = pl.ds(turn * piece, piece)
        patch_grad = matmul_tn(short_v[:, columns], patch_v[...])
        proj_grad = matmul_tn(z_rows[:, columns], feature_rows[...])
        position = total_v[:, columns].T
        vector_grad = vector_v[:, columns].T
        for part in range(piece // rows):
            shard, inside = turn * (piece // rows) + part, slice(part * rows, (part + 1) * rows)
            rows_v[shard, :, pl.ds(0, pixels)] = patch_grad[inside].astype(BF)
            rows_v[shard, :, pl.ds(pixels, embeds)] = proj_grad[inside].astype(BF)
            rows_v[shard, :, pl.ds(pixels + embeds, seq)] = position[inside].astype(BF)
            rows_v[shard, :, pl.ds(pixels + embeds + seq, 128)] = vector_grad[inside].astype(BF)
    for number in range(first_row_group, len(groups)):
        groups[number].begin()
    while last_turn[0] < len(groups) + max(LAGS):
        advance()

    def mail(number, slot):
        return pltpu.make_async_remote_copy(
            src_ref=note,
            dst_ref=inbox.at[slot],
            send_sem=mail_send.at[number],
            recv_sem=mail_recv.at[slot],
            device_id=place(number),
            device_id_type=MESH,
        )

    others(lambda number: mail(number, me).start())
    inbox[pl.ds(me, 1)] = note[...][None]
    links.finish()
    for dest, write, source in closers:
        pl.when(z == dest)(lambda write=write, source=source: write(source).wait())
    others(lambda number: mail(number, number).wait_recv())
    summed = jnp.sum(inbox[...], 0)
    others(lambda number: mail(number, me).wait_send())

    def pick(index):
        return jnp.sum(jnp.where(first & (lane == index), summed, 0.0))

    loss_sum, weight_sum = pick(1), pick(2)
    norm = jnp.sqrt(jnp.full((8, 128), pick(0) / sides)) / weight_sum
    clip = jnp.minimum(1.0, clip_bound / (norm + 1e-06)) / weight_sum
    totals[...] = jnp.where(
        lane == 0,
        loss_sum,
        jnp.where(lane == 1, weight_sum, jnp.where(lane == 2, norm, clip)),
    )


def backward(
    depth, sides, weights, saved, embedded, patches, vectors, keep, keep_column, head, start, stats
):
    layers, rows_all, width = weights.shape
    seq, pixels = patches.shape
    shards = PLANE * depth
    count, rows = rows_all // shards, width // shards
    lanes = -(-(pixels + EMB + SEQ + 4 + 12 * layers) // 128) * 128
    n = count // SUB
    p = n // 4 // 16 * 16
    m = n - p
    per_layer = depth * SUB
    blocks = layers * per_layer
    row_m = rows - 16
    everyone = shards * sides

    def room(*shape, dtype=BF):
        return pltpu.VMEM(shape, dtype)

    any_space = pl.BlockSpec(memory_space=pl.ANY)
    vmem = pl.BlockSpec(memory_space=pltpu.VMEM)
    slots = (blocks + depth) * 9
    return pl.pallas_call(
        functools.partial(backward_kernel, depth, sides, layers),
        out_shape=(
            jax.ShapeDtypeStruct((layers, count, width), BF),
            jax.ShapeDtypeStruct((rows, lanes), BF),
            jax.ShapeDtypeStruct((8, 128), F32),
        ),
        in_specs=[any_space] * (1 + len(saved) + 2) + [vmem] * 8,
        out_specs=[any_space, vmem, vmem],
        scratch_shapes=[
            room(2 * blocks + 2 * SUB, n, width),
            room(IN_FLIGHT, 2, n, width),
            room(blocks, 2, p, width),
            room(blocks, m, width),
            room(blocks, m, width),
            room(layers * SUB, m, width),
            room(layers * SUB, m, width),
            room(shards, rows, lanes),
            room(depth, 2, rows, lanes),
            room(depth, 2, rows, lanes),
            room(depth, 2, 16, lanes),
            room(depth, row_m, lanes),
            room(depth, row_m, lanes),
            room(row_m, lanes),
            room(row_m, lanes),
            room(seq, width, dtype=F32),
            room(seq, width),
            room(seq, 3 * width),
            room(seq, 128, dtype=F32),
            room(seq, width),
            room(seq, width, dtype=F32),
            room(seq, width),
            room(4, width, width),
            room(seq, pixels),
            room(seq, width),
            room(seq, 4 * width),
            room(seq, width, dtype=F32),
            room(seq, width),
            room(seq, width, dtype=F32),
            room(seq, width),
            room(128, width, dtype=F32),
            room(8, 128, dtype=F32),
            room(everyone, 8, 128, dtype=F32),
            pltpu.SemaphoreType.DMA((slots,)),
            pltpu.SemaphoreType.DMA((slots,)),
            pltpu.SemaphoreType.DMA((layers * SUB + 2 * depth,)),
            pltpu.SemaphoreType.DMA((4,)),
            pltpu.SemaphoreType.DMA((9,)),
            pltpu.SemaphoreType.DMA((everyone,)),
            pltpu.SemaphoreType.DMA((everyone,)),
            pltpu.SemaphoreType.REGULAR,
        ],
        name="backward_and_sum",
        compiler_params=pltpu.CompilerParams(
            collective_id=2, has_side_effects=True, vmem_limit_bytes=VMEM_LIMIT
        ),
    )(weights, *saved, embedded, patches, vectors, keep, keep_column, *head, start, stats)


def finish_kernel(
    hyper,
    totals,
    grad,
    momentum,
    mats,
    zero,
    ema,
    new_momentum,
    new_mats,
    new_ema,
    new_mixed,
    grad_v,
    m_v,
    mats_v,
    zero_v,
    ema_v,
    x_v,
    short_v,
    low_v,
    in_sem,
    out_sem,
):
    layers, count, width = grad.shape
    pairs = [(grad, grad_v), (momentum, m_v)]
    pairs += [(mats, mats_v), (zero, zero_v), (ema, ema_v)]
    loads = [pltpu.make_async_copy(a, b, in_sem.at[i]) for i, (a, b) in enumerate(pairs)]
    for load in loads:
        load.start()
    part = count // 3
    factor = totals[pl.ds(0, 1), pl.ds(3, 1)]
    loads[0].wait()
    loads[1].wait()
    stores = []
    for layer in range(layers):
        total = jnp.zeros((1, 1), F32)
        for third in range(3):
            rows = pl.ds(third * part, part)
            value = momentum_decay * m_v[layer, rows, :] + factor * grad_v[layer, rows, :].astype(F32)
            m_v[layer, rows, :] = value
            total += jnp.sum(value * value, keepdims=True)
        store = pltpu.make_async_copy(m_v.at[layer], new_momentum.at[layer], out_sem.at[layer])
        store.start()
        stores.append(store)
        inverse = 1.0 / (jnp.sqrt(total) + 1e-07)
        for third in range(3):
            rows = pl.ds(third * part, part)
            value = m_v[layer, rows, :] * inverse
            x_v[layer, rows, :] = value
            short_v[0, layer, rows, :] = value.astype(BF)

    row_id = lax.broadcasted_iota(jnp.int32, (part, count), 0)
    col_id = lax.broadcasted_iota(jnp.int32, (part, count), 1)

    @pl.loop(0, NS_STEPS)
    def _(turn):
        now, later = lax.rem(turn, 2), 1 - lax.rem(turn, 2)
        shift = jnp.where(turn >= NS_STEPS - 2, 1.0, 0.0)
        linear = coeff_cubic + 2.0 * shift * coeff_quintic
        stay = coeff_linear + shift * (coeff_cubic + shift * coeff_quintic)
        for layer in range(layers):
            for third in range(3):
                rows = pl.ds(third * part, part)
                gram = matmul_nt(short_v[now, layer, rows, :], short_v[now, layer])
                gram -= jnp.where(row_id + third * part == col_id, shift, 0.0)
                low_v[layer, rows, :] = gram.astype(BF)
        for layer in range(layers):
            for third in range(3):
                rows = pl.ds(third * part, part)
                low = low_v[layer, rows, :]
                poly = linear * low.astype(F32) + coeff_quintic * matmul(low, low_v[layer])
                value = stay * x_v[layer, rows, :] + matmul(poly.astype(BF), short_v[now, layer])
                x_v[layer, rows, :] = value
                short_v[later, layer, rows, :] = value.astype(BF)

    for load in loads[2:]:
        load.wait()
    for layer in range(layers):
        for third in range(3):
            rows = pl.ds(third * part, part)
            old = mats_v[layer, rows, :]
            value = old - muon_rate * (
                hyper * x_v[layer, rows, :] + weight_decay * old
            )
            mats_v[layer, rows, :] = value
            ema_v[layer, rows, :] = ema_decay * ema_v[layer, rows, :] + (1.0 - ema_decay) * value
            zero_v[layer, rows, :] = mix_share * value + (1.0 - mix_share) * zero_v[layer, rows, :]
            for turn, (source, target) in enumerate(
                ((mats_v, new_mats), (ema_v, new_ema), (zero_v, new_mixed))
            ):
                sem = out_sem.at[layers + (layer * 3 + third) * 3 + turn]
                store = pltpu.make_async_copy(source.at[layer, rows], target.at[layer, rows], sem)
                store.start()
                stores.append(store)
    for store in stores:
        store.wait()


def finish(totals, grad, momentum, mats, zero, ema):
    layers, count, width = grad.shape
    full = jax.ShapeDtypeStruct(mats.shape, F32)
    any_space = pl.BlockSpec(memory_space=pl.ANY)
    vmem = pl.BlockSpec(memory_space=pltpu.VMEM)
    return pl.pallas_call(
        functools.partial(finish_kernel, 0.2 * math.sqrt(width)),
        out_shape=(full, full, full, full),
        in_specs=[vmem] + [any_space] * 5,
        out_specs=[any_space] * 4,
        scratch_shapes=[
            pltpu.VMEM(grad.shape, BF),
            pltpu.VMEM(mats.shape, F32),
            pltpu.VMEM(mats.shape, F32),
            pltpu.VMEM(mats.shape, F32),
            pltpu.VMEM(mats.shape, F32),
            pltpu.VMEM(mats.shape, F32),
            pltpu.VMEM((2,) + mats.shape, BF),
            pltpu.VMEM((layers, count, count), BF),
            pltpu.SemaphoreType.DMA((5,)),
            pltpu.SemaphoreType.DMA((layers * 10,)),
        ],
        name="orthogonalize",
        compiler_params=pltpu.CompilerParams(vmem_limit_bytes=56 * 1024 * 1024),
    )(totals, grad, momentum, mats, zero, ema)


def gather_layer(shard):
    return lax.all_gather(shard.astype(jnp.bfloat16), "fsdp", axis=0, tiled=True)


def layer_forward(resid, weight_tensors, vector, valid_mask):
    images, seq = valid_mask.shape
    width = resid.shape[1]
    ffn = 4 * width
    normed = norm_forward(resid, vector[0], vector[1]).astype(jnp.bfloat16)
    bias = jnp.concatenate([vector[2], jnp.zeros_like(vector[2]), vector[3]])
    project = (matmul_nt(normed, weight_tensors[: 3 * width]) + bias).astype(jnp.bfloat16)
    parts = project.reshape(images, seq, 3, HEADS, HDIM)
    scores = attention_scores(parts, valid_mask)
    top_score = jnp.max(scores, -1, keepdims=True)
    expo = jnp.exp(scores - top_score)
    totals = jnp.sum(expo, -1, keepdims=True)
    log_total = top_score + jnp.log(totals)
    probs = (expo / totals).astype(jnp.bfloat16)
    context = jnp.einsum(
        "ihqk,ikhd->iqhd", probs, parts[:, :, 2], preferred_element_type=jnp.float32
    )
    context = context.reshape(images * seq, width).astype(jnp.bfloat16)
    mixed = resid + (matmul_nt(context, weight_tensors[3 * width : 4 * width]) + vector[4])
    normed_two = norm_forward(mixed, vector[5], vector[6]).astype(jnp.bfloat16)
    hidden_pre = matmul_nt(normed_two, weight_tensors[4 * width : 4 * width + ffn]) + vector[
        8:12
    ].reshape(ffn)
    hidden = (hidden_pre * jax.nn.sigmoid(1.702 * hidden_pre)).astype(jnp.bfloat16)
    output = mixed + (matmul(hidden, weight_tensors[4 * width + ffn :]) + vector[7])
    return (
        output,
        (resid, normed, project, log_total, context, mixed, normed_two, hidden_pre, hidden),
    )


def layer_backward(upstream, weight_tensors, vector, valid_mask, saved_activation):
    resid, normed, project, log_total, context, mixed, normed_two, hidden_pre, hidden = (
        saved_activation
    )
    images, seq = valid_mask.shape
    width = resid.shape[1]
    ffn = 4 * width
    out_grad = upstream.astype(jnp.bfloat16)
    grad_down = matmul_tn(hidden, out_grad)
    hidden_grad = matmul_nt(out_grad, weight_tensors[4 * width + ffn :])
    gate = jax.nn.sigmoid(1.702 * hidden_pre)
    pre_grad = (hidden_grad * (gate + 1.702 * hidden_pre * gate * (1.0 - gate))).astype(
        jnp.bfloat16
    )
    grad_up = matmul_tn(pre_grad, normed_two)
    second_in, gain_two, shift_two = norm_backward(
        mixed, vector[5], matmul(pre_grad, weight_tensors[4 * width : 4 * width + ffn])
    )
    mixed_grad = upstream + second_in
    attn_grad = mixed_grad.astype(jnp.bfloat16)
    grad_out = matmul_tn(attn_grad, context)
    context_grad = matmul(attn_grad, weight_tensors[3 * width : 4 * width]).astype(jnp.bfloat16)
    context_grad = context_grad.reshape(images, seq, HEADS, HDIM)
    parts = project.reshape(images, seq, 3, HEADS, HDIM)
    probs = jnp.exp(attention_scores(parts, valid_mask) - log_total)
    prob_grad = jnp.einsum(
        "iqhd,ikhd->ihqk", context_grad, parts[:, :, 2], preferred_element_type=jnp.float32
    )
    value_grad = jnp.einsum(
        "ihqk,iqhd->ikhd",
        probs.astype(jnp.bfloat16),
        context_grad,
        preferred_element_type=jnp.float32,
    )
    score_grad = (probs * (prob_grad - jnp.sum(prob_grad * probs, -1, keepdims=True))).astype(
        jnp.bfloat16
    )
    query_grad = jnp.einsum(
        "ihqk,ikhd->iqhd", score_grad, parts[:, :, 1], preferred_element_type=jnp.float32
    ) * HDIM ** (-0.5)
    key_grad = jnp.einsum(
        "ihqk,iqhd->ikhd", score_grad, parts[:, :, 0], preferred_element_type=jnp.float32
    ) * HDIM ** (-0.5)
    project_grad = (
        jnp.stack([query_grad, key_grad, value_grad], 2)
        .reshape(images * seq, 3 * width)
        .astype(jnp.bfloat16)
    )
    project_sum = jnp.sum(project_grad.astype(jnp.float32), 0)
    grad_qkv = matmul_tn(project_grad, normed)
    first_in, gain_one, shift_one = norm_backward(
        resid, vector[0], matmul(project_grad, weight_tensors[: 3 * width])
    )
    residual_gradient = mixed_grad + first_in
    grad_matrix = [part.astype(BF) for part in (grad_qkv, grad_out, grad_up, grad_down)]
    grad_vector = jnp.concatenate(
        [
            jnp.stack(
                [
                    gain_one,
                    shift_one,
                    project_sum[:width],
                    project_sum[2 * width :],
                    jnp.sum(attn_grad.astype(jnp.float32), 0),
                    gain_two,
                    shift_two,
                    jnp.sum(out_grad.astype(jnp.float32), 0),
                ]
            ),
            jnp.sum(pre_grad.astype(jnp.float32), 0).reshape(4, width),
        ],
        0,
    )
    return (residual_gradient, grad_matrix, grad_vector)


def newton_schulz(blocks):
    frob = jnp.sqrt(jnp.sum(blocks * blocks, axis=(1, 2), keepdims=True)) + 1e-07
    blocks = blocks / frob
    unit = jnp.eye(blocks.shape[1], dtype=jnp.float32)
    for turn in range(NS_STEPS):
        shift = 1.0 if turn >= NS_STEPS - 2 else 0.0
        short = blocks.astype(BF)
        gram = jnp.einsum("lcd,led->lce", short, short, preferred_element_type=F32) - shift * unit
        low = gram.astype(BF)
        square = jnp.einsum("lce,lef->lcf", low, low, preferred_element_type=F32)
        poly = (coeff_cubic + 2.0 * shift * coeff_quintic) * gram + coeff_quintic * square
        stay = coeff_linear + shift * (coeff_cubic + shift * coeff_quintic)
        blocks = stay * blocks + jnp.einsum(
            "lce,led->lcd", poly.astype(BF), short, preferred_element_type=F32
        )
    return blocks


def row_updates(clipped, layers, row_params, row_zero, row_ema, row_first, row_second):
    front = PIX + EMB + SEQ + 4
    new_first = first_decay * row_first + (1.0 - first_decay) * clipped
    new_second = second_decay * row_second + (1.0 - second_decay) * clipped * clipped
    down_bias_grad = clipped[front:].reshape(layers, 12, row_params.shape[1])[:, 7]
    step_size = (
        new_first
        / (1.0 - first_decay**STEPS_DONE)
        / (jnp.sqrt(new_second / (1.0 - second_decay**STEPS_DONE)) + adam_floor)
    )
    new_rows = row_params - adam_rate * (step_size + weight_decay * row_params)
    ema_rows = ema_decay * row_ema + (1.0 - ema_decay) * new_rows
    mixed_rows = mix_share * new_rows + (1.0 - mix_share) * row_zero
    return (new_rows, new_first, new_second, ema_rows, mixed_rows, down_bias_grad)


def plain_body(
    patches,
    pad_mask,
    labels,
    loss_weights,
    class_emb,
    layer_mats,
    layer_zero,
    layer_ema,
    layer_momentum,
    row_params,
    row_zero,
    row_ema,
    row_first,
    row_second,
):
    layers, columns, width = layer_mats.shape
    images, seq, pixels = patches.shape
    front = PIX + EMB + SEQ + 4
    valid_mask = pad_mask.astype(jnp.float32)
    gathered_rows = lax.all_gather(row_params.astype(jnp.bfloat16), "fsdp", axis=1, tiled=True)
    rows_value = gathered_rows.astype(jnp.float32)
    patch_weight = gathered_rows[:PIX]
    proj_rows = gathered_rows[PIX : PIX + EMB]
    position = rows_value[PIX + EMB : PIX + EMB + SEQ]
    head_vec = rows_value[PIX + EMB + SEQ : front]
    layer_vector_params = rows_value[front:].reshape(layers, 12, width)
    flat_patches = patches.reshape(images * seq, pixels)
    embedded = (matmul(flat_patches, patch_weight).reshape(images, seq, width) + position).reshape(
        images * seq, width
    )
    resid = norm_forward(embedded, head_vec[0], head_vec[1])
    kept_weights = []
    saved_activations = []
    for layer_number in range(layers):
        weight_tensors = gather_layer(layer_mats[layer_number])
        kept_weights.append(weight_tensors)
        resid, saved_activation = layer_forward(
            resid, weight_tensors, layer_vector_params[layer_number], valid_mask
        )
        saved_activations.append(saved_activation)
    counts = jnp.sum(valid_mask, -1, keepdims=True)
    pooled = jnp.sum(resid.reshape(images, seq, width) * valid_mask[..., None], 1) / counts
    pooled_norm = norm_forward(pooled, head_vec[2], head_vec[3]).astype(jnp.bfloat16)
    feature = matmul_nt(pooled_norm, proj_rows)
    inv_length = lax.rsqrt(jnp.sum(feature * feature, -1, keepdims=True) + unit_epsilon)
    unit_feat = (feature * inv_length).astype(jnp.bfloat16)
    classes = class_emb.astype(jnp.float32)
    class_unit = (
        classes * lax.rsqrt(jnp.sum(classes * classes, -1, keepdims=True) + unit_epsilon)
    ).astype(jnp.bfloat16)
    logits = logit_scale * matmul_nt(unit_feat, class_unit)
    top_logit = jnp.max(logits, -1, keepdims=True)
    shifted = jnp.exp(logits - top_logit)
    total_exp = jnp.sum(shifted, -1, keepdims=True)
    log_norm = top_logit + jnp.log(total_exp)
    onehot = (jnp.arange(logits.shape[1])[None, :] == labels[:, None]).astype(jnp.float32)
    losses = log_norm[:, 0] - jnp.sum(onehot * logits, -1)
    weights_value = loss_weights.astype(jnp.float32)
    loss_sum, weight_sum = lax.psum(
        (jnp.sum(weights_value * losses), jnp.sum(weights_value)), ("fsdp", "ns")
    )
    seed = weights_value / weight_sum
    logit_grad = seed[:, None] * (shifted / total_exp - onehot)
    unit_grad = logit_scale * jnp.dot(logit_grad, class_unit.astype(jnp.float32), precision=HIGHEST)
    feat_grad = inv_length * unit_grad - feature * inv_length**3 * jnp.sum(
        unit_grad * feature, -1, keepdims=True
    )
    grad_proj = jnp.dot(feat_grad.T, pooled_norm.astype(jnp.float32), precision=HIGHEST)
    pooled_grad, gain_post, shift_post = norm_backward(
        pooled, head_vec[2], jnp.dot(feat_grad, proj_rows.astype(jnp.float32), precision=HIGHEST)
    )
    residual_gradient = (valid_mask[..., None] * (pooled_grad / counts)[:, None, :]).reshape(
        images * seq, width
    )
    grad_mats = [None] * layers
    grad_vecs = [None] * layers
    for layer_number in reversed(range(layers)):
        weight_tensors = kept_weights[layer_number]
        residual_gradient, grad_matrix, grad_vector = layer_backward(
            residual_gradient,
            weight_tensors,
            layer_vector_params[layer_number],
            valid_mask,
            saved_activations[layer_number],
        )
        grad_mats[layer_number], grad_vecs[layer_number] = (
            lax.psum_scatter(
                jnp.concatenate(grad_matrix, 0), "fsdp", scatter_dimension=0, tiled=True
            ),
            lax.psum_scatter(grad_vector, "fsdp", scatter_dimension=1, tiled=True),
        )
    embed_grad, gain_pre, shift_pre = norm_backward(embedded, head_vec[0], residual_gradient)
    position_grad = jnp.sum(embed_grad.reshape(images, seq, width), 0)
    patch_grad = matmul_tn(flat_patches, embed_grad.astype(jnp.bfloat16))
    front_grad = jnp.concatenate(
        [
            patch_grad,
            grad_proj,
            position_grad,
            jnp.stack([gain_pre, shift_pre, gain_post, shift_post]),
        ],
        0,
    )
    front_shard = lax.psum_scatter(front_grad, "fsdp", scatter_dimension=1, tiled=True)
    mat_grad = jnp.stack(grad_mats)
    row_grad = jnp.concatenate([front_shard] + grad_vecs, 0)
    pairs = lax.axis_size("ns")
    side = lax.axis_index("ns")
    half_depth = width // pairs
    half_rows = row_grad.shape[0] // pairs
    mat_total, row_total = (
        lax.psum(mat_grad.astype(jnp.bfloat16), "ns").astype(jnp.float32),
        lax.psum(row_grad.astype(jnp.bfloat16), "ns").astype(jnp.float32),
    )
    mat_half = lax.dynamic_slice_in_dim(mat_total, side * half_depth, half_depth, 2)
    row_half = lax.dynamic_slice_in_dim(row_total, side * half_rows, half_rows, 0)
    squares = jnp.sum(mat_half * mat_half) + jnp.sum(row_half * row_half)
    grad_norm = jnp.sqrt(lax.psum(squares, ("fsdp", "ns")))
    clip = jnp.minimum(1.0, clip_bound / (grad_norm + 1e-06))
    momentum = momentum_decay * layer_momentum + clip * mat_total
    orth = newton_schulz(momentum)
    new_mats = layer_mats - muon_rate * (0.2 * math.sqrt(width) * orth + weight_decay * layer_mats)
    ema_mats = ema_decay * layer_ema + (1.0 - ema_decay) * new_mats
    mixed_mats = mix_share * new_mats + (1.0 - mix_share) * layer_zero
    return (loss_sum, weight_sum, grad_norm, new_mats, momentum, ema_mats, mixed_mats) + row_updates(
        clip * row_total, layers, row_params, row_zero, row_ema, row_first, row_second
    )


def fast_body(
    patches,
    pad_mask,
    labels,
    loss_weights,
    class_emb,
    layer_mats,
    layer_zero,
    layer_ema,
    layer_momentum,
    row_params,
    row_zero,
    row_ema,
    row_first,
    row_second,
):
    layers, columns, width = layer_mats.shape
    shards = lax.axis_size("fsdp")
    depth = shards // PLANE
    rows, share = row_params.shape
    lanes = -(-rows // 128) * 128
    valid_mask = pad_mask.astype(F32)
    sent_rows = jnp.pad(row_params.T.astype(BF), ((0, 0), (0, lanes - rows)))
    classes = jnp.pad(class_emb, ((0, -class_emb.shape[0] % 128), (0, 0)))
    weights, *saved, embedded, vectors, pooled_row, z_rows, feature_rows, start, stats = forward(
        depth,
        sent_rows,
        layer_mats.astype(BF),
        patches[0],
        valid_mask,
        valid_mask.T,
        classes,
        labels[:, None],
        loss_weights.astype(F32)[:, None],
    )
    mat_total, row_total, totals = backward(
        depth,
        lax.axis_size("ns"),
        weights,
        saved,
        embedded,
        patches[0],
        vectors,
        valid_mask,
        valid_mask.T,
        (pooled_row, z_rows, feature_rows),
        start,
        stats,
    )
    loss_sum, weight_sum, grad_norm, clip = (totals[0, turn] for turn in range(4))
    momentum, new_mats, ema_mats, mixed_mats = finish(
        totals, mat_total, layer_momentum, layer_mats, layer_zero, layer_ema
    )
    clipped = clip * row_total.astype(F32)[:, :rows].T
    return (loss_sum, weight_sum, grad_norm, new_mats, momentum, ema_mats, mixed_mats) + row_updates(
        clipped, layers, row_params, row_zero, row_ema, row_first, row_second
    )


def body(*args):
    count, share = args[5].shape[1], args[9].shape[1]
    planes = lax.axis_size("fsdp") == 4 * PLANE and lax.axis_size("ns") == 2
    if planes and count % 192 == 0 and share % 48 == 0 and args[0].shape[0] == 1:
        return fast_body(*args)
    return plain_body(*args)


def solution(mesh):
    in_specs = (
        P(("fsdp", "ns"), None, None),
        P(("fsdp", "ns"), None),
        P(("fsdp", "ns")),
        P(("fsdp", "ns")),
        P(),
        P(None, "fsdp", None),
        P(None, "fsdp", None),
        P(None, "fsdp", None),
        P(None, "fsdp", None),
        P(None, "fsdp"),
        P(None, "fsdp"),
        P(None, "fsdp"),
        P(None, "fsdp"),
        P(None, "fsdp"),
    )
    out_specs = (
        P(),
        P(),
        P(),
        P(None, "fsdp", None),
        P(None, "fsdp", None),
        P(None, "fsdp", None),
        P(None, "fsdp", None),
        P(None, "fsdp"),
        P(None, "fsdp"),
        P(None, "fsdp"),
        P(None, "fsdp"),
        P(None, "fsdp"),
        P(None, "fsdp"),
    )
    return jax.shard_map(body, mesh=mesh, in_specs=in_specs, out_specs=out_specs, check_vma=False)
```

```python
import functools
import math
from typing import NamedTuple

import jax
import jax.numpy as jnp
from jax import lax
from jax.experimental import pallas as pl
from jax.experimental.pallas import tpu as pltpu
from jax.sharding import PartitionSpec as P

HEADS = 12
HDIM = 64
PIX = 768
EMB = 512
SEQ = 256
NS_STEPS = 5
STEPS_DONE = 10


HIGHEST = lax.Precision.HIGHEST
norm_epsilon = 1e-05
unit_epsilon = 1e-06
logit_scale = 50.0
clip_bound = 0.001
momentum_decay = 0.95
muon_rate = 0.05
weight_decay = 0.05
adam_rate = 0.2
first_decay = 0.9
second_decay = 0.98
adam_floor = 1e-08
ema_decay = 0.9
mix_share = 0.5
coeff_linear = 3.4445
coeff_cubic = -4.775
coeff_quintic = 2.0315


def matmul(left, right):
    return jnp.dot(left, right, preferred_element_type=jnp.float32)


def matmul_nt(left, right):
    return lax.dot_general(
        left, right, (((1,), (1,)), ((), ())), preferred_element_type=jnp.float32
    )


def matmul_tn(left, right):
    return lax.dot_general(
        left, right, (((0,), (0,)), ((), ())), preferred_element_type=jnp.float32
    )


def norm_forward(inputs, gain, shift):
    center = inputs - jnp.mean(inputs, -1, keepdims=True)
    scale = lax.rsqrt(jnp.mean(center * center, -1, keepdims=True) + norm_epsilon)
    return center * scale * gain + shift


def norm_backward(inputs, gain, upstream):
    center = inputs - jnp.mean(inputs, -1, keepdims=True)
    scale = lax.rsqrt(jnp.mean(center * center, -1, keepdims=True) + norm_epsilon)
    normal = center * scale
    scaled_up = upstream * gain
    inner = scale * (
        scaled_up
        - jnp.mean(scaled_up, -1, keepdims=True)
        - normal * jnp.mean(scaled_up * normal, -1, keepdims=True)
    )
    return (inner, jnp.sum(upstream * normal, 0), jnp.sum(upstream, 0))


def attention_scores(parts, valid_mask):
    raw = jnp.einsum(
        "iqhd,ikhd->ihqk", parts[:, :, 0], parts[:, :, 1], preferred_element_type=jnp.float32
    )
    return jnp.where(valid_mask[:, None, None, :] > 0, raw * HDIM ** (-0.5), -1000000000.0)


BF = jnp.bfloat16
F32 = jnp.float32
MESH = pl.DeviceIdType.MESH
PLANE = 4


def guarded(pred, run):
    if pred is None:
        run()
    else:
        pl.when(pred)(run)


def both(first, second):
    if first is None:
        return second
    return first if second is None else jnp.logical_and(first, second)


def rows_at(start, count):
    return pl.ds(start if isinstance(start, int) else pl.multiple_of(start, 16), count)


class Links:
    def __init__(self, depth, send_sem, recv_sem):
        self.depth, self.send_sem, self.recv_sem = depth, send_sem, recv_sem
        self.me, self.x = lax.axis_index("fsdp"), lax.axis_index("ns")
        self.z, self.y, self.c = self.me // PLANE, lax.rem(self.me // 2, 2), lax.rem(self.me, 2)
        self.up = (self.at(self.z + 1, self.y, self.c), self.x)
        self.down = (self.at(self.z - 1, self.y, self.c), self.x)
        self.y_peer = (self.at(self.z, 1 - self.y, self.c), self.x)
        self.c_peer = (self.at(self.z, self.y, 1 - self.c), self.x)
        self.x_peer = (self.me, 1 - self.x)
        self.count, self.sent, self.waited = 0, [], set()

    def at(self, z, y, c):
        return PLANE * z + 2 * y + c

    def slot(self):
        self.count += 1
        return self.count - 1

    def greet(self):
        barrier = pltpu.get_barrier_semaphore()

        def signal(device):
            pl.semaphore_signal(barrier, inc=1, device_id=device, device_id_type=MESH)

        for device in (self.y_peer, self.x_peer, self.c_peer):
            signal(device)
        pl.when(self.z < self.depth - 1)(lambda: signal(self.up))
        pl.when(self.z > 0)(lambda: signal(self.down))
        inner = (self.z < self.depth - 1).astype(jnp.int32) + (self.z > 0).astype(jnp.int32)
        pl.semaphore_wait(barrier, 3 + inner)

    def copy(self, slot, source, target, device):
        return pltpu.make_async_remote_copy(
            src_ref=source,
            dst_ref=target,
            send_sem=self.send_sem.at[slot],
            recv_sem=self.recv_sem.at[slot],
            device_id=device,
            device_id_type=MESH,
        )

    def send(self, slot, source, target, device, pred=None):
        copy = self.copy(slot, source, target, device)
        guarded(pred, copy.start)
        self.sent.append((slot, pred, copy))

    def receive(self, slot, target, pred=None):
        guarded(pred, self.copy(slot, target, target, self.c_peer).wait_recv)

    def finish(self, slot=None):
        for number, pred, copy in self.sent:
            if number not in self.waited and (slot is None or number == slot):
                guarded(pred, copy.wait_send)
        if slot is not None:
            self.waited.add(slot)


def gather_item(links, own, target, count):
    depth, z, y, c, x = links.depth, links.z, links.y, links.c, links.x
    third = count // 3
    early = count // 9 // 16 * 16
    begin, amount = x * (third + early), 2 * third - early
    early_begin = amount - x * (third - early)
    origin = (0, 0)
    keys = [(side, far) for far in range(1, depth) for side in (-1, 1)]
    z_slot = {key: links.slot() for key in keys}
    y_slot = {key: links.slot() for key in keys + [origin]}
    e_slot = {(key, o): links.slot() for key in keys for o in (0, 1)}
    pair_slot = links.slot()
    x_slot = {(key, o): links.slot() for key in keys + [origin] for o in (0, 1)}
    c_slot = {(key, o): links.slot() for key in keys + [origin] for o in (0, 1)}

    def part(shard):
        return target(shard).at[rows_at(begin, amount)]

    def own_part():
        return own.at[rows_at(begin, amount)]

    def early_part(shard):
        return target(shard).at[rows_at(early_begin, early)]

    def third_of(shard, side):
        return target(shard).at[rows_at(side * 2 * third, third)]

    def shard(key, other, core=None):
        return links.at(z + key[0] * key[1], 1 - y if other else y, c if core is None else core)

    def exists(key):
        if key == origin:
            return None
        return z >= key[1] if key[0] < 0 else z + key[1] < depth

    def z_send(key):
        for side in (-1, 1) if key == origin else (key[0],):
            if key[1] + 1 < depth:
                source = own_part() if key == origin else part(shard(key, 0))
                links.send(
                    z_slot[(side, key[1] + 1)],
                    source,
                    part(shard(key, 0)),
                    links.up if side < 0 else links.down,
                    both(exists(key), z < depth - 1 if side < 0 else z > 0),
                )

    def e_send(key, other):
        for side in (-1, 1) if key == origin else (key[0],):
            if early and key[1] + 1 < depth:
                block = early_part(shard(key, other))
                mine = key == origin and other == 0
                links.send(
                    e_slot[((side, key[1] + 1), other)],
                    own.at[rows_at(early_begin, early)] if mine else block,
                    block,
                    links.up if side < 0 else links.down,
                    both(exists(key), z < depth - 1 if side < 0 else z > 0),
                )

    def e_receive(key, other):
        if early:
            links.receive(e_slot[(key, other)], early_part(shard(key, other)), exists(key))

    def y_send(key):
        source = own_part() if key == origin else part(shard(key, 0))
        links.send(y_slot[key], source, part(shard(key, 0)), links.y_peer, exists(key))

    def x_send(key, other):
        block = third_of(shard(key, other), x)
        links.send(x_slot[(key, other)], block, block, links.x_peer, exists(key))

    def c_send(key, other):
        whole = target(shard(key, other))
        source = own if (key, other) == (origin, 0) else whole
        links.send(c_slot[(key, other)], source, whole, links.c_peer, exists(key))

    order = []
    for far in range(1, depth):
        order += [((side, far), 0) for side in (-1, 1)]
        order += [(key, 1) for key in ([origin] if far == 1 else [(-1, far - 1), (1, far - 1)])]
    order += [((side, depth - 1), 1) for side in (-1, 1)]

    def start():
        if early:
            source = own.at[rows_at(early_begin, early)]
            links.send(pair_slot, source, early_part(shard(origin, 0)), links.y_peer)
        z_send(origin)
        e_send(origin, 0)
        y_send(origin)
        c_send(origin, 0)

    def cross(keys_now):
        for key in keys_now:
            links.receive(y_slot[key], part(shard(key, 1)), exists(key))
            x_send(key, 1)

    def step(far):
        if far == 1 and early:
            links.receive(pair_slot, early_part(shard(origin, 1)))
            e_send(origin, 1)
        for side in (-1, 1):
            key = (side, far)
            links.receive(z_slot[key], part(shard(key, 0)), exists(key))
            z_send(key)
            y_send(key)
            x_send(key, 0)
        cross([origin] if far == 1 else [(-1, far - 1), (1, far - 1)])
        for side in (-1, 1):
            for other in (0, 1):
                e_receive((side, far), other)
                e_send((side, far), other)
        if far == depth - 1:
            cross([(-1, far), (1, far)])

    def share():
        for key, other in order:
            links.receive(x_slot[(key, other)], third_of(shard(key, other), 1 - x), exists(key))
            c_send(key, other)

    def settle():
        for key, other in [(origin, 0)] + order:
            links.receive(c_slot[(key, other)], target(shard(key, other, 1 - c)), exists(key))

    return start, step, share, settle

def split(value):
    high = value.astype(BF)
    return high, (value - high.astype(F32)).astype(BF)


def forward_kernel(
    depth,
    halves,
    rows,
    mats,
    patches,
    keep,
    keep_column,
    classes,
    label,
    weight,
    all_mats,
    resid,
    normed,
    project,
    log_total,
    context,
    mixed,
    normed_two,
    embedded,
    vectors,
    pooled_row,
    z_rows,
    feature_rows,
    vector_start,
    stats,
    rows_v,
    mats_v,
    own_v,
    resid_v,
    normed_v,
    project_v,
    log_v,
    context_v,
    mixed_v,
    two_v,
    embed_v,
    weight_v,
    total_v,
    class_v,
    send_sem,
    recv_sem,
    local_sem,
    weight_sem,
    save_sem,
):
    links = Links(depth, send_sem, recv_sem)
    layers, count, width = mats.shape
    size = count // halves
    rows_v[pl.ds(links.me, 1)] = rows[...][None]
    items = [gather_item(links, rows, lambda shard: rows_v.at[shard], rows.shape[0])]
    own, loads = [], []
    for layer in range(layers):
        loads.append(pltpu.make_async_copy(mats.at[layer], mats_v, local_sem.at[0]))
        own.append(
            pltpu.make_async_copy(
                own_v.at[layer],
                all_mats.at[layer, rows_at(links.me * count, count)],
                local_sem.at[1 + layer],
            )
        )
        for half in range(halves):

            def target(shard, layer=layer, half=half):
                return all_mats.at[layer, rows_at(shard * count + half * size, size)]

            block = own_v.at[layer, pl.ds(half * size, size)]
            items.append(gather_item(links, block, target, size))
    saves = []

    def take(layer):
        loads[layer].wait()
        own_v[layer] = mats_v[...].astype(BF)
        own[layer].start()
        if layer + 1 < layers:
            loads[layer + 1].start()

    loads[0].start()
    links.greet()

    def save(source, target):
        copy = pltpu.make_async_copy(source, target, save_sem.at[len(saves)])
        copy.start()
        saves.append(copy)

    def table(begin, amount):
        return rows_v[:, :, pl.ds(begin, amount)].reshape(width, amount)

    pixels, seq = patches.shape[1], patches.shape[0]

    def column(index):
        return vectors[pl.ds(index, 1), :]

    def embed():
        vectors[...] = table(pixels + EMB + SEQ, 128).astype(F32).T
        position = table(pixels + EMB, SEQ).astype(F32).T
        embed_v[...] = matmul_nt(patches[...], table(0, pixels)) + position
        save(embed_v, embedded)
        resid_v[0] = norm_forward(embed_v[...], column(0), column(1))

    order = []
    for layer in range(layers):
        order += [(layer, index) for index in (0, 1, 2, 3, 4, 8, 5, 9, 6, 10, 7, 11)]

    def chunk_copy(number):
        layer, index = order[number]
        return pltpu.make_async_copy(
            all_mats.at[layer, pl.ds(index * width, width)],
            weight_v.at[number % 4],
            weight_sem.at[number % 4],
        )

    def chunk(number):
        chunk_copy(number).wait()
        return weight_v[number % 4]

    half_lane = lax.broadcasted_iota(jnp.int32, (1, 128), 1) < HDIM
    scale = HDIM ** (-0.5)

    def attention_pair(layer, pair):
        def lanes(base):
            return pl.ds(pl.multiple_of(base + pair * 128, 128), 128)

        query, key = project_v[layer, :, lanes(0)], project_v[layer, :, lanes(width)]
        value = project_v[layer, :, lanes(2 * width)]
        results = []
        kept = log_v[layer]
        lane = lax.broadcasted_iota(jnp.int32, kept.shape, 1)
        for head in range(2):
            here = half_lane if head == 0 else jnp.logical_not(half_lane)
            query_h = jnp.where(here, query, jnp.zeros_like(query))
            scores = jnp.where(keep[...] > 0, matmul_nt(query_h, key) * scale, -1000000000.0)
            top = jnp.max(scores, -1, keepdims=True)
            expo = jnp.exp(scores - top)
            total = jnp.sum(expo, -1, keepdims=True)
            kept = jnp.where(lane == 2 * pair + head, top + jnp.log(total), kept)
            results.append(matmul((expo / total).astype(BF), value))
        log_v[layer] = kept
        context_v[layer, :, lanes(0)] = jnp.where(half_lane, results[0], results[1]).astype(BF)

    def layer_steps(layer):
        base, first = 4 + 12 * layer, 12 * layer

        def vector(index):
            return column(base + index)

        for number in range(first, first + 4):
            chunk_copy(number).start()
        log_v[layer] = jnp.zeros_like(log_v[layer])
        save(resid_v.at[layer], resid.at[layer])
        normed_v[layer] = norm_forward(resid_v[layer], vector(0), vector(1)).astype(BF)
        save(normed_v.at[layer], normed.at[layer])
        for part in range(3):
            result = matmul_nt(normed_v[layer], chunk(first + part))
            if part != 1:
                result += vector(2 if part == 0 else 3)
            project_v[layer, :, pl.ds(part * width, width)] = result.astype(BF)
            chunk_copy(first + 4 + part).start()
        save(project_v.at[layer], project.at[layer])
        yield
        for third in range(3):

            @pl.loop(0, 2)
            def _(turn, third=third):
                attention_pair(layer, 2 * third + turn)

            yield
        save(context_v.at[layer], context.at[layer])
        save(log_v.at[layer], log_total.at[layer])
        mixed_v[layer] = resid_v[layer] + (
            matmul_nt(context_v[layer], chunk(first + 3)) + vector(4)
        )
        chunk_copy(first + 7).start()
        save(mixed_v.at[layer], mixed.at[layer])
        two_v[layer] = norm_forward(mixed_v[layer], vector(5), vector(6)).astype(BF)
        save(two_v.at[layer], normed_two.at[layer])
        yield
        total_v[...] = mixed_v[layer] + vector(7)
        for part in range(4):
            number = first + 4 + 2 * part
            pre = matmul_nt(two_v[layer], chunk(number)) + vector(8 + part)
            hidden = (pre * jax.nn.sigmoid(1.702 * pre)).astype(BF)
            total_v[...] += matmul(hidden, chunk(number + 1))
            for ahead in (number + 4, number + 5):
                if ahead < first + 12:
                    chunk_copy(ahead).start()
            if part < 3:
                yield
        resid_v[layer + 1] = total_v[...]
        yield

    def class_units():
        value = classes[...].astype(F32)
        length = lax.rsqrt(jnp.sum(value * value, -1, keepdims=True) + unit_epsilon)
        class_v[...] = (value * length).astype(BF)

    def head():
        number = jnp.sum(keep[...], -1, keepdims=True)
        pooled = jnp.sum(resid_v[layers] * keep_column[...], 0, keepdims=True) / number
        center = pooled - jnp.mean(pooled, -1, keepdims=True)
        spread = lax.rsqrt(jnp.mean(center * center, -1, keepdims=True) + norm_epsilon)
        normal = center * spread
        z_value = jnp.broadcast_to(normal * column(2) + column(3), (16, width)).astype(BF)
        proj = table(pixels, EMB)
        feature = matmul(z_value, proj)
        inverse = lax.rsqrt(jnp.sum(feature * feature, -1, keepdims=True) + unit_epsilon)
        unit = (feature * inverse).astype(BF)
        logits = logit_scale * matmul_nt(unit, class_v[...])
        lane = lax.broadcasted_iota(jnp.int32, logits.shape, 1)
        top = jnp.max(logits, -1, keepdims=True)
        shifted = jnp.exp(logits - top)
        total = jnp.sum(shifted, -1, keepdims=True)
        chosen = lane == label[...]
        loss = top + jnp.log(total) - jnp.sum(jnp.where(chosen, logits, 0.0), -1, keepdims=True)
        logit_grad = weight[...] * (shifted / total - chosen.astype(F32))
        high, low = split(logit_grad)
        unit_grad = logit_scale * (matmul(high, class_v[...]) + matmul(low, class_v[...]))
        feature_grad = inverse * unit_grad - feature * inverse**3 * jnp.sum(
            unit_grad * feature, -1, keepdims=True
        )
        high, low = split(feature_grad)
        z_grad = (matmul_nt(high, proj) + matmul_nt(low, proj))[:1]
        scaled = z_grad * column(2)
        inner = spread * (
            scaled
            - jnp.mean(scaled, -1, keepdims=True)
            - normal * jnp.mean(scaled * normal, -1, keepdims=True)
        )
        pooled_row[...] = jnp.broadcast_to(inner / number, pooled_row.shape)
        spot = lax.broadcasted_iota(jnp.int32, (16, 1), 0)
        z_rows[...] = jnp.where(spot < 2, z_value, jnp.zeros_like(z_value))
        picked = jnp.where(spot == 0, high, jnp.where(spot == 1, low, jnp.zeros_like(low)))
        feature_rows[...] = picked
        vector_start[...] = jnp.zeros_like(vector_start)
        vector_start[pl.ds(2, 1), :] = z_grad * normal
        vector_start[pl.ds(3, 1), :] = z_grad
        here = lax.broadcasted_iota(jnp.int32, (8, 128), 1)
        first = lax.broadcasted_iota(jnp.int32, (8, 128), 0) == 0
        value = jnp.where(first & (here == 1), (loss * weight[...])[:8], 0.0)
        stats[...] = jnp.where(first & (here == 2), jnp.broadcast_to(weight[...], (8, 128)), value)

    running = None

    def work(amount):
        nonlocal running
        for _ in range(amount):
            if running is None:
                return
            if next(running, 0) == 0:
                running = None

    items[0][0]()
    take(0)
    class_units()
    for number, (_, step, _, _) in enumerate(items):
        step(1)
        work(1)
        step(2)
        if number + 1 < len(items):
            if number > 0 and number % halves == 0:
                take(number // halves)
            items[number + 1][0]()
        work(1)
        if number > 0:
            items[number - 1][2]()
        work(1)
        for far in range(3, depth):
            step(far)
        work(1)
        if number > 0:
            items[number - 1][3]()
            if number == 1:
                embed()
            for layer in range(layers - 1):
                if number - 1 == halves * (layer + 1):
                    own[layer].wait()
                    work(1000)
                    running = counted(layer_steps(layer))
        work(1)
    items[-1][2]()
    work(2)
    items[-1][3]()
    work(1000)
    own[layers - 1].wait()
    for _ in layer_steps(layers - 1):
        pass
    head()
    links.finish()
    for copy in saves:
        copy.wait()


def counted(steps):
    for _ in steps:
        yield 1


def forward(depth, rows, mats, patches, keep, keep_column, classes, label, weight):
    layers, count, width = mats.shape
    shards = PLANE * depth
    halves = 2
    seq = patches.shape[0]
    slots = (1 + layers * halves) * 60
    any_space = pl.BlockSpec(memory_space=pl.ANY)
    vmem = pl.BlockSpec(memory_space=pltpu.VMEM)

    def shape(*sizes, dtype=F32):
        return jax.ShapeDtypeStruct(sizes, dtype)

    saved = (
        shape(layers, seq, width),
        shape(layers, seq, width, dtype=BF),
        shape(layers, seq, 3 * width, dtype=BF),
        shape(layers, seq, 128),
        shape(layers, seq, width, dtype=BF),
        shape(layers, seq, width),
        shape(layers, seq, width, dtype=BF),
    )
    return pl.pallas_call(
        functools.partial(forward_kernel, depth, halves),
        out_shape=(shape(layers, shards * count, width, dtype=BF),)
        + saved
        + (
            shape(seq, width),
            shape(128, width),
            shape(8, width),
            shape(16, width, dtype=BF),
            shape(16, EMB, dtype=BF),
            shape(128, width),
            shape(8, 128),
        ),
        in_specs=[vmem, any_space] + [vmem] * 6,
        out_specs=[any_space] * 9 + [vmem] * 6,
        scratch_shapes=[
            pltpu.VMEM((shards,) + rows.shape, BF),
            pltpu.VMEM(mats.shape[1:], F32),
            pltpu.VMEM(mats.shape, BF),
            pltpu.VMEM((layers + 1, seq, width), F32),
        ]
        + [pltpu.VMEM(array.shape, array.dtype) for array in saved[1:]]
        + [
            pltpu.VMEM((seq, width), F32),
            pltpu.VMEM((4, width, width), BF),
            pltpu.VMEM((seq, width), F32),
            pltpu.VMEM(classes.shape, BF),
            pltpu.SemaphoreType.DMA((slots,)),
            pltpu.SemaphoreType.DMA((slots,)),
            pltpu.SemaphoreType.DMA((1 + layers,)),
            pltpu.SemaphoreType.DMA((4,)),
            pltpu.SemaphoreType.DMA((1 + 7 * layers,)),
        ],
        name="gather_and_forward",
        compiler_params=pltpu.CompilerParams(
            collective_id=1, has_side_effects=True, vmem_limit_bytes=56 * 1024 * 1024
        ),
    )(rows, mats, patches, keep, keep_column, classes, label, weight)


def accumulate(target, start, source, begin, count, step):
    @pl.loop(0, count // step)
    def _(turn):
        here = rows_at(start + turn * step, step)
        there = rows_at(begin + turn * step, step)
        target[here, :] = (target[here, :].astype(F32) + source[there, :].astype(F32)).astype(BF)


class Group(NamedTuple):
    begin: object
    stages: list
    core_slot: list


def scatter_group(links, dest, load, sizes, bufs, emit, used=None):
    depth, z, y, c, x = links.depth, links.z, links.y, links.c, links.x
    n, p, q, step = sizes
    mine, core_in, x_in, y_in, z_in, z_last, final = bufs
    core_slot, x_slot = [links.slot(), links.slot()], [links.slot(), links.slot()]
    q_slot, p_slot, low_slot, high_slot, last_slot = (links.slot() for _ in range(5))
    m = p + q
    first = x * p
    own_p, peer_p = x * m, (1 - x) * m
    sides = ((0, 1 - y), (1, y))

    def begin():
        for i, side in sides:
            load(i, side, mine.at[side], core_in.at[side], core_slot[i])

    def stage_core():
        for i, side in sides:
            load(i, side, mine.at[side], None, None)
            links.receive(core_slot[i], core_in.at[side])
            accumulate(mine.at[side], 0, core_in.at[side], 0, n, step)
            links.send(x_slot[i], mine.at[side, rows_at(peer_p, p)], x_in.at[side], links.x_peer)
            if i == 0:
                links.send(q_slot, mine.at[side, pl.ds(p, q)], y_in.at[pl.ds(0, q)], links.y_peer)
        if used is not None:
            used()

    def stage_x():
        for i, side in sides:
            links.receive(x_slot[i], x_in.at[side])
            accumulate(mine.at[side], own_p, x_in.at[side], 0, p, step)
            if i == 0:
                links.send(
                    p_slot, mine.at[side, rows_at(own_p, p)], y_in.at[pl.ds(q, p)], links.y_peer
                )
        links.receive(q_slot, y_in.at[pl.ds(0, q)])
        accumulate(mine.at[y], p, y_in, 0, q, step)

    def stage_y():
        links.receive(p_slot, y_in.at[pl.ds(q, p)])
        accumulate(mine.at[y], own_p, y_in, q, p, step)

    def stage_z(hop):
        block = mine.at[y, rows_at(first, m)]

        def take(slot, source, pred):
            @pl.when(pred)
            def _():
                links.receive(slot, source)
                accumulate(mine.at[y], first, source, 0, m, step)

        if dest > 0:
            if 1 <= hop <= dest:
                take(low_slot, z_in, z == hop)
            if hop < dest:
                links.send(low_slot, block, z_in, links.up, z == hop)
        if dest < depth - 1:
            turn = depth - 1 - hop
            if hop >= 1 and turn > dest:
                take(high_slot, z_in, z == turn)
            if turn > dest + 1:
                links.send(high_slot, block, z_in, links.down, z == turn)
            if turn == dest + 1:
                links.send(high_slot, block, z_last, links.down, z == turn)
            if turn == dest and hop >= 1:
                take(high_slot, z_last, z == dest)
        if hop == max(dest, depth - 1 - dest):
            links.send(last_slot, block, final, links.x_peer, z == dest)

    def stage_last():
        links.finish(x_slot[1])
        links.finish(last_slot)

        @pl.when(z == dest)
        def _():
            links.receive(last_slot, final)
            accumulate(mine.at[y], p, final, jnp.where(x == 0, 0, p), q, step)

            @pl.loop(0, p // 16)
            def _(turn):
                there = rows_at(jnp.where(x == 0, q, 0) + turn * 16, 16)
                mine[y, rows_at(peer_p + turn * 16, 16), :] = final[there, :]

            emit(mine.at[y])

    hops = [functools.partial(stage_z, hop) for hop in range(depth)]
    return Group(begin, [stage_core, stage_x, stage_y] + hops + [stage_last], core_slot)

def norm_back(value, gain, upstream):
    center = value - jnp.mean(value, -1, keepdims=True)
    scale = lax.rsqrt(jnp.mean(center * center, -1, keepdims=True) + norm_epsilon)
    normal = center * scale
    scaled = upstream * gain
    inner = scale * (
        scaled
        - jnp.mean(scaled, -1, keepdims=True)
        - normal * jnp.mean(scaled * normal, -1, keepdims=True)
    )
    return (
        inner,
        jnp.sum(upstream * normal, 0, keepdims=True),
        jnp.sum(upstream, 0, keepdims=True),
    )


VMEM_LIMIT = 62 * 1024 * 1024
SUB = 3
IN_FLIGHT = 2 * SUB
LAGS = (1, 3, 5, 7, 9, 11, 13, 15)


def backward_kernel(
    depth,
    sides,
    layers,
    weights,
    resid,
    normed,
    project,
    log_total,
    context,
    mixed,
    normed_two,
    embedded,
    patches,
    vectors,
    keep,
    keep_column,
    pooled_row,
    z_rows,
    feature_rows,
    vector_start,
    stats,
    out,
    clipped,
    totals,
    row_out,
    blocks_v,
    core_in,
    x_in,
    y_in,
    z_in,
    z_last,
    final,
    rows_v,
    row_mine,
    row_core,
    row_x,
    row_y,
    row_z,
    row_z_last,
    row_final,
    resid_v,
    normed_v,
    project_v,
    log_v,
    context_v,
    mixed_v,
    two_v,
    weight_v,
    patch_v,
    hidden_v,
    pre_v,
    up_v,
    short_v,
    total_v,
    context_grad_v,
    vector_v,
    note,
    inbox,
    send_sem,
    recv_sem,
    local_sem,
    weight_sem,
    load_sem,
    mail_send,
    mail_recv,
    free_sem,
):
    links = Links(depth, send_sem, recv_sem)
    y, c, z = links.y, links.c, links.z
    me = links.me * sides + links.x
    everyone = PLANE * depth * sides
    width = up_v.shape[1]
    count = out.shape[1]
    n = count // SUB
    p = n // 4 // 16 * 16
    per_layer = depth * SUB
    own = 2 * layers * per_layer
    piece = 2 * n

    saved = (
        (normed_two, two_v),
        (mixed, mixed_v),
        (context, context_v),
        (resid, resid_v),
        (normed, normed_v),
        (project, project_v),
        (log_total, log_v),
    )

    def load(layer, which):
        source, target = saved[which]
        return pltpu.make_async_copy(source.at[layer], target, load_sem.at[which])

    chunks = []
    for layer in reversed(range(layers)):
        for turn in (3, 2, 1, 0):
            chunks += [(layer, 8 + turn), (layer, 4 + turn)]
        chunks += [(layer, 3), (layer, 0), (layer, 1), (layer, 2)]

    def chunk_copy(number):
        layer, index = chunks[number]
        return pltpu.make_async_copy(
            weights.at[layer, pl.ds(index * width, width)],
            weight_v.at[number % 4],
            weight_sem.at[number % 4],
        )

    def chunk(number):
        chunk_copy(number).wait()
        return weight_v[number % 4]

    def refill(*numbers):
        for number in numbers:
            if number < len(chunks):
                chunk_copy(number).start()

    for which in range(len(saved)):
        load(layers - 1, which).start()
    refill(0, 1, 2, 3)
    patch_load = pltpu.make_async_copy(patches, patch_v, load_sem.at[7])
    patch_load.start()

    def others(run):
        for number in range(everyone):
            pl.when(me != number)(functools.partial(run, number))

    def place(number):
        return (number // sides, number % sides)

    barrier = pltpu.get_barrier_semaphore()
    others(
        lambda number: pl.semaphore_signal(
            barrier, inc=1, device_id=place(number), device_id_type=MESH
        )
    )
    note[...] = stats[...]
    vector_v[...] = vector_start[...]
    up_v[...] = keep_column[...] * pooled_row[pl.ds(0, 1), :]
    lane = lax.broadcasted_iota(jnp.int32, (8, 128), 1)
    first = lax.broadcasted_iota(jnp.int32, (8, 128), 0) == 0

    def add_squares(block):
        value = block.astype(F32)
        note[...] += jnp.where(first & (lane == 0), jnp.sum(value * value), 0.0)

    groups, closers = [], []
    starts = {}

    def add_group(dest, send_out, take_in, sizes, bufs, emit, used=None):
        def load_block(i, side, mine, target, slot):
            if target is None:
                take_in(i, side, mine)
            else:
                send_out(i, side, mine, target, slot)

        groups.append(scatter_group(links, dest, load_block, sizes, bufs, emit, used))

    for order, layer in enumerate(reversed(range(layers))):
        for turn, dest in enumerate(reversed(range(depth))):
            ring = own
            for part in range(SUB):
                number, spot = len(groups), layer * SUB + part
                starts[(layer, dest, part)] = number
                slot = number % IN_FLIGHT

                def send_out(i, side, mine, target, sem_slot, ring=ring, part=part):
                    source = blocks_v.at[ring + 2 * part + side]
                    links.send(sem_slot, source, target, links.c_peer)

                def write(source, layer=layer, part=part, spot=spot):
                    target = out.at[layer, pl.ds(part * n, n)]
                    return pltpu.make_async_copy(source, target, local_sem.at[spot])

                def emit(result, write=write):
                    add_squares(result[...])
                    write(result).start()

                closers.append((dest, write, blocks_v.at[2 * number]))

                def used(number=number):
                    if number < layers * per_layer - IN_FLIGHT:
                        pl.semaphore_signal(
                            free_sem, inc=1, device_id=links.c_peer, device_id_type=MESH
                        )

                add_group(
                    dest,
                    send_out,
                    lambda i, side, mine: None,
                    (n, p, n - 2 * p, n // 4),
                    [blocks_v.at[pl.ds(2 * number, 2)], core_in.at[slot]]
                    + [ref.at[number] for ref in (x_in, y_in, z_in)]
                    + [z_last.at[spot], final.at[spot]],
                    emit,
                    used,
                )
    first_row_group = len(groups)
    rows = row_out.shape[0]
    for dest in reversed(range(depth)):
        number = len(groups)

        def row_copy(i, side, mine, dest=dest):
            sem = local_sem.at[layers * SUB + 2 * dest + i]
            return pltpu.make_async_copy(rows_v.at[links.at(dest, side, c)], mine, sem)

        def row_send(i, side, mine, target, slot, dest=dest, row_copy=row_copy):
            row_copy(i, side, mine).start()
            source = rows_v.at[links.at(dest, side, 1 - c)]
            links.send(slot, source, target, links.c_peer)

        def row_emit(result, dest=dest):
            add_squares(result[...])
            row_out[...] = result[...]

        add_group(
            dest,
            row_send,
            lambda i, side, mine, row_copy=row_copy: row_copy(i, side, mine).wait(),
            (rows, 16, rows - 32, 16),
            [ref.at[dest] for ref in (row_mine, row_core, row_x, row_y, row_z)]
            + [row_z_last, row_final],
            row_emit,
        )

    begun = []

    def release(layer, dest):
        for part in range(SUB):
            number = starts[(layer, dest, part)]
            if number >= IN_FLIGHT:
                pl.semaphore_wait(free_sem, 1)
            groups[number].begin()
            begun.append(number)

    def recycle(layer, dest):
        for part in range(SUB):
            number = starts[(layer, dest, part)]
            if number >= SUB:
                for slot in groups[number - SUB].core_slot:
                    links.finish(slot)

    last_turn = [0]

    def advance():
        turn = last_turn[0]
        for stage, lag in enumerate(LAGS):
            if 0 <= turn - lag < len(groups):
                groups[turn - lag].stages[stage]()
        last_turn[0] += 1

    def grad_pieces(layer, dest, left, column, amount, right, begin):
        number = starts[(layer, dest, 0)]
        ring = own

        @pl.loop(0, amount)
        def _(turn):
            columns = pl.ds(pl.multiple_of(column + turn * piece, 128), piece)
            result = matmul_tn(left[:, columns], right[...])
            for half in range(2):
                block = 2 * (begin + turn) + half
                shard = block // SUB
                part = lax.rem(block, SUB)
                side, core = shard // 2, lax.rem(shard, 2)
                index = jnp.where(
                    core == c, 2 * (number + part) + side, ring + 2 * part + side
                )
                blocks_v[index] = result[half * n : (half + 1) * n].astype(BF)

    half_lane = lax.broadcasted_iota(jnp.int32, (1, 128), 1) < HDIM
    scale = HDIM ** (-0.5)

    def attention_pair(pair):
        def lanes(base):
            return pl.ds(pl.multiple_of(base + pair * 128, 128), 128)

        query, key = project_v[:, lanes(0)], project_v[:, lanes(width)]
        value, grad = project_v[:, lanes(2 * width)], context_grad_v[:, lanes(0)]
        totals_now = log_v[...]
        column = lax.broadcasted_iota(jnp.int32, totals_now.shape, 1)
        query_grad = key_grad = value_grad = 0.0
        zero = jnp.zeros_like(query)
        for head in range(2):
            here = half_lane if head == 0 else jnp.logical_not(half_lane)
            query_h, key_h = jnp.where(here, query, zero), jnp.where(here, key, zero)
            grad_h = jnp.where(here, grad, zero)
            total = jnp.sum(
                jnp.where(column == 2 * pair + head, totals_now, 0.0), -1, keepdims=True
            )
            scores = jnp.where(keep[...] > 0, matmul_nt(query_h, key) * scale, -1000000000.0)
            probs = jnp.exp(scores - total)
            prob_grad = matmul_nt(grad_h, value)
            value_grad += matmul_tn(probs.astype(BF), grad_h)
            score_grad = (
                probs * (prob_grad - jnp.sum(prob_grad * probs, -1, keepdims=True))
            ).astype(BF)
            query_grad += matmul(score_grad, key_h)
            key_grad += matmul_tn(score_grad, query_h)
        pre_v[:, lanes(0)] = (query_grad * scale).astype(BF)
        pre_v[:, lanes(width)] = (key_grad * scale).astype(BF)
        pre_v[:, lanes(2 * width)] = value_grad.astype(BF)

    def layer_steps(order, layer):
        base = 4 + 12 * layer
        chunk0 = 12 * order

        def vector(index):
            return vectors[pl.ds(base + index, 1), :]

        def put(index, value):
            vector_v[pl.ds(base + index, 1), :] = value

        def column_sum(value):
            return jnp.sum(value.astype(F32), 0, keepdims=True)

        load(layer, 0).wait()
        short_v[...] = up_v[...].astype(BF)
        put(7, column_sum(short_v[...]))
        total_v[...] = jnp.zeros_like(total_v)
        recycle(layer, 3)
        for turn, part in enumerate((3, 2, 1, 0)):
            number = chunk0 + 2 * turn
            down, up = chunk(number), chunk(number + 1)
            pre = matmul_nt(two_v[...], up) + vector(8 + part)
            gate = jax.nn.sigmoid(1.702 * pre)
            hidden_v[...] = (pre * gate).astype(BF)
            slope = gate + 1.702 * pre * gate * (1.0 - gate)
            pre_grad = (matmul_nt(short_v[...], down) * slope).astype(BF)
            pre_v[:, pl.ds(part * width, width)] = pre_grad
            put(8 + part, column_sum(pre_grad))
            total_v[...] += matmul(pre_grad, up)
            refill(number + 4, number + 5)
            yield None
            if part == 0:
                recycle(layer, 2)
            if part > 0:
                grad_pieces(layer, 3, hidden_v, 0, 2, short_v, 2 * (part - 1))
            else:
                grad_pieces(layer, 2, hidden_v, 0, 2, short_v, 4)
            if part == 1:
                release(layer, 3)
                yield 3
            else:
                yield None
        grad_pieces(layer, 2, pre_v, 2 * width, 2, two_v, 0)
        yield None
        grad_pieces(layer, 2, pre_v, 3 * width, 2, two_v, 2)
        release(layer, 2)
        yield 2
        load(layer, 1).wait()
        inner, gain, shift = norm_back(mixed_v[...], vector(5), total_v[...])
        put(5, gain)
        put(6, shift)
        up_v[...] += inner
        short_v[...] = up_v[...].astype(BF)
        put(4, column_sum(short_v[...]))
        yield None
        load(layer, 2).wait()
        recycle(layer, 1)
        grad_pieces(layer, 1, short_v, 0, 2, context_v, 0)
        context_grad_v[...] = matmul(short_v[...], chunk(chunk0 + 8)).astype(BF)
        refill(chunk0 + 12)
        yield None
        grad_pieces(layer, 1, pre_v, 0, 2, two_v, 2)
        yield None
        grad_pieces(layer, 1, pre_v, width, 2, two_v, 4)
        release(layer, 1)
        if layer > 0:
            for which in range(3):
                load(layer - 1, which).start()
        else:
            embed_load.start()
        yield 1
        load(layer, 5).wait()
        load(layer, 6).wait()
        for third in range(3):

            @pl.loop(0, 2)
            def _(turn, third=third):
                attention_pair(2 * third + turn)

            yield None
        load(layer, 4).wait()
        recycle(layer, 0)
        put(2, column_sum(pre_v[:, pl.ds(0, width)]))
        put(3, column_sum(pre_v[:, pl.ds(2 * width, width)]))
        for third in range(3):
            grad_pieces(layer, 0, pre_v, third * width, 2, normed_v, 2 * third)
            if third < 2:
                yield None
        release(layer, 0)
        yield 0
        load(layer, 3).wait()
        back = matmul(pre_v[:, pl.ds(0, width)], chunk(chunk0 + 9))
        back += matmul(pre_v[:, pl.ds(width, width)], chunk(chunk0 + 10))
        back += matmul(pre_v[:, pl.ds(2 * width, width)], chunk(chunk0 + 11))
        refill(chunk0 + 13, chunk0 + 14, chunk0 + 15)
        inner, gain, shift = norm_back(resid_v[...], vector(0), back)
        put(0, gain)
        put(1, shift)
        up_v[...] += inner
        if layer > 0:
            for which in range(3, len(saved)):
                load(layer - 1, which).start()
        yield None

    embed_load = pltpu.make_async_copy(embedded, mixed_v, load_sem.at[8])
    pl.semaphore_wait(barrier, everyone - 1)
    pending = 0
    for order, layer in enumerate(reversed(range(layers))):
        for ready in layer_steps(order, layer):
            if ready is not None:
                pending += SUB
            if pending > 0:
                advance()
                pending -= 1
    embed_load.wait()
    inner, gain, shift = norm_back(mixed_v[...], vectors[pl.ds(0, 1), :], up_v[...])
    vector_v[pl.ds(0, 1), :] = gain
    vector_v[pl.ds(1, 1), :] = shift
    short_v[...] = inner.astype(BF)
    total_v[...] = inner
    patch_load.wait()
    pixels, embeds, seq = patch_v.shape[1], feature_rows.shape[1], inner.shape[0]
    for turn in range(width // piece):
        columns = pl.ds(turn * piece, piece)
        patch_grad = matmul_tn(short_v[:, columns], patch_v[...])
        proj_grad = matmul_tn(z_rows[:, columns], feature_rows[...])
        position = total_v[:, columns].T
        vector_grad = vector_v[:, columns].T
        for part in range(piece // rows):
            shard, inside = turn * (piece // rows) + part, slice(part * rows, (part + 1) * rows)
            rows_v[shard, :, pl.ds(0, pixels)] = patch_grad[inside].astype(BF)
            rows_v[shard, :, pl.ds(pixels, embeds)] = proj_grad[inside].astype(BF)
            rows_v[shard, :, pl.ds(pixels + embeds, seq)] = position[inside].astype(BF)
            rows_v[shard, :, pl.ds(pixels + embeds + seq, 128)] = vector_grad[inside].astype(BF)
    for number in range(first_row_group, len(groups)):
        groups[number].begin()
    while last_turn[0] < len(groups) + max(LAGS):
        advance()

    def mail(number, slot):
        return pltpu.make_async_remote_copy(
            src_ref=note,
            dst_ref=inbox.at[slot],
            send_sem=mail_send.at[number],
            recv_sem=mail_recv.at[slot],
            device_id=place(number),
            device_id_type=MESH,
        )

    others(lambda number: mail(number, me).start())
    inbox[pl.ds(me, 1)] = note[...][None]
    links.finish()
    for dest, write, source in closers:
        pl.when(z == dest)(lambda write=write, source=source: write(source).wait())
    others(lambda number: mail(number, number).wait_recv())
    summed = jnp.sum(inbox[...], 0)
    others(lambda number: mail(number, me).wait_send())

    def pick(index):
        return jnp.sum(jnp.where(first & (lane == index), summed, 0.0))

    loss_sum, weight_sum = pick(1), pick(2)
    norm = jnp.sqrt(jnp.full((8, 128), pick(0) / sides)) / weight_sum
    clip = jnp.minimum(1.0, clip_bound / (norm + 1e-06)) / weight_sum
    totals[...] = jnp.where(
        lane == 0,
        loss_sum,
        jnp.where(lane == 1, weight_sum, jnp.where(lane == 2, norm, clip)),
    )
    clipped[...] = (row_out[...].astype(F32) * clip[:1, :1]).T


def backward(
    depth, sides, weights, saved, embedded, patches, vectors, keep, keep_column, head, start, stats
):
    layers, rows_all, width = weights.shape
    seq, pixels = patches.shape
    shards = PLANE * depth
    count, rows = rows_all // shards, width // shards
    lanes = -(-(pixels + EMB + SEQ + 4 + 12 * layers) // 128) * 128
    n = count // SUB
    p = n // 4 // 16 * 16
    m = n - p
    per_layer = depth * SUB
    blocks = layers * per_layer
    row_m = rows - 16
    everyone = shards * sides

    def room(*shape, dtype=BF):
        return pltpu.VMEM(shape, dtype)

    any_space = pl.BlockSpec(memory_space=pl.ANY)
    vmem = pl.BlockSpec(memory_space=pltpu.VMEM)
    slots = (blocks + depth) * 9
    return pl.pallas_call(
        functools.partial(backward_kernel, depth, sides, layers),
        out_shape=(
            jax.ShapeDtypeStruct((layers, count, width), BF),
            jax.ShapeDtypeStruct((lanes, rows), F32),
            jax.ShapeDtypeStruct((8, 128), F32),
        ),
        in_specs=[any_space] * (1 + len(saved) + 2) + [vmem] * 8,
        out_specs=[any_space, vmem, vmem],
        scratch_shapes=[
            room(rows, lanes),
            room(2 * blocks + 2 * SUB, n, width),
            room(IN_FLIGHT, 2, n, width),
            room(blocks, 2, p, width),
            room(blocks, m, width),
            room(blocks, m, width),
            room(layers * SUB, m, width),
            room(layers * SUB, m, width),
            room(shards, rows, lanes),
            room(depth, 2, rows, lanes),
            room(depth, 2, rows, lanes),
            room(depth, 2, 16, lanes),
            room(depth, row_m, lanes),
            room(depth, row_m, lanes),
            room(row_m, lanes),
            room(row_m, lanes),
            room(seq, width, dtype=F32),
            room(seq, width),
            room(seq, 3 * width),
            room(seq, 128, dtype=F32),
            room(seq, width),
            room(seq, width, dtype=F32),
            room(seq, width),
            room(4, width, width),
            room(seq, pixels),
            room(seq, width),
            room(seq, 4 * width),
            room(seq, width, dtype=F32),
            room(seq, width),
            room(seq, width, dtype=F32),
            room(seq, width),
            room(128, width, dtype=F32),
            room(8, 128, dtype=F32),
            room(everyone, 8, 128, dtype=F32),
            pltpu.SemaphoreType.DMA((slots,)),
            pltpu.SemaphoreType.DMA((slots,)),
            pltpu.SemaphoreType.DMA((layers * SUB + 2 * depth,)),
            pltpu.SemaphoreType.DMA((4,)),
            pltpu.SemaphoreType.DMA((9,)),
            pltpu.SemaphoreType.DMA((everyone,)),
            pltpu.SemaphoreType.DMA((everyone,)),
            pltpu.SemaphoreType.REGULAR,
        ],
        name="backward_and_sum",
        compiler_params=pltpu.CompilerParams(
            collective_id=2, has_side_effects=True, vmem_limit_bytes=VMEM_LIMIT
        ),
    )(weights, *saved, embedded, patches, vectors, keep, keep_column, *head, start, stats)


def finish_kernel(
    hyper,
    totals,
    grad,
    momentum,
    mats,
    zero,
    ema,
    new_momentum,
    new_mats,
    new_ema,
    new_mixed,
    grad_v,
    m_v,
    mats_v,
    zero_v,
    ema_v,
    x_v,
    short_v,
    low_v,
    in_sem,
    out_sem,
):
    layers, count, width = grad.shape
    pairs = [(grad, grad_v), (momentum, m_v)]
    pairs += [(mats, mats_v), (zero, zero_v), (ema, ema_v)]
    loads = [pltpu.make_async_copy(a, b, in_sem.at[i]) for i, (a, b) in enumerate(pairs)]
    for load in loads:
        load.start()
    part = count // 3
    factor = totals[pl.ds(0, 1), pl.ds(3, 1)]
    loads[0].wait()
    loads[1].wait()
    stores = []
    for layer in range(layers):
        total = jnp.zeros((1, 1), F32)
        for third in range(3):
            rows = pl.ds(third * part, part)
            value = momentum_decay * m_v[layer, rows, :] + factor * grad_v[layer, rows, :].astype(F32)
            m_v[layer, rows, :] = value
            total += jnp.sum(value * value, keepdims=True)
        store = pltpu.make_async_copy(m_v.at[layer], new_momentum.at[layer], out_sem.at[layer])
        store.start()
        stores.append(store)
        inverse = 1.0 / (jnp.sqrt(total) + 1e-07)
        for third in range(3):
            rows = pl.ds(third * part, part)
            value = m_v[layer, rows, :] * inverse
            x_v[layer, rows, :] = value
            short_v[0, layer, rows, :] = value.astype(BF)

    row_id = lax.broadcasted_iota(jnp.int32, (part, count), 0)
    col_id = lax.broadcasted_iota(jnp.int32, (part, count), 1)

    def step(turn, shift, use):
        now = lax.rem(turn, 2)
        linear = coeff_cubic + 2.0 * shift * coeff_quintic
        stay = coeff_linear + shift * (coeff_cubic + shift * coeff_quintic)
        for layer in range(layers):
            for third in range(3):
                rows = pl.ds(third * part, part)
                gram = matmul_nt(short_v[now, layer, rows, :], short_v[now, layer])
                gram -= jnp.where(row_id + third * part == col_id, shift, 0.0)
                low_v[layer, rows, :] = gram.astype(BF)
        for layer in range(layers):
            for third in range(3):
                rows = pl.ds(third * part, part)
                low = low_v[layer, rows, :]
                poly = linear * low.astype(F32) + coeff_quintic * matmul(low, low_v[layer])
                value = stay * x_v[layer, rows, :] + matmul(poly.astype(BF), short_v[now, layer])
                use(layer, third, rows, value)

    @pl.loop(0, NS_STEPS - 1)
    def _(turn):
        def keep(layer, third, rows, value):
            x_v[layer, rows, :] = value
            short_v[1 - lax.rem(turn, 2), layer, rows, :] = value.astype(BF)

        step(turn, jnp.where(turn >= NS_STEPS - 2, 1.0, 0.0), keep)

    for load in loads[2:]:
        load.wait()

    def update(layer, third, rows, orth):
        old = mats_v[layer, rows, :]
        value = old - muon_rate * (hyper * orth + weight_decay * old)
        mats_v[layer, rows, :] = value
        ema_v[layer, rows, :] = ema_decay * ema_v[layer, rows, :] + (1.0 - ema_decay) * value
        zero_v[layer, rows, :] = mix_share * value + (1.0 - mix_share) * zero_v[layer, rows, :]
        for turn, (source, target) in enumerate(
            ((mats_v, new_mats), (ema_v, new_ema), (zero_v, new_mixed))
        ):
            sem = out_sem.at[layers + (layer * 3 + third) * 3 + turn]
            store = pltpu.make_async_copy(source.at[layer, rows], target.at[layer, rows], sem)
            store.start()
            stores.append(store)

    step(NS_STEPS - 1, 1.0, update)
    for store in stores:
        store.wait()


def finish(totals, grad, momentum, mats, zero, ema):
    layers, count, width = grad.shape
    full = jax.ShapeDtypeStruct(mats.shape, F32)
    any_space = pl.BlockSpec(memory_space=pl.ANY)
    vmem = pl.BlockSpec(memory_space=pltpu.VMEM)
    return pl.pallas_call(
        functools.partial(finish_kernel, 0.2 * math.sqrt(width)),
        out_shape=(full, full, full, full),
        in_specs=[vmem] + [any_space] * 5,
        out_specs=[any_space] * 4,
        scratch_shapes=[
            pltpu.VMEM(grad.shape, BF),
            pltpu.VMEM(mats.shape, F32),
            pltpu.VMEM(mats.shape, F32),
            pltpu.VMEM(mats.shape, F32),
            pltpu.VMEM(mats.shape, F32),
            pltpu.VMEM(mats.shape, F32),
            pltpu.VMEM((2,) + mats.shape, BF),
            pltpu.VMEM((layers, count, count), BF),
            pltpu.SemaphoreType.DMA((5,)),
            pltpu.SemaphoreType.DMA((layers * 10,)),
        ],
        name="orthogonalize",
        compiler_params=pltpu.CompilerParams(vmem_limit_bytes=56 * 1024 * 1024),
    )(totals, grad, momentum, mats, zero, ema)


def gather_layer(shard):
    return lax.all_gather(shard.astype(jnp.bfloat16), "fsdp", axis=0, tiled=True)


def layer_forward(resid, weight_tensors, vector, valid_mask):
    images, seq = valid_mask.shape
    width = resid.shape[1]
    ffn = 4 * width
    normed = norm_forward(resid, vector[0], vector[1]).astype(jnp.bfloat16)
    bias = jnp.concatenate([vector[2], jnp.zeros_like(vector[2]), vector[3]])
    project = (matmul_nt(normed, weight_tensors[: 3 * width]) + bias).astype(jnp.bfloat16)
    parts = project.reshape(images, seq, 3, HEADS, HDIM)
    scores = attention_scores(parts, valid_mask)
    top_score = jnp.max(scores, -1, keepdims=True)
    expo = jnp.exp(scores - top_score)
    totals = jnp.sum(expo, -1, keepdims=True)
    log_total = top_score + jnp.log(totals)
    probs = (expo / totals).astype(jnp.bfloat16)
    context = jnp.einsum(
        "ihqk,ikhd->iqhd", probs, parts[:, :, 2], preferred_element_type=jnp.float32
    )
    context = context.reshape(images * seq, width).astype(jnp.bfloat16)
    mixed = resid + (matmul_nt(context, weight_tensors[3 * width : 4 * width]) + vector[4])
    normed_two = norm_forward(mixed, vector[5], vector[6]).astype(jnp.bfloat16)
    hidden_pre = matmul_nt(normed_two, weight_tensors[4 * width : 4 * width + ffn]) + vector[
        8:12
    ].reshape(ffn)
    hidden = (hidden_pre * jax.nn.sigmoid(1.702 * hidden_pre)).astype(jnp.bfloat16)
    output = mixed + (matmul(hidden, weight_tensors[4 * width + ffn :]) + vector[7])
    return (
        output,
        (resid, normed, project, log_total, context, mixed, normed_two, hidden_pre, hidden),
    )


def layer_backward(upstream, weight_tensors, vector, valid_mask, saved_activation):
    resid, normed, project, log_total, context, mixed, normed_two, hidden_pre, hidden = (
        saved_activation
    )
    images, seq = valid_mask.shape
    width = resid.shape[1]
    ffn = 4 * width
    out_grad = upstream.astype(jnp.bfloat16)
    grad_down = matmul_tn(hidden, out_grad)
    hidden_grad = matmul_nt(out_grad, weight_tensors[4 * width + ffn :])
    gate = jax.nn.sigmoid(1.702 * hidden_pre)
    pre_grad = (hidden_grad * (gate + 1.702 * hidden_pre * gate * (1.0 - gate))).astype(
        jnp.bfloat16
    )
    grad_up = matmul_tn(pre_grad, normed_two)
    second_in, gain_two, shift_two = norm_backward(
        mixed, vector[5], matmul(pre_grad, weight_tensors[4 * width : 4 * width + ffn])
    )
    mixed_grad = upstream + second_in
    attn_grad = mixed_grad.astype(jnp.bfloat16)
    grad_out = matmul_tn(attn_grad, context)
    context_grad = matmul(attn_grad, weight_tensors[3 * width : 4 * width]).astype(jnp.bfloat16)
    context_grad = context_grad.reshape(images, seq, HEADS, HDIM)
    parts = project.reshape(images, seq, 3, HEADS, HDIM)
    probs = jnp.exp(attention_scores(parts, valid_mask) - log_total)
    prob_grad = jnp.einsum(
        "iqhd,ikhd->ihqk", context_grad, parts[:, :, 2], preferred_element_type=jnp.float32
    )
    value_grad = jnp.einsum(
        "ihqk,iqhd->ikhd",
        probs.astype(jnp.bfloat16),
        context_grad,
        preferred_element_type=jnp.float32,
    )
    score_grad = (probs * (prob_grad - jnp.sum(prob_grad * probs, -1, keepdims=True))).astype(
        jnp.bfloat16
    )
    query_grad = jnp.einsum(
        "ihqk,ikhd->iqhd", score_grad, parts[:, :, 1], preferred_element_type=jnp.float32
    ) * HDIM ** (-0.5)
    key_grad = jnp.einsum(
        "ihqk,iqhd->ikhd", score_grad, parts[:, :, 0], preferred_element_type=jnp.float32
    ) * HDIM ** (-0.5)
    project_grad = (
        jnp.stack([query_grad, key_grad, value_grad], 2)
        .reshape(images * seq, 3 * width)
        .astype(jnp.bfloat16)
    )
    project_sum = jnp.sum(project_grad.astype(jnp.float32), 0)
    grad_qkv = matmul_tn(project_grad, normed)
    first_in, gain_one, shift_one = norm_backward(
        resid, vector[0], matmul(project_grad, weight_tensors[: 3 * width])
    )
    residual_gradient = mixed_grad + first_in
    grad_matrix = [part.astype(BF) for part in (grad_qkv, grad_out, grad_up, grad_down)]
    grad_vector = jnp.concatenate(
        [
            jnp.stack(
                [
                    gain_one,
                    shift_one,
                    project_sum[:width],
                    project_sum[2 * width :],
                    jnp.sum(attn_grad.astype(jnp.float32), 0),
                    gain_two,
                    shift_two,
                    jnp.sum(out_grad.astype(jnp.float32), 0),
                ]
            ),
            jnp.sum(pre_grad.astype(jnp.float32), 0).reshape(4, width),
        ],
        0,
    )
    return (residual_gradient, grad_matrix, grad_vector)


def newton_schulz(blocks):
    frob = jnp.sqrt(jnp.sum(blocks * blocks, axis=(1, 2), keepdims=True)) + 1e-07
    blocks = blocks / frob
    unit = jnp.eye(blocks.shape[1], dtype=jnp.float32)
    for turn in range(NS_STEPS):
        shift = 1.0 if turn >= NS_STEPS - 2 else 0.0
        short = blocks.astype(BF)
        gram = jnp.einsum("lcd,led->lce", short, short, preferred_element_type=F32) - shift * unit
        low = gram.astype(BF)
        square = jnp.einsum("lce,lef->lcf", low, low, preferred_element_type=F32)
        poly = (coeff_cubic + 2.0 * shift * coeff_quintic) * gram + coeff_quintic * square
        stay = coeff_linear + shift * (coeff_cubic + shift * coeff_quintic)
        blocks = stay * blocks + jnp.einsum(
            "lce,led->lcd", poly.astype(BF), short, preferred_element_type=F32
        )
    return blocks


def row_updates(clipped, layers, row_params, row_zero, row_ema, row_first, row_second):
    front = PIX + EMB + SEQ + 4
    new_first = first_decay * row_first + (1.0 - first_decay) * clipped
    new_second = second_decay * row_second + (1.0 - second_decay) * clipped * clipped
    down_bias_grad = clipped[front:].reshape(layers, 12, row_params.shape[1])[:, 7]
    step_size = (
        new_first
        / (1.0 - first_decay**STEPS_DONE)
        / (jnp.sqrt(new_second / (1.0 - second_decay**STEPS_DONE)) + adam_floor)
    )
    new_rows = row_params - adam_rate * (step_size + weight_decay * row_params)
    ema_rows = ema_decay * row_ema + (1.0 - ema_decay) * new_rows
    mixed_rows = mix_share * new_rows + (1.0 - mix_share) * row_zero
    return (new_rows, new_first, new_second, ema_rows, mixed_rows, down_bias_grad)


def plain_body(
    patches,
    pad_mask,
    labels,
    loss_weights,
    class_emb,
    layer_mats,
    layer_zero,
    layer_ema,
    layer_momentum,
    row_params,
    row_zero,
    row_ema,
    row_first,
    row_second,
):
    layers, columns, width = layer_mats.shape
    images, seq, pixels = patches.shape
    front = PIX + EMB + SEQ + 4
    valid_mask = pad_mask.astype(jnp.float32)
    gathered_rows = lax.all_gather(row_params.astype(jnp.bfloat16), "fsdp", axis=1, tiled=True)
    rows_value = gathered_rows.astype(jnp.float32)
    patch_weight = gathered_rows[:PIX]
    proj_rows = gathered_rows[PIX : PIX + EMB]
    position = rows_value[PIX + EMB : PIX + EMB + SEQ]
    head_vec = rows_value[PIX + EMB + SEQ : front]
    layer_vector_params = rows_value[front:].reshape(layers, 12, width)
    flat_patches = patches.reshape(images * seq, pixels)
    embedded = (matmul(flat_patches, patch_weight).reshape(images, seq, width) + position).reshape(
        images * seq, width
    )
    resid = norm_forward(embedded, head_vec[0], head_vec[1])
    kept_weights = []
    saved_activations = []
    for layer_number in range(layers):
        weight_tensors = gather_layer(layer_mats[layer_number])
        kept_weights.append(weight_tensors)
        resid, saved_activation = layer_forward(
            resid, weight_tensors, layer_vector_params[layer_number], valid_mask
        )
        saved_activations.append(saved_activation)
    counts = jnp.sum(valid_mask, -1, keepdims=True)
    pooled = jnp.sum(resid.reshape(images, seq, width) * valid_mask[..., None], 1) / counts
    pooled_norm = norm_forward(pooled, head_vec[2], head_vec[3]).astype(jnp.bfloat16)
    feature = matmul_nt(pooled_norm, proj_rows)
    inv_length = lax.rsqrt(jnp.sum(feature * feature, -1, keepdims=True) + unit_epsilon)
    unit_feat = (feature * inv_length).astype(jnp.bfloat16)
    classes = class_emb.astype(jnp.float32)
    class_unit = (
        classes * lax.rsqrt(jnp.sum(classes * classes, -1, keepdims=True) + unit_epsilon)
    ).astype(jnp.bfloat16)
    logits = logit_scale * matmul_nt(unit_feat, class_unit)
    top_logit = jnp.max(logits, -1, keepdims=True)
    shifted = jnp.exp(logits - top_logit)
    total_exp = jnp.sum(shifted, -1, keepdims=True)
    log_norm = top_logit + jnp.log(total_exp)
    onehot = (jnp.arange(logits.shape[1])[None, :] == labels[:, None]).astype(jnp.float32)
    losses = log_norm[:, 0] - jnp.sum(onehot * logits, -1)
    weights_value = loss_weights.astype(jnp.float32)
    loss_sum, weight_sum = lax.psum(
        (jnp.sum(weights_value * losses), jnp.sum(weights_value)), ("fsdp", "ns")
    )
    seed = weights_value / weight_sum
    logit_grad = seed[:, None] * (shifted / total_exp - onehot)
    unit_grad = logit_scale * jnp.dot(logit_grad, class_unit.astype(jnp.float32), precision=HIGHEST)
    feat_grad = inv_length * unit_grad - feature * inv_length**3 * jnp.sum(
        unit_grad * feature, -1, keepdims=True
    )
    grad_proj = jnp.dot(feat_grad.T, pooled_norm.astype(jnp.float32), precision=HIGHEST)
    pooled_grad, gain_post, shift_post = norm_backward(
        pooled, head_vec[2], jnp.dot(feat_grad, proj_rows.astype(jnp.float32), precision=HIGHEST)
    )
    residual_gradient = (valid_mask[..., None] * (pooled_grad / counts)[:, None, :]).reshape(
        images * seq, width
    )
    grad_mats = [None] * layers
    grad_vecs = [None] * layers
    for layer_number in reversed(range(layers)):
        weight_tensors = kept_weights[layer_number]
        residual_gradient, grad_matrix, grad_vector = layer_backward(
            residual_gradient,
            weight_tensors,
            layer_vector_params[layer_number],
            valid_mask,
            saved_activations[layer_number],
        )
        grad_mats[layer_number], grad_vecs[layer_number] = (
            lax.psum_scatter(
                jnp.concatenate(grad_matrix, 0), "fsdp", scatter_dimension=0, tiled=True
            ),
            lax.psum_scatter(grad_vector, "fsdp", scatter_dimension=1, tiled=True),
        )
    embed_grad, gain_pre, shift_pre = norm_backward(embedded, head_vec[0], residual_gradient)
    position_grad = jnp.sum(embed_grad.reshape(images, seq, width), 0)
    patch_grad = matmul_tn(flat_patches, embed_grad.astype(jnp.bfloat16))
    front_grad = jnp.concatenate(
        [
            patch_grad,
            grad_proj,
            position_grad,
            jnp.stack([gain_pre, shift_pre, gain_post, shift_post]),
        ],
        0,
    )
    front_shard = lax.psum_scatter(front_grad, "fsdp", scatter_dimension=1, tiled=True)
    mat_grad = jnp.stack(grad_mats)
    row_grad = jnp.concatenate([front_shard] + grad_vecs, 0)
    pairs = lax.axis_size("ns")
    side = lax.axis_index("ns")
    half_depth = width // pairs
    half_rows = row_grad.shape[0] // pairs
    mat_total, row_total = (
        lax.psum(mat_grad.astype(jnp.bfloat16), "ns").astype(jnp.float32),
        lax.psum(row_grad.astype(jnp.bfloat16), "ns").astype(jnp.float32),
    )
    mat_half = lax.dynamic_slice_in_dim(mat_total, side * half_depth, half_depth, 2)
    row_half = lax.dynamic_slice_in_dim(row_total, side * half_rows, half_rows, 0)
    squares = jnp.sum(mat_half * mat_half) + jnp.sum(row_half * row_half)
    grad_norm = jnp.sqrt(lax.psum(squares, ("fsdp", "ns")))
    clip = jnp.minimum(1.0, clip_bound / (grad_norm + 1e-06))
    momentum = momentum_decay * layer_momentum + clip * mat_total
    orth = newton_schulz(momentum)
    new_mats = layer_mats - muon_rate * (0.2 * math.sqrt(width) * orth + weight_decay * layer_mats)
    ema_mats = ema_decay * layer_ema + (1.0 - ema_decay) * new_mats
    mixed_mats = mix_share * new_mats + (1.0 - mix_share) * layer_zero
    return (loss_sum, weight_sum, grad_norm, new_mats, momentum, ema_mats, mixed_mats) + row_updates(
        clip * row_total, layers, row_params, row_zero, row_ema, row_first, row_second
    )


def fast_body(
    patches,
    pad_mask,
    labels,
    loss_weights,
    class_emb,
    layer_mats,
    layer_zero,
    layer_ema,
    layer_momentum,
    row_params,
    row_zero,
    row_ema,
    row_first,
    row_second,
):
    layers, columns, width = layer_mats.shape
    shards = lax.axis_size("fsdp")
    depth = shards // PLANE
    rows, share = row_params.shape
    lanes = -(-rows // 128) * 128
    valid_mask = pad_mask.astype(F32)
    sent_rows = jnp.pad(row_params.T.astype(BF), ((0, 0), (0, lanes - rows)))
    weights, *saved, embedded, vectors, pooled_row, z_rows, feature_rows, start, stats = forward(
        depth,
        sent_rows,
        layer_mats,
        patches[0],
        valid_mask,
        valid_mask.T,
        class_emb,
        labels[:, None],
        loss_weights.astype(F32)[:, None],
    )
    mat_total, clipped, totals = backward(
        depth,
        lax.axis_size("ns"),
        weights,
        saved,
        embedded,
        patches[0],
        vectors,
        valid_mask,
        valid_mask.T,
        (pooled_row, z_rows, feature_rows),
        start,
        stats,
    )
    loss_sum, weight_sum, grad_norm = (totals[0, turn] for turn in range(3))
    momentum, new_mats, ema_mats, mixed_mats = finish(
        totals, mat_total, layer_momentum, layer_mats, layer_zero, layer_ema
    )
    return (loss_sum, weight_sum, grad_norm, new_mats, momentum, ema_mats, mixed_mats) + row_updates(
        clipped[:rows], layers, row_params, row_zero, row_ema, row_first, row_second
    )


def body(*args):
    count, share = args[5].shape[1], args[9].shape[1]
    planes = lax.axis_size("fsdp") == 4 * PLANE and lax.axis_size("ns") == 2
    if planes and count % 192 == 0 and share % 48 == 0 and args[0].shape[0] == 1:
        return fast_body(*args)
    return plain_body(*args)


def solution(mesh):
    in_specs = (
        P(("fsdp", "ns"), None, None),
        P(("fsdp", "ns"), None),
        P(("fsdp", "ns")),
        P(("fsdp", "ns")),
        P(),
        P(None, "fsdp", None),
        P(None, "fsdp", None),
        P(None, "fsdp", None),
        P(None, "fsdp", None),
        P(None, "fsdp"),
        P(None, "fsdp"),
        P(None, "fsdp"),
        P(None, "fsdp"),
        P(None, "fsdp"),
    )
    out_specs = (
        P(),
        P(),
        P(),
        P(None, "fsdp", None),
        P(None, "fsdp", None),
        P(None, "fsdp", None),
        P(None, "fsdp", None),
        P(None, "fsdp"),
        P(None, "fsdp"),
        P(None, "fsdp"),
        P(None, "fsdp"),
        P(None, "fsdp"),
        P(None, "fsdp"),
    )
    return jax.shard_map(body, mesh=mesh, in_specs=in_specs, out_specs=out_specs, check_vma=False)
```

```python
import functools
import math
from typing import NamedTuple

import jax
import jax.numpy as jnp
from jax import lax
from jax.experimental import pallas as pl
from jax.experimental.pallas import tpu as pltpu
from jax.sharding import PartitionSpec as P

HEADS = 12
HDIM = 64
PIX = 768
EMB = 512
SEQ = 256
NS_STEPS = 5
STEPS_DONE = 10


HIGHEST = lax.Precision.HIGHEST
norm_epsilon = 1e-05
unit_epsilon = 1e-06
logit_scale = 50.0
clip_bound = 0.001
momentum_decay = 0.95
muon_rate = 0.05
weight_decay = 0.05
adam_rate = 0.2
first_decay = 0.9
second_decay = 0.98
adam_floor = 1e-08
ema_decay = 0.9
mix_share = 0.5
coeff_linear = 3.4445
coeff_cubic = -4.775
coeff_quintic = 2.0315


def matmul(left, right):
    return jnp.dot(left, right, preferred_element_type=jnp.float32)


def matmul_nt(left, right):
    return lax.dot_general(
        left, right, (((1,), (1,)), ((), ())), preferred_element_type=jnp.float32
    )


def matmul_tn(left, right):
    return lax.dot_general(
        left, right, (((0,), (0,)), ((), ())), preferred_element_type=jnp.float32
    )


def norm_forward(inputs, gain, shift):
    center = inputs - jnp.mean(inputs, -1, keepdims=True)
    scale = lax.rsqrt(jnp.mean(center * center, -1, keepdims=True) + norm_epsilon)
    return center * scale * gain + shift


def norm_backward(inputs, gain, upstream):
    center = inputs - jnp.mean(inputs, -1, keepdims=True)
    scale = lax.rsqrt(jnp.mean(center * center, -1, keepdims=True) + norm_epsilon)
    normal = center * scale
    scaled_up = upstream * gain
    inner = scale * (
        scaled_up
        - jnp.mean(scaled_up, -1, keepdims=True)
        - normal * jnp.mean(scaled_up * normal, -1, keepdims=True)
    )
    return (inner, jnp.sum(upstream * normal, 0), jnp.sum(upstream, 0))


def attention_scores(parts, valid_mask):
    raw = jnp.einsum(
        "iqhd,ikhd->ihqk", parts[:, :, 0], parts[:, :, 1], preferred_element_type=jnp.float32
    )
    return jnp.where(valid_mask[:, None, None, :] > 0, raw * HDIM ** (-0.5), -1000000000.0)


BF = jnp.bfloat16
F32 = jnp.float32
MESH = pl.DeviceIdType.MESH
PLANE = 4


def guarded(pred, run):
    if pred is None:
        run()
    else:
        pl.when(pred)(run)


def both(first, second):
    if first is None:
        return second
    return first if second is None else jnp.logical_and(first, second)


def rows_at(start, count):
    return pl.ds(start if isinstance(start, int) else pl.multiple_of(start, 16), count)


class Links:
    def __init__(self, depth, send_sem, recv_sem):
        self.depth, self.send_sem, self.recv_sem = depth, send_sem, recv_sem
        self.me, self.x = lax.axis_index("fsdp"), lax.axis_index("ns")
        self.z, self.y, self.c = self.me // PLANE, lax.rem(self.me // 2, 2), lax.rem(self.me, 2)
        self.up = (self.at(self.z + 1, self.y, self.c), self.x)
        self.down = (self.at(self.z - 1, self.y, self.c), self.x)
        self.y_peer = (self.at(self.z, 1 - self.y, self.c), self.x)
        self.c_peer = (self.at(self.z, self.y, 1 - self.c), self.x)
        self.x_peer = (self.me, 1 - self.x)
        self.count, self.sent, self.waited = 0, [], set()

    def at(self, z, y, c):
        return PLANE * z + 2 * y + c

    def slot(self):
        self.count += 1
        return self.count - 1

    def greet(self):
        barrier = pltpu.get_barrier_semaphore()

        def signal(device):
            pl.semaphore_signal(barrier, inc=1, device_id=device, device_id_type=MESH)

        for device in (self.y_peer, self.x_peer, self.c_peer):
            signal(device)
        pl.when(self.z < self.depth - 1)(lambda: signal(self.up))
        pl.when(self.z > 0)(lambda: signal(self.down))
        inner = (self.z < self.depth - 1).astype(jnp.int32) + (self.z > 0).astype(jnp.int32)
        pl.semaphore_wait(barrier, 3 + inner)

    def copy(self, slot, source, target, device):
        return pltpu.make_async_remote_copy(
            src_ref=source,
            dst_ref=target,
            send_sem=self.send_sem.at[slot],
            recv_sem=self.recv_sem.at[slot],
            device_id=device,
            device_id_type=MESH,
        )

    def send(self, slot, source, target, device, pred=None):
        copy = self.copy(slot, source, target, device)
        guarded(pred, copy.start)
        self.sent.append((slot, pred, copy))

    def receive(self, slot, target, pred=None):
        guarded(pred, self.copy(slot, target, target, self.c_peer).wait_recv)

    def finish(self, slot=None):
        for number, pred, copy in self.sent:
            if number not in self.waited and (slot is None or number == slot):
                guarded(pred, copy.wait_send)
        if slot is not None:
            self.waited.add(slot)


def gather_item(links, own, target, count):
    depth, z, y, c, x = links.depth, links.z, links.y, links.c, links.x
    third = count // 3
    early = count // 9 // 16 * 16
    begin, amount = x * (third + early), 2 * third - early
    early_begin = amount - x * (third - early)
    origin = (0, 0)
    keys = [(side, far) for far in range(1, depth) for side in (-1, 1)]
    z_slot = {key: links.slot() for key in keys}
    y_slot = {key: links.slot() for key in keys + [origin]}
    e_slot = {(key, o): links.slot() for key in keys for o in (0, 1)}
    pair_slot = links.slot()
    x_slot = {(key, o): links.slot() for key in keys + [origin] for o in (0, 1)}
    c_slot = {(key, o): links.slot() for key in keys + [origin] for o in (0, 1)}

    def part(shard):
        return target(shard).at[rows_at(begin, amount)]

    def own_part():
        return own.at[rows_at(begin, amount)]

    def early_part(shard):
        return target(shard).at[rows_at(early_begin, early)]

    def third_of(shard, side):
        return target(shard).at[rows_at(side * 2 * third, third)]

    def shard(key, other, core=None):
        return links.at(z + key[0] * key[1], 1 - y if other else y, c if core is None else core)

    def exists(key):
        if key == origin:
            return None
        return z >= key[1] if key[0] < 0 else z + key[1] < depth

    def z_send(key):
        for side in (-1, 1) if key == origin else (key[0],):
            if key[1] + 1 < depth:
                source = own_part() if key == origin else part(shard(key, 0))
                links.send(
                    z_slot[(side, key[1] + 1)],
                    source,
                    part(shard(key, 0)),
                    links.up if side < 0 else links.down,
                    both(exists(key), z < depth - 1 if side < 0 else z > 0),
                )

    def e_send(key, other):
        for side in (-1, 1) if key == origin else (key[0],):
            if early and key[1] + 1 < depth:
                block = early_part(shard(key, other))
                mine = key == origin and other == 0
                links.send(
                    e_slot[((side, key[1] + 1), other)],
                    own.at[rows_at(early_begin, early)] if mine else block,
                    block,
                    links.up if side < 0 else links.down,
                    both(exists(key), z < depth - 1 if side < 0 else z > 0),
                )

    def e_receive(key, other):
        if early:
            links.receive(e_slot[(key, other)], early_part(shard(key, other)), exists(key))

    def y_send(key):
        source = own_part() if key == origin else part(shard(key, 0))
        links.send(y_slot[key], source, part(shard(key, 0)), links.y_peer, exists(key))

    def x_send(key, other):
        block = third_of(shard(key, other), x)
        links.send(x_slot[(key, other)], block, block, links.x_peer, exists(key))

    def c_send(key, other):
        whole = target(shard(key, other))
        source = own if (key, other) == (origin, 0) else whole
        links.send(c_slot[(key, other)], source, whole, links.c_peer, exists(key))

    order = []
    for far in range(1, depth):
        order += [((side, far), 0) for side in (-1, 1)]
        order += [(key, 1) for key in ([origin] if far == 1 else [(-1, far - 1), (1, far - 1)])]
    order += [((side, depth - 1), 1) for side in (-1, 1)]

    def start():
        if early:
            source = own.at[rows_at(early_begin, early)]
            links.send(pair_slot, source, early_part(shard(origin, 0)), links.y_peer)
        z_send(origin)
        e_send(origin, 0)
        y_send(origin)
        c_send(origin, 0)

    def cross(keys_now):
        for key in keys_now:
            links.receive(y_slot[key], part(shard(key, 1)), exists(key))
            x_send(key, 1)

    def step(far):
        if far == 1 and early:
            links.receive(pair_slot, early_part(shard(origin, 1)))
            e_send(origin, 1)
        for side in (-1, 1):
            key = (side, far)
            links.receive(z_slot[key], part(shard(key, 0)), exists(key))
            z_send(key)
            y_send(key)
            x_send(key, 0)
        cross([origin] if far == 1 else [(-1, far - 1), (1, far - 1)])
        for side in (-1, 1):
            for other in (0, 1):
                e_receive((side, far), other)
                e_send((side, far), other)
        if far == depth - 1:
            cross([(-1, far), (1, far)])

    def share():
        for key, other in order:
            links.receive(x_slot[(key, other)], third_of(shard(key, other), 1 - x), exists(key))
            c_send(key, other)

    def settle():
        for key, other in [(origin, 0)] + order:
            links.receive(c_slot[(key, other)], target(shard(key, other, 1 - c)), exists(key))

    return start, step, share, settle

def split(value):
    high = value.astype(BF)
    return high, (value - high.astype(F32)).astype(BF)


def forward_kernel(
    depth,
    halves,
    rows,
    mats,
    patches,
    keep,
    keep_column,
    classes,
    label,
    weight,
    all_mats,
    resid,
    normed,
    project,
    log_total,
    context,
    mixed,
    normed_two,
    embedded,
    vectors,
    pooled_row,
    z_rows,
    feature_rows,
    vector_start,
    stats,
    rows_v,
    mats_v,
    own_v,
    resid_v,
    normed_v,
    project_v,
    log_v,
    context_v,
    mixed_v,
    two_v,
    embed_v,
    weight_v,
    total_v,
    class_v,
    send_sem,
    recv_sem,
    local_sem,
    weight_sem,
    save_sem,
):
    links = Links(depth, send_sem, recv_sem)
    layers, count, width = mats.shape
    size = count // halves
    rows_v[pl.ds(links.me, 1)] = rows[...][None]
    items = [gather_item(links, rows, lambda shard: rows_v.at[shard], rows.shape[0])]
    own, loads = [], []
    for layer in range(layers):
        loads.append(pltpu.make_async_copy(mats.at[layer], mats_v, local_sem.at[0]))
        own.append(
            pltpu.make_async_copy(
                own_v.at[layer],
                all_mats.at[layer, rows_at(links.me * count, count)],
                local_sem.at[1 + layer],
            )
        )
        for half in range(halves):

            def target(shard, layer=layer, half=half):
                return all_mats.at[layer, rows_at(shard * count + half * size, size)]

            block = own_v.at[layer, pl.ds(half * size, size)]
            items.append(gather_item(links, block, target, size))
    saves = []

    def take(layer):
        loads[layer].wait()
        own_v[layer] = mats_v[...].astype(BF)
        own[layer].start()
        if layer + 1 < layers:
            loads[layer + 1].start()

    loads[0].start()
    links.greet()

    def save(source, target):
        copy = pltpu.make_async_copy(source, target, save_sem.at[len(saves)])
        copy.start()
        saves.append(copy)

    def table(begin, amount):
        return rows_v[:, :, pl.ds(begin, amount)].reshape(width, amount)

    pixels, seq = patches.shape[1], patches.shape[0]

    def column(index):
        return vectors[pl.ds(index, 1), :]

    def embed():
        vectors[...] = table(pixels + EMB + SEQ, 128).astype(F32).T
        position = table(pixels + EMB, SEQ).astype(F32).T
        embed_v[...] = matmul_nt(patches[...], table(0, pixels)) + position
        save(embed_v, embedded)
        resid_v[0] = norm_forward(embed_v[...], column(0), column(1))

    order = []
    for layer in range(layers):
        order += [(layer, index) for index in (0, 1, 2, 3, 4, 8, 5, 9, 6, 10, 7, 11)]

    def chunk_copy(number):
        layer, index = order[number]
        return pltpu.make_async_copy(
            all_mats.at[layer, pl.ds(index * width, width)],
            weight_v.at[number % 4],
            weight_sem.at[number % 4],
        )

    def chunk(number):
        chunk_copy(number).wait()
        return weight_v[number % 4]

    half_lane = lax.broadcasted_iota(jnp.int32, (1, 128), 1) < HDIM
    scale = HDIM ** (-0.5)

    def attention_pair(layer, pair):
        def lanes(base):
            return pl.ds(pl.multiple_of(base + pair * 128, 128), 128)

        query, key = project_v[layer, :, lanes(0)], project_v[layer, :, lanes(width)]
        value = project_v[layer, :, lanes(2 * width)]
        results = []
        kept = log_v[layer]
        lane = lax.broadcasted_iota(jnp.int32, kept.shape, 1)
        for head in range(2):
            here = half_lane if head == 0 else jnp.logical_not(half_lane)
            query_h = jnp.where(here, query, jnp.zeros_like(query))
            scores = jnp.where(keep[...] > 0, matmul_nt(query_h, key) * scale, -1000000000.0)
            top = jnp.max(scores, -1, keepdims=True)
            expo = jnp.exp(scores - top)
            total = jnp.sum(expo, -1, keepdims=True)
            kept = jnp.where(lane == 2 * pair + head, top + jnp.log(total), kept)
            results.append(matmul((expo / total).astype(BF), value))
        log_v[layer] = kept
        context_v[layer, :, lanes(0)] = jnp.where(half_lane, results[0], results[1]).astype(BF)

    def layer_steps(layer):
        base, first = 4 + 12 * layer, 12 * layer

        def vector(index):
            return column(base + index)

        for number in range(first, first + 4):
            chunk_copy(number).start()
        log_v[layer] = jnp.zeros_like(log_v[layer])
        save(resid_v.at[layer], resid.at[layer])
        normed_v[layer] = norm_forward(resid_v[layer], vector(0), vector(1)).astype(BF)
        save(normed_v.at[layer], normed.at[layer])
        for part in range(3):
            result = matmul_nt(normed_v[layer], chunk(first + part))
            if part != 1:
                result += vector(2 if part == 0 else 3)
            project_v[layer, :, pl.ds(part * width, width)] = result.astype(BF)
            chunk_copy(first + 4 + part).start()
        save(project_v.at[layer], project.at[layer])
        yield
        for third in range(3):

            @pl.loop(0, 2)
            def _(turn, third=third):
                attention_pair(layer, 2 * third + turn)

            yield
        save(context_v.at[layer], context.at[layer])
        save(log_v.at[layer], log_total.at[layer])
        mixed_v[layer] = resid_v[layer] + (
            matmul_nt(context_v[layer], chunk(first + 3)) + vector(4)
        )
        chunk_copy(first + 7).start()
        save(mixed_v.at[layer], mixed.at[layer])
        two_v[layer] = norm_forward(mixed_v[layer], vector(5), vector(6)).astype(BF)
        save(two_v.at[layer], normed_two.at[layer])
        yield
        total_v[...] = mixed_v[layer] + vector(7)
        for part in range(4):
            number = first + 4 + 2 * part
            pre = matmul_nt(two_v[layer], chunk(number)) + vector(8 + part)
            hidden = (pre * jax.nn.sigmoid(1.702 * pre)).astype(BF)
            total_v[...] += matmul(hidden, chunk(number + 1))
            for ahead in (number + 4, number + 5):
                if ahead < first + 12:
                    chunk_copy(ahead).start()
            if part < 3:
                yield
        resid_v[layer + 1] = total_v[...]
        yield

    def class_units():
        value = classes[...].astype(F32)
        length = lax.rsqrt(jnp.sum(value * value, -1, keepdims=True) + unit_epsilon)
        class_v[...] = (value * length).astype(BF)

    def head():
        number = jnp.sum(keep[...], -1, keepdims=True)
        pooled = jnp.sum(resid_v[layers] * keep_column[...], 0, keepdims=True) / number
        center = pooled - jnp.mean(pooled, -1, keepdims=True)
        spread = lax.rsqrt(jnp.mean(center * center, -1, keepdims=True) + norm_epsilon)
        normal = center * spread
        z_value = jnp.broadcast_to(normal * column(2) + column(3), (16, width)).astype(BF)
        proj = table(pixels, EMB)
        feature = matmul(z_value, proj)
        inverse = lax.rsqrt(jnp.sum(feature * feature, -1, keepdims=True) + unit_epsilon)
        unit = (feature * inverse).astype(BF)
        logits = logit_scale * matmul_nt(unit, class_v[...])
        lane = lax.broadcasted_iota(jnp.int32, logits.shape, 1)
        top = jnp.max(logits, -1, keepdims=True)
        shifted = jnp.exp(logits - top)
        total = jnp.sum(shifted, -1, keepdims=True)
        chosen = lane == label[...]
        loss = top + jnp.log(total) - jnp.sum(jnp.where(chosen, logits, 0.0), -1, keepdims=True)
        logit_grad = weight[...] * (shifted / total - chosen.astype(F32))
        high, low = split(logit_grad)
        unit_grad = logit_scale * (matmul(high, class_v[...]) + matmul(low, class_v[...]))
        feature_grad = inverse * unit_grad - feature * inverse**3 * jnp.sum(
            unit_grad * feature, -1, keepdims=True
        )
        high, low = split(feature_grad)
        z_grad = (matmul_nt(high, proj) + matmul_nt(low, proj))[:1]
        scaled = z_grad * column(2)
        inner = spread * (
            scaled
            - jnp.mean(scaled, -1, keepdims=True)
            - normal * jnp.mean(scaled * normal, -1, keepdims=True)
        )
        pooled_row[...] = jnp.broadcast_to(inner / number, pooled_row.shape)
        spot = lax.broadcasted_iota(jnp.int32, (16, 1), 0)
        z_rows[...] = jnp.where(spot < 2, z_value, jnp.zeros_like(z_value))
        picked = jnp.where(spot == 0, high, jnp.where(spot == 1, low, jnp.zeros_like(low)))
        feature_rows[...] = picked
        vector_start[...] = jnp.zeros_like(vector_start)
        vector_start[pl.ds(2, 1), :] = z_grad * normal
        vector_start[pl.ds(3, 1), :] = z_grad
        here = lax.broadcasted_iota(jnp.int32, (8, 128), 1)
        first = lax.broadcasted_iota(jnp.int32, (8, 128), 0) == 0
        value = jnp.where(first & (here == 1), (loss * weight[...])[:8], 0.0)
        stats[...] = jnp.where(first & (here == 2), jnp.broadcast_to(weight[...], (8, 128)), value)

    running = None

    def work(amount):
        nonlocal running
        for _ in range(amount):
            if running is None:
                return
            if next(running, 0) == 0:
                running = None

    items[0][0]()
    take(0)
    class_units()
    for number, (_, step, _, _) in enumerate(items):
        step(1)
        work(1)
        step(2)
        if number + 1 < len(items):
            if number > 0 and number % halves == 0:
                take(number // halves)
            items[number + 1][0]()
        work(1)
        if number > 0:
            items[number - 1][2]()
        work(1)
        for far in range(3, depth):
            step(far)
        work(1)
        if number > 0:
            items[number - 1][3]()
            if number == 1:
                embed()
            for layer in range(layers - 1):
                if number - 1 == halves * (layer + 1):
                    own[layer].wait()
                    work(1000)
                    running = counted(layer_steps(layer))
        work(1)
    items[-1][2]()
    work(2)
    items[-1][3]()
    work(1000)
    own[layers - 1].wait()
    for _ in layer_steps(layers - 1):
        pass
    head()
    links.finish()
    for copy in saves:
        copy.wait()


def counted(steps):
    for _ in steps:
        yield 1


def forward(depth, rows, mats, patches, keep, keep_column, classes, label, weight):
    layers, count, width = mats.shape
    shards = PLANE * depth
    halves = 2
    seq = patches.shape[0]
    slots = (1 + layers * halves) * 60
    any_space = pl.BlockSpec(memory_space=pl.ANY)
    vmem = pl.BlockSpec(memory_space=pltpu.VMEM)

    def shape(*sizes, dtype=F32):
        return jax.ShapeDtypeStruct(sizes, dtype)

    saved = (
        shape(layers, seq, width),
        shape(layers, seq, width, dtype=BF),
        shape(layers, seq, 3 * width, dtype=BF),
        shape(layers, seq, 128),
        shape(layers, seq, width, dtype=BF),
        shape(layers, seq, width),
        shape(layers, seq, width, dtype=BF),
    )
    return pl.pallas_call(
        functools.partial(forward_kernel, depth, halves),
        out_shape=(shape(layers, shards * count, width, dtype=BF),)
        + saved
        + (
            shape(seq, width),
            shape(128, width),
            shape(8, width),
            shape(16, width, dtype=BF),
            shape(16, EMB, dtype=BF),
            shape(128, width),
            shape(8, 128),
        ),
        in_specs=[vmem, any_space] + [vmem] * 6,
        out_specs=[any_space] * 9 + [vmem] * 6,
        scratch_shapes=[
            pltpu.VMEM((shards,) + rows.shape, BF),
            pltpu.VMEM(mats.shape[1:], F32),
            pltpu.VMEM(mats.shape, BF),
            pltpu.VMEM((layers + 1, seq, width), F32),
        ]
        + [pltpu.VMEM(array.shape, array.dtype) for array in saved[1:]]
        + [
            pltpu.VMEM((seq, width), F32),
            pltpu.VMEM((4, width, width), BF),
            pltpu.VMEM((seq, width), F32),
            pltpu.VMEM(classes.shape, BF),
            pltpu.SemaphoreType.DMA((slots,)),
            pltpu.SemaphoreType.DMA((slots,)),
            pltpu.SemaphoreType.DMA((1 + layers,)),
            pltpu.SemaphoreType.DMA((4,)),
            pltpu.SemaphoreType.DMA((1 + 7 * layers,)),
        ],
        name="gather_and_forward",
        compiler_params=pltpu.CompilerParams(
            collective_id=1, has_side_effects=True, vmem_limit_bytes=56 * 1024 * 1024
        ),
    )(rows, mats, patches, keep, keep_column, classes, label, weight)


def accumulate(target, start, source, begin, count, step):
    @pl.loop(0, count // step)
    def _(turn):
        here = rows_at(start + turn * step, step)
        there = rows_at(begin + turn * step, step)
        target[here, :] = (target[here, :].astype(F32) + source[there, :].astype(F32)).astype(BF)


class Group(NamedTuple):
    begin: object
    stages: list
    core_slot: list


def scatter_group(links, dest, load, sizes, bufs, emit, used=None):
    depth, z, y, c, x = links.depth, links.z, links.y, links.c, links.x
    n, p, q, step = sizes
    mine, core_in, x_in, y_in, z_in, z_last, final = bufs
    core_slot, x_slot = [links.slot(), links.slot()], [links.slot(), links.slot()]
    q_slot, p_slot, low_slot, high_slot, last_slot = (links.slot() for _ in range(5))
    m = p + q
    first = x * p
    own_p, peer_p = x * m, (1 - x) * m
    sides = ((0, 1 - y), (1, y))

    def begin():
        for i, side in sides:
            load(i, side, mine.at[side], core_in.at[side], core_slot[i])

    def stage_core():
        for i, side in sides:
            load(i, side, mine.at[side], None, None)
            links.receive(core_slot[i], core_in.at[side])
            accumulate(mine.at[side], 0, core_in.at[side], 0, n, step)
            links.send(x_slot[i], mine.at[side, rows_at(peer_p, p)], x_in.at[side], links.x_peer)
            if i == 0:
                links.send(q_slot, mine.at[side, pl.ds(p, q)], y_in.at[pl.ds(0, q)], links.y_peer)
        if used is not None:
            used()

    def stage_x():
        for i, side in sides:
            links.receive(x_slot[i], x_in.at[side])
            accumulate(mine.at[side], own_p, x_in.at[side], 0, p, step)
            if i == 0:
                links.send(
                    p_slot, mine.at[side, rows_at(own_p, p)], y_in.at[pl.ds(q, p)], links.y_peer
                )
        links.receive(q_slot, y_in.at[pl.ds(0, q)])
        accumulate(mine.at[y], p, y_in, 0, q, step)

    def stage_y():
        links.receive(p_slot, y_in.at[pl.ds(q, p)])
        accumulate(mine.at[y], own_p, y_in, q, p, step)

    def stage_z(hop):
        block = mine.at[y, rows_at(first, m)]

        def take(slot, source, pred):
            @pl.when(pred)
            def _():
                links.receive(slot, source)
                accumulate(mine.at[y], first, source, 0, m, step)

        if dest > 0:
            if 1 <= hop <= dest:
                take(low_slot, z_in, z == hop)
            if hop < dest:
                links.send(low_slot, block, z_in, links.up, z == hop)
        if dest < depth - 1:
            turn = depth - 1 - hop
            if hop >= 1 and turn > dest:
                take(high_slot, z_in, z == turn)
            if turn > dest + 1:
                links.send(high_slot, block, z_in, links.down, z == turn)
            if turn == dest + 1:
                links.send(high_slot, block, z_last, links.down, z == turn)
            if turn == dest and hop >= 1:
                take(high_slot, z_last, z == dest)
        if hop == max(dest, depth - 1 - dest):
            links.send(last_slot, block, final, links.x_peer, z == dest)

    def stage_last():
        links.finish(x_slot[1])
        links.finish(last_slot)

        @pl.when(z == dest)
        def _():
            links.receive(last_slot, final)
            accumulate(mine.at[y], p, final, jnp.where(x == 0, 0, p), q, step)

            @pl.loop(0, p // 16)
            def _(turn):
                there = rows_at(jnp.where(x == 0, q, 0) + turn * 16, 16)
                mine[y, rows_at(peer_p + turn * 16, 16), :] = final[there, :]

            emit(mine.at[y])

    hops = [functools.partial(stage_z, hop) for hop in range(depth)]
    return Group(begin, [stage_core, stage_x, stage_y] + hops + [stage_last], core_slot)

def norm_back(value, gain, upstream):
    center = value - jnp.mean(value, -1, keepdims=True)
    scale = lax.rsqrt(jnp.mean(center * center, -1, keepdims=True) + norm_epsilon)
    normal = center * scale
    scaled = upstream * gain
    inner = scale * (
        scaled
        - jnp.mean(scaled, -1, keepdims=True)
        - normal * jnp.mean(scaled * normal, -1, keepdims=True)
    )
    return (
        inner,
        jnp.sum(upstream * normal, 0, keepdims=True),
        jnp.sum(upstream, 0, keepdims=True),
    )


VMEM_LIMIT = 62 * 1024 * 1024
SUB = 3
IN_FLIGHT = 2 * SUB
LAGS = (1, 3, 5, 7, 9, 11, 13, 15)


def backward_kernel(
    depth,
    sides,
    layers,
    weights,
    resid,
    normed,
    project,
    log_total,
    context,
    mixed,
    normed_two,
    embedded,
    patches,
    vectors,
    keep,
    keep_column,
    pooled_row,
    z_rows,
    feature_rows,
    vector_start,
    stats,
    out,
    clipped,
    totals,
    row_out,
    blocks_v,
    core_in,
    x_in,
    y_in,
    z_in,
    z_last,
    final,
    rows_v,
    row_mine,
    row_core,
    row_x,
    row_y,
    row_z,
    row_z_last,
    row_final,
    resid_v,
    normed_v,
    project_v,
    log_v,
    context_v,
    mixed_v,
    two_v,
    weight_v,
    patch_v,
    hidden_v,
    pre_v,
    up_v,
    short_v,
    total_v,
    context_grad_v,
    vector_v,
    note,
    inbox,
    send_sem,
    recv_sem,
    local_sem,
    weight_sem,
    load_sem,
    mail_send,
    mail_recv,
    free_sem,
):
    links = Links(depth, send_sem, recv_sem)
    y, c, z = links.y, links.c, links.z
    me = links.me * sides + links.x
    everyone = PLANE * depth * sides
    width = up_v.shape[1]
    count = out.shape[1]
    n = count // SUB
    p = n // 4 // 16 * 16
    per_layer = depth * SUB
    own = 2 * layers * per_layer
    piece = 2 * n

    saved = (
        (normed_two, two_v),
        (mixed, mixed_v),
        (context, context_v),
        (resid, resid_v),
        (normed, normed_v),
        (project, project_v),
        (log_total, log_v),
    )

    def load(layer, which):
        source, target = saved[which]
        return pltpu.make_async_copy(source.at[layer], target, load_sem.at[which])

    chunks = []
    for layer in reversed(range(layers)):
        for turn in (3, 2, 1, 0):
            chunks += [(layer, 8 + turn), (layer, 4 + turn)]
        chunks += [(layer, 3), (layer, 0), (layer, 1), (layer, 2)]

    def chunk_copy(number):
        layer, index = chunks[number]
        return pltpu.make_async_copy(
            weights.at[layer, pl.ds(index * width, width)],
            weight_v.at[number % 4],
            weight_sem.at[number % 4],
        )

    def chunk(number):
        chunk_copy(number).wait()
        return weight_v[number % 4]

    def refill(*numbers):
        for number in numbers:
            if number < len(chunks):
                chunk_copy(number).start()

    for which in range(len(saved)):
        load(layers - 1, which).start()
    refill(0, 1, 2, 3)
    patch_load = pltpu.make_async_copy(patches, patch_v, load_sem.at[7])
    patch_load.start()

    def others(run):
        for number in range(everyone):
            pl.when(me != number)(functools.partial(run, number))

    def place(number):
        return (number // sides, number % sides)

    barrier = pltpu.get_barrier_semaphore()
    others(
        lambda number: pl.semaphore_signal(
            barrier, inc=1, device_id=place(number), device_id_type=MESH
        )
    )
    note[...] = stats[...]
    vector_v[...] = vector_start[...]
    up_v[...] = keep_column[...] * pooled_row[pl.ds(0, 1), :]
    lane = lax.broadcasted_iota(jnp.int32, (8, 128), 1)
    first = lax.broadcasted_iota(jnp.int32, (8, 128), 0) == 0

    def add_squares(block):
        value = block.astype(F32)
        note[...] += jnp.where(first & (lane == 0), jnp.sum(value * value), 0.0)

    groups, closers = [], []
    starts = {}

    def add_group(dest, send_out, take_in, sizes, bufs, emit, used=None):
        def load_block(i, side, mine, target, slot):
            if target is None:
                take_in(i, side, mine)
            else:
                send_out(i, side, mine, target, slot)

        groups.append(scatter_group(links, dest, load_block, sizes, bufs, emit, used))

    for order, layer in enumerate(reversed(range(layers))):
        for turn, dest in enumerate(reversed(range(depth))):
            ring = own
            for part in range(SUB):
                number, spot = len(groups), layer * SUB + part
                starts[(layer, dest, part)] = number
                slot = number % IN_FLIGHT

                def send_out(i, side, mine, target, sem_slot, ring=ring, part=part):
                    source = blocks_v.at[ring + 2 * part + side]
                    links.send(sem_slot, source, target, links.c_peer)

                def write(source, layer=layer, part=part, spot=spot):
                    target = out.at[layer, pl.ds(part * n, n)]
                    return pltpu.make_async_copy(source, target, local_sem.at[spot])

                def emit(result, write=write):
                    add_squares(result[...])
                    write(result).start()

                closers.append((dest, write, blocks_v.at[2 * number]))

                def used(number=number):
                    if number < layers * per_layer - IN_FLIGHT:
                        pl.semaphore_signal(
                            free_sem, inc=1, device_id=links.c_peer, device_id_type=MESH
                        )

                add_group(
                    dest,
                    send_out,
                    lambda i, side, mine: None,
                    (n, p, n - 2 * p, n // 4),
                    [blocks_v.at[pl.ds(2 * number, 2)], core_in.at[slot]]
                    + [ref.at[number] for ref in (x_in, y_in, z_in)]
                    + [z_last.at[spot], final.at[spot]],
                    emit,
                    used,
                )
    first_row_group = len(groups)
    rows = row_out.shape[0]
    for dest in reversed(range(depth)):
        number = len(groups)

        def row_copy(i, side, mine, dest=dest):
            sem = local_sem.at[layers * SUB + 2 * dest + i]
            return pltpu.make_async_copy(rows_v.at[links.at(dest, side, c)], mine, sem)

        def row_send(i, side, mine, target, slot, dest=dest, row_copy=row_copy):
            row_copy(i, side, mine).start()
            source = rows_v.at[links.at(dest, side, 1 - c)]
            links.send(slot, source, target, links.c_peer)

        def row_emit(result, dest=dest):
            add_squares(result[...])
            row_out[...] = result[...]

        add_group(
            dest,
            row_send,
            lambda i, side, mine, row_copy=row_copy: row_copy(i, side, mine).wait(),
            (rows, 16, rows - 32, 16),
            [ref.at[dest] for ref in (row_mine, row_core, row_x, row_y, row_z)]
            + [row_z_last, row_final],
            row_emit,
        )

    begun = []

    def release(layer, dest):
        for part in range(SUB):
            number = starts[(layer, dest, part)]
            if number >= IN_FLIGHT:
                pl.semaphore_wait(free_sem, 1)
            groups[number].begin()
            begun.append(number)

    def recycle(layer, dest):
        for part in range(SUB):
            number = starts[(layer, dest, part)]
            if number >= SUB:
                for slot in groups[number - SUB].core_slot:
                    links.finish(slot)

    last_turn = [0]

    def advance():
        turn = last_turn[0]
        for stage, lag in enumerate(LAGS):
            if 0 <= turn - lag < len(groups):
                groups[turn - lag].stages[stage]()
        last_turn[0] += 1

    def grad_pieces(layer, dest, left, column, amount, right, begin):
        number = starts[(layer, dest, 0)]
        ring = own

        @pl.loop(0, amount)
        def _(turn):
            columns = pl.ds(pl.multiple_of(column + turn * piece, 128), piece)
            result = matmul_tn(left[:, columns], right[...])
            for half in range(2):
                block = 2 * (begin + turn) + half
                shard = block // SUB
                part = lax.rem(block, SUB)
                side, core = shard // 2, lax.rem(shard, 2)
                index = jnp.where(
                    core == c, 2 * (number + part) + side, ring + 2 * part + side
                )
                blocks_v[index] = result[half * n : (half + 1) * n].astype(BF)

    half_lane = lax.broadcasted_iota(jnp.int32, (1, 128), 1) < HDIM
    scale = HDIM ** (-0.5)

    def attention_pair(pair):
        def lanes(base):
            return pl.ds(pl.multiple_of(base + pair * 128, 128), 128)

        query, key = project_v[:, lanes(0)], project_v[:, lanes(width)]
        value, grad = project_v[:, lanes(2 * width)], context_grad_v[:, lanes(0)]
        totals_now = log_v[...]
        column = lax.broadcasted_iota(jnp.int32, totals_now.shape, 1)
        query_grad = key_grad = value_grad = 0.0
        zero = jnp.zeros_like(query)
        for head in range(2):
            here = half_lane if head == 0 else jnp.logical_not(half_lane)
            query_h, key_h = jnp.where(here, query, zero), jnp.where(here, key, zero)
            grad_h = jnp.where(here, grad, zero)
            total = jnp.sum(
                jnp.where(column == 2 * pair + head, totals_now, 0.0), -1, keepdims=True
            )
            scores = jnp.where(keep[...] > 0, matmul_nt(query_h, key) * scale, -1000000000.0)
            probs = jnp.exp(scores - total)
            prob_grad = matmul_nt(grad_h, value)
            value_grad += matmul_tn(probs.astype(BF), grad_h)
            score_grad = (
                probs * (prob_grad - jnp.sum(prob_grad * probs, -1, keepdims=True))
            ).astype(BF)
            query_grad += matmul(score_grad, key_h)
            key_grad += matmul_tn(score_grad, query_h)
        pre_v[:, lanes(0)] = (query_grad * scale).astype(BF)
        pre_v[:, lanes(width)] = (key_grad * scale).astype(BF)
        pre_v[:, lanes(2 * width)] = value_grad.astype(BF)

    def layer_steps(order, layer):
        base = 4 + 12 * layer
        chunk0 = 12 * order

        def vector(index):
            return vectors[pl.ds(base + index, 1), :]

        def put(index, value):
            vector_v[pl.ds(base + index, 1), :] = value

        def column_sum(value):
            return jnp.sum(value.astype(F32), 0, keepdims=True)

        load(layer, 0).wait()
        short_v[...] = up_v[...].astype(BF)
        put(7, column_sum(short_v[...]))
        total_v[...] = jnp.zeros_like(total_v)
        recycle(layer, 3)
        for turn, part in enumerate((3, 2, 1, 0)):
            number = chunk0 + 2 * turn
            down, up = chunk(number), chunk(number + 1)
            pre = matmul_nt(two_v[...], up) + vector(8 + part)
            gate = jax.nn.sigmoid(1.702 * pre)
            hidden_v[...] = (pre * gate).astype(BF)
            slope = gate + 1.702 * pre * gate * (1.0 - gate)
            pre_grad = (matmul_nt(short_v[...], down) * slope).astype(BF)
            pre_v[:, pl.ds(part * width, width)] = pre_grad
            put(8 + part, column_sum(pre_grad))
            total_v[...] += matmul(pre_grad, up)
            refill(number + 4, number + 5)
            yield None
            if part == 0:
                recycle(layer, 2)
            if part > 0:
                grad_pieces(layer, 3, hidden_v, 0, 2, short_v, 2 * (part - 1))
            else:
                grad_pieces(layer, 2, hidden_v, 0, 2, short_v, 4)
            if part == 1:
                release(layer, 3)
                yield 3
            else:
                yield None
        grad_pieces(layer, 2, pre_v, 2 * width, 2, two_v, 0)
        yield None
        grad_pieces(layer, 2, pre_v, 3 * width, 2, two_v, 2)
        release(layer, 2)
        yield 2
        load(layer, 1).wait()
        inner, gain, shift = norm_back(mixed_v[...], vector(5), total_v[...])
        put(5, gain)
        put(6, shift)
        up_v[...] += inner
        short_v[...] = up_v[...].astype(BF)
        put(4, column_sum(short_v[...]))
        yield None
        load(layer, 2).wait()
        recycle(layer, 1)
        grad_pieces(layer, 1, short_v, 0, 2, context_v, 0)
        context_grad_v[...] = matmul(short_v[...], chunk(chunk0 + 8)).astype(BF)
        refill(chunk0 + 12)
        yield None
        grad_pieces(layer, 1, pre_v, 0, 2, two_v, 2)
        yield None
        grad_pieces(layer, 1, pre_v, width, 2, two_v, 4)
        release(layer, 1)
        if layer > 0:
            for which in range(3):
                load(layer - 1, which).start()
        else:
            embed_load.start()
        yield 1
        load(layer, 5).wait()
        load(layer, 6).wait()
        for third in range(3):

            @pl.loop(0, 2)
            def _(turn, third=third):
                attention_pair(2 * third + turn)

            yield None
        load(layer, 4).wait()
        recycle(layer, 0)
        put(2, column_sum(pre_v[:, pl.ds(0, width)]))
        put(3, column_sum(pre_v[:, pl.ds(2 * width, width)]))
        for third in range(3):
            grad_pieces(layer, 0, pre_v, third * width, 2, normed_v, 2 * third)
            if third < 2:
                yield None
        release(layer, 0)
        yield 0
        load(layer, 3).wait()
        back = matmul(pre_v[:, pl.ds(0, width)], chunk(chunk0 + 9))
        back += matmul(pre_v[:, pl.ds(width, width)], chunk(chunk0 + 10))
        back += matmul(pre_v[:, pl.ds(2 * width, width)], chunk(chunk0 + 11))
        refill(chunk0 + 13, chunk0 + 14, chunk0 + 15)
        inner, gain, shift = norm_back(resid_v[...], vector(0), back)
        put(0, gain)
        put(1, shift)
        up_v[...] += inner
        if layer > 0:
            for which in range(3, len(saved)):
                load(layer - 1, which).start()
        yield None

    embed_load = pltpu.make_async_copy(embedded, mixed_v, load_sem.at[8])
    pl.semaphore_wait(barrier, everyone - 1)
    pending = 0
    for order, layer in enumerate(reversed(range(layers))):
        for ready in layer_steps(order, layer):
            if ready is not None:
                pending += SUB
            if pending > 0:
                advance()
                pending -= 1
    embed_load.wait()
    inner, gain, shift = norm_back(mixed_v[...], vectors[pl.ds(0, 1), :], up_v[...])
    vector_v[pl.ds(0, 1), :] = gain
    vector_v[pl.ds(1, 1), :] = shift
    short_v[...] = inner.astype(BF)
    total_v[...] = inner
    patch_load.wait()
    pixels, embeds, seq = patch_v.shape[1], feature_rows.shape[1], inner.shape[0]
    for turn in range(width // piece):
        columns = pl.ds(turn * piece, piece)
        patch_grad = matmul_tn(short_v[:, columns], patch_v[...])
        proj_grad = matmul_tn(z_rows[:, columns], feature_rows[...])
        position = total_v[:, columns].T
        vector_grad = vector_v[:, columns].T
        for part in range(piece // rows):
            shard, inside = turn * (piece // rows) + part, slice(part * rows, (part + 1) * rows)
            rows_v[shard, :, pl.ds(0, pixels)] = patch_grad[inside].astype(BF)
            rows_v[shard, :, pl.ds(pixels, embeds)] = proj_grad[inside].astype(BF)
            rows_v[shard, :, pl.ds(pixels + embeds, seq)] = position[inside].astype(BF)
            rows_v[shard, :, pl.ds(pixels + embeds + seq, 128)] = vector_grad[inside].astype(BF)
    for number in range(first_row_group, len(groups)):
        groups[number].begin()
    while last_turn[0] < len(groups) + max(LAGS):
        advance()

    def mail(number, slot):
        return pltpu.make_async_remote_copy(
            src_ref=note,
            dst_ref=inbox.at[slot],
            send_sem=mail_send.at[number],
            recv_sem=mail_recv.at[slot],
            device_id=place(number),
            device_id_type=MESH,
        )

    others(lambda number: mail(number, me).start())
    inbox[pl.ds(me, 1)] = note[...][None]
    links.finish()
    for dest, write, source in closers:
        pl.when(z == dest)(lambda write=write, source=source: write(source).wait())
    others(lambda number: mail(number, number).wait_recv())
    summed = jnp.sum(inbox[...], 0)
    others(lambda number: mail(number, me).wait_send())

    def pick(index):
        return jnp.sum(jnp.where(first & (lane == index), summed, 0.0))

    loss_sum, weight_sum = pick(1), pick(2)
    norm = jnp.sqrt(jnp.full((8, 128), pick(0) / sides)) / weight_sum
    clip = jnp.minimum(1.0, clip_bound / (norm + 1e-06)) / weight_sum
    totals[...] = jnp.where(
        lane == 0,
        loss_sum,
        jnp.where(lane == 1, weight_sum, jnp.where(lane == 2, norm, clip)),
    )
    clipped[...] = row_out[...].astype(F32) * clip[:1, :1]


def backward(
    depth, sides, weights, saved, embedded, patches, vectors, keep, keep_column, head, start, stats
):
    layers, rows_all, width = weights.shape
    seq, pixels = patches.shape
    shards = PLANE * depth
    count, rows = rows_all // shards, width // shards
    lanes = -(-(pixels + EMB + SEQ + 4 + 12 * layers) // 128) * 128
    n = count // SUB
    p = n // 4 // 16 * 16
    m = n - p
    per_layer = depth * SUB
    blocks = layers * per_layer
    row_m = rows - 16
    everyone = shards * sides

    def room(*shape, dtype=BF):
        return pltpu.VMEM(shape, dtype)

    any_space = pl.BlockSpec(memory_space=pl.ANY)
    vmem = pl.BlockSpec(memory_space=pltpu.VMEM)
    slots = (blocks + depth) * 9
    return pl.pallas_call(
        functools.partial(backward_kernel, depth, sides, layers),
        out_shape=(
            jax.ShapeDtypeStruct((layers, count, width), BF),
            jax.ShapeDtypeStruct((rows, lanes), F32),
            jax.ShapeDtypeStruct((8, 128), F32),
        ),
        in_specs=[any_space] * (1 + len(saved) + 2) + [vmem] * 8,
        out_specs=[any_space, vmem, vmem],
        scratch_shapes=[
            room(rows, lanes),
            room(2 * blocks + 2 * SUB, n, width),
            room(IN_FLIGHT, 2, n, width),
            room(blocks, 2, p, width),
            room(blocks, m, width),
            room(blocks, m, width),
            room(layers * SUB, m, width),
            room(layers * SUB, m, width),
            room(shards, rows, lanes),
            room(depth, 2, rows, lanes),
            room(depth, 2, rows, lanes),
            room(depth, 2, 16, lanes),
            room(depth, row_m, lanes),
            room(depth, row_m, lanes),
            room(row_m, lanes),
            room(row_m, lanes),
            room(seq, width, dtype=F32),
            room(seq, width),
            room(seq, 3 * width),
            room(seq, 128, dtype=F32),
            room(seq, width),
            room(seq, width, dtype=F32),
            room(seq, width),
            room(4, width, width),
            room(seq, pixels),
            room(seq, width),
            room(seq, 4 * width),
            room(seq, width, dtype=F32),
            room(seq, width),
            room(seq, width, dtype=F32),
            room(seq, width),
            room(128, width, dtype=F32),
            room(8, 128, dtype=F32),
            room(everyone, 8, 128, dtype=F32),
            pltpu.SemaphoreType.DMA((slots,)),
            pltpu.SemaphoreType.DMA((slots,)),
            pltpu.SemaphoreType.DMA((layers * SUB + 2 * depth,)),
            pltpu.SemaphoreType.DMA((4,)),
            pltpu.SemaphoreType.DMA((9,)),
            pltpu.SemaphoreType.DMA((everyone,)),
            pltpu.SemaphoreType.DMA((everyone,)),
            pltpu.SemaphoreType.REGULAR,
        ],
        name="backward_and_sum",
        compiler_params=pltpu.CompilerParams(
            collective_id=2, has_side_effects=True, vmem_limit_bytes=VMEM_LIMIT
        ),
    )(weights, *saved, embedded, patches, vectors, keep, keep_column, *head, start, stats)


def adam(clipped, row_params, row_zero, row_ema, row_first, row_second):
    new_first = first_decay * row_first + (1.0 - first_decay) * clipped
    new_second = second_decay * row_second + (1.0 - second_decay) * clipped * clipped
    step_size = (
        new_first
        / (1.0 - first_decay**STEPS_DONE)
        / (jnp.sqrt(new_second / (1.0 - second_decay**STEPS_DONE)) + adam_floor)
    )
    new_rows = row_params - adam_rate * (step_size + weight_decay * row_params)
    ema_rows = ema_decay * row_ema + (1.0 - ema_decay) * new_rows
    mixed_rows = mix_share * new_rows + (1.0 - mix_share) * row_zero
    return (new_rows, new_first, new_second, ema_rows, mixed_rows)


def finish_kernel(
    hyper,
    totals,
    clipped,
    row_params,
    row_zero,
    row_ema,
    row_first,
    row_second,
    grad,
    momentum,
    mats,
    zero,
    ema,
    new_rows,
    new_first,
    new_second,
    ema_rows,
    mixed_rows,
    bias_grad,
    new_momentum,
    new_mats,
    new_ema,
    new_mixed,
    grad_v,
    m_v,
    mats_v,
    zero_v,
    ema_v,
    x_v,
    short_v,
    low_v,
    in_sem,
    out_sem,
):
    layers, count, width = grad.shape
    pairs = [(grad, grad_v), (momentum, m_v)]
    pairs += [(mats, mats_v), (zero, zero_v), (ema, ema_v)]
    loads = [pltpu.make_async_copy(a, b, in_sem.at[i]) for i, (a, b) in enumerate(pairs)]
    for load in loads:
        load.start()
    rows = row_params.shape[1]
    row_grad = clipped[:, pl.ds(0, rows)]
    news = adam(row_grad, *(ref[...] for ref in (row_params, row_zero, row_ema, row_first, row_second)))
    for target, value in zip((new_rows, new_first, new_second, ema_rows, mixed_rows), news):
        target[...] = value
    lane = lax.broadcasted_iota(jnp.int32, clipped.shape, 1)
    spot = lax.broadcasted_iota(jnp.int32, bias_grad.shape, 1)
    bias = jnp.zeros(bias_grad.shape, F32)
    for layer in range(layers):
        index = PIX + EMB + SEQ + 4 + 12 * layer + 7
        column = jnp.sum(jnp.where(lane == index, clipped[...], 0.0), -1, keepdims=True)
        bias = jnp.where(spot == layer, column, bias)
    bias_grad[...] = bias
    part = count // 3
    factor = totals[pl.ds(0, 1), pl.ds(3, 1)]
    loads[0].wait()
    loads[1].wait()
    stores = []
    for layer in range(layers):
        total = jnp.zeros((1, 1), F32)
        for third in range(3):
            rows = pl.ds(third * part, part)
            value = momentum_decay * m_v[layer, rows, :] + factor * grad_v[layer, rows, :].astype(F32)
            m_v[layer, rows, :] = value
            total += jnp.sum(value * value, keepdims=True)
        store = pltpu.make_async_copy(m_v.at[layer], new_momentum.at[layer], out_sem.at[layer])
        store.start()
        stores.append(store)
        inverse = 1.0 / (jnp.sqrt(total) + 1e-07)
        for third in range(3):
            rows = pl.ds(third * part, part)
            value = m_v[layer, rows, :] * inverse
            x_v[layer, rows, :] = value
            short_v[0, layer, rows, :] = value.astype(BF)

    row_id = lax.broadcasted_iota(jnp.int32, (part, count), 0)
    col_id = lax.broadcasted_iota(jnp.int32, (part, count), 1)

    def step(turn, shift, use):
        now = lax.rem(turn, 2)
        linear = coeff_cubic + 2.0 * shift * coeff_quintic
        stay = coeff_linear + shift * (coeff_cubic + shift * coeff_quintic)
        for layer in range(layers):
            for third in range(3):
                rows = pl.ds(third * part, part)
                gram = matmul_nt(short_v[now, layer, rows, :], short_v[now, layer])
                gram -= jnp.where(row_id + third * part == col_id, shift, 0.0)
                low_v[layer, rows, :] = gram.astype(BF)
        for layer in range(layers):
            for third in range(3):
                rows = pl.ds(third * part, part)
                low = low_v[layer, rows, :]
                poly = linear * low.astype(F32) + coeff_quintic * matmul(low, low_v[layer])
                value = stay * x_v[layer, rows, :] + matmul(poly.astype(BF), short_v[now, layer])
                use(layer, third, rows, value)

    @pl.loop(0, NS_STEPS - 1)
    def _(turn):
        def keep(layer, third, rows, value):
            x_v[layer, rows, :] = value
            short_v[1 - lax.rem(turn, 2), layer, rows, :] = value.astype(BF)

        step(turn, jnp.where(turn >= NS_STEPS - 2, 1.0, 0.0), keep)

    for load in loads[2:]:
        load.wait()

    def update(layer, third, rows, orth):
        old = mats_v[layer, rows, :]
        value = old - muon_rate * (hyper * orth + weight_decay * old)
        mats_v[layer, rows, :] = value
        ema_v[layer, rows, :] = ema_decay * ema_v[layer, rows, :] + (1.0 - ema_decay) * value
        zero_v[layer, rows, :] = mix_share * value + (1.0 - mix_share) * zero_v[layer, rows, :]
        for turn, (source, target) in enumerate(
            ((mats_v, new_mats), (ema_v, new_ema), (zero_v, new_mixed))
        ):
            sem = out_sem.at[layers + (layer * 3 + third) * 3 + turn]
            store = pltpu.make_async_copy(source.at[layer, rows], target.at[layer, rows], sem)
            store.start()
            stores.append(store)

    step(NS_STEPS - 1, 1.0, update)
    for store in stores:
        store.wait()


def finish(totals, clipped, tables, grad, momentum, mats, zero, ema):
    layers, count, width = grad.shape
    full = jax.ShapeDtypeStruct(mats.shape, F32)
    table = jax.ShapeDtypeStruct(tables[0].shape, F32)
    any_space = pl.BlockSpec(memory_space=pl.ANY)
    vmem = pl.BlockSpec(memory_space=pltpu.VMEM)
    return pl.pallas_call(
        functools.partial(finish_kernel, 0.2 * math.sqrt(width)),
        out_shape=(table,) * 5
        + (jax.ShapeDtypeStruct((clipped.shape[0], 128), F32), full, full, full, full),
        in_specs=[vmem] * (2 + len(tables)) + [any_space] * 5,
        out_specs=[vmem] * 6 + [any_space] * 4,
        scratch_shapes=[
            pltpu.VMEM(grad.shape, BF),
            pltpu.VMEM(mats.shape, F32),
            pltpu.VMEM(mats.shape, F32),
            pltpu.VMEM(mats.shape, F32),
            pltpu.VMEM(mats.shape, F32),
            pltpu.VMEM(mats.shape, F32),
            pltpu.VMEM((2,) + mats.shape, BF),
            pltpu.VMEM((layers, count, count), BF),
            pltpu.SemaphoreType.DMA((5,)),
            pltpu.SemaphoreType.DMA((layers * 10,)),
        ],
        name="orthogonalize",
        compiler_params=pltpu.CompilerParams(vmem_limit_bytes=56 * 1024 * 1024),
    )(totals, clipped, *tables, grad, momentum, mats, zero, ema)


def gather_layer(shard):
    return lax.all_gather(shard.astype(jnp.bfloat16), "fsdp", axis=0, tiled=True)


def layer_forward(resid, weight_tensors, vector, valid_mask):
    images, seq = valid_mask.shape
    width = resid.shape[1]
    ffn = 4 * width
    normed = norm_forward(resid, vector[0], vector[1]).astype(jnp.bfloat16)
    bias = jnp.concatenate([vector[2], jnp.zeros_like(vector[2]), vector[3]])
    project = (matmul_nt(normed, weight_tensors[: 3 * width]) + bias).astype(jnp.bfloat16)
    parts = project.reshape(images, seq, 3, HEADS, HDIM)
    scores = attention_scores(parts, valid_mask)
    top_score = jnp.max(scores, -1, keepdims=True)
    expo = jnp.exp(scores - top_score)
    totals = jnp.sum(expo, -1, keepdims=True)
    log_total = top_score + jnp.log(totals)
    probs = (expo / totals).astype(jnp.bfloat16)
    context = jnp.einsum(
        "ihqk,ikhd->iqhd", probs, parts[:, :, 2], preferred_element_type=jnp.float32
    )
    context = context.reshape(images * seq, width).astype(jnp.bfloat16)
    mixed = resid + (matmul_nt(context, weight_tensors[3 * width : 4 * width]) + vector[4])
    normed_two = norm_forward(mixed, vector[5], vector[6]).astype(jnp.bfloat16)
    hidden_pre = matmul_nt(normed_two, weight_tensors[4 * width : 4 * width + ffn]) + vector[
        8:12
    ].reshape(ffn)
    hidden = (hidden_pre * jax.nn.sigmoid(1.702 * hidden_pre)).astype(jnp.bfloat16)
    output = mixed + (matmul(hidden, weight_tensors[4 * width + ffn :]) + vector[7])
    return (
        output,
        (resid, normed, project, log_total, context, mixed, normed_two, hidden_pre, hidden),
    )


def layer_backward(upstream, weight_tensors, vector, valid_mask, saved_activation):
    resid, normed, project, log_total, context, mixed, normed_two, hidden_pre, hidden = (
        saved_activation
    )
    images, seq = valid_mask.shape
    width = resid.shape[1]
    ffn = 4 * width
    out_grad = upstream.astype(jnp.bfloat16)
    grad_down = matmul_tn(hidden, out_grad)
    hidden_grad = matmul_nt(out_grad, weight_tensors[4 * width + ffn :])
    gate = jax.nn.sigmoid(1.702 * hidden_pre)
    pre_grad = (hidden_grad * (gate + 1.702 * hidden_pre * gate * (1.0 - gate))).astype(
        jnp.bfloat16
    )
    grad_up = matmul_tn(pre_grad, normed_two)
    second_in, gain_two, shift_two = norm_backward(
        mixed, vector[5], matmul(pre_grad, weight_tensors[4 * width : 4 * width + ffn])
    )
    mixed_grad = upstream + second_in
    attn_grad = mixed_grad.astype(jnp.bfloat16)
    grad_out = matmul_tn(attn_grad, context)
    context_grad = matmul(attn_grad, weight_tensors[3 * width : 4 * width]).astype(jnp.bfloat16)
    context_grad = context_grad.reshape(images, seq, HEADS, HDIM)
    parts = project.reshape(images, seq, 3, HEADS, HDIM)
    probs = jnp.exp(attention_scores(parts, valid_mask) - log_total)
    prob_grad = jnp.einsum(
        "iqhd,ikhd->ihqk", context_grad, parts[:, :, 2], preferred_element_type=jnp.float32
    )
    value_grad = jnp.einsum(
        "ihqk,iqhd->ikhd",
        probs.astype(jnp.bfloat16),
        context_grad,
        preferred_element_type=jnp.float32,
    )
    score_grad = (probs * (prob_grad - jnp.sum(prob_grad * probs, -1, keepdims=True))).astype(
        jnp.bfloat16
    )
    query_grad = jnp.einsum(
        "ihqk,ikhd->iqhd", score_grad, parts[:, :, 1], preferred_element_type=jnp.float32
    ) * HDIM ** (-0.5)
    key_grad = jnp.einsum(
        "ihqk,iqhd->ikhd", score_grad, parts[:, :, 0], preferred_element_type=jnp.float32
    ) * HDIM ** (-0.5)
    project_grad = (
        jnp.stack([query_grad, key_grad, value_grad], 2)
        .reshape(images * seq, 3 * width)
        .astype(jnp.bfloat16)
    )
    project_sum = jnp.sum(project_grad.astype(jnp.float32), 0)
    grad_qkv = matmul_tn(project_grad, normed)
    first_in, gain_one, shift_one = norm_backward(
        resid, vector[0], matmul(project_grad, weight_tensors[: 3 * width])
    )
    residual_gradient = mixed_grad + first_in
    grad_matrix = [part.astype(BF) for part in (grad_qkv, grad_out, grad_up, grad_down)]
    grad_vector = jnp.concatenate(
        [
            jnp.stack(
                [
                    gain_one,
                    shift_one,
                    project_sum[:width],
                    project_sum[2 * width :],
                    jnp.sum(attn_grad.astype(jnp.float32), 0),
                    gain_two,
                    shift_two,
                    jnp.sum(out_grad.astype(jnp.float32), 0),
                ]
            ),
            jnp.sum(pre_grad.astype(jnp.float32), 0).reshape(4, width),
        ],
        0,
    )
    return (residual_gradient, grad_matrix, grad_vector)


def newton_schulz(blocks):
    frob = jnp.sqrt(jnp.sum(blocks * blocks, axis=(1, 2), keepdims=True)) + 1e-07
    blocks = blocks / frob
    unit = jnp.eye(blocks.shape[1], dtype=jnp.float32)
    for turn in range(NS_STEPS):
        shift = 1.0 if turn >= NS_STEPS - 2 else 0.0
        short = blocks.astype(BF)
        gram = jnp.einsum("lcd,led->lce", short, short, preferred_element_type=F32) - shift * unit
        low = gram.astype(BF)
        square = jnp.einsum("lce,lef->lcf", low, low, preferred_element_type=F32)
        poly = (coeff_cubic + 2.0 * shift * coeff_quintic) * gram + coeff_quintic * square
        stay = coeff_linear + shift * (coeff_cubic + shift * coeff_quintic)
        blocks = stay * blocks + jnp.einsum(
            "lce,led->lcd", poly.astype(BF), short, preferred_element_type=F32
        )
    return blocks


def row_updates(clipped, layers, *tables):
    front = PIX + EMB + SEQ + 4
    down_bias_grad = clipped[front:].reshape(layers, 12, clipped.shape[1])[:, 7]
    return adam(clipped, *tables) + (down_bias_grad,)


def plain_body(
    patches,
    pad_mask,
    labels,
    loss_weights,
    class_emb,
    layer_mats,
    layer_zero,
    layer_ema,
    layer_momentum,
    row_params,
    row_zero,
    row_ema,
    row_first,
    row_second,
):
    layers, columns, width = layer_mats.shape
    images, seq, pixels = patches.shape
    front = PIX + EMB + SEQ + 4
    valid_mask = pad_mask.astype(jnp.float32)
    gathered_rows = lax.all_gather(row_params.astype(jnp.bfloat16), "fsdp", axis=1, tiled=True)
    rows_value = gathered_rows.astype(jnp.float32)
    patch_weight = gathered_rows[:PIX]
    proj_rows = gathered_rows[PIX : PIX + EMB]
    position = rows_value[PIX + EMB : PIX + EMB + SEQ]
    head_vec = rows_value[PIX + EMB + SEQ : front]
    layer_vector_params = rows_value[front:].reshape(layers, 12, width)
    flat_patches = patches.reshape(images * seq, pixels)
    embedded = (matmul(flat_patches, patch_weight).reshape(images, seq, width) + position).reshape(
        images * seq, width
    )
    resid = norm_forward(embedded, head_vec[0], head_vec[1])
    kept_weights = []
    saved_activations = []
    for layer_number in range(layers):
        weight_tensors = gather_layer(layer_mats[layer_number])
        kept_weights.append(weight_tensors)
        resid, saved_activation = layer_forward(
            resid, weight_tensors, layer_vector_params[layer_number], valid_mask
        )
        saved_activations.append(saved_activation)
    counts = jnp.sum(valid_mask, -1, keepdims=True)
    pooled = jnp.sum(resid.reshape(images, seq, width) * valid_mask[..., None], 1) / counts
    pooled_norm = norm_forward(pooled, head_vec[2], head_vec[3]).astype(jnp.bfloat16)
    feature = matmul_nt(pooled_norm, proj_rows)
    inv_length = lax.rsqrt(jnp.sum(feature * feature, -1, keepdims=True) + unit_epsilon)
    unit_feat = (feature * inv_length).astype(jnp.bfloat16)
    classes = class_emb.astype(jnp.float32)
    class_unit = (
        classes * lax.rsqrt(jnp.sum(classes * classes, -1, keepdims=True) + unit_epsilon)
    ).astype(jnp.bfloat16)
    logits = logit_scale * matmul_nt(unit_feat, class_unit)
    top_logit = jnp.max(logits, -1, keepdims=True)
    shifted = jnp.exp(logits - top_logit)
    total_exp = jnp.sum(shifted, -1, keepdims=True)
    log_norm = top_logit + jnp.log(total_exp)
    onehot = (jnp.arange(logits.shape[1])[None, :] == labels[:, None]).astype(jnp.float32)
    losses = log_norm[:, 0] - jnp.sum(onehot * logits, -1)
    weights_value = loss_weights.astype(jnp.float32)
    loss_sum, weight_sum = lax.psum(
        (jnp.sum(weights_value * losses), jnp.sum(weights_value)), ("fsdp", "ns")
    )
    seed = weights_value / weight_sum
    logit_grad = seed[:, None] * (shifted / total_exp - onehot)
    unit_grad = logit_scale * jnp.dot(logit_grad, class_unit.astype(jnp.float32), precision=HIGHEST)
    feat_grad = inv_length * unit_grad - feature * inv_length**3 * jnp.sum(
        unit_grad * feature, -1, keepdims=True
    )
    grad_proj = jnp.dot(feat_grad.T, pooled_norm.astype(jnp.float32), precision=HIGHEST)
    pooled_grad, gain_post, shift_post = norm_backward(
        pooled, head_vec[2], jnp.dot(feat_grad, proj_rows.astype(jnp.float32), precision=HIGHEST)
    )
    residual_gradient = (valid_mask[..., None] * (pooled_grad / counts)[:, None, :]).reshape(
        images * seq, width
    )
    grad_mats = [None] * layers
    grad_vecs = [None] * layers
    for layer_number in reversed(range(layers)):
        weight_tensors = kept_weights[layer_number]
        residual_gradient, grad_matrix, grad_vector = layer_backward(
            residual_gradient,
            weight_tensors,
            layer_vector_params[layer_number],
            valid_mask,
            saved_activations[layer_number],
        )
        grad_mats[layer_number], grad_vecs[layer_number] = (
            lax.psum_scatter(
                jnp.concatenate(grad_matrix, 0), "fsdp", scatter_dimension=0, tiled=True
            ),
            lax.psum_scatter(grad_vector, "fsdp", scatter_dimension=1, tiled=True),
        )
    embed_grad, gain_pre, shift_pre = norm_backward(embedded, head_vec[0], residual_gradient)
    position_grad = jnp.sum(embed_grad.reshape(images, seq, width), 0)
    patch_grad = matmul_tn(flat_patches, embed_grad.astype(jnp.bfloat16))
    front_grad = jnp.concatenate(
        [
            patch_grad,
            grad_proj,
            position_grad,
            jnp.stack([gain_pre, shift_pre, gain_post, shift_post]),
        ],
        0,
    )
    front_shard = lax.psum_scatter(front_grad, "fsdp", scatter_dimension=1, tiled=True)
    mat_grad = jnp.stack(grad_mats)
    row_grad = jnp.concatenate([front_shard] + grad_vecs, 0)
    pairs = lax.axis_size("ns")
    side = lax.axis_index("ns")
    half_depth = width // pairs
    half_rows = row_grad.shape[0] // pairs
    mat_total, row_total = (
        lax.psum(mat_grad.astype(jnp.bfloat16), "ns").astype(jnp.float32),
        lax.psum(row_grad.astype(jnp.bfloat16), "ns").astype(jnp.float32),
    )
    mat_half = lax.dynamic_slice_in_dim(mat_total, side * half_depth, half_depth, 2)
    row_half = lax.dynamic_slice_in_dim(row_total, side * half_rows, half_rows, 0)
    squares = jnp.sum(mat_half * mat_half) + jnp.sum(row_half * row_half)
    grad_norm = jnp.sqrt(lax.psum(squares, ("fsdp", "ns")))
    clip = jnp.minimum(1.0, clip_bound / (grad_norm + 1e-06))
    momentum = momentum_decay * layer_momentum + clip * mat_total
    orth = newton_schulz(momentum)
    new_mats = layer_mats - muon_rate * (0.2 * math.sqrt(width) * orth + weight_decay * layer_mats)
    ema_mats = ema_decay * layer_ema + (1.0 - ema_decay) * new_mats
    mixed_mats = mix_share * new_mats + (1.0 - mix_share) * layer_zero
    return (loss_sum, weight_sum, grad_norm, new_mats, momentum, ema_mats, mixed_mats) + row_updates(
        clip * row_total, layers, row_params, row_zero, row_ema, row_first, row_second
    )


def fast_body(
    patches,
    pad_mask,
    labels,
    loss_weights,
    class_emb,
    layer_mats,
    layer_zero,
    layer_ema,
    layer_momentum,
    row_params,
    row_zero,
    row_ema,
    row_first,
    row_second,
):
    layers, columns, width = layer_mats.shape
    shards = lax.axis_size("fsdp")
    depth = shards // PLANE
    rows, share = row_params.shape
    lanes = -(-rows // 128) * 128
    valid_mask = pad_mask.astype(F32)
    sent_rows = jnp.pad(row_params.T.astype(BF), ((0, 0), (0, lanes - rows)))
    weights, *saved, embedded, vectors, pooled_row, z_rows, feature_rows, start, stats = forward(
        depth,
        sent_rows,
        layer_mats,
        patches[0],
        valid_mask,
        valid_mask.T,
        class_emb,
        labels[:, None],
        loss_weights.astype(F32)[:, None],
    )
    mat_total, clipped, totals = backward(
        depth,
        lax.axis_size("ns"),
        weights,
        saved,
        embedded,
        patches[0],
        vectors,
        valid_mask,
        valid_mask.T,
        (pooled_row, z_rows, feature_rows),
        start,
        stats,
    )
    loss_sum, weight_sum, grad_norm = (totals[0, turn] for turn in range(3))
    tables = [table.T for table in (row_params, row_zero, row_ema, row_first, row_second)]
    *news, bias, momentum, new_mats, ema_mats, mixed_mats = finish(
        totals, clipped, tables, mat_total, layer_momentum, layer_mats, layer_zero, layer_ema
    )
    news = [table.T for table in news] + [bias[:, :layers].T]
    return (loss_sum, weight_sum, grad_norm, new_mats, momentum, ema_mats, mixed_mats, *news)


def body(*args):
    count, share = args[5].shape[1], args[9].shape[1]
    planes = lax.axis_size("fsdp") == 4 * PLANE and lax.axis_size("ns") == 2
    if planes and count % 192 == 0 and share % 48 == 0 and args[0].shape[0] == 1:
        return fast_body(*args)
    return plain_body(*args)


def solution(mesh):
    in_specs = (
        P(("fsdp", "ns"), None, None),
        P(("fsdp", "ns"), None),
        P(("fsdp", "ns")),
        P(("fsdp", "ns")),
        P(),
        P(None, "fsdp", None),
        P(None, "fsdp", None),
        P(None, "fsdp", None),
        P(None, "fsdp", None),
        P(None, "fsdp"),
        P(None, "fsdp"),
        P(None, "fsdp"),
        P(None, "fsdp"),
        P(None, "fsdp"),
    )
    out_specs = (
        P(),
        P(),
        P(),
        P(None, "fsdp", None),
        P(None, "fsdp", None),
        P(None, "fsdp", None),
        P(None, "fsdp", None),
        P(None, "fsdp"),
        P(None, "fsdp"),
        P(None, "fsdp"),
        P(None, "fsdp"),
        P(None, "fsdp"),
        P(None, "fsdp"),
    )
    return jax.shard_map(body, mesh=mesh, in_specs=in_specs, out_specs=out_specs, check_vma=False)
```

```python
import functools
import math
from typing import NamedTuple

import jax
import jax.numpy as jnp
from jax import lax
from jax.experimental import pallas as pl
from jax.experimental.pallas import tpu as pltpu
from jax.sharding import PartitionSpec as P

HEADS = 12
HDIM = 64
PIX = 768
EMB = 512
SEQ = 256
NS_STEPS = 5
STEPS_DONE = 10


HIGHEST = lax.Precision.HIGHEST
norm_epsilon = 1e-05
unit_epsilon = 1e-06
logit_scale = 50.0
clip_bound = 0.001
momentum_decay = 0.95
muon_rate = 0.05
weight_decay = 0.05
adam_rate = 0.2
first_decay = 0.9
second_decay = 0.98
adam_floor = 1e-08
ema_decay = 0.9
mix_share = 0.5
coeff_linear = 3.4445
coeff_cubic = -4.775
coeff_quintic = 2.0315


def matmul(left, right):
    return jnp.dot(left, right, preferred_element_type=jnp.float32)


def matmul_nt(left, right):
    return lax.dot_general(
        left, right, (((1,), (1,)), ((), ())), preferred_element_type=jnp.float32
    )


def matmul_tn(left, right):
    return lax.dot_general(
        left, right, (((0,), (0,)), ((), ())), preferred_element_type=jnp.float32
    )


def norm_forward(inputs, gain, shift):
    center = inputs - jnp.mean(inputs, -1, keepdims=True)
    scale = lax.rsqrt(jnp.mean(center * center, -1, keepdims=True) + norm_epsilon)
    return center * scale * gain + shift


def norm_backward(inputs, gain, upstream):
    center = inputs - jnp.mean(inputs, -1, keepdims=True)
    scale = lax.rsqrt(jnp.mean(center * center, -1, keepdims=True) + norm_epsilon)
    normal = center * scale
    scaled_up = upstream * gain
    inner = scale * (
        scaled_up
        - jnp.mean(scaled_up, -1, keepdims=True)
        - normal * jnp.mean(scaled_up * normal, -1, keepdims=True)
    )
    return (inner, jnp.sum(upstream * normal, 0), jnp.sum(upstream, 0))


def attention_scores(parts, valid_mask):
    raw = jnp.einsum(
        "iqhd,ikhd->ihqk", parts[:, :, 0], parts[:, :, 1], preferred_element_type=jnp.float32
    )
    return jnp.where(valid_mask[:, None, None, :] > 0, raw * HDIM ** (-0.5), -1000000000.0)


BF = jnp.bfloat16
F32 = jnp.float32
MESH = pl.DeviceIdType.MESH
PLANE = 4


def guarded(pred, run):
    if pred is None:
        run()
    else:
        pl.when(pred)(run)


def both(first, second):
    if first is None:
        return second
    return first if second is None else jnp.logical_and(first, second)


def rows_at(start, count):
    return pl.ds(start if isinstance(start, int) else pl.multiple_of(start, 16), count)


class Links:
    def __init__(self, depth, send_sem, recv_sem):
        self.depth, self.send_sem, self.recv_sem = depth, send_sem, recv_sem
        self.me, self.x = lax.axis_index("fsdp"), lax.axis_index("ns")
        self.z, self.y, self.c = self.me // PLANE, lax.rem(self.me // 2, 2), lax.rem(self.me, 2)
        self.up = (self.at(self.z + 1, self.y, self.c), self.x)
        self.down = (self.at(self.z - 1, self.y, self.c), self.x)
        self.y_peer = (self.at(self.z, 1 - self.y, self.c), self.x)
        self.c_peer = (self.at(self.z, self.y, 1 - self.c), self.x)
        self.x_peer = (self.me, 1 - self.x)
        self.count, self.sent, self.waited = 0, [], set()

    def at(self, z, y, c):
        return PLANE * z + 2 * y + c

    def slot(self):
        self.count += 1
        return self.count - 1

    def greet(self):
        barrier = pltpu.get_barrier_semaphore()

        def signal(device):
            pl.semaphore_signal(barrier, inc=1, device_id=device, device_id_type=MESH)

        for device in (self.y_peer, self.x_peer, self.c_peer):
            signal(device)
        pl.when(self.z < self.depth - 1)(lambda: signal(self.up))
        pl.when(self.z > 0)(lambda: signal(self.down))
        inner = (self.z < self.depth - 1).astype(jnp.int32) + (self.z > 0).astype(jnp.int32)
        pl.semaphore_wait(barrier, 3 + inner)

    def copy(self, slot, source, target, device):
        return pltpu.make_async_remote_copy(
            src_ref=source,
            dst_ref=target,
            send_sem=self.send_sem.at[slot],
            recv_sem=self.recv_sem.at[slot],
            device_id=device,
            device_id_type=MESH,
        )

    def send(self, slot, source, target, device, pred=None):
        copy = self.copy(slot, source, target, device)
        guarded(pred, copy.start)
        self.sent.append((slot, pred, copy))

    def receive(self, slot, target, pred=None):
        guarded(pred, self.copy(slot, target, target, self.c_peer).wait_recv)

    def finish(self, slot=None):
        for number, pred, copy in self.sent:
            if number not in self.waited and (slot is None or number == slot):
                guarded(pred, copy.wait_send)
        if slot is not None:
            self.waited.add(slot)


def gather_item(links, own, target, count):
    depth, z, y, c, x = links.depth, links.z, links.y, links.c, links.x
    third = count // 3
    early = count // 9 // 16 * 16
    begin, amount = x * (third + early), 2 * third - early
    early_begin = amount - x * (third - early)
    origin = (0, 0)
    keys = [(side, far) for far in range(1, depth) for side in (-1, 1)]
    z_slot = {key: links.slot() for key in keys}
    y_slot = {key: links.slot() for key in keys + [origin]}
    e_slot = {(key, o): links.slot() for key in keys for o in (0, 1)}
    pair_slot = links.slot()
    x_slot = {(key, o): links.slot() for key in keys + [origin] for o in (0, 1)}
    c_slot = {(key, o): links.slot() for key in keys + [origin] for o in (0, 1)}

    def part(shard):
        return target(shard).at[rows_at(begin, amount)]

    def own_part():
        return own.at[rows_at(begin, amount)]

    def early_part(shard):
        return target(shard).at[rows_at(early_begin, early)]

    def third_of(shard, side):
        return target(shard).at[rows_at(side * 2 * third, third)]

    def shard(key, other, core=None):
        return links.at(z + key[0] * key[1], 1 - y if other else y, c if core is None else core)

    def exists(key):
        if key == origin:
            return None
        return z >= key[1] if key[0] < 0 else z + key[1] < depth

    def z_send(key):
        for side in (-1, 1) if key == origin else (key[0],):
            if key[1] + 1 < depth:
                source = own_part() if key == origin else part(shard(key, 0))
                links.send(
                    z_slot[(side, key[1] + 1)],
                    source,
                    part(shard(key, 0)),
                    links.up if side < 0 else links.down,
                    both(exists(key), z < depth - 1 if side < 0 else z > 0),
                )

    def e_send(key, other):
        for side in (-1, 1) if key == origin else (key[0],):
            if early and key[1] + 1 < depth:
                block = early_part(shard(key, other))
                mine = key == origin and other == 0
                links.send(
                    e_slot[((side, key[1] + 1), other)],
                    own.at[rows_at(early_begin, early)] if mine else block,
                    block,
                    links.up if side < 0 else links.down,
                    both(exists(key), z < depth - 1 if side < 0 else z > 0),
                )

    def e_receive(key, other):
        if early:
            links.receive(e_slot[(key, other)], early_part(shard(key, other)), exists(key))

    def y_send(key):
        source = own_part() if key == origin else part(shard(key, 0))
        links.send(y_slot[key], source, part(shard(key, 0)), links.y_peer, exists(key))

    def x_send(key, other):
        block = third_of(shard(key, other), x)
        links.send(x_slot[(key, other)], block, block, links.x_peer, exists(key))

    def c_send(key, other):
        whole = target(shard(key, other))
        source = own if (key, other) == (origin, 0) else whole
        links.send(c_slot[(key, other)], source, whole, links.c_peer, exists(key))

    order = []
    for far in range(1, depth):
        order += [((side, far), 0) for side in (-1, 1)]
        order += [(key, 1) for key in ([origin] if far == 1 else [(-1, far - 1), (1, far - 1)])]
    order += [((side, depth - 1), 1) for side in (-1, 1)]

    def start():
        if early:
            source = own.at[rows_at(early_begin, early)]
            links.send(pair_slot, source, early_part(shard(origin, 0)), links.y_peer)
        z_send(origin)
        e_send(origin, 0)
        y_send(origin)
        c_send(origin, 0)

    def cross(keys_now):
        for key in keys_now:
            links.receive(y_slot[key], part(shard(key, 1)), exists(key))
            x_send(key, 1)

    def step(far):
        if far == 1 and early:
            links.receive(pair_slot, early_part(shard(origin, 1)))
            e_send(origin, 1)
        for side in (-1, 1):
            key = (side, far)
            links.receive(z_slot[key], part(shard(key, 0)), exists(key))
            z_send(key)
            y_send(key)
            x_send(key, 0)
        cross([origin] if far == 1 else [(-1, far - 1), (1, far - 1)])
        for side in (-1, 1):
            for other in (0, 1):
                e_receive((side, far), other)
                e_send((side, far), other)
        if far == depth - 1:
            cross([(-1, far), (1, far)])

    def share():
        for key, other in order:
            links.receive(x_slot[(key, other)], third_of(shard(key, other), 1 - x), exists(key))
            c_send(key, other)

    def settle():
        for key, other in [(origin, 0)] + order:
            links.receive(c_slot[(key, other)], target(shard(key, other, 1 - c)), exists(key))

    return start, step, share, settle

def split(value):
    high = value.astype(BF)
    return high, (value - high.astype(F32)).astype(BF)


def forward_kernel(
    depth,
    halves,
    rows,
    mats,
    patches,
    mask,
    classes,
    label,
    weight,
    all_mats,
    resid,
    normed,
    project,
    log_total,
    context,
    mixed,
    normed_two,
    embedded,
    vectors,
    pooled_row,
    z_rows,
    feature_rows,
    vector_start,
    stats,
    row_own,
    tail_v,
    rows_v,
    mats_v,
    own_v,
    resid_v,
    normed_v,
    project_v,
    log_v,
    context_v,
    mixed_v,
    two_v,
    embed_v,
    weight_v,
    total_v,
    class_v,
    send_sem,
    recv_sem,
    local_sem,
    weight_sem,
    save_sem,
):
    links = Links(depth, send_sem, recv_sem)
    layers, count, width = mats.shape
    size = count // halves
    whole = rows.shape[1] // 128 * 128
    tail_v[...] = jnp.zeros_like(tail_v)
    tail_v[:, pl.ds(0, rows.shape[1] - whole)] = rows[:, pl.ds(whole, rows.shape[1] - whole)]
    row_own[:, pl.ds(0, whole)] = rows[:, pl.ds(0, whole)].astype(BF)
    row_own[:, pl.ds(whole, 128)] = tail_v[...].astype(BF)
    rows_v[pl.ds(links.me, 1)] = row_own[...][None]
    items = [gather_item(links, row_own, lambda shard: rows_v.at[shard], rows.shape[0])]
    keep = mask[...].astype(F32)
    own, loads = [], []
    for layer in range(layers):
        loads.append(pltpu.make_async_copy(mats.at[layer], mats_v, local_sem.at[0]))
        own.append(
            pltpu.make_async_copy(
                own_v.at[layer],
                all_mats.at[layer, rows_at(links.me * count, count)],
                local_sem.at[1 + layer],
            )
        )
        for half in range(halves):

            def target(shard, layer=layer, half=half):
                return all_mats.at[layer, rows_at(shard * count + half * size, size)]

            block = own_v.at[layer, pl.ds(half * size, size)]
            items.append(gather_item(links, block, target, size))
    saves = []

    def take(layer):
        loads[layer].wait()
        own_v[layer] = mats_v[...].astype(BF)
        own[layer].start()
        if layer + 1 < layers:
            loads[layer + 1].start()

    loads[0].start()
    links.greet()

    def save(source, target):
        copy = pltpu.make_async_copy(source, target, save_sem.at[len(saves)])
        copy.start()
        saves.append(copy)

    def table(begin, amount):
        return rows_v[:, :, pl.ds(begin, amount)].reshape(width, amount)

    pixels, seq = patches.shape[1], patches.shape[0]

    def column(index):
        return vectors[pl.ds(index, 1), :]

    def embed():
        vectors[...] = table(pixels + EMB + SEQ, 128).astype(F32).T
        position = table(pixels + EMB, SEQ).astype(F32).T
        embed_v[...] = matmul_nt(patches[...], table(0, pixels)) + position
        save(embed_v, embedded)
        resid_v[0] = norm_forward(embed_v[...], column(0), column(1))

    order = []
    for layer in range(layers):
        order += [(layer, index) for index in (0, 1, 2, 3, 4, 8, 5, 9, 6, 10, 7, 11)]

    def chunk_copy(number):
        layer, index = order[number]
        return pltpu.make_async_copy(
            all_mats.at[layer, pl.ds(index * width, width)],
            weight_v.at[number % 4],
            weight_sem.at[number % 4],
        )

    def chunk(number):
        chunk_copy(number).wait()
        return weight_v[number % 4]

    half_lane = lax.broadcasted_iota(jnp.int32, (1, 128), 1) < HDIM
    scale = HDIM ** (-0.5)

    def attention_pair(layer, pair):
        def lanes(base):
            return pl.ds(pl.multiple_of(base + pair * 128, 128), 128)

        query, key = project_v[layer, :, lanes(0)], project_v[layer, :, lanes(width)]
        value = project_v[layer, :, lanes(2 * width)]
        results = []
        kept = log_v[layer]
        lane = lax.broadcasted_iota(jnp.int32, kept.shape, 1)
        for head in range(2):
            here = half_lane if head == 0 else jnp.logical_not(half_lane)
            query_h = jnp.where(here, query, jnp.zeros_like(query))
            scores = jnp.where(keep > 0, matmul_nt(query_h, key) * scale, -1000000000.0)
            top = jnp.max(scores, -1, keepdims=True)
            expo = jnp.exp(scores - top)
            total = jnp.sum(expo, -1, keepdims=True)
            kept = jnp.where(lane == 2 * pair + head, top + jnp.log(total), kept)
            results.append(matmul((expo / total).astype(BF), value))
        log_v[layer] = kept
        context_v[layer, :, lanes(0)] = jnp.where(half_lane, results[0], results[1]).astype(BF)

    def layer_steps(layer):
        base, first = 4 + 12 * layer, 12 * layer

        def vector(index):
            return column(base + index)

        for number in range(first, first + 4):
            chunk_copy(number).start()
        log_v[layer] = jnp.zeros_like(log_v[layer])
        save(resid_v.at[layer], resid.at[layer])
        normed_v[layer] = norm_forward(resid_v[layer], vector(0), vector(1)).astype(BF)
        save(normed_v.at[layer], normed.at[layer])
        for part in range(3):
            result = matmul_nt(normed_v[layer], chunk(first + part))
            if part != 1:
                result += vector(2 if part == 0 else 3)
            project_v[layer, :, pl.ds(part * width, width)] = result.astype(BF)
            chunk_copy(first + 4 + part).start()
        save(project_v.at[layer], project.at[layer])
        yield
        for third in range(3):

            @pl.loop(0, 2)
            def _(turn, third=third):
                attention_pair(layer, 2 * third + turn)

            yield
        save(context_v.at[layer], context.at[layer])
        save(log_v.at[layer], log_total.at[layer])
        mixed_v[layer] = resid_v[layer] + (
            matmul_nt(context_v[layer], chunk(first + 3)) + vector(4)
        )
        chunk_copy(first + 7).start()
        save(mixed_v.at[layer], mixed.at[layer])
        two_v[layer] = norm_forward(mixed_v[layer], vector(5), vector(6)).astype(BF)
        save(two_v.at[layer], normed_two.at[layer])
        yield
        total_v[...] = mixed_v[layer] + vector(7)
        for part in range(4):
            number = first + 4 + 2 * part
            pre = matmul_nt(two_v[layer], chunk(number)) + vector(8 + part)
            hidden = (pre * jax.nn.sigmoid(1.702 * pre)).astype(BF)
            total_v[...] += matmul(hidden, chunk(number + 1))
            for ahead in (number + 4, number + 5):
                if ahead < first + 12:
                    chunk_copy(ahead).start()
            if part < 3:
                yield
        resid_v[layer + 1] = total_v[...]
        yield

    def class_units():
        value = classes[...].astype(F32)
        length = lax.rsqrt(jnp.sum(value * value, -1, keepdims=True) + unit_epsilon)
        class_v[...] = (value * length).astype(BF)

    def head():
        number = jnp.sum(keep, -1, keepdims=True)
        keep_column = jnp.broadcast_to(keep, (8, seq)).T[:, :1]
        pooled = jnp.sum(resid_v[layers] * keep_column, 0, keepdims=True) / number
        center = pooled - jnp.mean(pooled, -1, keepdims=True)
        spread = lax.rsqrt(jnp.mean(center * center, -1, keepdims=True) + norm_epsilon)
        normal = center * spread
        z_value = jnp.broadcast_to(normal * column(2) + column(3), (16, width)).astype(BF)
        proj = table(pixels, EMB)
        feature = matmul(z_value, proj)
        inverse = lax.rsqrt(jnp.sum(feature * feature, -1, keepdims=True) + unit_epsilon)
        unit = (feature * inverse).astype(BF)
        logits = logit_scale * matmul_nt(unit, class_v[...])
        lane = lax.broadcasted_iota(jnp.int32, logits.shape, 1)
        top = jnp.max(logits, -1, keepdims=True)
        shifted = jnp.exp(logits - top)
        total = jnp.sum(shifted, -1, keepdims=True)
        chosen = lane == label[...]
        loss = top + jnp.log(total) - jnp.sum(jnp.where(chosen, logits, 0.0), -1, keepdims=True)
        logit_grad = weight[...] * (shifted / total - chosen.astype(F32))
        high, low = split(logit_grad)
        unit_grad = logit_scale * (matmul(high, class_v[...]) + matmul(low, class_v[...]))
        feature_grad = inverse * unit_grad - feature * inverse**3 * jnp.sum(
            unit_grad * feature, -1, keepdims=True
        )
        high, low = split(feature_grad)
        z_grad = (matmul_nt(high, proj) + matmul_nt(low, proj))[:1]
        scaled = z_grad * column(2)
        inner = spread * (
            scaled
            - jnp.mean(scaled, -1, keepdims=True)
            - normal * jnp.mean(scaled * normal, -1, keepdims=True)
        )
        pooled_row[...] = jnp.broadcast_to(inner / number, pooled_row.shape)
        spot = lax.broadcasted_iota(jnp.int32, (16, 1), 0)
        z_rows[...] = jnp.where(spot < 2, z_value, jnp.zeros_like(z_value))
        picked = jnp.where(spot == 0, high, jnp.where(spot == 1, low, jnp.zeros_like(low)))
        feature_rows[...] = picked
        vector_start[...] = jnp.zeros_like(vector_start)
        vector_start[pl.ds(2, 1), :] = z_grad * normal
        vector_start[pl.ds(3, 1), :] = z_grad
        here = lax.broadcasted_iota(jnp.int32, (8, 128), 1)
        first = lax.broadcasted_iota(jnp.int32, (8, 128), 0) == 0
        value = jnp.where(first & (here == 1), (loss * weight[...])[:8], 0.0)
        stats[...] = jnp.where(first & (here == 2), jnp.broadcast_to(weight[...], (8, 128)), value)

    running = None

    def work(amount):
        nonlocal running
        for _ in range(amount):
            if running is None:
                return
            if next(running, 0) == 0:
                running = None

    items[0][0]()
    take(0)
    class_units()
    for number, (_, step, _, _) in enumerate(items):
        step(1)
        work(1)
        step(2)
        if number + 1 < len(items):
            if number > 0 and number % halves == 0:
                take(number // halves)
            items[number + 1][0]()
        work(1)
        if number > 0:
            items[number - 1][2]()
        work(1)
        for far in range(3, depth):
            step(far)
        work(1)
        if number > 0:
            items[number - 1][3]()
            if number == 1:
                embed()
            for layer in range(layers - 1):
                if number - 1 == halves * (layer + 1):
                    own[layer].wait()
                    work(1000)
                    running = counted(layer_steps(layer))
        work(1)
    items[-1][2]()
    work(2)
    items[-1][3]()
    work(1000)
    own[layers - 1].wait()
    for _ in layer_steps(layers - 1):
        pass
    head()
    links.finish()
    for copy in saves:
        copy.wait()


def counted(steps):
    for _ in steps:
        yield 1


def forward(depth, rows, mats, patches, mask, classes, label, weight):
    layers, count, width = mats.shape
    lanes = (rows.shape[1] // 128 + 1) * 128
    shards = PLANE * depth
    halves = 2
    seq = patches.shape[0]
    slots = (1 + layers * halves) * 60
    any_space = pl.BlockSpec(memory_space=pl.ANY)
    vmem = pl.BlockSpec(memory_space=pltpu.VMEM)

    def shape(*sizes, dtype=F32):
        return jax.ShapeDtypeStruct(sizes, dtype)

    saved = (
        shape(layers, seq, width),
        shape(layers, seq, width, dtype=BF),
        shape(layers, seq, 3 * width, dtype=BF),
        shape(layers, seq, 128),
        shape(layers, seq, width, dtype=BF),
        shape(layers, seq, width),
        shape(layers, seq, width, dtype=BF),
    )
    return pl.pallas_call(
        functools.partial(forward_kernel, depth, halves),
        out_shape=(shape(layers, shards * count, width, dtype=BF),)
        + saved
        + (
            shape(seq, width),
            shape(128, width),
            shape(8, width),
            shape(16, width, dtype=BF),
            shape(16, EMB, dtype=BF),
            shape(128, width),
            shape(8, 128),
        ),
        in_specs=[vmem, any_space] + [vmem] * 5,
        out_specs=[any_space] * 9 + [vmem] * 6,
        scratch_shapes=[
            pltpu.VMEM((rows.shape[0], lanes), BF),
            pltpu.VMEM((rows.shape[0], 128), F32),
            pltpu.VMEM((shards, rows.shape[0], lanes), BF),
            pltpu.VMEM(mats.shape[1:], F32),
            pltpu.VMEM(mats.shape, BF),
            pltpu.VMEM((layers + 1, seq, width), F32),
        ]
        + [pltpu.VMEM(array.shape, array.dtype) for array in saved[1:]]
        + [
            pltpu.VMEM((seq, width), F32),
            pltpu.VMEM((4, width, width), BF),
            pltpu.VMEM((seq, width), F32),
            pltpu.VMEM(classes.shape, BF),
            pltpu.SemaphoreType.DMA((slots,)),
            pltpu.SemaphoreType.DMA((slots,)),
            pltpu.SemaphoreType.DMA((1 + layers,)),
            pltpu.SemaphoreType.DMA((4,)),
            pltpu.SemaphoreType.DMA((1 + 7 * layers,)),
        ],
        name="gather_and_forward",
        compiler_params=pltpu.CompilerParams(
            collective_id=1, has_side_effects=True, vmem_limit_bytes=56 * 1024 * 1024
        ),
    )(rows, mats, patches, mask, classes, label, weight)


def accumulate(target, start, source, begin, count, step):
    @pl.loop(0, count // step)
    def _(turn):
        here = rows_at(start + turn * step, step)
        there = rows_at(begin + turn * step, step)
        target[here, :] = (target[here, :].astype(F32) + source[there, :].astype(F32)).astype(BF)


class Group(NamedTuple):
    begin: object
    stages: list
    core_slot: list


def scatter_group(links, dest, load, sizes, bufs, emit, used=None):
    depth, z, y, c, x = links.depth, links.z, links.y, links.c, links.x
    n, p, q, step = sizes
    mine, core_in, x_in, y_in, z_in, z_last, final = bufs
    core_slot, x_slot = [links.slot(), links.slot()], [links.slot(), links.slot()]
    q_slot, p_slot, low_slot, high_slot, last_slot = (links.slot() for _ in range(5))
    m = p + q
    first = x * p
    own_p, peer_p = x * m, (1 - x) * m
    sides = ((0, 1 - y), (1, y))

    def begin():
        for i, side in sides:
            load(i, side, mine.at[side], core_in.at[side], core_slot[i])

    def stage_core():
        for i, side in sides:
            load(i, side, mine.at[side], None, None)
            links.receive(core_slot[i], core_in.at[side])
            accumulate(mine.at[side], 0, core_in.at[side], 0, n, step)
            links.send(x_slot[i], mine.at[side, rows_at(peer_p, p)], x_in.at[side], links.x_peer)
            if i == 0:
                links.send(q_slot, mine.at[side, pl.ds(p, q)], y_in.at[pl.ds(0, q)], links.y_peer)
        if used is not None:
            used()

    def stage_x():
        for i, side in sides:
            links.receive(x_slot[i], x_in.at[side])
            accumulate(mine.at[side], own_p, x_in.at[side], 0, p, step)
            if i == 0:
                links.send(
                    p_slot, mine.at[side, rows_at(own_p, p)], y_in.at[pl.ds(q, p)], links.y_peer
                )
        links.receive(q_slot, y_in.at[pl.ds(0, q)])
        accumulate(mine.at[y], p, y_in, 0, q, step)

    def stage_y():
        links.receive(p_slot, y_in.at[pl.ds(q, p)])
        accumulate(mine.at[y], own_p, y_in, q, p, step)

    def stage_z(hop):
        block = mine.at[y, rows_at(first, m)]

        def take(slot, source, pred):
            @pl.when(pred)
            def _():
                links.receive(slot, source)
                accumulate(mine.at[y], first, source, 0, m, step)

        if dest > 0:
            if 1 <= hop <= dest:
                take(low_slot, z_in, z == hop)
            if hop < dest:
                links.send(low_slot, block, z_in, links.up, z == hop)
        if dest < depth - 1:
            turn = depth - 1 - hop
            if hop >= 1 and turn > dest:
                take(high_slot, z_in, z == turn)
            if turn > dest + 1:
                links.send(high_slot, block, z_in, links.down, z == turn)
            if turn == dest + 1:
                links.send(high_slot, block, z_last, links.down, z == turn)
            if turn == dest and hop >= 1:
                take(high_slot, z_last, z == dest)
        if hop == max(dest, depth - 1 - dest):
            links.send(last_slot, block, final, links.x_peer, z == dest)

    def stage_last():
        links.finish(x_slot[1])
        links.finish(last_slot)

        @pl.when(z == dest)
        def _():
            links.receive(last_slot, final)
            accumulate(mine.at[y], p, final, jnp.where(x == 0, 0, p), q, step)

            @pl.loop(0, p // 16)
            def _(turn):
                there = rows_at(jnp.where(x == 0, q, 0) + turn * 16, 16)
                mine[y, rows_at(peer_p + turn * 16, 16), :] = final[there, :]

            emit(mine.at[y])

    hops = [functools.partial(stage_z, hop) for hop in range(depth)]
    return Group(begin, [stage_core, stage_x, stage_y] + hops + [stage_last], core_slot)

def norm_back(value, gain, upstream):
    center = value - jnp.mean(value, -1, keepdims=True)
    scale = lax.rsqrt(jnp.mean(center * center, -1, keepdims=True) + norm_epsilon)
    normal = center * scale
    scaled = upstream * gain
    inner = scale * (
        scaled
        - jnp.mean(scaled, -1, keepdims=True)
        - normal * jnp.mean(scaled * normal, -1, keepdims=True)
    )
    return (
        inner,
        jnp.sum(upstream * normal, 0, keepdims=True),
        jnp.sum(upstream, 0, keepdims=True),
    )


VMEM_LIMIT = 62 * 1024 * 1024
SUB = 3
IN_FLIGHT = 2 * SUB
LAGS = (1, 3, 5, 7, 9, 11, 13, 15)


def backward_kernel(
    depth,
    sides,
    layers,
    weights,
    resid,
    normed,
    project,
    log_total,
    context,
    mixed,
    normed_two,
    embedded,
    patches,
    vectors,
    mask,
    pooled_row,
    z_rows,
    feature_rows,
    vector_start,
    stats,
    out,
    clipped,
    totals,
    row_out,
    blocks_v,
    core_in,
    x_in,
    y_in,
    z_in,
    z_last,
    final,
    rows_v,
    row_mine,
    row_core,
    row_x,
    row_y,
    row_z,
    row_z_last,
    row_final,
    resid_v,
    normed_v,
    project_v,
    log_v,
    context_v,
    mixed_v,
    two_v,
    weight_v,
    patch_v,
    hidden_v,
    pre_v,
    up_v,
    short_v,
    total_v,
    context_grad_v,
    vector_v,
    note,
    inbox,
    send_sem,
    recv_sem,
    local_sem,
    weight_sem,
    load_sem,
    mail_send,
    mail_recv,
    free_sem,
):
    links = Links(depth, send_sem, recv_sem)
    y, c, z = links.y, links.c, links.z
    me = links.me * sides + links.x
    everyone = PLANE * depth * sides
    width = up_v.shape[1]
    count = out.shape[1]
    n = count // SUB
    p = n // 4 // 16 * 16
    per_layer = depth * SUB
    own = 2 * layers * per_layer
    piece = 2 * n

    saved = (
        (normed_two, two_v),
        (mixed, mixed_v),
        (context, context_v),
        (resid, resid_v),
        (normed, normed_v),
        (project, project_v),
        (log_total, log_v),
    )

    def load(layer, which):
        source, target = saved[which]
        return pltpu.make_async_copy(source.at[layer], target, load_sem.at[which])

    chunks = []
    for layer in reversed(range(layers)):
        for turn in (3, 2, 1, 0):
            chunks += [(layer, 8 + turn), (layer, 4 + turn)]
        chunks += [(layer, 3), (layer, 0), (layer, 1), (layer, 2)]

    def chunk_copy(number):
        layer, index = chunks[number]
        return pltpu.make_async_copy(
            weights.at[layer, pl.ds(index * width, width)],
            weight_v.at[number % 4],
            weight_sem.at[number % 4],
        )

    def chunk(number):
        chunk_copy(number).wait()
        return weight_v[number % 4]

    def refill(*numbers):
        for number in numbers:
            if number < len(chunks):
                chunk_copy(number).start()

    for which in range(len(saved)):
        load(layers - 1, which).start()
    refill(0, 1, 2, 3)
    patch_load = pltpu.make_async_copy(patches, patch_v, load_sem.at[7])
    patch_load.start()

    def others(run):
        for number in range(everyone):
            pl.when(me != number)(functools.partial(run, number))

    def place(number):
        return (number // sides, number % sides)

    barrier = pltpu.get_barrier_semaphore()
    others(
        lambda number: pl.semaphore_signal(
            barrier, inc=1, device_id=place(number), device_id_type=MESH
        )
    )
    note[...] = stats[...]
    vector_v[...] = vector_start[...]
    keep = mask[...].astype(F32)
    keep_column = jnp.broadcast_to(keep, (8, keep.shape[1])).T[:, :1]
    up_v[...] = keep_column * pooled_row[pl.ds(0, 1), :]
    lane = lax.broadcasted_iota(jnp.int32, (8, 128), 1)
    first = lax.broadcasted_iota(jnp.int32, (8, 128), 0) == 0

    def add_squares(block):
        value = block.astype(F32)
        note[...] += jnp.where(first & (lane == 0), jnp.sum(value * value), 0.0)

    groups, closers = [], []
    starts, members = {}, {}

    def add_group(dest, send_out, take_in, sizes, bufs, emit, used=None):
        def load_block(i, side, mine, target, slot):
            if target is None:
                take_in(i, side, mine)
            else:
                send_out(i, side, mine, target, slot)

        groups.append(scatter_group(links, dest, load_block, sizes, bufs, emit, used))

    total_blocks = layers * per_layer
    for order, layer in enumerate(reversed(range(layers))):
        for turn, dest in enumerate(reversed(range(depth))):
            for part in range(SUB):
                number, spot = (order * depth + turn) * SUB + part, layer * SUB + part
                starts[(layer, dest, part)] = number
                pieces = 2 if number >= total_blocks - SUB else 1
                size = n // pieces
                edge = (size // 4 + 15) // 16 * 16
                middle = size - edge
                members[number] = []
                for half in range(pieces):
                    members[number].append(len(groups))
                    inside = pl.ds(half * size, size)
                    window = pl.ds(half * middle, middle)

                    def send_out(i, side, mine, target, slot, part=part, inside=inside):
                        source = blocks_v.at[own + 2 * part + side, inside]
                        links.send(slot, source, target, links.c_peer)

                    def write(source, layer=layer, at=part * n + half * size, size=size, sem=spot + half * (layers * SUB + 2 * depth)):
                        target = out.at[layer, pl.ds(at, size)]
                        return pltpu.make_async_copy(source, target, local_sem.at[sem])

                    def emit(result, write=write):
                        add_squares(result[...])
                        write(result).start()

                    closers.append((dest, write, blocks_v.at[2 * number, inside]))

                    def used(number=number):
                        if number < total_blocks - IN_FLIGHT:
                            pl.semaphore_signal(
                                free_sem, inc=1, device_id=links.c_peer, device_id_type=MESH
                            )

                    add_group(
                        dest,
                        send_out,
                        lambda i, side, mine: None,
                        (size, edge, size - 2 * edge, 48 if pieces == 1 else 32),
                        [
                            blocks_v.at[pl.ds(2 * number, 2), inside],
                            core_in.at[number % IN_FLIGHT, :, inside],
                            x_in.at[number if half == 0 else total_blocks + part, :, pl.ds(0, edge)],
                            y_in.at[number, window],
                            z_in.at[number, window],
                            z_last.at[spot, window],
                            final.at[spot, window],
                        ],
                        emit,
                        used,
                    )
    first_row_group = len(groups)
    rows = row_out.shape[0]
    for dest in reversed(range(depth)):
        number = len(groups)

        def row_copy(i, side, mine, dest=dest):
            sem = local_sem.at[layers * SUB + 2 * dest + i]
            return pltpu.make_async_copy(rows_v.at[links.at(dest, side, c)], mine, sem)

        def row_send(i, side, mine, target, slot, dest=dest, row_copy=row_copy):
            row_copy(i, side, mine).start()
            source = rows_v.at[links.at(dest, side, 1 - c)]
            links.send(slot, source, target, links.c_peer)

        def row_emit(result, dest=dest):
            add_squares(result[...])
            row_out[...] = result[...]

        add_group(
            dest,
            row_send,
            lambda i, side, mine, row_copy=row_copy: row_copy(i, side, mine).wait(),
            (rows, 16, rows - 32, 16),
            [ref.at[dest] for ref in (row_mine, row_core, row_x, row_y, row_z)]
            + [row_z_last, row_final],
            row_emit,
        )

    def release(layer, dest):
        begun = 0
        for part in range(SUB):
            number = starts[(layer, dest, part)]
            if number >= IN_FLIGHT:
                pl.semaphore_wait(free_sem, 1)
            for index in members[number]:
                groups[index].begin()
                begun += 1
        return begun

    def recycle(layer, dest):
        for part in range(SUB):
            number = starts[(layer, dest, part)]
            if number >= SUB:
                for index in members[number - SUB]:
                    for slot in groups[index].core_slot:
                        links.finish(slot)

    last_turn = [0]

    def advance():
        turn = last_turn[0]
        for stage, lag in enumerate(LAGS):
            if 0 <= turn - lag < len(groups):
                groups[turn - lag].stages[stage]()
        last_turn[0] += 1

    def grad_pieces(layer, dest, left, column, amount, right, begin):
        number = starts[(layer, dest, 0)]
        ring = own

        @pl.loop(0, amount)
        def _(turn):
            columns = pl.ds(pl.multiple_of(column + turn * piece, 128), piece)
            result = matmul_tn(left[:, columns], right[...])
            for half in range(2):
                block = 2 * (begin + turn) + half
                shard = block // SUB
                part = lax.rem(block, SUB)
                side, core = shard // 2, lax.rem(shard, 2)
                index = jnp.where(
                    core == c, 2 * (number + part) + side, ring + 2 * part + side
                )
                blocks_v[index] = result[half * n : (half + 1) * n].astype(BF)

    half_lane = lax.broadcasted_iota(jnp.int32, (1, 128), 1) < HDIM
    scale = HDIM ** (-0.5)

    def attention_pair(pair):
        def lanes(base):
            return pl.ds(pl.multiple_of(base + pair * 128, 128), 128)

        query, key = project_v[:, lanes(0)], project_v[:, lanes(width)]
        value, grad = project_v[:, lanes(2 * width)], context_grad_v[:, lanes(0)]
        totals_now = log_v[...]
        column = lax.broadcasted_iota(jnp.int32, totals_now.shape, 1)
        query_grad = key_grad = value_grad = 0.0
        zero = jnp.zeros_like(query)
        for head in range(2):
            here = half_lane if head == 0 else jnp.logical_not(half_lane)
            query_h, key_h = jnp.where(here, query, zero), jnp.where(here, key, zero)
            grad_h = jnp.where(here, grad, zero)
            total = jnp.sum(
                jnp.where(column == 2 * pair + head, totals_now, 0.0), -1, keepdims=True
            )
            scores = jnp.where(keep > 0, matmul_nt(query_h, key) * scale, -1000000000.0)
            probs = jnp.exp(scores - total)
            prob_grad = matmul_nt(grad_h, value)
            value_grad += matmul_tn(probs.astype(BF), grad_h)
            score_grad = (
                probs * (prob_grad - jnp.sum(prob_grad * probs, -1, keepdims=True))
            ).astype(BF)
            query_grad += matmul(score_grad, key_h)
            key_grad += matmul_tn(score_grad, query_h)
        pre_v[:, lanes(0)] = (query_grad * scale).astype(BF)
        pre_v[:, lanes(width)] = (key_grad * scale).astype(BF)
        pre_v[:, lanes(2 * width)] = value_grad.astype(BF)

    def layer_steps(order, layer):
        base = 4 + 12 * layer
        chunk0 = 12 * order

        def vector(index):
            return vectors[pl.ds(base + index, 1), :]

        def put(index, value):
            vector_v[pl.ds(base + index, 1), :] = value

        def column_sum(value):
            return jnp.sum(value.astype(F32), 0, keepdims=True)

        load(layer, 0).wait()
        short_v[...] = up_v[...].astype(BF)
        put(7, column_sum(short_v[...]))
        total_v[...] = jnp.zeros_like(total_v)
        recycle(layer, 3)
        for turn, part in enumerate((3, 2, 1, 0)):
            number = chunk0 + 2 * turn
            down, up = chunk(number), chunk(number + 1)
            pre = matmul_nt(two_v[...], up) + vector(8 + part)
            gate = jax.nn.sigmoid(1.702 * pre)
            hidden_v[...] = (pre * gate).astype(BF)
            slope = gate + 1.702 * pre * gate * (1.0 - gate)
            pre_grad = (matmul_nt(short_v[...], down) * slope).astype(BF)
            pre_v[:, pl.ds(part * width, width)] = pre_grad
            put(8 + part, column_sum(pre_grad))
            total_v[...] += matmul(pre_grad, up)
            refill(number + 4, number + 5)
            yield None
            if part == 0:
                recycle(layer, 2)
            if part > 0:
                grad_pieces(layer, 3, hidden_v, 0, 2, short_v, 2 * (part - 1))
            else:
                grad_pieces(layer, 2, hidden_v, 0, 2, short_v, 4)
            if part == 1:
                begun = release(layer, 3)
                yield begun
            else:
                yield None
        grad_pieces(layer, 2, pre_v, 2 * width, 2, two_v, 0)
        yield None
        grad_pieces(layer, 2, pre_v, 3 * width, 2, two_v, 2)
        begun = release(layer, 2)
        yield begun
        load(layer, 1).wait()
        inner, gain, shift = norm_back(mixed_v[...], vector(5), total_v[...])
        put(5, gain)
        put(6, shift)
        up_v[...] += inner
        short_v[...] = up_v[...].astype(BF)
        put(4, column_sum(short_v[...]))
        yield None
        load(layer, 2).wait()
        recycle(layer, 1)
        grad_pieces(layer, 1, short_v, 0, 2, context_v, 0)
        context_grad_v[...] = matmul(short_v[...], chunk(chunk0 + 8)).astype(BF)
        refill(chunk0 + 12)
        yield None
        grad_pieces(layer, 1, pre_v, 0, 2, two_v, 2)
        yield None
        grad_pieces(layer, 1, pre_v, width, 2, two_v, 4)
        begun = release(layer, 1)
        if layer > 0:
            for which in range(3):
                load(layer - 1, which).start()
        else:
            embed_load.start()
        yield begun
        load(layer, 5).wait()
        load(layer, 6).wait()
        for third in range(3):

            @pl.loop(0, 2)
            def _(turn, third=third):
                attention_pair(2 * third + turn)

            yield None
        load(layer, 4).wait()
        recycle(layer, 0)
        put(2, column_sum(pre_v[:, pl.ds(0, width)]))
        put(3, column_sum(pre_v[:, pl.ds(2 * width, width)]))
        for third in range(3):
            grad_pieces(layer, 0, pre_v, third * width, 2, normed_v, 2 * third)
            if third < 2:
                yield None
        begun = release(layer, 0)
        yield begun
        load(layer, 3).wait()
        back = matmul(pre_v[:, pl.ds(0, width)], chunk(chunk0 + 9))
        back += matmul(pre_v[:, pl.ds(width, width)], chunk(chunk0 + 10))
        back += matmul(pre_v[:, pl.ds(2 * width, width)], chunk(chunk0 + 11))
        refill(chunk0 + 13, chunk0 + 14, chunk0 + 15)
        inner, gain, shift = norm_back(resid_v[...], vector(0), back)
        put(0, gain)
        put(1, shift)
        up_v[...] += inner
        if layer > 0:
            for which in range(3, len(saved)):
                load(layer - 1, which).start()
        yield None

    embed_load = pltpu.make_async_copy(embedded, mixed_v, load_sem.at[8])
    pl.semaphore_wait(barrier, everyone - 1)
    pending = 0
    for order, layer in enumerate(reversed(range(layers))):
        for ready in layer_steps(order, layer):
            if ready is not None:
                pending += ready
            if pending > 0:
                advance()
                pending -= 1
    embed_load.wait()
    inner, gain, shift = norm_back(mixed_v[...], vectors[pl.ds(0, 1), :], up_v[...])
    vector_v[pl.ds(0, 1), :] = gain
    vector_v[pl.ds(1, 1), :] = shift
    short_v[...] = inner.astype(BF)
    total_v[...] = inner
    patch_load.wait()
    pixels, embeds, seq = patch_v.shape[1], feature_rows.shape[1], inner.shape[0]
    for turn in range(width // piece):
        columns = pl.ds(turn * piece, piece)
        patch_grad = matmul_tn(short_v[:, columns], patch_v[...])
        proj_grad = matmul_tn(z_rows[:, columns], feature_rows[...])
        position = total_v[:, columns].T
        vector_grad = vector_v[:, columns].T
        for part in range(piece // rows):
            shard, inside = turn * (piece // rows) + part, slice(part * rows, (part + 1) * rows)
            rows_v[shard, :, pl.ds(0, pixels)] = patch_grad[inside].astype(BF)
            rows_v[shard, :, pl.ds(pixels, embeds)] = proj_grad[inside].astype(BF)
            rows_v[shard, :, pl.ds(pixels + embeds, seq)] = position[inside].astype(BF)
            rows_v[shard, :, pl.ds(pixels + embeds + seq, 128)] = vector_grad[inside].astype(BF)
    for number in range(first_row_group, len(groups)):
        groups[number].begin()
    while last_turn[0] < len(groups) + max(LAGS):
        advance()

    def mail(number, slot):
        return pltpu.make_async_remote_copy(
            src_ref=note,
            dst_ref=inbox.at[slot],
            send_sem=mail_send.at[number],
            recv_sem=mail_recv.at[slot],
            device_id=place(number),
            device_id_type=MESH,
        )

    others(lambda number: mail(number, me).start())
    inbox[pl.ds(me, 1)] = note[...][None]
    links.finish()
    for dest, write, source in closers:
        pl.when(z == dest)(lambda write=write, source=source: write(source).wait())
    others(lambda number: mail(number, number).wait_recv())
    summed = jnp.sum(inbox[...], 0)
    others(lambda number: mail(number, me).wait_send())

    def pick(index):
        return jnp.sum(jnp.where(first & (lane == index), summed, 0.0))

    loss_sum, weight_sum = pick(1), pick(2)
    norm = jnp.sqrt(jnp.full((8, 128), pick(0) / sides)) / weight_sum
    clip = jnp.minimum(1.0, clip_bound / (norm + 1e-06)) / weight_sum
    totals[...] = jnp.where(
        lane == 0,
        loss_sum,
        jnp.where(lane == 1, weight_sum, jnp.where(lane == 2, norm, clip)),
    )
    clipped[...] = row_out[...].astype(F32) * clip[:1, :1]


def backward(
    depth, sides, weights, saved, embedded, patches, vectors, mask, head, start, stats
):
    layers, rows_all, width = weights.shape
    seq, pixels = patches.shape
    shards = PLANE * depth
    count, rows = rows_all // shards, width // shards
    lanes = -(-(pixels + EMB + SEQ + 4 + 12 * layers) // 128) * 128
    n = count // SUB
    p = n // 4 // 16 * 16
    m = n - p
    per_layer = depth * SUB
    blocks = layers * per_layer
    row_m = rows - 16
    everyone = shards * sides

    def room(*shape, dtype=BF):
        return pltpu.VMEM(shape, dtype)

    any_space = pl.BlockSpec(memory_space=pl.ANY)
    vmem = pl.BlockSpec(memory_space=pltpu.VMEM)
    slots = (blocks + SUB + depth) * 9
    return pl.pallas_call(
        functools.partial(backward_kernel, depth, sides, layers),
        out_shape=(
            jax.ShapeDtypeStruct((layers, count, width), BF),
            jax.ShapeDtypeStruct((rows, lanes), F32),
            jax.ShapeDtypeStruct((8, 128), F32),
        ),
        in_specs=[any_space] * (1 + len(saved) + 2) + [vmem] * 7,
        out_specs=[any_space, vmem, vmem],
        scratch_shapes=[
            room(rows, lanes),
            room(2 * blocks + 2 * SUB, n, width),
            room(IN_FLIGHT, 2, n, width),
            room(blocks + SUB, 2, p, width),
            room(blocks, m, width),
            room(blocks, m, width),
            room(layers * SUB, m, width),
            room(layers * SUB, m, width),
            room(shards, rows, lanes),
            room(depth, 2, rows, lanes),
            room(depth, 2, rows, lanes),
            room(depth, 2, 16, lanes),
            room(depth, row_m, lanes),
            room(depth, row_m, lanes),
            room(row_m, lanes),
            room(row_m, lanes),
            room(seq, width, dtype=F32),
            room(seq, width),
            room(seq, 3 * width),
            room(seq, 128, dtype=F32),
            room(seq, width),
            room(seq, width, dtype=F32),
            room(seq, width),
            room(4, width, width),
            room(seq, pixels),
            room(seq, width),
            room(seq, 4 * width),
            room(seq, width, dtype=F32),
            room(seq, width),
            room(seq, width, dtype=F32),
            room(seq, width),
            room(128, width, dtype=F32),
            room(8, 128, dtype=F32),
            room(everyone, 8, 128, dtype=F32),
            pltpu.SemaphoreType.DMA((slots,)),
            pltpu.SemaphoreType.DMA((slots,)),
            pltpu.SemaphoreType.DMA((2 * layers * SUB + 2 * depth,)),
            pltpu.SemaphoreType.DMA((4,)),
            pltpu.SemaphoreType.DMA((9,)),
            pltpu.SemaphoreType.DMA((everyone,)),
            pltpu.SemaphoreType.DMA((everyone,)),
            pltpu.SemaphoreType.REGULAR,
        ],
        name="backward_and_sum",
        compiler_params=pltpu.CompilerParams(
            collective_id=2, has_side_effects=True, vmem_limit_bytes=VMEM_LIMIT
        ),
    )(weights, *saved, embedded, patches, vectors, mask, *head, start, stats)


def adam(clipped, row_params, row_zero, row_ema, row_first, row_second):
    new_first = first_decay * row_first + (1.0 - first_decay) * clipped
    new_second = second_decay * row_second + (1.0 - second_decay) * clipped * clipped
    step_size = (
        new_first
        / (1.0 - first_decay**STEPS_DONE)
        / (jnp.sqrt(new_second / (1.0 - second_decay**STEPS_DONE)) + adam_floor)
    )
    new_rows = row_params - adam_rate * (step_size + weight_decay * row_params)
    ema_rows = ema_decay * row_ema + (1.0 - ema_decay) * new_rows
    mixed_rows = mix_share * new_rows + (1.0 - mix_share) * row_zero
    return (new_rows, new_first, new_second, ema_rows, mixed_rows)


def finish_kernel(
    hyper,
    totals,
    clipped,
    row_params,
    row_zero,
    row_ema,
    row_first,
    row_second,
    grad,
    momentum,
    mats,
    zero,
    ema,
    new_rows,
    new_first,
    new_second,
    ema_rows,
    mixed_rows,
    bias_grad,
    new_momentum,
    new_mats,
    new_ema,
    new_mixed,
    grad_v,
    m_v,
    mats_v,
    zero_v,
    ema_v,
    x_v,
    short_v,
    low_v,
    in_sem,
    out_sem,
):
    layers, count, width = grad.shape
    pairs = [(grad, grad_v), (momentum, m_v)]
    pairs += [(mats, mats_v), (zero, zero_v), (ema, ema_v)]
    loads = [pltpu.make_async_copy(a, b, in_sem.at[i]) for i, (a, b) in enumerate(pairs)]
    for load in loads:
        load.start()
    rows = row_params.shape[1]
    row_grad = clipped[:, pl.ds(0, rows)]
    news = adam(row_grad, *(ref[...] for ref in (row_params, row_zero, row_ema, row_first, row_second)))
    for target, value in zip((new_rows, new_first, new_second, ema_rows, mixed_rows), news):
        target[...] = value
    lane = lax.broadcasted_iota(jnp.int32, clipped.shape, 1)
    spot = lax.broadcasted_iota(jnp.int32, bias_grad.shape, 1)
    bias = jnp.zeros(bias_grad.shape, F32)
    for layer in range(layers):
        index = PIX + EMB + SEQ + 4 + 12 * layer + 7
        column = jnp.sum(jnp.where(lane == index, clipped[...], 0.0), -1, keepdims=True)
        bias = jnp.where(spot == layer, column, bias)
    bias_grad[...] = bias
    part = count // 3
    factor = totals[pl.ds(0, 1), pl.ds(3, 1)]
    loads[0].wait()
    loads[1].wait()
    stores = []
    for layer in range(layers):
        total = jnp.zeros((1, 1), F32)
        for third in range(3):
            rows = pl.ds(third * part, part)
            value = momentum_decay * m_v[layer, rows, :] + factor * grad_v[layer, rows, :].astype(F32)
            m_v[layer, rows, :] = value
            total += jnp.sum(value * value, keepdims=True)
        store = pltpu.make_async_copy(m_v.at[layer], new_momentum.at[layer], out_sem.at[layer])
        store.start()
        stores.append(store)
        inverse = 1.0 / (jnp.sqrt(total) + 1e-07)
        for third in range(3):
            rows = pl.ds(third * part, part)
            value = m_v[layer, rows, :] * inverse
            x_v[layer, rows, :] = value
            short_v[0, layer, rows, :] = value.astype(BF)

    row_id = lax.broadcasted_iota(jnp.int32, (part, count), 0)
    col_id = lax.broadcasted_iota(jnp.int32, (part, count), 1)

    def step(turn, shift, use):
        now = lax.rem(turn, 2)
        linear = coeff_cubic + 2.0 * shift * coeff_quintic
        stay = coeff_linear + shift * (coeff_cubic + shift * coeff_quintic)
        for layer in range(layers):
            for third in range(3):
                rows = pl.ds(third * part, part)
                gram = matmul_nt(short_v[now, layer, rows, :], short_v[now, layer])
                gram -= jnp.where(row_id + third * part == col_id, shift, 0.0)
                low_v[layer, rows, :] = gram.astype(BF)
        for layer in range(layers):
            for third in range(3):
                rows = pl.ds(third * part, part)
                low = low_v[layer, rows, :]
                poly = linear * low.astype(F32) + coeff_quintic * matmul(low, low_v[layer])
                value = stay * x_v[layer, rows, :] + matmul(poly.astype(BF), short_v[now, layer])
                use(layer, third, rows, value)

    @pl.loop(0, NS_STEPS - 1)
    def _(turn):
        def keep(layer, third, rows, value):
            x_v[layer, rows, :] = value
            short_v[1 - lax.rem(turn, 2), layer, rows, :] = value.astype(BF)

        step(turn, jnp.where(turn >= NS_STEPS - 2, 1.0, 0.0), keep)

    for load in loads[2:]:
        load.wait()

    def update(layer, third, rows, orth):
        old = mats_v[layer, rows, :]
        value = old - muon_rate * (hyper * orth + weight_decay * old)
        mats_v[layer, rows, :] = value
        ema_v[layer, rows, :] = ema_decay * ema_v[layer, rows, :] + (1.0 - ema_decay) * value
        zero_v[layer, rows, :] = mix_share * value + (1.0 - mix_share) * zero_v[layer, rows, :]
        for turn, (source, target) in enumerate(
            ((mats_v, new_mats), (ema_v, new_ema), (zero_v, new_mixed))
        ):
            sem = out_sem.at[layers + (layer * 3 + third) * 3 + turn]
            store = pltpu.make_async_copy(source.at[layer, rows], target.at[layer, rows], sem)
            store.start()
            stores.append(store)

    step(NS_STEPS - 1, 1.0, update)
    for store in stores:
        store.wait()


def finish(totals, clipped, tables, grad, momentum, mats, zero, ema):
    layers, count, width = grad.shape
    full = jax.ShapeDtypeStruct(mats.shape, F32)
    table = jax.ShapeDtypeStruct(tables[0].shape, F32)
    any_space = pl.BlockSpec(memory_space=pl.ANY)
    vmem = pl.BlockSpec(memory_space=pltpu.VMEM)
    return pl.pallas_call(
        functools.partial(finish_kernel, 0.2 * math.sqrt(width)),
        out_shape=(table,) * 5
        + (jax.ShapeDtypeStruct((clipped.shape[0], 128), F32), full, full, full, full),
        in_specs=[vmem] * (2 + len(tables)) + [any_space] * 5,
        out_specs=[vmem] * 6 + [any_space] * 4,
        scratch_shapes=[
            pltpu.VMEM(grad.shape, BF),
            pltpu.VMEM(mats.shape, F32),
            pltpu.VMEM(mats.shape, F32),
            pltpu.VMEM(mats.shape, F32),
            pltpu.VMEM(mats.shape, F32),
            pltpu.VMEM(mats.shape, F32),
            pltpu.VMEM((2,) + mats.shape, BF),
            pltpu.VMEM((layers, count, count), BF),
            pltpu.SemaphoreType.DMA((5,)),
            pltpu.SemaphoreType.DMA((layers * 10,)),
        ],
        name="orthogonalize",
        compiler_params=pltpu.CompilerParams(vmem_limit_bytes=56 * 1024 * 1024),
    )(totals, clipped, *tables, grad, momentum, mats, zero, ema)


def gather_layer(shard):
    return lax.all_gather(shard.astype(jnp.bfloat16), "fsdp", axis=0, tiled=True)


def layer_forward(resid, weight_tensors, vector, valid_mask):
    images, seq = valid_mask.shape
    width = resid.shape[1]
    ffn = 4 * width
    normed = norm_forward(resid, vector[0], vector[1]).astype(jnp.bfloat16)
    bias = jnp.concatenate([vector[2], jnp.zeros_like(vector[2]), vector[3]])
    project = (matmul_nt(normed, weight_tensors[: 3 * width]) + bias).astype(jnp.bfloat16)
    parts = project.reshape(images, seq, 3, HEADS, HDIM)
    scores = attention_scores(parts, valid_mask)
    top_score = jnp.max(scores, -1, keepdims=True)
    expo = jnp.exp(scores - top_score)
    totals = jnp.sum(expo, -1, keepdims=True)
    log_total = top_score + jnp.log(totals)
    probs = (expo / totals).astype(jnp.bfloat16)
    context = jnp.einsum(
        "ihqk,ikhd->iqhd", probs, parts[:, :, 2], preferred_element_type=jnp.float32
    )
    context = context.reshape(images * seq, width).astype(jnp.bfloat16)
    mixed = resid + (matmul_nt(context, weight_tensors[3 * width : 4 * width]) + vector[4])
    normed_two = norm_forward(mixed, vector[5], vector[6]).astype(jnp.bfloat16)
    hidden_pre = matmul_nt(normed_two, weight_tensors[4 * width : 4 * width + ffn]) + vector[
        8:12
    ].reshape(ffn)
    hidden = (hidden_pre * jax.nn.sigmoid(1.702 * hidden_pre)).astype(jnp.bfloat16)
    output = mixed + (matmul(hidden, weight_tensors[4 * width + ffn :]) + vector[7])
    return (
        output,
        (resid, normed, project, log_total, context, mixed, normed_two, hidden_pre, hidden),
    )


def layer_backward(upstream, weight_tensors, vector, valid_mask, saved_activation):
    resid, normed, project, log_total, context, mixed, normed_two, hidden_pre, hidden = (
        saved_activation
    )
    images, seq = valid_mask.shape
    width = resid.shape[1]
    ffn = 4 * width
    out_grad = upstream.astype(jnp.bfloat16)
    grad_down = matmul_tn(hidden, out_grad)
    hidden_grad = matmul_nt(out_grad, weight_tensors[4 * width + ffn :])
    gate = jax.nn.sigmoid(1.702 * hidden_pre)
    pre_grad = (hidden_grad * (gate + 1.702 * hidden_pre * gate * (1.0 - gate))).astype(
        jnp.bfloat16
    )
    grad_up = matmul_tn(pre_grad, normed_two)
    second_in, gain_two, shift_two = norm_backward(
        mixed, vector[5], matmul(pre_grad, weight_tensors[4 * width : 4 * width + ffn])
    )
    mixed_grad = upstream + second_in
    attn_grad = mixed_grad.astype(jnp.bfloat16)
    grad_out = matmul_tn(attn_grad, context)
    context_grad = matmul(attn_grad, weight_tensors[3 * width : 4 * width]).astype(jnp.bfloat16)
    context_grad = context_grad.reshape(images, seq, HEADS, HDIM)
    parts = project.reshape(images, seq, 3, HEADS, HDIM)
    probs = jnp.exp(attention_scores(parts, valid_mask) - log_total)
    prob_grad = jnp.einsum(
        "iqhd,ikhd->ihqk", context_grad, parts[:, :, 2], preferred_element_type=jnp.float32
    )
    value_grad = jnp.einsum(
        "ihqk,iqhd->ikhd",
        probs.astype(jnp.bfloat16),
        context_grad,
        preferred_element_type=jnp.float32,
    )
    score_grad = (probs * (prob_grad - jnp.sum(prob_grad * probs, -1, keepdims=True))).astype(
        jnp.bfloat16
    )
    query_grad = jnp.einsum(
        "ihqk,ikhd->iqhd", score_grad, parts[:, :, 1], preferred_element_type=jnp.float32
    ) * HDIM ** (-0.5)
    key_grad = jnp.einsum(
        "ihqk,iqhd->ikhd", score_grad, parts[:, :, 0], preferred_element_type=jnp.float32
    ) * HDIM ** (-0.5)
    project_grad = (
        jnp.stack([query_grad, key_grad, value_grad], 2)
        .reshape(images * seq, 3 * width)
        .astype(jnp.bfloat16)
    )
    project_sum = jnp.sum(project_grad.astype(jnp.float32), 0)
    grad_qkv = matmul_tn(project_grad, normed)
    first_in, gain_one, shift_one = norm_backward(
        resid, vector[0], matmul(project_grad, weight_tensors[: 3 * width])
    )
    residual_gradient = mixed_grad + first_in
    grad_matrix = [part.astype(BF) for part in (grad_qkv, grad_out, grad_up, grad_down)]
    grad_vector = jnp.concatenate(
        [
            jnp.stack(
                [
                    gain_one,
                    shift_one,
                    project_sum[:width],
                    project_sum[2 * width :],
                    jnp.sum(attn_grad.astype(jnp.float32), 0),
                    gain_two,
                    shift_two,
                    jnp.sum(out_grad.astype(jnp.float32), 0),
                ]
            ),
            jnp.sum(pre_grad.astype(jnp.float32), 0).reshape(4, width),
        ],
        0,
    )
    return (residual_gradient, grad_matrix, grad_vector)


def newton_schulz(blocks):
    frob = jnp.sqrt(jnp.sum(blocks * blocks, axis=(1, 2), keepdims=True)) + 1e-07
    blocks = blocks / frob
    unit = jnp.eye(blocks.shape[1], dtype=jnp.float32)
    for turn in range(NS_STEPS):
        shift = 1.0 if turn >= NS_STEPS - 2 else 0.0
        short = blocks.astype(BF)
        gram = jnp.einsum("lcd,led->lce", short, short, preferred_element_type=F32) - shift * unit
        low = gram.astype(BF)
        square = jnp.einsum("lce,lef->lcf", low, low, preferred_element_type=F32)
        poly = (coeff_cubic + 2.0 * shift * coeff_quintic) * gram + coeff_quintic * square
        stay = coeff_linear + shift * (coeff_cubic + shift * coeff_quintic)
        blocks = stay * blocks + jnp.einsum(
            "lce,led->lcd", poly.astype(BF), short, preferred_element_type=F32
        )
    return blocks


def row_updates(clipped, layers, *tables):
    front = PIX + EMB + SEQ + 4
    down_bias_grad = clipped[front:].reshape(layers, 12, clipped.shape[1])[:, 7]
    return adam(clipped, *tables) + (down_bias_grad,)


def plain_body(
    patches,
    pad_mask,
    labels,
    loss_weights,
    class_emb,
    layer_mats,
    layer_zero,
    layer_ema,
    layer_momentum,
    row_params,
    row_zero,
    row_ema,
    row_first,
    row_second,
):
    layers, columns, width = layer_mats.shape
    images, seq, pixels = patches.shape
    front = PIX + EMB + SEQ + 4
    valid_mask = pad_mask.astype(jnp.float32)
    gathered_rows = lax.all_gather(row_params.astype(jnp.bfloat16), "fsdp", axis=1, tiled=True)
    rows_value = gathered_rows.astype(jnp.float32)
    patch_weight = gathered_rows[:PIX]
    proj_rows = gathered_rows[PIX : PIX + EMB]
    position = rows_value[PIX + EMB : PIX + EMB + SEQ]
    head_vec = rows_value[PIX + EMB + SEQ : front]
    layer_vector_params = rows_value[front:].reshape(layers, 12, width)
    flat_patches = patches.reshape(images * seq, pixels)
    embedded = (matmul(flat_patches, patch_weight).reshape(images, seq, width) + position).reshape(
        images * seq, width
    )
    resid = norm_forward(embedded, head_vec[0], head_vec[1])
    kept_weights = []
    saved_activations = []
    for layer_number in range(layers):
        weight_tensors = gather_layer(layer_mats[layer_number])
        kept_weights.append(weight_tensors)
        resid, saved_activation = layer_forward(
            resid, weight_tensors, layer_vector_params[layer_number], valid_mask
        )
        saved_activations.append(saved_activation)
    counts = jnp.sum(valid_mask, -1, keepdims=True)
    pooled = jnp.sum(resid.reshape(images, seq, width) * valid_mask[..., None], 1) / counts
    pooled_norm = norm_forward(pooled, head_vec[2], head_vec[3]).astype(jnp.bfloat16)
    feature = matmul_nt(pooled_norm, proj_rows)
    inv_length = lax.rsqrt(jnp.sum(feature * feature, -1, keepdims=True) + unit_epsilon)
    unit_feat = (feature * inv_length).astype(jnp.bfloat16)
    classes = class_emb.astype(jnp.float32)
    class_unit = (
        classes * lax.rsqrt(jnp.sum(classes * classes, -1, keepdims=True) + unit_epsilon)
    ).astype(jnp.bfloat16)
    logits = logit_scale * matmul_nt(unit_feat, class_unit)
    top_logit = jnp.max(logits, -1, keepdims=True)
    shifted = jnp.exp(logits - top_logit)
    total_exp = jnp.sum(shifted, -1, keepdims=True)
    log_norm = top_logit + jnp.log(total_exp)
    onehot = (jnp.arange(logits.shape[1])[None, :] == labels[:, None]).astype(jnp.float32)
    losses = log_norm[:, 0] - jnp.sum(onehot * logits, -1)
    weights_value = loss_weights.astype(jnp.float32)
    loss_sum, weight_sum = lax.psum(
        (jnp.sum(weights_value * losses), jnp.sum(weights_value)), ("fsdp", "ns")
    )
    seed = weights_value / weight_sum
    logit_grad = seed[:, None] * (shifted / total_exp - onehot)
    unit_grad = logit_scale * jnp.dot(logit_grad, class_unit.astype(jnp.float32), precision=HIGHEST)
    feat_grad = inv_length * unit_grad - feature * inv_length**3 * jnp.sum(
        unit_grad * feature, -1, keepdims=True
    )
    grad_proj = jnp.dot(feat_grad.T, pooled_norm.astype(jnp.float32), precision=HIGHEST)
    pooled_grad, gain_post, shift_post = norm_backward(
        pooled, head_vec[2], jnp.dot(feat_grad, proj_rows.astype(jnp.float32), precision=HIGHEST)
    )
    residual_gradient = (valid_mask[..., None] * (pooled_grad / counts)[:, None, :]).reshape(
        images * seq, width
    )
    grad_mats = [None] * layers
    grad_vecs = [None] * layers
    for layer_number in reversed(range(layers)):
        weight_tensors = kept_weights[layer_number]
        residual_gradient, grad_matrix, grad_vector = layer_backward(
            residual_gradient,
            weight_tensors,
            layer_vector_params[layer_number],
            valid_mask,
            saved_activations[layer_number],
        )
        grad_mats[layer_number], grad_vecs[layer_number] = (
            lax.psum_scatter(
                jnp.concatenate(grad_matrix, 0), "fsdp", scatter_dimension=0, tiled=True
            ),
            lax.psum_scatter(grad_vector, "fsdp", scatter_dimension=1, tiled=True),
        )
    embed_grad, gain_pre, shift_pre = norm_backward(embedded, head_vec[0], residual_gradient)
    position_grad = jnp.sum(embed_grad.reshape(images, seq, width), 0)
    patch_grad = matmul_tn(flat_patches, embed_grad.astype(jnp.bfloat16))
    front_grad = jnp.concatenate(
        [
            patch_grad,
            grad_proj,
            position_grad,
            jnp.stack([gain_pre, shift_pre, gain_post, shift_post]),
        ],
        0,
    )
    front_shard = lax.psum_scatter(front_grad, "fsdp", scatter_dimension=1, tiled=True)
    mat_grad = jnp.stack(grad_mats)
    row_grad = jnp.concatenate([front_shard] + grad_vecs, 0)
    pairs = lax.axis_size("ns")
    side = lax.axis_index("ns")
    half_depth = width // pairs
    half_rows = row_grad.shape[0] // pairs
    mat_total, row_total = (
        lax.psum(mat_grad.astype(jnp.bfloat16), "ns").astype(jnp.float32),
        lax.psum(row_grad.astype(jnp.bfloat16), "ns").astype(jnp.float32),
    )
    mat_half = lax.dynamic_slice_in_dim(mat_total, side * half_depth, half_depth, 2)
    row_half = lax.dynamic_slice_in_dim(row_total, side * half_rows, half_rows, 0)
    squares = jnp.sum(mat_half * mat_half) + jnp.sum(row_half * row_half)
    grad_norm = jnp.sqrt(lax.psum(squares, ("fsdp", "ns")))
    clip = jnp.minimum(1.0, clip_bound / (grad_norm + 1e-06))
    momentum = momentum_decay * layer_momentum + clip * mat_total
    orth = newton_schulz(momentum)
    new_mats = layer_mats - muon_rate * (0.2 * math.sqrt(width) * orth + weight_decay * layer_mats)
    ema_mats = ema_decay * layer_ema + (1.0 - ema_decay) * new_mats
    mixed_mats = mix_share * new_mats + (1.0 - mix_share) * layer_zero
    return (loss_sum, weight_sum, grad_norm, new_mats, momentum, ema_mats, mixed_mats) + row_updates(
        clip * row_total, layers, row_params, row_zero, row_ema, row_first, row_second
    )


def fast_body(
    patches,
    pad_mask,
    labels,
    loss_weights,
    class_emb,
    layer_mats,
    layer_zero,
    layer_ema,
    layer_momentum,
    row_params,
    row_zero,
    row_ema,
    row_first,
    row_second,
):
    layers, columns, width = layer_mats.shape
    shards = lax.axis_size("fsdp")
    depth = shards // PLANE
    weights, *saved, embedded, vectors, pooled_row, z_rows, feature_rows, start, stats = forward(
        depth,
        row_params.T,
        layer_mats,
        patches[0],
        pad_mask,
        class_emb,
        labels[:, None],
        loss_weights.astype(F32)[:, None],
    )
    mat_total, clipped, totals = backward(
        depth,
        lax.axis_size("ns"),
        weights,
        saved,
        embedded,
        patches[0],
        vectors,
        pad_mask,
        (pooled_row, z_rows, feature_rows),
        start,
        stats,
    )
    loss_sum, weight_sum, grad_norm = (totals[0, turn] for turn in range(3))
    tables = [table.T for table in (row_params, row_zero, row_ema, row_first, row_second)]
    *news, bias, momentum, new_mats, ema_mats, mixed_mats = finish(
        totals, clipped, tables, mat_total, layer_momentum, layer_mats, layer_zero, layer_ema
    )
    news = [table.T for table in news] + [bias[:, :layers].T]
    return (loss_sum, weight_sum, grad_norm, new_mats, momentum, ema_mats, mixed_mats, *news)


def body(*args):
    count, share = args[5].shape[1], args[9].shape[1]
    planes = lax.axis_size("fsdp") == 4 * PLANE and lax.axis_size("ns") == 2
    if planes and count % 192 == 0 and share % 48 == 0 and args[0].shape[0] == 1:
        return fast_body(*args)
    return plain_body(*args)


def solution(mesh):
    in_specs = (
        P(("fsdp", "ns"), None, None),
        P(("fsdp", "ns"), None),
        P(("fsdp", "ns")),
        P(("fsdp", "ns")),
        P(),
        P(None, "fsdp", None),
        P(None, "fsdp", None),
        P(None, "fsdp", None),
        P(None, "fsdp", None),
        P(None, "fsdp"),
        P(None, "fsdp"),
        P(None, "fsdp"),
        P(None, "fsdp"),
        P(None, "fsdp"),
    )
    out_specs = (
        P(),
        P(),
        P(),
        P(None, "fsdp", None),
        P(None, "fsdp", None),
        P(None, "fsdp", None),
        P(None, "fsdp", None),
        P(None, "fsdp"),
        P(None, "fsdp"),
        P(None, "fsdp"),
        P(None, "fsdp"),
        P(None, "fsdp"),
        P(None, "fsdp"),
    )
    return jax.shard_map(body, mesh=mesh, in_specs=in_specs, out_specs=out_specs, check_vma=False)
```

```python
import functools
import math
from typing import NamedTuple

import jax
import jax.numpy as jnp
from jax import lax
from jax.experimental import pallas as pl
from jax.experimental.pallas import tpu as pltpu
from jax.sharding import PartitionSpec as P

HEADS = 12
HDIM = 64
PIX = 768
EMB = 512
SEQ = 256
NS_STEPS = 5
STEPS_DONE = 10


HIGHEST = lax.Precision.HIGHEST
norm_epsilon = 1e-05
unit_epsilon = 1e-06
logit_scale = 50.0
clip_bound = 0.001
momentum_decay = 0.95
muon_rate = 0.05
weight_decay = 0.05
adam_rate = 0.2
first_decay = 0.9
second_decay = 0.98
adam_floor = 1e-08
ema_decay = 0.9
mix_share = 0.5
coeff_linear = 3.4445
coeff_cubic = -4.775
coeff_quintic = 2.0315


def matmul(left, right):
    return jnp.dot(left, right, preferred_element_type=jnp.float32)


def matmul_nt(left, right):
    return lax.dot_general(
        left, right, (((1,), (1,)), ((), ())), preferred_element_type=jnp.float32
    )


def matmul_tn(left, right):
    return lax.dot_general(
        left, right, (((0,), (0,)), ((), ())), preferred_element_type=jnp.float32
    )


def norm_forward(inputs, gain, shift):
    center = inputs - jnp.mean(inputs, -1, keepdims=True)
    scale = lax.rsqrt(jnp.mean(center * center, -1, keepdims=True) + norm_epsilon)
    return center * scale * gain + shift


def norm_backward(inputs, gain, upstream):
    center = inputs - jnp.mean(inputs, -1, keepdims=True)
    scale = lax.rsqrt(jnp.mean(center * center, -1, keepdims=True) + norm_epsilon)
    normal = center * scale
    scaled_up = upstream * gain
    inner = scale * (
        scaled_up
        - jnp.mean(scaled_up, -1, keepdims=True)
        - normal * jnp.mean(scaled_up * normal, -1, keepdims=True)
    )
    return (inner, jnp.sum(upstream * normal, 0), jnp.sum(upstream, 0))


def attention_scores(parts, valid_mask):
    raw = jnp.einsum(
        "iqhd,ikhd->ihqk", parts[:, :, 0], parts[:, :, 1], preferred_element_type=jnp.float32
    )
    return jnp.where(valid_mask[:, None, None, :] > 0, raw * HDIM ** (-0.5), -1000000000.0)


BF = jnp.bfloat16
F32 = jnp.float32
MESH = pl.DeviceIdType.MESH
PLANE = 4


def guarded(pred, run):
    if pred is None:
        run()
    else:
        pl.when(pred)(run)


def both(first, second):
    if first is None:
        return second
    return first if second is None else jnp.logical_and(first, second)


def rows_at(start, count):
    return pl.ds(start if isinstance(start, int) else pl.multiple_of(start, 16), count)


class Links:
    def __init__(self, depth, send_sem, recv_sem):
        self.depth, self.send_sem, self.recv_sem = depth, send_sem, recv_sem
        self.me, self.x = lax.axis_index("fsdp"), lax.axis_index("ns")
        self.z, self.y, self.c = self.me // PLANE, lax.rem(self.me // 2, 2), lax.rem(self.me, 2)
        self.up = (self.at(self.z + 1, self.y, self.c), self.x)
        self.down = (self.at(self.z - 1, self.y, self.c), self.x)
        self.y_peer = (self.at(self.z, 1 - self.y, self.c), self.x)
        self.c_peer = (self.at(self.z, self.y, 1 - self.c), self.x)
        self.x_peer = (self.me, 1 - self.x)
        self.count, self.sent, self.waited = 0, [], set()

    def at(self, z, y, c):
        return PLANE * z + 2 * y + c

    def slot(self):
        self.count += 1
        return self.count - 1

    def greet(self):
        barrier = pltpu.get_barrier_semaphore()

        def signal(device):
            pl.semaphore_signal(barrier, inc=1, device_id=device, device_id_type=MESH)

        for device in (self.y_peer, self.x_peer, self.c_peer):
            signal(device)
        pl.when(self.z < self.depth - 1)(lambda: signal(self.up))
        pl.when(self.z > 0)(lambda: signal(self.down))
        inner = (self.z < self.depth - 1).astype(jnp.int32) + (self.z > 0).astype(jnp.int32)
        pl.semaphore_wait(barrier, 3 + inner)

    def copy(self, slot, source, target, device):
        return pltpu.make_async_remote_copy(
            src_ref=source,
            dst_ref=target,
            send_sem=self.send_sem.at[slot],
            recv_sem=self.recv_sem.at[slot],
            device_id=device,
            device_id_type=MESH,
        )

    def send(self, slot, source, target, device, pred=None):
        copy = self.copy(slot, source, target, device)
        guarded(pred, copy.start)
        self.sent.append((slot, pred, copy))

    def receive(self, slot, target, pred=None):
        guarded(pred, self.copy(slot, target, target, self.c_peer).wait_recv)

    def finish(self, slot=None):
        for number, pred, copy in self.sent:
            if number not in self.waited and (slot is None or number == slot):
                guarded(pred, copy.wait_send)
        if slot is not None:
            self.waited.add(slot)


def gather_item(links, own, target, count):
    depth, z, y, c, x = links.depth, links.z, links.y, links.c, links.x
    third = count // 3
    early = count // 9 // 16 * 16
    begin, amount = x * (third + early), 2 * third - early
    early_begin = amount - x * (third - early)
    origin = (0, 0)
    keys = [(side, far) for far in range(1, depth) for side in (-1, 1)]
    z_slot = {key: links.slot() for key in keys}
    y_slot = {key: links.slot() for key in keys + [origin]}
    e_slot = {(key, o): links.slot() for key in keys for o in (0, 1)}
    pair_slot = links.slot()
    x_slot = {(key, o): links.slot() for key in keys + [origin] for o in (0, 1)}
    c_slot = {(key, o): links.slot() for key in keys + [origin] for o in (0, 1)}

    def part(shard):
        return target(shard).at[rows_at(begin, amount)]

    def own_part():
        return own.at[rows_at(begin, amount)]

    def early_part(shard):
        return target(shard).at[rows_at(early_begin, early)]

    def third_of(shard, side):
        return target(shard).at[rows_at(side * 2 * third, third)]

    def shard(key, other, core=None):
        return links.at(z + key[0] * key[1], 1 - y if other else y, c if core is None else core)

    def exists(key):
        if key == origin:
            return None
        return z >= key[1] if key[0] < 0 else z + key[1] < depth

    def z_send(key):
        for side in (-1, 1) if key == origin else (key[0],):
            if key[1] + 1 < depth:
                source = own_part() if key == origin else part(shard(key, 0))
                links.send(
                    z_slot[(side, key[1] + 1)],
                    source,
                    part(shard(key, 0)),
                    links.up if side < 0 else links.down,
                    both(exists(key), z < depth - 1 if side < 0 else z > 0),
                )

    def e_send(key, other):
        for side in (-1, 1) if key == origin else (key[0],):
            if early and key[1] + 1 < depth:
                block = early_part(shard(key, other))
                mine = key == origin and other == 0
                links.send(
                    e_slot[((side, key[1] + 1), other)],
                    own.at[rows_at(early_begin, early)] if mine else block,
                    block,
                    links.up if side < 0 else links.down,
                    both(exists(key), z < depth - 1 if side < 0 else z > 0),
                )

    def e_receive(key, other):
        if early:
            links.receive(e_slot[(key, other)], early_part(shard(key, other)), exists(key))

    def y_send(key):
        source = own_part() if key == origin else part(shard(key, 0))
        links.send(y_slot[key], source, part(shard(key, 0)), links.y_peer, exists(key))

    def x_send(key, other):
        block = third_of(shard(key, other), x)
        links.send(x_slot[(key, other)], block, block, links.x_peer, exists(key))

    def c_send(key, other):
        whole = target(shard(key, other))
        source = own if (key, other) == (origin, 0) else whole
        links.send(c_slot[(key, other)], source, whole, links.c_peer, exists(key))

    order = []
    for far in range(1, depth):
        order += [((side, far), 0) for side in (-1, 1)]
        order += [(key, 1) for key in ([origin] if far == 1 else [(-1, far - 1), (1, far - 1)])]
    order += [((side, depth - 1), 1) for side in (-1, 1)]

    def start():
        if early:
            source = own.at[rows_at(early_begin, early)]
            links.send(pair_slot, source, early_part(shard(origin, 0)), links.y_peer)
        z_send(origin)
        e_send(origin, 0)
        y_send(origin)
        c_send(origin, 0)

    def cross(keys_now):
        for key in keys_now:
            links.receive(y_slot[key], part(shard(key, 1)), exists(key))
            x_send(key, 1)

    def step(far):
        if far == 1 and early:
            links.receive(pair_slot, early_part(shard(origin, 1)))
            e_send(origin, 1)
        for side in (-1, 1):
            key = (side, far)
            links.receive(z_slot[key], part(shard(key, 0)), exists(key))
            z_send(key)
            y_send(key)
            x_send(key, 0)
        cross([origin] if far == 1 else [(-1, far - 1), (1, far - 1)])
        for side in (-1, 1):
            for other in (0, 1):
                e_receive((side, far), other)
                e_send((side, far), other)
        if far == depth - 1:
            cross([(-1, far), (1, far)])

    def share():
        for key, other in order:
            links.receive(x_slot[(key, other)], third_of(shard(key, other), 1 - x), exists(key))
            c_send(key, other)

    def settle():
        for key, other in [(origin, 0)] + order:
            links.receive(c_slot[(key, other)], target(shard(key, other, 1 - c)), exists(key))

    return start, step, share, settle

def split(value):
    high = value.astype(BF)
    return high, (value - high.astype(F32)).astype(BF)


def forward_kernel(
    depth,
    halves,
    rows,
    mats,
    patches,
    mask,
    classes,
    label,
    weight,
    all_mats,
    resid,
    normed,
    project,
    log_total,
    context,
    mixed,
    normed_two,
    embedded,
    vectors,
    pooled_row,
    z_rows,
    feature_rows,
    vector_start,
    stats,
    row_own,
    tail_v,
    rows_v,
    mats_v,
    own_v,
    resid_v,
    normed_v,
    project_v,
    log_v,
    context_v,
    mixed_v,
    two_v,
    embed_v,
    weight_v,
    total_v,
    class_v,
    send_sem,
    recv_sem,
    local_sem,
    weight_sem,
    save_sem,
):
    links = Links(depth, send_sem, recv_sem)
    layers, count, width = mats.shape
    size = count // halves
    whole = rows.shape[1] // 128 * 128
    tail_v[...] = jnp.zeros_like(tail_v)
    tail_v[:, pl.ds(0, rows.shape[1] - whole)] = rows[:, pl.ds(whole, rows.shape[1] - whole)]
    row_own[:, pl.ds(0, whole)] = rows[:, pl.ds(0, whole)].astype(BF)
    row_own[:, pl.ds(whole, 128)] = tail_v[...].astype(BF)
    rows_v[pl.ds(links.me, 1)] = row_own[...][None]
    items = [gather_item(links, row_own, lambda shard: rows_v.at[shard], rows.shape[0])]
    keep = mask[...].astype(F32)
    own, loads = [], []
    for layer in range(layers):
        loads.append(pltpu.make_async_copy(mats.at[layer], mats_v, local_sem.at[0]))
        own.append(
            pltpu.make_async_copy(
                own_v.at[layer],
                all_mats.at[layer, rows_at(links.me * count, count)],
                local_sem.at[1 + layer],
            )
        )
        for half in range(halves):

            def target(shard, layer=layer, half=half):
                return all_mats.at[layer, rows_at(shard * count + half * size, size)]

            block = own_v.at[layer, pl.ds(half * size, size)]
            items.append(gather_item(links, block, target, size))
    saves = []

    def take(layer):
        loads[layer].wait()
        own_v[layer] = mats_v[...].astype(BF)
        own[layer].start()
        if layer + 1 < layers:
            loads[layer + 1].start()

    loads[0].start()
    links.greet()

    def save(source, target):
        copy = pltpu.make_async_copy(source, target, save_sem.at[len(saves)])
        copy.start()
        saves.append(copy)

    def table(begin, amount):
        return rows_v[:, :, pl.ds(begin, amount)].reshape(width, amount)

    pixels, seq = patches.shape[1], patches.shape[0]

    def column(index):
        return vectors[pl.ds(index, 1), :]

    def embed():
        vectors[...] = table(pixels + EMB + SEQ, 128).astype(F32).T
        position = table(pixels + EMB, SEQ).astype(F32).T
        embed_v[...] = matmul_nt(patches[...], table(0, pixels)) + position
        save(embed_v, embedded)
        resid_v[0] = norm_forward(embed_v[...], column(0), column(1))

    order = []
    for layer in range(layers):
        order += [(layer, index) for index in (0, 1, 2, 3, 4, 8, 5, 9, 6, 10, 7, 11)]

    def chunk_copy(number):
        layer, index = order[number]
        return pltpu.make_async_copy(
            all_mats.at[layer, pl.ds(index * width, width)],
            weight_v.at[number % 4],
            weight_sem.at[number % 4],
        )

    def chunk(number):
        chunk_copy(number).wait()
        return weight_v[number % 4]

    half_lane = lax.broadcasted_iota(jnp.int32, (1, 128), 1) < HDIM
    scale = HDIM ** (-0.5)

    def attention_pair(layer, pair):
        def lanes(base):
            return pl.ds(pl.multiple_of(base + pair * 128, 128), 128)

        query, key = project_v[layer, :, lanes(0)], project_v[layer, :, lanes(width)]
        value = project_v[layer, :, lanes(2 * width)]
        results = []
        kept = log_v[layer]
        lane = lax.broadcasted_iota(jnp.int32, kept.shape, 1)
        for head in range(2):
            here = half_lane if head == 0 else jnp.logical_not(half_lane)
            query_h = jnp.where(here, query, jnp.zeros_like(query))
            scores = jnp.where(keep > 0, matmul_nt(query_h, key) * scale, -1000000000.0)
            top = jnp.max(scores, -1, keepdims=True)
            expo = jnp.exp(scores - top)
            total = jnp.sum(expo, -1, keepdims=True)
            kept = jnp.where(lane == 2 * pair + head, top + jnp.log(total), kept)
            results.append(matmul((expo / total).astype(BF), value))
        log_v[layer] = kept
        context_v[layer, :, lanes(0)] = jnp.where(half_lane, results[0], results[1]).astype(BF)

    def layer_steps(layer):
        base, first = 4 + 12 * layer, 12 * layer

        def vector(index):
            return column(base + index)

        for number in range(first, first + 4):
            chunk_copy(number).start()
        log_v[layer] = jnp.zeros_like(log_v[layer])
        save(resid_v.at[layer], resid.at[layer])
        normed_v[layer] = norm_forward(resid_v[layer], vector(0), vector(1)).astype(BF)
        save(normed_v.at[layer], normed.at[layer])
        for part in range(3):
            result = matmul_nt(normed_v[layer], chunk(first + part))
            if part != 1:
                result += vector(2 if part == 0 else 3)
            project_v[layer, :, pl.ds(part * width, width)] = result.astype(BF)
            chunk_copy(first + 4 + part).start()
        save(project_v.at[layer], project.at[layer])
        yield
        for third in range(3):

            @pl.loop(0, 2)
            def _(turn, third=third):
                attention_pair(layer, 2 * third + turn)

            yield
        save(context_v.at[layer], context.at[layer])
        save(log_v.at[layer], log_total.at[layer])
        mixed_v[layer] = resid_v[layer] + (
            matmul_nt(context_v[layer], chunk(first + 3)) + vector(4)
        )
        chunk_copy(first + 7).start()
        save(mixed_v.at[layer], mixed.at[layer])
        two_v[layer] = norm_forward(mixed_v[layer], vector(5), vector(6)).astype(BF)
        save(two_v.at[layer], normed_two.at[layer])
        yield
        total_v[...] = mixed_v[layer] + vector(7)
        for part in range(4):
            number = first + 4 + 2 * part
            pre = matmul_nt(two_v[layer], chunk(number)) + vector(8 + part)
            hidden = (pre * jax.nn.sigmoid(1.702 * pre)).astype(BF)
            total_v[...] += matmul(hidden, chunk(number + 1))
            for ahead in (number + 4, number + 5):
                if ahead < first + 12:
                    chunk_copy(ahead).start()
            if part < 3:
                yield
        resid_v[layer + 1] = total_v[...]
        yield

    def class_units():
        value = classes[...].astype(F32)
        length = lax.rsqrt(jnp.sum(value * value, -1, keepdims=True) + unit_epsilon)
        class_v[...] = (value * length).astype(BF)

    def head():
        number = jnp.sum(keep, -1, keepdims=True)
        keep_column = jnp.broadcast_to(keep, (8, seq)).T[:, :1]
        pooled = jnp.sum(resid_v[layers] * keep_column, 0, keepdims=True) / number
        center = pooled - jnp.mean(pooled, -1, keepdims=True)
        spread = lax.rsqrt(jnp.mean(center * center, -1, keepdims=True) + norm_epsilon)
        normal = center * spread
        z_value = jnp.broadcast_to(normal * column(2) + column(3), (16, width)).astype(BF)
        proj = table(pixels, EMB)
        feature = matmul(z_value, proj)
        inverse = lax.rsqrt(jnp.sum(feature * feature, -1, keepdims=True) + unit_epsilon)
        unit = (feature * inverse).astype(BF)
        logits = logit_scale * matmul_nt(unit, class_v[...])
        lane = lax.broadcasted_iota(jnp.int32, logits.shape, 1)
        top = jnp.max(logits, -1, keepdims=True)
        shifted = jnp.exp(logits - top)
        total = jnp.sum(shifted, -1, keepdims=True)
        chosen = lane == label[...]
        loss = top + jnp.log(total) - jnp.sum(jnp.where(chosen, logits, 0.0), -1, keepdims=True)
        logit_grad = weight[...] * (shifted / total - chosen.astype(F32))
        high, low = split(logit_grad)
        unit_grad = logit_scale * (matmul(high, class_v[...]) + matmul(low, class_v[...]))
        feature_grad = inverse * unit_grad - feature * inverse**3 * jnp.sum(
            unit_grad * feature, -1, keepdims=True
        )
        high, low = split(feature_grad)
        z_grad = (matmul_nt(high, proj) + matmul_nt(low, proj))[:1]
        scaled = z_grad * column(2)
        inner = spread * (
            scaled
            - jnp.mean(scaled, -1, keepdims=True)
            - normal * jnp.mean(scaled * normal, -1, keepdims=True)
        )
        pooled_row[...] = jnp.broadcast_to(inner / number, pooled_row.shape)
        spot = lax.broadcasted_iota(jnp.int32, (16, 1), 0)
        z_rows[...] = jnp.where(spot < 2, z_value, jnp.zeros_like(z_value))
        picked = jnp.where(spot == 0, high, jnp.where(spot == 1, low, jnp.zeros_like(low)))
        feature_rows[...] = picked
        vector_start[...] = jnp.zeros_like(vector_start)
        vector_start[pl.ds(2, 1), :] = z_grad * normal
        vector_start[pl.ds(3, 1), :] = z_grad
        here = lax.broadcasted_iota(jnp.int32, (8, 128), 1)
        first = lax.broadcasted_iota(jnp.int32, (8, 128), 0) == 0
        value = jnp.where(first & (here == 1), (loss * weight[...])[:8], 0.0)
        stats[...] = jnp.where(first & (here == 2), jnp.broadcast_to(weight[...], (8, 128)), value)

    running = None

    def work(amount):
        nonlocal running
        for _ in range(amount):
            if running is None:
                return
            if next(running, 0) == 0:
                running = None

    items[0][0]()
    take(0)
    class_units()
    for number, (_, step, _, _) in enumerate(items):
        step(1)
        work(1)
        step(2)
        if number + 1 < len(items):
            if number > 0 and number % halves == 0:
                take(number // halves)
            items[number + 1][0]()
        work(1)
        if number > 0:
            items[number - 1][2]()
        work(1)
        for far in range(3, depth):
            step(far)
        work(1)
        if number > 0:
            items[number - 1][3]()
            if number == 1:
                embed()
            for layer in range(layers - 1):
                if number - 1 == halves * (layer + 1):
                    own[layer].wait()
                    work(1000)
                    running = counted(layer_steps(layer))
        work(1)
    items[-1][2]()
    work(2)
    items[-1][3]()
    work(1000)
    own[layers - 1].wait()
    for _ in layer_steps(layers - 1):
        pass
    head()
    links.finish()
    for copy in saves:
        copy.wait()


def counted(steps):
    for _ in steps:
        yield 1


def forward(depth, rows, mats, patches, mask, classes, label, weight):
    layers, count, width = mats.shape
    lanes = (rows.shape[1] // 128 + 1) * 128
    shards = PLANE * depth
    halves = 2
    seq = patches.shape[0]
    slots = (1 + layers * halves) * 60
    any_space = pl.BlockSpec(memory_space=pl.ANY)
    vmem = pl.BlockSpec(memory_space=pltpu.VMEM)

    def shape(*sizes, dtype=F32):
        return jax.ShapeDtypeStruct(sizes, dtype)

    saved = (
        shape(layers, seq, width),
        shape(layers, seq, width, dtype=BF),
        shape(layers, seq, 3 * width, dtype=BF),
        shape(layers, seq, 128),
        shape(layers, seq, width, dtype=BF),
        shape(layers, seq, width),
        shape(layers, seq, width, dtype=BF),
    )
    return pl.pallas_call(
        functools.partial(forward_kernel, depth, halves),
        out_shape=(shape(layers, shards * count, width, dtype=BF),)
        + saved
        + (
            shape(seq, width),
            shape(128, width),
            shape(8, width),
            shape(16, width, dtype=BF),
            shape(16, EMB, dtype=BF),
            shape(128, width),
            shape(8, 128),
        ),
        in_specs=[vmem, any_space] + [vmem] * 5,
        out_specs=[any_space] * 9 + [vmem] * 6,
        scratch_shapes=[
            pltpu.VMEM((rows.shape[0], lanes), BF),
            pltpu.VMEM((rows.shape[0], 128), F32),
            pltpu.VMEM((shards, rows.shape[0], lanes), BF),
            pltpu.VMEM(mats.shape[1:], F32),
            pltpu.VMEM(mats.shape, BF),
            pltpu.VMEM((layers + 1, seq, width), F32),
        ]
        + [pltpu.VMEM(array.shape, array.dtype) for array in saved[1:]]
        + [
            pltpu.VMEM((seq, width), F32),
            pltpu.VMEM((4, width, width), BF),
            pltpu.VMEM((seq, width), F32),
            pltpu.VMEM(classes.shape, BF),
            pltpu.SemaphoreType.DMA((slots,)),
            pltpu.SemaphoreType.DMA((slots,)),
            pltpu.SemaphoreType.DMA((1 + layers,)),
            pltpu.SemaphoreType.DMA((4,)),
            pltpu.SemaphoreType.DMA((1 + 7 * layers,)),
        ],
        name="gather_and_forward",
        compiler_params=pltpu.CompilerParams(
            collective_id=1, has_side_effects=True, vmem_limit_bytes=56 * 1024 * 1024
        ),
    )(rows, mats, patches, mask, classes, label, weight)


def accumulate(target, start, source, begin, count, step):
    @pl.loop(0, count // step)
    def _(turn):
        here = rows_at(start + turn * step, step)
        there = rows_at(begin + turn * step, step)
        target[here, :] = (target[here, :].astype(F32) + source[there, :].astype(F32)).astype(BF)


class Group(NamedTuple):
    begin: object
    stages: list
    core_slot: list


def scatter_group(links, dest, load, sizes, bufs, emit, used=None):
    depth, z, y, c, x = links.depth, links.z, links.y, links.c, links.x
    n, p, q, step = sizes
    mine, core_in, x_in, y_in, z_in, z_last, final = bufs
    core_slot, x_slot = [links.slot(), links.slot()], [links.slot(), links.slot()]
    q_slot, p_slot, low_slot, high_slot, last_slot = (links.slot() for _ in range(5))
    m = p + q
    first = x * p
    own_p, peer_p = x * m, (1 - x) * m
    sides = ((0, 1 - y), (1, y))

    def begin():
        for i, side in sides:
            load(i, side, mine.at[side], core_in.at[side], core_slot[i])

    def stage_core():
        for i, side in sides:
            load(i, side, mine.at[side], None, None)
            links.receive(core_slot[i], core_in.at[side])
            accumulate(mine.at[side], 0, core_in.at[side], 0, n, step)
            links.send(x_slot[i], mine.at[side, rows_at(peer_p, p)], x_in.at[side], links.x_peer)
            if i == 0:
                links.send(q_slot, mine.at[side, pl.ds(p, q)], y_in.at[pl.ds(0, q)], links.y_peer)
        if used is not None:
            used()

    def stage_x():
        for i, side in sides:
            links.receive(x_slot[i], x_in.at[side])
            accumulate(mine.at[side], own_p, x_in.at[side], 0, p, step)
            if i == 0:
                links.send(
                    p_slot, mine.at[side, rows_at(own_p, p)], y_in.at[pl.ds(q, p)], links.y_peer
                )
        links.receive(q_slot, y_in.at[pl.ds(0, q)])
        accumulate(mine.at[y], p, y_in, 0, q, step)

    def stage_y():
        links.receive(p_slot, y_in.at[pl.ds(q, p)])
        accumulate(mine.at[y], own_p, y_in, q, p, step)

    def stage_z(hop):
        block = mine.at[y, rows_at(first, m)]

        def take(slot, source, pred):
            @pl.when(pred)
            def _():
                links.receive(slot, source)
                accumulate(mine.at[y], first, source, 0, m, step)

        if dest > 0:
            if 1 <= hop <= dest:
                take(low_slot, z_in, z == hop)
            if hop < dest:
                links.send(low_slot, block, z_in, links.up, z == hop)
        if dest < depth - 1:
            turn = depth - 1 - hop
            if hop >= 1 and turn > dest:
                take(high_slot, z_in, z == turn)
            if turn > dest + 1:
                links.send(high_slot, block, z_in, links.down, z == turn)
            if turn == dest + 1:
                links.send(high_slot, block, z_last, links.down, z == turn)
            if turn == dest and hop >= 1:
                take(high_slot, z_last, z == dest)
        if hop == max(dest, depth - 1 - dest):
            links.send(last_slot, block, final, links.x_peer, z == dest)

    def stage_last():
        links.finish(x_slot[1])
        links.finish(last_slot)

        @pl.when(z == dest)
        def _():
            links.receive(last_slot, final)
            accumulate(mine.at[y], p, final, jnp.where(x == 0, 0, p), q, step)

            @pl.loop(0, p // 16)
            def _(turn):
                there = rows_at(jnp.where(x == 0, q, 0) + turn * 16, 16)
                mine[y, rows_at(peer_p + turn * 16, 16), :] = final[there, :]

            emit(mine.at[y])

    hops = [functools.partial(stage_z, hop) for hop in range(depth)]
    return Group(begin, [stage_core, stage_x, stage_y] + hops + [stage_last], core_slot)

def norm_back(value, gain, upstream):
    center = value - jnp.mean(value, -1, keepdims=True)
    scale = lax.rsqrt(jnp.mean(center * center, -1, keepdims=True) + norm_epsilon)
    normal = center * scale
    scaled = upstream * gain
    inner = scale * (
        scaled
        - jnp.mean(scaled, -1, keepdims=True)
        - normal * jnp.mean(scaled * normal, -1, keepdims=True)
    )
    return (
        inner,
        jnp.sum(upstream * normal, 0, keepdims=True),
        jnp.sum(upstream, 0, keepdims=True),
    )


VMEM_LIMIT = 62 * 1024 * 1024
SUB = 3
IN_FLIGHT = 2 * SUB
LAGS = (1, 3, 5, 7, 9, 11, 13, 15)


def backward_kernel(
    depth,
    sides,
    layers,
    weights,
    resid,
    normed,
    project,
    log_total,
    context,
    mixed,
    normed_two,
    embedded,
    patches,
    vectors,
    mask,
    pooled_row,
    z_rows,
    feature_rows,
    vector_start,
    stats,
    out,
    clipped,
    totals,
    row_out,
    blocks_v,
    core_in,
    x_in,
    y_in,
    z_in,
    z_last,
    final,
    rows_v,
    row_mine,
    row_core,
    row_x,
    row_y,
    row_z,
    row_z_last,
    row_final,
    resid_v,
    normed_v,
    project_v,
    log_v,
    context_v,
    mixed_v,
    two_v,
    weight_v,
    patch_v,
    hidden_v,
    pre_v,
    up_v,
    short_v,
    total_v,
    context_grad_v,
    vector_v,
    note,
    inbox,
    send_sem,
    recv_sem,
    local_sem,
    weight_sem,
    load_sem,
    mail_send,
    mail_recv,
    free_sem,
):
    links = Links(depth, send_sem, recv_sem)
    y, c, z = links.y, links.c, links.z
    me = links.me * sides + links.x
    everyone = PLANE * depth * sides
    width = up_v.shape[1]
    count = out.shape[1]
    n = count // SUB
    p = n // 4 // 16 * 16
    per_layer = depth * SUB
    own = 2 * layers * per_layer
    piece = 2 * n

    saved = (
        (normed_two, two_v),
        (mixed, mixed_v),
        (context, context_v),
        (resid, resid_v),
        (normed, normed_v),
        (project, project_v),
        (log_total, log_v),
    )

    def load(layer, which):
        source, target = saved[which]
        return pltpu.make_async_copy(source.at[layer], target, load_sem.at[which])

    chunks = []
    for layer in reversed(range(layers)):
        for turn in (3, 2, 1, 0):
            chunks += [(layer, 8 + turn), (layer, 4 + turn)]
        chunks += [(layer, 3), (layer, 0), (layer, 1), (layer, 2)]

    def chunk_copy(number):
        layer, index = chunks[number]
        return pltpu.make_async_copy(
            weights.at[layer, pl.ds(index * width, width)],
            weight_v.at[number % 4],
            weight_sem.at[number % 4],
        )

    def chunk(number):
        chunk_copy(number).wait()
        return weight_v[number % 4]

    def refill(*numbers):
        for number in numbers:
            if number < len(chunks):
                chunk_copy(number).start()

    for which in range(len(saved)):
        load(layers - 1, which).start()
    refill(0, 1, 2, 3)
    patch_load = pltpu.make_async_copy(patches, patch_v, load_sem.at[7])
    patch_load.start()

    def others(run):
        for number in range(everyone):
            pl.when(me != number)(functools.partial(run, number))

    def place(number):
        return (number // sides, number % sides)

    barrier = pltpu.get_barrier_semaphore()
    others(
        lambda number: pl.semaphore_signal(
            barrier, inc=1, device_id=place(number), device_id_type=MESH
        )
    )
    note[...] = stats[...]
    vector_v[...] = vector_start[...]
    keep = mask[...].astype(F32)
    keep_column = jnp.broadcast_to(keep, (8, keep.shape[1])).T[:, :1]
    up_v[...] = keep_column * pooled_row[pl.ds(0, 1), :]
    lane = lax.broadcasted_iota(jnp.int32, (8, 128), 1)
    first = lax.broadcasted_iota(jnp.int32, (8, 128), 0) == 0

    def add_squares(block):
        value = block.astype(F32)
        note[...] += jnp.where(first & (lane == 0), jnp.sum(value * value), 0.0)

    groups, closers = [], []
    starts, members = {}, {}

    def add_group(dest, send_out, take_in, sizes, bufs, emit, used=None):
        def load_block(i, side, mine, target, slot):
            if target is None:
                take_in(i, side, mine)
            else:
                send_out(i, side, mine, target, slot)

        groups.append(scatter_group(links, dest, load_block, sizes, bufs, emit, used))

    total_blocks = layers * per_layer
    for order, layer in enumerate(reversed(range(layers))):
        for turn, dest in enumerate(reversed(range(depth))):
            for part in range(SUB):
                number, spot = (order * depth + turn) * SUB + part, layer * SUB + part
                starts[(layer, dest, part)] = number
                pieces = 2 if number >= total_blocks - SUB else 1
                size = n // pieces
                edge = (size // 4 + 15) // 16 * 16
                middle = size - edge
                members[number] = []
                for half in range(pieces):
                    members[number].append(len(groups))
                    inside = pl.ds(half * size, size)
                    window = pl.ds(half * middle, middle)

                    def send_out(i, side, mine, target, slot, part=part, inside=inside):
                        source = blocks_v.at[own + 2 * part + side, inside]
                        links.send(slot, source, target, links.c_peer)

                    def write(source, layer=layer, at=part * n + half * size, size=size, sem=spot + half * (layers * SUB + 2 * depth)):
                        target = out.at[layer, pl.ds(at, size)]
                        return pltpu.make_async_copy(source, target, local_sem.at[sem])

                    def emit(result, write=write):
                        add_squares(result[...])
                        write(result).start()

                    closers.append((dest, write, blocks_v.at[2 * number, inside]))

                    def used(number=number):
                        if number < total_blocks - IN_FLIGHT:
                            pl.semaphore_signal(
                                free_sem, inc=1, device_id=links.c_peer, device_id_type=MESH
                            )

                    add_group(
                        dest,
                        send_out,
                        lambda i, side, mine: None,
                        (size, edge, size - 2 * edge, 48 if pieces == 1 else 32),
                        [
                            blocks_v.at[pl.ds(2 * number, 2), inside],
                            core_in.at[number % IN_FLIGHT, :, inside],
                            x_in.at[number if half == 0 else total_blocks + part, :, pl.ds(0, edge)],
                            y_in.at[number, window],
                            z_in.at[number, window],
                            z_last.at[spot, window],
                            final.at[spot, window],
                        ],
                        emit,
                        used,
                    )
    first_row_group = len(groups)
    rows = row_out.shape[0]
    for dest in reversed(range(depth)):
        number = len(groups)

        def row_copy(i, side, mine, dest=dest):
            sem = local_sem.at[layers * SUB + 2 * dest + i]
            return pltpu.make_async_copy(rows_v.at[links.at(dest, side, c)], mine, sem)

        def row_send(i, side, mine, target, slot, dest=dest, row_copy=row_copy):
            row_copy(i, side, mine).start()
            source = rows_v.at[links.at(dest, side, 1 - c)]
            links.send(slot, source, target, links.c_peer)

        def row_emit(result, dest=dest):
            add_squares(result[...])
            row_out[...] = result[...]

        add_group(
            dest,
            row_send,
            lambda i, side, mine, row_copy=row_copy: row_copy(i, side, mine).wait(),
            (rows, 16, rows - 32, 16),
            [ref.at[dest] for ref in (row_mine, row_core, row_x, row_y, row_z)]
            + [row_z_last, row_final],
            row_emit,
        )

    def release(layer, dest):
        begun = 0
        for part in range(SUB):
            number = starts[(layer, dest, part)]
            if number >= IN_FLIGHT:
                pl.semaphore_wait(free_sem, 1)
            for index in members[number]:
                groups[index].begin()
                begun += 1
        return begun

    def recycle(layer, dest):
        for part in range(SUB):
            number = starts[(layer, dest, part)]
            if number >= SUB:
                for index in members[number - SUB]:
                    for slot in groups[index].core_slot:
                        links.finish(slot)

    last_turn = [0]

    def advance():
        turn = last_turn[0]
        for stage, lag in enumerate(LAGS):
            if 0 <= turn - lag < len(groups):
                groups[turn - lag].stages[stage]()
        last_turn[0] += 1

    def grad_pieces(layer, dest, left, column, amount, right, begin):
        number = starts[(layer, dest, 0)]
        ring = own

        @pl.loop(0, amount)
        def _(turn):
            columns = pl.ds(pl.multiple_of(column + turn * piece, 128), piece)
            result = matmul_tn(left[:, columns], right[...])
            for half in range(2):
                block = 2 * (begin + turn) + half
                shard = block // SUB
                part = lax.rem(block, SUB)
                side, core = shard // 2, lax.rem(shard, 2)
                index = jnp.where(
                    core == c, 2 * (number + part) + side, ring + 2 * part + side
                )
                blocks_v[index] = result[half * n : (half + 1) * n].astype(BF)

    half_lane = lax.broadcasted_iota(jnp.int32, (1, 128), 1) < HDIM
    scale = HDIM ** (-0.5)

    def attention_pair(pair):
        def lanes(base):
            return pl.ds(pl.multiple_of(base + pair * 128, 128), 128)

        query, key = project_v[:, lanes(0)], project_v[:, lanes(width)]
        value, grad = project_v[:, lanes(2 * width)], context_grad_v[:, lanes(0)]
        totals_now = log_v[...]
        column = lax.broadcasted_iota(jnp.int32, totals_now.shape, 1)
        query_grad = key_grad = value_grad = 0.0
        zero = jnp.zeros_like(query)
        for head in range(2):
            here = half_lane if head == 0 else jnp.logical_not(half_lane)
            query_h, key_h = jnp.where(here, query, zero), jnp.where(here, key, zero)
            grad_h = jnp.where(here, grad, zero)
            total = jnp.sum(
                jnp.where(column == 2 * pair + head, totals_now, 0.0), -1, keepdims=True
            )
            scores = jnp.where(keep > 0, matmul_nt(query_h, key) * scale, -1000000000.0)
            probs = jnp.exp(scores - total)
            prob_grad = matmul_nt(grad_h, value)
            value_grad += matmul_tn(probs.astype(BF), grad_h)
            score_grad = (
                probs * (prob_grad - jnp.sum(prob_grad * probs, -1, keepdims=True))
            ).astype(BF)
            query_grad += matmul(score_grad, key_h)
            key_grad += matmul_tn(score_grad, query_h)
        pre_v[:, lanes(0)] = (query_grad * scale).astype(BF)
        pre_v[:, lanes(width)] = (key_grad * scale).astype(BF)
        pre_v[:, lanes(2 * width)] = value_grad.astype(BF)

    def layer_steps(order, layer):
        base = 4 + 12 * layer
        chunk0 = 12 * order

        def vector(index):
            return vectors[pl.ds(base + index, 1), :]

        def put(index, value):
            vector_v[pl.ds(base + index, 1), :] = value

        def column_sum(value):
            return jnp.sum(value.astype(F32), 0, keepdims=True)

        load(layer, 0).wait()
        short_v[...] = up_v[...].astype(BF)
        put(7, column_sum(short_v[...]))
        total_v[...] = jnp.zeros_like(total_v)
        recycle(layer, 3)
        for turn, part in enumerate((3, 2, 1, 0)):
            number = chunk0 + 2 * turn
            down, up = chunk(number), chunk(number + 1)
            pre = matmul_nt(two_v[...], up) + vector(8 + part)
            gate = jax.nn.sigmoid(1.702 * pre)
            hidden_v[...] = (pre * gate).astype(BF)
            slope = gate + 1.702 * pre * gate * (1.0 - gate)
            pre_grad = (matmul_nt(short_v[...], down) * slope).astype(BF)
            pre_v[:, pl.ds(part * width, width)] = pre_grad
            put(8 + part, column_sum(pre_grad))
            total_v[...] += matmul(pre_grad, up)
            refill(number + 4, number + 5)
            yield None
            if part == 0:
                recycle(layer, 2)
            if part > 0:
                grad_pieces(layer, 3, hidden_v, 0, 2, short_v, 2 * (part - 1))
            else:
                grad_pieces(layer, 2, hidden_v, 0, 2, short_v, 4)
            if part == 1:
                begun = release(layer, 3)
                yield begun
            else:
                yield None
        grad_pieces(layer, 2, pre_v, 2 * width, 2, two_v, 0)
        yield None
        grad_pieces(layer, 2, pre_v, 3 * width, 2, two_v, 2)
        begun = release(layer, 2)
        yield begun
        load(layer, 1).wait()
        inner, gain, shift = norm_back(mixed_v[...], vector(5), total_v[...])
        put(5, gain)
        put(6, shift)
        up_v[...] += inner
        short_v[...] = up_v[...].astype(BF)
        put(4, column_sum(short_v[...]))
        yield None
        load(layer, 2).wait()
        recycle(layer, 1)
        grad_pieces(layer, 1, short_v, 0, 2, context_v, 0)
        context_grad_v[...] = matmul(short_v[...], chunk(chunk0 + 8)).astype(BF)
        refill(chunk0 + 12)
        yield None
        grad_pieces(layer, 1, pre_v, 0, 2, two_v, 2)
        yield None
        grad_pieces(layer, 1, pre_v, width, 2, two_v, 4)
        begun = release(layer, 1)
        if layer > 0:
            for which in range(3):
                load(layer - 1, which).start()
        else:
            embed_load.start()
        yield begun
        load(layer, 5).wait()
        load(layer, 6).wait()
        for third in range(3):

            @pl.loop(0, 2)
            def _(turn, third=third):
                attention_pair(2 * third + turn)

            yield None
        load(layer, 4).wait()
        recycle(layer, 0)
        put(2, column_sum(pre_v[:, pl.ds(0, width)]))
        put(3, column_sum(pre_v[:, pl.ds(2 * width, width)]))
        for third in range(3):
            grad_pieces(layer, 0, pre_v, third * width, 2, normed_v, 2 * third)
            if third < 2:
                yield None
        begun = release(layer, 0)
        yield begun
        load(layer, 3).wait()
        back = matmul(pre_v[:, pl.ds(0, width)], chunk(chunk0 + 9))
        back += matmul(pre_v[:, pl.ds(width, width)], chunk(chunk0 + 10))
        back += matmul(pre_v[:, pl.ds(2 * width, width)], chunk(chunk0 + 11))
        refill(chunk0 + 13, chunk0 + 14, chunk0 + 15)
        inner, gain, shift = norm_back(resid_v[...], vector(0), back)
        put(0, gain)
        put(1, shift)
        up_v[...] += inner
        if layer > 0:
            for which in range(3, len(saved)):
                load(layer - 1, which).start()
        yield None

    embed_load = pltpu.make_async_copy(embedded, mixed_v, load_sem.at[8])
    pl.semaphore_wait(barrier, everyone - 1)
    pending = 0
    for order, layer in enumerate(reversed(range(layers))):
        for ready in layer_steps(order, layer):
            if ready is not None:
                pending += ready
            if pending > 0:
                advance()
                pending -= 1
    embed_load.wait()
    inner, gain, shift = norm_back(mixed_v[...], vectors[pl.ds(0, 1), :], up_v[...])
    vector_v[pl.ds(0, 1), :] = gain
    vector_v[pl.ds(1, 1), :] = shift
    short_v[...] = inner.astype(BF)
    total_v[...] = inner
    patch_load.wait()
    pixels, embeds, seq = patch_v.shape[1], feature_rows.shape[1], inner.shape[0]
    for turn in range(width // piece):
        columns = pl.ds(turn * piece, piece)
        patch_grad = matmul_tn(short_v[:, columns], patch_v[...])
        proj_grad = matmul_tn(z_rows[:, columns], feature_rows[...])
        position = total_v[:, columns].T
        vector_grad = vector_v[:, columns].T
        for part in range(piece // rows):
            shard, inside = turn * (piece // rows) + part, slice(part * rows, (part + 1) * rows)
            rows_v[shard, :, pl.ds(0, pixels)] = patch_grad[inside].astype(BF)
            rows_v[shard, :, pl.ds(pixels, embeds)] = proj_grad[inside].astype(BF)
            rows_v[shard, :, pl.ds(pixels + embeds, seq)] = position[inside].astype(BF)
            rows_v[shard, :, pl.ds(pixels + embeds + seq, 128)] = vector_grad[inside].astype(BF)
    for number in range(first_row_group, len(groups)):
        groups[number].begin()
    while last_turn[0] < len(groups) + max(LAGS):
        advance()

    def mail(number, slot):
        return pltpu.make_async_remote_copy(
            src_ref=note,
            dst_ref=inbox.at[slot],
            send_sem=mail_send.at[number],
            recv_sem=mail_recv.at[slot],
            device_id=place(number),
            device_id_type=MESH,
        )

    others(lambda number: mail(number, me).start())
    inbox[pl.ds(me, 1)] = note[...][None]
    links.finish()
    for dest, write, source in closers:
        pl.when(z == dest)(lambda write=write, source=source: write(source).wait())
    others(lambda number: mail(number, number).wait_recv())
    summed = jnp.sum(inbox[...], 0)
    others(lambda number: mail(number, me).wait_send())

    def pick(index):
        return jnp.sum(jnp.where(first & (lane == index), summed, 0.0))

    loss_sum, weight_sum = pick(1), pick(2)
    norm = jnp.sqrt(jnp.full((8, 128), pick(0) / sides)) / weight_sum
    clip = jnp.minimum(1.0, clip_bound / (norm + 1e-06)) / weight_sum
    totals[...] = jnp.where(
        lane == 0,
        loss_sum,
        jnp.where(lane == 1, weight_sum, jnp.where(lane == 2, norm, clip)),
    )
    clipped[...] = row_out[...].astype(F32) * clip[:1, :1]


def backward(
    depth, sides, weights, saved, embedded, patches, vectors, mask, head, start, stats
):
    layers, rows_all, width = weights.shape
    seq, pixels = patches.shape
    shards = PLANE * depth
    count, rows = rows_all // shards, width // shards
    lanes = -(-(pixels + EMB + SEQ + 4 + 12 * layers) // 128) * 128
    n = count // SUB
    p = n // 4 // 16 * 16
    m = n - p
    per_layer = depth * SUB
    blocks = layers * per_layer
    row_m = rows - 16
    everyone = shards * sides

    def room(*shape, dtype=BF):
        return pltpu.VMEM(shape, dtype)

    any_space = pl.BlockSpec(memory_space=pl.ANY)
    vmem = pl.BlockSpec(memory_space=pltpu.VMEM)
    slots = (blocks + SUB + depth) * 9
    return pl.pallas_call(
        functools.partial(backward_kernel, depth, sides, layers),
        out_shape=(
            jax.ShapeDtypeStruct((layers, count, width), BF),
            jax.ShapeDtypeStruct((rows, lanes), F32),
            jax.ShapeDtypeStruct((8, 128), F32),
        ),
        in_specs=[any_space] * (1 + len(saved) + 2) + [vmem] * 7,
        out_specs=[any_space, vmem, vmem],
        scratch_shapes=[
            room(rows, lanes),
            room(2 * blocks + 2 * SUB, n, width),
            room(IN_FLIGHT, 2, n, width),
            room(blocks + SUB, 2, p, width),
            room(blocks, m, width),
            room(blocks, m, width),
            room(layers * SUB, m, width),
            room(layers * SUB, m, width),
            room(shards, rows, lanes),
            room(depth, 2, rows, lanes),
            room(depth, 2, rows, lanes),
            room(depth, 2, 16, lanes),
            room(depth, row_m, lanes),
            room(depth, row_m, lanes),
            room(row_m, lanes),
            room(row_m, lanes),
            room(seq, width, dtype=F32),
            room(seq, width),
            room(seq, 3 * width),
            room(seq, 128, dtype=F32),
            room(seq, width),
            room(seq, width, dtype=F32),
            room(seq, width),
            room(4, width, width),
            room(seq, pixels),
            room(seq, width),
            room(seq, 4 * width),
            room(seq, width, dtype=F32),
            room(seq, width),
            room(seq, width, dtype=F32),
            room(seq, width),
            room(128, width, dtype=F32),
            room(8, 128, dtype=F32),
            room(everyone, 8, 128, dtype=F32),
            pltpu.SemaphoreType.DMA((slots,)),
            pltpu.SemaphoreType.DMA((slots,)),
            pltpu.SemaphoreType.DMA((2 * layers * SUB + 2 * depth,)),
            pltpu.SemaphoreType.DMA((4,)),
            pltpu.SemaphoreType.DMA((9,)),
            pltpu.SemaphoreType.DMA((everyone,)),
            pltpu.SemaphoreType.DMA((everyone,)),
            pltpu.SemaphoreType.REGULAR,
        ],
        name="backward_and_sum",
        compiler_params=pltpu.CompilerParams(
            collective_id=2, has_side_effects=True, vmem_limit_bytes=VMEM_LIMIT
        ),
    )(weights, *saved, embedded, patches, vectors, mask, *head, start, stats)


def adam(clipped, row_params, row_zero, row_ema, row_first, row_second):
    new_first = first_decay * row_first + (1.0 - first_decay) * clipped
    new_second = second_decay * row_second + (1.0 - second_decay) * clipped * clipped
    step_size = (
        new_first
        / (1.0 - first_decay**STEPS_DONE)
        / (jnp.sqrt(new_second / (1.0 - second_decay**STEPS_DONE)) + adam_floor)
    )
    new_rows = row_params - adam_rate * (step_size + weight_decay * row_params)
    ema_rows = ema_decay * row_ema + (1.0 - ema_decay) * new_rows
    mixed_rows = mix_share * new_rows + (1.0 - mix_share) * row_zero
    return (new_rows, new_first, new_second, ema_rows, mixed_rows)


def finish_kernel(
    hyper,
    totals,
    clipped,
    row_params,
    row_zero,
    row_ema,
    row_first,
    row_second,
    grad,
    momentum,
    mats,
    zero,
    ema,
    new_rows,
    new_first,
    new_second,
    ema_rows,
    mixed_rows,
    bias_grad,
    new_momentum,
    new_mats,
    new_ema,
    new_mixed,
    grad_v,
    m_v,
    mats_v,
    zero_v,
    ema_v,
    x_v,
    short_v,
    low_v,
    in_sem,
    out_sem,
):
    layers, count, width = grad.shape
    pairs = [(grad, grad_v), (momentum, m_v)]
    pairs += [(mats, mats_v), (zero, zero_v), (ema, ema_v)]
    loads = [pltpu.make_async_copy(a, b, in_sem.at[i]) for i, (a, b) in enumerate(pairs)]
    for load in loads:
        load.start()
    rows = row_params.shape[1]
    row_grad = clipped[:, pl.ds(0, rows)]
    news = adam(row_grad, *(ref[...] for ref in (row_params, row_zero, row_ema, row_first, row_second)))
    for target, value in zip((new_rows, new_first, new_second, ema_rows, mixed_rows), news):
        target[...] = value
    lane = lax.broadcasted_iota(jnp.int32, clipped.shape, 1)
    spot = lax.broadcasted_iota(jnp.int32, bias_grad.shape, 1)
    bias = jnp.zeros(bias_grad.shape, F32)
    for layer in range(layers):
        index = PIX + EMB + SEQ + 4 + 12 * layer + 7
        column = jnp.sum(jnp.where(lane == index, clipped[...], 0.0), -1, keepdims=True)
        bias = jnp.where(spot == layer, column, bias)
    bias_grad[...] = bias
    part = count // 2
    factor = totals[pl.ds(0, 1), pl.ds(3, 1)]
    loads[0].wait()
    loads[1].wait()
    stores = []
    for layer in range(layers):
        total = jnp.zeros((1, 1), F32)
        for third in range(2):
            rows = pl.ds(third * part, part)
            value = momentum_decay * m_v[layer, rows, :] + factor * grad_v[layer, rows, :].astype(F32)
            m_v[layer, rows, :] = value
            total += jnp.sum(value * value, keepdims=True)
        store = pltpu.make_async_copy(m_v.at[layer], new_momentum.at[layer], out_sem.at[layer])
        store.start()
        stores.append(store)
        inverse = 1.0 / (jnp.sqrt(total) + 1e-07)
        for third in range(2):
            rows = pl.ds(third * part, part)
            value = m_v[layer, rows, :] * inverse
            x_v[layer, rows, :] = value
            short_v[0, layer, rows, :] = value.astype(BF)

    row_id = lax.broadcasted_iota(jnp.int32, (part, count), 0)
    col_id = lax.broadcasted_iota(jnp.int32, (part, count), 1)

    def step(turn, shift, use):
        now = lax.rem(turn, 2)
        linear = coeff_cubic + 2.0 * shift * coeff_quintic
        stay = coeff_linear + shift * (coeff_cubic + shift * coeff_quintic)
        for layer in range(layers):
            for third in range(2):
                rows = pl.ds(third * part, part)
                gram = matmul_nt(short_v[now, layer, rows, :], short_v[now, layer])
                gram -= jnp.where(row_id + third * part == col_id, shift, 0.0)
                low_v[layer, rows, :] = gram.astype(BF)
        for layer in range(layers):
            for third in range(2):
                rows = pl.ds(third * part, part)
                low = low_v[layer, rows, :]
                poly = linear * low.astype(F32) + coeff_quintic * matmul(low, low_v[layer])
                value = stay * x_v[layer, rows, :] + matmul(poly.astype(BF), short_v[now, layer])
                use(layer, third, rows, value)

    @pl.loop(0, NS_STEPS - 1)
    def _(turn):
        def keep(layer, third, rows, value):
            x_v[layer, rows, :] = value
            short_v[1 - lax.rem(turn, 2), layer, rows, :] = value.astype(BF)

        step(turn, jnp.where(turn >= NS_STEPS - 2, 1.0, 0.0), keep)

    for load in loads[2:]:
        load.wait()

    def update(layer, third, rows, orth):
        old = mats_v[layer, rows, :]
        value = old - muon_rate * (hyper * orth + weight_decay * old)
        mats_v[layer, rows, :] = value
        ema_v[layer, rows, :] = ema_decay * ema_v[layer, rows, :] + (1.0 - ema_decay) * value
        zero_v[layer, rows, :] = mix_share * value + (1.0 - mix_share) * zero_v[layer, rows, :]
        for turn, (source, target) in enumerate(
            ((mats_v, new_mats), (ema_v, new_ema), (zero_v, new_mixed))
        ):
            sem = out_sem.at[layers + (layer * 3 + third) * 3 + turn]
            store = pltpu.make_async_copy(source.at[layer, rows], target.at[layer, rows], sem)
            store.start()
            stores.append(store)

    step(NS_STEPS - 1, 1.0, update)
    for store in stores:
        store.wait()


def finish(totals, clipped, tables, grad, momentum, mats, zero, ema):
    layers, count, width = grad.shape
    full = jax.ShapeDtypeStruct(mats.shape, F32)
    table = jax.ShapeDtypeStruct(tables[0].shape, F32)
    any_space = pl.BlockSpec(memory_space=pl.ANY)
    vmem = pl.BlockSpec(memory_space=pltpu.VMEM)
    return pl.pallas_call(
        functools.partial(finish_kernel, 0.2 * math.sqrt(width)),
        out_shape=(table,) * 5
        + (jax.ShapeDtypeStruct((clipped.shape[0], 128), F32), full, full, full, full),
        in_specs=[vmem] * (2 + len(tables)) + [any_space] * 5,
        out_specs=[vmem] * 6 + [any_space] * 4,
        scratch_shapes=[
            pltpu.VMEM(grad.shape, BF),
            pltpu.VMEM(mats.shape, F32),
            pltpu.VMEM(mats.shape, F32),
            pltpu.VMEM(mats.shape, F32),
            pltpu.VMEM(mats.shape, F32),
            pltpu.VMEM(mats.shape, F32),
            pltpu.VMEM((2,) + mats.shape, BF),
            pltpu.VMEM((layers, count, count), BF),
            pltpu.SemaphoreType.DMA((5,)),
            pltpu.SemaphoreType.DMA((layers * 10,)),
        ],
        name="orthogonalize",
        compiler_params=pltpu.CompilerParams(vmem_limit_bytes=56 * 1024 * 1024),
    )(totals, clipped, *tables, grad, momentum, mats, zero, ema)


def gather_layer(shard):
    return lax.all_gather(shard.astype(jnp.bfloat16), "fsdp", axis=0, tiled=True)


def layer_forward(resid, weight_tensors, vector, valid_mask):
    images, seq = valid_mask.shape
    width = resid.shape[1]
    ffn = 4 * width
    normed = norm_forward(resid, vector[0], vector[1]).astype(jnp.bfloat16)
    bias = jnp.concatenate([vector[2], jnp.zeros_like(vector[2]), vector[3]])
    project = (matmul_nt(normed, weight_tensors[: 3 * width]) + bias).astype(jnp.bfloat16)
    parts = project.reshape(images, seq, 3, HEADS, HDIM)
    scores = attention_scores(parts, valid_mask)
    top_score = jnp.max(scores, -1, keepdims=True)
    expo = jnp.exp(scores - top_score)
    totals = jnp.sum(expo, -1, keepdims=True)
    log_total = top_score + jnp.log(totals)
    probs = (expo / totals).astype(jnp.bfloat16)
    context = jnp.einsum(
        "ihqk,ikhd->iqhd", probs, parts[:, :, 2], preferred_element_type=jnp.float32
    )
    context = context.reshape(images * seq, width).astype(jnp.bfloat16)
    mixed = resid + (matmul_nt(context, weight_tensors[3 * width : 4 * width]) + vector[4])
    normed_two = norm_forward(mixed, vector[5], vector[6]).astype(jnp.bfloat16)
    hidden_pre = matmul_nt(normed_two, weight_tensors[4 * width : 4 * width + ffn]) + vector[
        8:12
    ].reshape(ffn)
    hidden = (hidden_pre * jax.nn.sigmoid(1.702 * hidden_pre)).astype(jnp.bfloat16)
    output = mixed + (matmul(hidden, weight_tensors[4 * width + ffn :]) + vector[7])
    return (
        output,
        (resid, normed, project, log_total, context, mixed, normed_two, hidden_pre, hidden),
    )


def layer_backward(upstream, weight_tensors, vector, valid_mask, saved_activation):
    resid, normed, project, log_total, context, mixed, normed_two, hidden_pre, hidden = (
        saved_activation
    )
    images, seq = valid_mask.shape
    width = resid.shape[1]
    ffn = 4 * width
    out_grad = upstream.astype(jnp.bfloat16)
    grad_down = matmul_tn(hidden, out_grad)
    hidden_grad = matmul_nt(out_grad, weight_tensors[4 * width + ffn :])
    gate = jax.nn.sigmoid(1.702 * hidden_pre)
    pre_grad = (hidden_grad * (gate + 1.702 * hidden_pre * gate * (1.0 - gate))).astype(
        jnp.bfloat16
    )
    grad_up = matmul_tn(pre_grad, normed_two)
    second_in, gain_two, shift_two = norm_backward(
        mixed, vector[5], matmul(pre_grad, weight_tensors[4 * width : 4 * width + ffn])
    )
    mixed_grad = upstream + second_in
    attn_grad = mixed_grad.astype(jnp.bfloat16)
    grad_out = matmul_tn(attn_grad, context)
    context_grad = matmul(attn_grad, weight_tensors[3 * width : 4 * width]).astype(jnp.bfloat16)
    context_grad = context_grad.reshape(images, seq, HEADS, HDIM)
    parts = project.reshape(images, seq, 3, HEADS, HDIM)
    probs = jnp.exp(attention_scores(parts, valid_mask) - log_total)
    prob_grad = jnp.einsum(
        "iqhd,ikhd->ihqk", context_grad, parts[:, :, 2], preferred_element_type=jnp.float32
    )
    value_grad = jnp.einsum(
        "ihqk,iqhd->ikhd",
        probs.astype(jnp.bfloat16),
        context_grad,
        preferred_element_type=jnp.float32,
    )
    score_grad = (probs * (prob_grad - jnp.sum(prob_grad * probs, -1, keepdims=True))).astype(
        jnp.bfloat16
    )
    query_grad = jnp.einsum(
        "ihqk,ikhd->iqhd", score_grad, parts[:, :, 1], preferred_element_type=jnp.float32
    ) * HDIM ** (-0.5)
    key_grad = jnp.einsum(
        "ihqk,iqhd->ikhd", score_grad, parts[:, :, 0], preferred_element_type=jnp.float32
    ) * HDIM ** (-0.5)
    project_grad = (
        jnp.stack([query_grad, key_grad, value_grad], 2)
        .reshape(images * seq, 3 * width)
        .astype(jnp.bfloat16)
    )
    project_sum = jnp.sum(project_grad.astype(jnp.float32), 0)
    grad_qkv = matmul_tn(project_grad, normed)
    first_in, gain_one, shift_one = norm_backward(
        resid, vector[0], matmul(project_grad, weight_tensors[: 3 * width])
    )
    residual_gradient = mixed_grad + first_in
    grad_matrix = [part.astype(BF) for part in (grad_qkv, grad_out, grad_up, grad_down)]
    grad_vector = jnp.concatenate(
        [
            jnp.stack(
                [
                    gain_one,
                    shift_one,
                    project_sum[:width],
                    project_sum[2 * width :],
                    jnp.sum(attn_grad.astype(jnp.float32), 0),
                    gain_two,
                    shift_two,
                    jnp.sum(out_grad.astype(jnp.float32), 0),
                ]
            ),
            jnp.sum(pre_grad.astype(jnp.float32), 0).reshape(4, width),
        ],
        0,
    )
    return (residual_gradient, grad_matrix, grad_vector)


def newton_schulz(blocks):
    frob = jnp.sqrt(jnp.sum(blocks * blocks, axis=(1, 2), keepdims=True)) + 1e-07
    blocks = blocks / frob
    unit = jnp.eye(blocks.shape[1], dtype=jnp.float32)
    for turn in range(NS_STEPS):
        shift = 1.0 if turn >= NS_STEPS - 2 else 0.0
        short = blocks.astype(BF)
        gram = jnp.einsum("lcd,led->lce", short, short, preferred_element_type=F32) - shift * unit
        low = gram.astype(BF)
        square = jnp.einsum("lce,lef->lcf", low, low, preferred_element_type=F32)
        poly = (coeff_cubic + 2.0 * shift * coeff_quintic) * gram + coeff_quintic * square
        stay = coeff_linear + shift * (coeff_cubic + shift * coeff_quintic)
        blocks = stay * blocks + jnp.einsum(
            "lce,led->lcd", poly.astype(BF), short, preferred_element_type=F32
        )
    return blocks


def row_updates(clipped, layers, *tables):
    front = PIX + EMB + SEQ + 4
    down_bias_grad = clipped[front:].reshape(layers, 12, clipped.shape[1])[:, 7]
    return adam(clipped, *tables) + (down_bias_grad,)


def plain_body(
    patches,
    pad_mask,
    labels,
    loss_weights,
    class_emb,
    layer_mats,
    layer_zero,
    layer_ema,
    layer_momentum,
    row_params,
    row_zero,
    row_ema,
    row_first,
    row_second,
):
    layers, columns, width = layer_mats.shape
    images, seq, pixels = patches.shape
    front = PIX + EMB + SEQ + 4
    valid_mask = pad_mask.astype(jnp.float32)
    gathered_rows = lax.all_gather(row_params.astype(jnp.bfloat16), "fsdp", axis=1, tiled=True)
    rows_value = gathered_rows.astype(jnp.float32)
    patch_weight = gathered_rows[:PIX]
    proj_rows = gathered_rows[PIX : PIX + EMB]
    position = rows_value[PIX + EMB : PIX + EMB + SEQ]
    head_vec = rows_value[PIX + EMB + SEQ : front]
    layer_vector_params = rows_value[front:].reshape(layers, 12, width)
    flat_patches = patches.reshape(images * seq, pixels)
    embedded = (matmul(flat_patches, patch_weight).reshape(images, seq, width) + position).reshape(
        images * seq, width
    )
    resid = norm_forward(embedded, head_vec[0], head_vec[1])
    kept_weights = []
    saved_activations = []
    for layer_number in range(layers):
        weight_tensors = gather_layer(layer_mats[layer_number])
        kept_weights.append(weight_tensors)
        resid, saved_activation = layer_forward(
            resid, weight_tensors, layer_vector_params[layer_number], valid_mask
        )
        saved_activations.append(saved_activation)
    counts = jnp.sum(valid_mask, -1, keepdims=True)
    pooled = jnp.sum(resid.reshape(images, seq, width) * valid_mask[..., None], 1) / counts
    pooled_norm = norm_forward(pooled, head_vec[2], head_vec[3]).astype(jnp.bfloat16)
    feature = matmul_nt(pooled_norm, proj_rows)
    inv_length = lax.rsqrt(jnp.sum(feature * feature, -1, keepdims=True) + unit_epsilon)
    unit_feat = (feature * inv_length).astype(jnp.bfloat16)
    classes = class_emb.astype(jnp.float32)
    class_unit = (
        classes * lax.rsqrt(jnp.sum(classes * classes, -1, keepdims=True) + unit_epsilon)
    ).astype(jnp.bfloat16)
    logits = logit_scale * matmul_nt(unit_feat, class_unit)
    top_logit = jnp.max(logits, -1, keepdims=True)
    shifted = jnp.exp(logits - top_logit)
    total_exp = jnp.sum(shifted, -1, keepdims=True)
    log_norm = top_logit + jnp.log(total_exp)
    onehot = (jnp.arange(logits.shape[1])[None, :] == labels[:, None]).astype(jnp.float32)
    losses = log_norm[:, 0] - jnp.sum(onehot * logits, -1)
    weights_value = loss_weights.astype(jnp.float32)
    loss_sum, weight_sum = lax.psum(
        (jnp.sum(weights_value * losses), jnp.sum(weights_value)), ("fsdp", "ns")
    )
    seed = weights_value / weight_sum
    logit_grad = seed[:, None] * (shifted / total_exp - onehot)
    unit_grad = logit_scale * jnp.dot(logit_grad, class_unit.astype(jnp.float32), precision=HIGHEST)
    feat_grad = inv_length * unit_grad - feature * inv_length**3 * jnp.sum(
        unit_grad * feature, -1, keepdims=True
    )
    grad_proj = jnp.dot(feat_grad.T, pooled_norm.astype(jnp.float32), precision=HIGHEST)
    pooled_grad, gain_post, shift_post = norm_backward(
        pooled, head_vec[2], jnp.dot(feat_grad, proj_rows.astype(jnp.float32), precision=HIGHEST)
    )
    residual_gradient = (valid_mask[..., None] * (pooled_grad / counts)[:, None, :]).reshape(
        images * seq, width
    )
    grad_mats = [None] * layers
    grad_vecs = [None] * layers
    for layer_number in reversed(range(layers)):
        weight_tensors = kept_weights[layer_number]
        residual_gradient, grad_matrix, grad_vector = layer_backward(
            residual_gradient,
            weight_tensors,
            layer_vector_params[layer_number],
            valid_mask,
            saved_activations[layer_number],
        )
        grad_mats[layer_number], grad_vecs[layer_number] = (
            lax.psum_scatter(
                jnp.concatenate(grad_matrix, 0), "fsdp", scatter_dimension=0, tiled=True
            ),
            lax.psum_scatter(grad_vector, "fsdp", scatter_dimension=1, tiled=True),
        )
    embed_grad, gain_pre, shift_pre = norm_backward(embedded, head_vec[0], residual_gradient)
    position_grad = jnp.sum(embed_grad.reshape(images, seq, width), 0)
    patch_grad = matmul_tn(flat_patches, embed_grad.astype(jnp.bfloat16))
    front_grad = jnp.concatenate(
        [
            patch_grad,
            grad_proj,
            position_grad,
            jnp.stack([gain_pre, shift_pre, gain_post, shift_post]),
        ],
        0,
    )
    front_shard = lax.psum_scatter(front_grad, "fsdp", scatter_dimension=1, tiled=True)
    mat_grad = jnp.stack(grad_mats)
    row_grad = jnp.concatenate([front_shard] + grad_vecs, 0)
    pairs = lax.axis_size("ns")
    side = lax.axis_index("ns")
    half_depth = width // pairs
    half_rows = row_grad.shape[0] // pairs
    mat_total, row_total = (
        lax.psum(mat_grad.astype(jnp.bfloat16), "ns").astype(jnp.float32),
        lax.psum(row_grad.astype(jnp.bfloat16), "ns").astype(jnp.float32),
    )
    mat_half = lax.dynamic_slice_in_dim(mat_total, side * half_depth, half_depth, 2)
    row_half = lax.dynamic_slice_in_dim(row_total, side * half_rows, half_rows, 0)
    squares = jnp.sum(mat_half * mat_half) + jnp.sum(row_half * row_half)
    grad_norm = jnp.sqrt(lax.psum(squares, ("fsdp", "ns")))
    clip = jnp.minimum(1.0, clip_bound / (grad_norm + 1e-06))
    momentum = momentum_decay * layer_momentum + clip * mat_total
    orth = newton_schulz(momentum)
    new_mats = layer_mats - muon_rate * (0.2 * math.sqrt(width) * orth + weight_decay * layer_mats)
    ema_mats = ema_decay * layer_ema + (1.0 - ema_decay) * new_mats
    mixed_mats = mix_share * new_mats + (1.0 - mix_share) * layer_zero
    return (loss_sum, weight_sum, grad_norm, new_mats, momentum, ema_mats, mixed_mats) + row_updates(
        clip * row_total, layers, row_params, row_zero, row_ema, row_first, row_second
    )


def fast_body(
    patches,
    pad_mask,
    labels,
    loss_weights,
    class_emb,
    layer_mats,
    layer_zero,
    layer_ema,
    layer_momentum,
    row_params,
    row_zero,
    row_ema,
    row_first,
    row_second,
):
    layers, columns, width = layer_mats.shape
    shards = lax.axis_size("fsdp")
    depth = shards // PLANE
    weights, *saved, embedded, vectors, pooled_row, z_rows, feature_rows, start, stats = forward(
        depth,
        row_params.T,
        layer_mats,
        patches[0],
        pad_mask,
        class_emb,
        labels[:, None],
        loss_weights.astype(F32)[:, None],
    )
    mat_total, clipped, totals = backward(
        depth,
        lax.axis_size("ns"),
        weights,
        saved,
        embedded,
        patches[0],
        vectors,
        pad_mask,
        (pooled_row, z_rows, feature_rows),
        start,
        stats,
    )
    loss_sum, weight_sum, grad_norm = (totals[0, turn] for turn in range(3))
    tables = [table.T for table in (row_params, row_zero, row_ema, row_first, row_second)]
    *news, bias, momentum, new_mats, ema_mats, mixed_mats = finish(
        totals, clipped, tables, mat_total, layer_momentum, layer_mats, layer_zero, layer_ema
    )
    news = [table.T for table in news] + [bias[:, :layers].T]
    return (loss_sum, weight_sum, grad_norm, new_mats, momentum, ema_mats, mixed_mats, *news)


def body(*args):
    count, share = args[5].shape[1], args[9].shape[1]
    planes = lax.axis_size("fsdp") == 4 * PLANE and lax.axis_size("ns") == 2
    if planes and count % 192 == 0 and share % 48 == 0 and args[0].shape[0] == 1:
        return fast_body(*args)
    return plain_body(*args)


def solution(mesh):
    in_specs = (
        P(("fsdp", "ns"), None, None),
        P(("fsdp", "ns"), None),
        P(("fsdp", "ns")),
        P(("fsdp", "ns")),
        P(),
        P(None, "fsdp", None),
        P(None, "fsdp", None),
        P(None, "fsdp", None),
        P(None, "fsdp", None),
        P(None, "fsdp"),
        P(None, "fsdp"),
        P(None, "fsdp"),
        P(None, "fsdp"),
        P(None, "fsdp"),
    )
    out_specs = (
        P(),
        P(),
        P(),
        P(None, "fsdp", None),
        P(None, "fsdp", None),
        P(None, "fsdp", None),
        P(None, "fsdp", None),
        P(None, "fsdp"),
        P(None, "fsdp"),
        P(None, "fsdp"),
        P(None, "fsdp"),
        P(None, "fsdp"),
        P(None, "fsdp"),
    )
    return jax.shard_map(body, mesh=mesh, in_specs=in_specs, out_specs=out_specs, check_vma=False)
```
